32 devices in a mesh: wide: 8 (over y, x, core), narrow: 4 (over z).
Axes of the slice: x: 2, y: 2, z: 4, core: 2. Of those that a mesh axis runs over, the one named last changes fastest.
Arguments:
- layer_input: bfloat16 [16384, 1024], P(('wide', 'narrow')), may hold values from -6 to 6
- out_grad: bfloat16 [16384, 1024], P(('wide', 'narrow')), may hold values from -6 to 6
- norm_attn_gain: bfloat16 [1024], replicated, may hold values from 0.5 to 1.5
- w_query: bfloat16 [1024, 1024], P(None, 'narrow'), may hold values from -0.0234375 to 0.0234375
- w_key: bfloat16 [1024, 1024], P(None, 'narrow'), may hold values from -0.1875 to 0.1875
- w_value: bfloat16 [1024, 1024], P(None, 'narrow'), may hold values from -0.1875 to 0.1875
- w_out: bfloat16 [1024, 1024], P('narrow'), may hold values from -1 to 1
- rel_table: bfloat16 [32, 16], P(None, 'narrow'), may hold values from -4 to 4
- layout_table: bfloat16 [64, 16], P(None, 'narrow'), may hold values from -4 to 4
- norm_ffn_gain: bfloat16 [1024], replicated, may hold values from 0.5 to 1.5
- w_gate: bfloat16 [1024, 2816], P(None, 'narrow'), may hold values from -0.1875 to 0.1875
- w_up: bfloat16 [1024, 2816], P(None, 'narrow'), may hold values from -0.1875 to 0.1875
- down_projection_weight: bfloat16 [2816, 1024], P('narrow'), may hold values from -0.109375 to 0.109375
- page_lengths: int32 [8, 4], P('wide'), may hold values from 1 to 1024, 2048 in all within a row
- key_mask: int32 [16384], P('wide'), may hold values 0 or 1
- rel_bucket: int32 [16384, 2048], P('wide'), may hold values from 0 to 31
- layout_bucket: int32 [16384, 2048], P('wide'), may hold values from 0 to 63
Outputs:
- layer_out: bfloat16 [16384, 1024], P(('wide', 'narrow'))
- in_grad: float32 [16384, 1024], P(('wide', 'narrow'))
- grad_norm_attn: float32 [1024], P(('wide', 'narrow'))
- grad_query: float32 [1024, 1024], P('wide', 'narrow')
- grad_key: float32 [1024, 1024], P('wide', 'narrow')
- grad_value: float32 [1024, 1024], P('wide', 'narrow')
- grad_out_proj: float32 [1024, 1024], P('narrow', 'wide')
- grad_rel_table: float32 [32, 16], P('wide', 'narrow')
- grad_layout_table: float32 [64, 16], P('wide', 'narrow')
- grad_norm_ffn: float32 [1024], P(('wide', 'narrow'))
- grad_gate: float32 [1024, 2816], P('wide', 'narrow')
- grad_up: float32 [1024, 2816], P('wide', 'narrow')
- grad_down: float32 [2816, 1024], P('narrow', 'wide')
The draws below stay inside these ranges and needn't reach their ends.
Inputs may be any that keep to these rules, and one draw needn't show every extreme that they name: `page_lengths`: each row sums to 2048; the pages fill the block of tokens of that index of wide in order, and one of them has exactly 1024 tokens.
All inputs are finite; a program needn't handle non-finite values. No bound on the sum of `key_mask` on one device may be relied on, other than what follows from the above.
Results may differ from the reference program's by a relative error of at most 0.015.
Values may be sent and summed in bfloat16 or wider, within the bound.
No kernel may reach another device: no remote copies, remote signals or barrier semaphores. Data moves between devices by JAX's collectives and lax.ppermute only.
A program may use at most 320 MiB of HBM per device.

```python
import math
import jax
import jax.numpy as jnp
import numpy as np
from jax import lax

D = 1024
H = 16
DH = 64
FF = 2816
NB_REL = 32
NB_LAY = 64
TOK_DEV = 2048
PAGE_MOST = 1024
PAGES_DEV = 4
TOKENS = 16384
N_WIDE = 8


def touch_ends(entries, rng, smallest, largest):
    longest = entries.shape.index(max(entries.shape))
    spots = []
    for shift in (0, 1):
        where = [jax.random.randint(jax.random.fold_in(rng, axis), (), 0, length) for axis, length in enumerate(entries.shape)]
        where[longest] = (where[longest] + shift) % entries.shape[longest]
        spots.append(tuple(where))
    return entries.at[spots[0]].set(smallest).at[spots[1]].set(largest)


def shard_levels(rng, extent, shards, least, largest):
    factor_of, own = 1.0, jax.random.fold_in(rng, 6)
    for dim, parts in shards:
        steps = jnp.exp(jax.random.uniform(jax.random.fold_in(own, dim), (parts,), jnp.float32, least / len(shards), largest / len(shards)))
        factor_of = factor_of * jnp.repeat(steps, extent[dim] // parts).reshape([-1 if axis == dim else 1 for axis in range(len(extent))])
    return factor_of


def split_up(amount, total, most, slope):
    weights = [(1 << 20) // math.isqrt(grade ** slope) + 1 for grade in range(2, amount + 1)]
    spare, counts = total - most - (amount - 1), [1] * (amount - 1)
    while spare > 0:
        movable = [i for i in range(amount - 1) if counts[i] < most]
        whole, left = sum([weights[i] for i in movable]), spare
        for i in movable:
            addition = min(most - counts[i], max(1, left * weights[i] // whole), spare)
            counts[i] = counts[i] + addition
            spare = spare - addition
    return np.array([most] + counts)


def ragged(key, count, total, most, slope):
    if count == 2:
        one = jax.random.randint(key, (), max(1, total - most), min(most, total - 1) + 1)
        return jnp.stack([one, total - one])
    tallies = jnp.asarray(split_up(count, total, most, slope), jnp.int32)
    twos = (count - 1) // 2
    giver, taker = tallies[1:1 + 2 * twos:2], tallies[2:2 + 2 * twos:2]
    margin = jnp.minimum(giver - 1, most - taker)
    moved = jax.random.randint(jax.random.fold_in(key, 1), (twos,), 0, 1 << 20) % (margin + 1)
    tallies = tallies.at[1:1 + 2 * twos:2].set(giver - moved).at[2:2 + 2 * twos:2].set(taker + moved)
    return tallies[jax.random.permutation(jax.random.fold_in(key, 2), count)]


def centred(own_key, dims, scale, bound, cuts=(), held_as=jnp.bfloat16):
    values = jax.random.normal(own_key, dims, jnp.float32) * scale
    if len(cuts) > 0:
        values = shard_levels(own_key, dims, cuts, -0.22, 0.18) * values
    return jnp.clip(values, min=-bound, max=bound).astype(held_as)


def setup_inputs(seed: int = 0) -> dict:
    key_list = jax.random.split(jax.random.key(seed), 18)
    layer_input = centred(key_list[0], (TOKENS, D), 1.0, 6.0, ((0, 32),))
    out_grad = centred(key_list[1], (TOKENS, D), 1.0, 6.0, ((0, 32),))
    norm_attn_gain = jnp.clip(1.0 + 0.1 * jax.random.normal(key_list[2], (D,), jnp.float32), 0.5, 1.5).astype(jnp.bfloat16)
    w_query = centred(key_list[3], (D, H * DH), (D * DH) ** -0.5, 0.0234375, ((1, 4),))
    w_key = centred(key_list[4], (D, H * DH), D ** -0.5, 0.1875, ((1, 4),))
    w_value = centred(key_list[5], (D, H * DH), D ** -0.5, 0.1875, ((1, 4),))
    w_out = centred(key_list[6], (H * DH, D), (H * DH // 32) ** -0.5, 1.0, ((0, 4),))
    rel_table = centred(key_list[7], (NB_REL, H), 0.7, 4.0, ((1, 4),))
    layout_table = centred(key_list[8], (NB_LAY, H), 0.7, 4.0, ((1, 4),))
    norm_ffn_gain = jnp.clip(1.0 + 0.1 * jax.random.normal(key_list[9], (D,), jnp.float32), 0.5, 1.5).astype(jnp.bfloat16)
    w_gate = centred(key_list[10], (D, FF), D ** -0.5, 0.1875, ((1, 4),))
    w_up = centred(key_list[11], (D, FF), D ** -0.5, 0.1875, ((1, 4),))
    down_projection_weight = centred(key_list[12], (FF, D), FF ** -0.5, 0.109375, ((0, 4),))
    page_lengths = jax.vmap(lambda own: ragged(own, PAGES_DEV, TOK_DEV, PAGE_MOST, 2))(jax.random.split(key_list[13], N_WIDE)).reshape((N_WIDE, PAGES_DEV)).astype(jnp.int32)
    key_mask = touch_ends((jax.random.randint(key_list[14], (TOKENS,), 0, 8) < 7).astype(jnp.int32), jax.random.fold_in(key_list[14], 1), 0, 1)
    rel_bucket = touch_ends(jax.random.randint(key_list[15], (TOKENS, TOK_DEV), 0, NB_REL), jax.random.fold_in(key_list[15], 1), 0, NB_REL - 1).astype(jnp.int32)
    layout_bucket = touch_ends(jax.random.randint(key_list[16], (TOKENS, TOK_DEV), 0, NB_LAY), jax.random.fold_in(key_list[16], 1), 0, NB_LAY - 1).astype(jnp.int32)
    return dict(layer_input=layer_input, out_grad=out_grad, norm_attn_gain=norm_attn_gain, w_query=w_query, w_key=w_key, w_value=w_value, w_out=w_out, rel_table=rel_table, layout_table=layout_table, norm_ffn_gain=norm_ffn_gain, w_gate=w_gate, w_up=w_up, down_projection_weight=down_projection_weight, page_lengths=page_lengths, key_mask=key_mask, rel_bucket=rel_bucket, layout_bucket=layout_bucket)


epsilon = 1e-06
masked_score = -1e+30
highest = lax.Precision.HIGHEST

@jax.custom_vjp
def low(v):
    return lax.optimization_barrier(v.astype(jnp.bfloat16)).astype(jnp.float32)

@jax.custom_vjp
def low_back(v):
    return v

def low_keep(v):
    return (low(v), None)

def low_pass(kept, grad):
    return (grad,)

def back_keep(v):
    return (v, None)

def back_low(kept, grad):
    return (low(grad),)
low.defvjp(low_keep, low_pass)
low_back.defvjp(back_keep, back_low)

def product(left, right):
    return jnp.dot(left, right, precision=highest, preferred_element_type=jnp.float32)

def rms_norm(rows, gain):
    scale = lax.rsqrt(lax.optimization_barrier(jnp.mean(rows * rows, axis=-1, keepdims=True)) + epsilon)
    return rows * scale * gain

def gated(gate, upward):
    return jax.nn.gelu(gate, approximate=True) * upward

def one_block(pieces, relative_heads, layout_heads):
    query_block, keys_block, values_block, allow_block, relative_bucket_index, layout_ids = pieces
    query_heads = query_block.reshape(TOK_DEV, H, DH)
    key_heads_split = keys_block.reshape(TOK_DEV, H, DH)
    values_heads = values_block.reshape(TOK_DEV, H, DH)
    raw = low_back(jnp.einsum('qhd,khd->hqk', query_heads, key_heads_split, precision=highest))
    biased = raw + relative_heads[:, relative_bucket_index] + layout_heads[:, layout_ids]
    scores = jnp.where(allow_block[None], biased, masked_score)
    top = lax.optimization_barrier(jnp.max(scores, axis=-1, keepdims=True))
    exponent = jnp.exp(scores - top)
    probs = low(exponent / lax.optimization_barrier(jnp.sum(exponent, axis=-1, keepdims=True)))
    mixed = jnp.einsum('hqk,khd->qhd', probs, values_heads, precision=highest)
    return mixed.reshape(TOK_DEV, H * DH)

def reference(layer_input, out_grad, norm_attn_gain, w_query, w_key, w_value, w_out, rel_table, layout_table, norm_ffn_gain, w_gate, w_up, down_projection_weight, page_lengths, key_mask, rel_bucket, layout_bucket):
    ends = jnp.cumsum(page_lengths, axis=1, dtype=jnp.int32)
    position = jnp.arange(TOK_DEV, dtype=jnp.int32)
    page_of = lax.optimization_barrier(jnp.sum((position[None, :, None] >= ends[:, None, :]).astype(jnp.int32), axis=2, dtype=jnp.int32))
    visible_key = key_mask.reshape(N_WIDE, TOK_DEV) == 1
    diagonal_band = position[:, None] == position[None, :]
    allowed = (page_of[:, :, None] == page_of[:, None, :]) & (visible_key[:, None, :] | diagonal_band[None])
    relative_bucket_index = rel_bucket.reshape(N_WIDE, TOK_DEV, TOK_DEV)
    layout_ids = layout_bucket.reshape(N_WIDE, TOK_DEV, TOK_DEV)
    checked = jax.checkpoint(one_block)

    def forward(resid, gain_attn, query_matrix, key_weight, value_weight, out_weight, relative_weight, layout_weight, gain_ffn, gate_weight, up_weight, down_weight):
        normed_attn = low(rms_norm(resid, gain_attn))
        query = low_back(low(product(normed_attn, query_matrix)))
        keys = low_back(low(product(normed_attn, key_weight)))
        values = low_back(low(product(normed_attn, value_weight)))
        relative_heads = relative_weight.T
        layout_heads = layout_weight.T
        blocks = (query.reshape(N_WIDE, TOK_DEV, H * DH), keys.reshape(N_WIDE, TOK_DEV, H * DH), values.reshape(N_WIDE, TOK_DEV, H * DH), allowed, relative_bucket_index, layout_ids)
        mixed = lax.map(lambda pieces: checked(pieces, relative_heads, layout_heads), blocks)
        attended = low_back(low(mixed.reshape(TOKENS, H * DH)))
        middle = resid + low_back(product(attended, out_weight))
        normed_ffn = low(rms_norm(middle, gain_ffn))
        gate = low_back(product(normed_ffn, gate_weight))
        upward = low_back(product(normed_ffn, up_weight))
        hidden = low(gated(gate, upward))
        return middle + low_back(product(hidden, down_weight))
    arrays = (layer_input, norm_attn_gain, w_query, w_key, w_value, w_out, rel_table, layout_table, norm_ffn_gain, w_gate, w_up, down_projection_weight)
    floats = [array.astype(jnp.float32) for array in arrays]
    block_out, pullback = jax.vjp(forward, *floats)
    grads = pullback(out_grad.astype(jnp.float32))
    return (block_out.astype(jnp.bfloat16), grads[0], grads[1], grads[2], grads[3], grads[4], grads[5], grads[6], grads[7], grads[8], grads[9], grads[10], grads[11])
```

```python
import functools
import jax
import jax.numpy as jnp
from jax import lax
from jax.experimental import pallas as pl
from jax.experimental.pallas import tpu as pltpu
from jax.sharding import PartitionSpec as P

DH = 64
BIAS_SCALE = 4096.0
LOG2E = 1.4426950408889634
f32 = jnp.float32
bf16 = jnp.bfloat16
NT = (((1,), (1,)), ((), ()))
NN = (((1,), (0,)), ((), ()))


def dot(a, b, dims=NN):
    return lax.dot_general(a, b, dims, preferred_element_type=f32)


def key_window(len_ref, first, last, count, width):
    ends = []
    total = 0
    for p in range(len_ref.shape[1]):
        total = total + len_ref[0, p]
        ends.append(total)
    start = 0
    stop = count
    for e in ends:
        start = jnp.where(e <= first, e, start)
    for e in reversed(ends):
        stop = jnp.where(e > last, e, stop)
    base = (start // 128) * 128
    steps = (stop - base + width - 1) // width
    base = jnp.minimum(base, count - steps * width)
    return ends, base, steps


def own_half(shape, head):
    lane = lax.broadcasted_iota(jnp.int32, shape, len(shape) - 1)
    return (lane < DH) if head % 2 == 0 else (lane >= DH)


def fill_values(vext, v_ref, heads):
    for h in range(heads):
        vp = v_ref[:, (h // 2) * 128:(h // 2 + 1) * 128]
        vext[h] = jnp.where(own_half(vp.shape, h), vp, jnp.ones_like(vp))


def forward_kernel(len_ref, q_ref, k_ref, v_ref, rel_ref, lay_ref, tab_ref, kmask_ref,
                   att_ref, rinv_ref, e_ref, code_ref,
                   s_scr, m_scr, vext, colcode, *, width, heads):
    tq, count = rel_ref.shape
    pairs = heads // 2
    i = pl.program_id(0)
    t0 = i * tq
    ends, base, steps = key_window(len_ref, t0, t0 + tq - 1, count, width)

    @pl.when(i == 0)
    def _():
        fill_values(vext, v_ref, heads)
        pos = lax.broadcasted_iota(jnp.int32, (8, count), 1)
        page = jnp.zeros((8, count), jnp.int32)
        for e in ends:
            page = page + (pos >= e).astype(jnp.int32)
        colcode[...] = jnp.where(kmask_ref[...] == 1, page, -1)

    rowpos = lax.broadcasted_iota(jnp.int32, (tq, 128), 0) + t0
    rowpage = jnp.zeros((tq, 128), jnp.int32)
    for e in ends:
        rowpage = rowpage + (rowpos >= e).astype(jnp.int32)
    lanes = lax.broadcasted_iota(jnp.int32, (tq, 128), 1)
    scaled = []
    for h in range(heads):
        qp = q_ref[:, (h // 2) * 128:(h // 2 + 1) * 128]
        scaled.append(jnp.where(own_half(qp.shape, h), qp * bf16(BIAS_SCALE), jnp.zeros_like(qp)))
        m_scr[h] = jnp.full((tq, 128), -3e38, f32)
    tabs = [[jnp.broadcast_to(tab_ref[2 * p + r:2 * p + r + 1, :], (tq, 128)) for r in range(2)]
            for p in range(pairs)]

    def scores(j, carry):
        c0 = pl.multiple_of(base + j * width, 128)
        raw = [dot(scaled[h], k_ref[pl.ds(c0, width), (h // 2) * 128:(h // 2 + 1) * 128], NT)
               for h in range(heads)]
        for half in range(width // 128):
            cc = pl.multiple_of(c0 + half * 128, 128)
            rel = rel_ref[:, pl.ds(cc, 128)]
            lay = lay_ref[:, pl.ds(cc, 128)]
            code_ref[:, pl.ds(cc, 128)] = (rel + lay * 32).astype(jnp.int16)
            col = jnp.broadcast_to(colcode[0:1, pl.ds(cc, 128)], (tq, 128))
            seen = (rowpage == col) | (rowpos == lanes + cc)
            hide = jnp.where(seen, f32(0.0), f32(-1e30))
            for p in range(pairs):
                word = (jnp.take_along_axis(tabs[p][0], rel, axis=1, mode="promise_in_bounds")
                        + jnp.take_along_axis(tabs[p][1], lay, axis=1, mode="promise_in_bounds"))
                parts = ((word & 0xFFFF).astype(f32), (word >> 16).astype(f32))
                for r in range(2):
                    h = 2 * p + r
                    s = raw[h][:, half * 128:(half + 1) * 128] + parts[r] + hide
                    s_scr[h, :, pl.ds(cc, 128)] = s
                    m_scr[h] = jnp.maximum(m_scr[h], s)
        return carry

    lax.fori_loop(0, steps, scores, 0)

    for p in range(pairs):
        accs = []
        for h in (2 * p, 2 * p + 1):
            top = jnp.max(m_scr[h], axis=1, keepdims=True)

            def values(j, acc):
                c0 = pl.multiple_of(base + j * width, 128)
                e = jnp.exp2((s_scr[h, :, pl.ds(c0, width)] - top) * f32(LOG2E / BIAS_SCALE)).astype(bf16)
                e_ref[h, :, pl.ds(c0, width)] = e
                return acc + dot(e, vext[h, pl.ds(c0, width), :])

            accs.append(lax.fori_loop(0, steps, values, jnp.zeros((tq, 128), f32)))
        low = own_half((tq, 128), 0)
        mixed = jnp.where(low, accs[0], accs[1])
        total = pltpu.roll(jnp.where(low, accs[1], accs[0]), DH, 1)
        rinv = 1.0 / total
        att_ref[:, p * 128:(p + 1) * 128] = (mixed * rinv).astype(bf16)
        rinv_ref[:, p * 128:(p + 1) * 128] = rinv


def attention_forward(page_lengths, proj, rel, lay, tab, kmask, tq=256, width=256):
    count = proj.shape[0]
    hc = proj.shape[1] // 3
    heads = hc // DH
    grid = (count // tq,)
    return pl.pallas_call(
        functools.partial(forward_kernel, width=width, heads=heads),
        grid=grid,
        in_specs=[
            pl.BlockSpec(memory_space=pltpu.SMEM),
            pl.BlockSpec((tq, hc), lambda i: (i, 0)),
            pl.BlockSpec((count, hc), lambda i: (0, 1)),
            pl.BlockSpec((count, hc), lambda i: (0, 2)),
            pl.BlockSpec((tq, count), lambda i: (i, 0)),
            pl.BlockSpec((tq, count), lambda i: (i, 0)),
            pl.BlockSpec(tab.shape, lambda i: (0, 0)),
            pl.BlockSpec((1, count), lambda i: (0, 0)),
        ],
        out_specs=[
            pl.BlockSpec((tq, hc), lambda i: (i, 0)),
            pl.BlockSpec((tq, hc), lambda i: (i, 0)),
            pl.BlockSpec((heads, tq, count), lambda i: (0, i, 0)),
            pl.BlockSpec((tq, count), lambda i: (i, 0)),
        ],
        out_shape=[
            jax.ShapeDtypeStruct((count, hc), bf16),
            jax.ShapeDtypeStruct((count, hc), f32),
            jax.ShapeDtypeStruct((heads, count, count), bf16),
            jax.ShapeDtypeStruct((count, count), jnp.int16),
        ],
        scratch_shapes=[
            pltpu.VMEM((heads, tq, count), f32),
            pltpu.VMEM((heads, tq, 128), f32),
            pltpu.VMEM((heads, count, 128), bf16),
            pltpu.VMEM((8, count), jnp.int32),
        ],
        compiler_params=pltpu.CompilerParams(vmem_limit_bytes=56 << 20),
        name="attention_forward",
    )(page_lengths, proj, proj, proj, rel, lay, tab, kmask.reshape(1, count))


def bias_words(rel_table, layout_table):
    def pack(table):
        whole = jnp.round(table.astype(f32) * BIAS_SCALE).astype(jnp.int32)
        low = jnp.clip(whole[:, 0::2] + 16384, 0, 32767)
        high = jnp.clip(whole[:, 1::2], -16384, 16383)
        words = (high * 65536 + low).T
        return jnp.pad(words, ((0, 0), (0, 128 - words.shape[1])))
    both = jnp.stack([pack(rel_table), pack(layout_table)], axis=1)
    return both.reshape(-1, 128)


def signs(code, shift, bits):
    return [jnp.where((code & jnp.int16(1 << (shift + b))) == 0, bf16(1.0), bf16(-1.0))
            for b in range(bits)]


def walsh(sign_list):
    out = [None]
    for s in sign_list:
        out = out + [s if o is None else o * s for o in out]
    return out


def backward_kernel(len_ref, q_ref, k_ref, v_ref, e_ref, code_ref, da_ref, att_ref, rinv_ref,
                    dq_ref, dk_ref, dv_ref, hl_ref, hr_ref,
                    vext, lhs_scr, dat_scr, qt_scr, ds_scr, dq_scr, dkt, dvt, left, blay, brel,
                    *, width, heads):
    tq, count = code_ref.shape
    pairs = heads // 2
    i = pl.program_id(0)
    t0 = i * tq
    ends, base, steps = key_window(len_ref, t0, t0 + tq - 1, count, width)

    @pl.when(i == 0)
    def _():
        fill_values(vext, v_ref, heads)
        dkt[...] = jnp.zeros_like(dkt)
        dvt[...] = jnp.zeros_like(dvt)
        hl_ref[...] = jnp.zeros_like(hl_ref)
        hr_ref[...] = jnp.zeros_like(hr_ref)

    low = own_half((tq, 128), 0)
    lane = lax.broadcasted_iota(jnp.int32, (tq, 128), 1)
    first_part = (lane & 32) == 0
    for p in range(pairs):
        cols = slice(p * 128, (p + 1) * 128)
        da = (da_ref[:, cols].astype(f32) * rinv_ref[:, cols]).astype(bf16)
        daf = da.astype(f32)
        prod = daf * att_ref[:, cols].astype(f32)
        for r in range(2):
            own = low if r == 0 else jnp.logical_not(low)
            delta = jnp.sum(jnp.where(own, prod, 0.0), axis=1, keepdims=True) * f32(-1.0 / 32)
            high = delta.astype(bf16).astype(f32)
            rest = delta - high
            lhs_scr[2 * p + r] = jnp.where(own, daf, jnp.where(first_part, high, rest)).astype(bf16)
        dat_scr[p] = daf.T.astype(bf16)
        qt_scr[p] = q_ref[:, cols].astype(f32).T.astype(bf16)
        dq_scr[p] = jnp.zeros((tq, 128), f32)

    def chunk(j, carry):
        c0 = pl.multiple_of(base + j * width, 128)
        here = pl.ds(c0, width)
        for p in range(pairs):
            cols = slice(p * 128, (p + 1) * 128)
            kp = k_ref[here, cols]
            dqs = []
            for r in range(2):
                h = 2 * p + r
                rows = slice(r * DH, (r + 1) * DH)
                e = e_ref[h, :, here]
                d = dot(lhs_scr[h], vext[h, here, :], NT)
                ds = (e.astype(f32) * d).astype(bf16)
                ds_scr[h] = ds
                dqs.append(dot(ds, kp))
                dkt[p, rows, here] += dot(qt_scr[p, rows, :], ds)
                dvt[p, rows, here] += dot(dat_scr[p, rows, :], e)
            dq_scr[p] += jnp.where(low, dqs[0], dqs[1])
        for b in range(tq // 16):
            rows = slice(16 * b, 16 * (b + 1))
            span = slice(b * width, (b + 1) * width)
            code = code_ref[rows, here]
            rel_signs = signs(code, 0, 5)
            lay_signs = signs(code, 5, 6)
            left_lay = walsh(lay_signs[:2])[1:]
            left_rel = walsh(rel_signs[:2])[1:]
            for h in range(heads):
                ds = ds_scr[h, rows, :]
                place = 16 * (3 * heads + h)
                left[place:place + 16, span] = ds
                for a in range(3):
                    place = 16 * (a * heads + h)
                    left[place:place + 16, span] = ds * left_lay[a]
                    place = 16 * ((4 + a) * heads + h)
                    left[place:place + 16, span] = ds * left_rel[a]
            for n, func in enumerate(walsh(lay_signs[2:])):
                blay[16 * n:16 * (n + 1), span] = jnp.ones((16, width), bf16) if func is None else func
            for n, func in enumerate(walsh(rel_signs[2:])):
                brel[16 * n:16 * (n + 1), span] = jnp.ones((16, width), bf16) if func is None else func
        group = 64 * heads
        hl_ref[...] += dot(left[:group, :], blay[...], NT)
        hr_ref[...] += dot(left[48 * heads:48 * heads + group, :], brel[...], NT)
        return carry

    lax.fori_loop(0, steps, chunk, 0)
    for p in range(pairs):
        dq_ref[:, p * 128:(p + 1) * 128] = dq_scr[p].astype(bf16)

    @pl.when(i == pl.num_programs(0) - 1)
    def _():
        for p in range(pairs):
            for c in range(0, count, 256):
                dk_ref[c:c + 256, p * 128:(p + 1) * 128] = dkt[p, :, c:c + 256].T.astype(bf16)
                dv_ref[c:c + 256, p * 128:(p + 1) * 128] = dvt[p, :, c:c + 256].T.astype(bf16)


def attention_backward(page_lengths, proj, e, code, d_att, att, rinv, tq=256, width=256):
    count = proj.shape[0]
    hc = proj.shape[1] // 3
    heads = hc // DH
    pairs = heads // 2
    grid = (count // tq,)
    deep = tq // 16 * width
    tile = lambda i: (i, 0)
    fixed = lambda i: (0, 0)
    return pl.pallas_call(
        functools.partial(backward_kernel, width=width, heads=heads),
        grid=grid,
        in_specs=[
            pl.BlockSpec(memory_space=pltpu.SMEM),
            pl.BlockSpec((tq, hc), tile),
            pl.BlockSpec((count, hc), lambda i: (0, 1)),
            pl.BlockSpec((count, hc), lambda i: (0, 2)),
            pl.BlockSpec((heads, tq, count), lambda i: (0, i, 0)),
            pl.BlockSpec((tq, count), tile),
            pl.BlockSpec((tq, hc), tile),
            pl.BlockSpec((tq, hc), tile),
            pl.BlockSpec((tq, hc), tile),
        ],
        out_specs=[
            pl.BlockSpec((tq, hc), tile),
            pl.BlockSpec((count, hc), fixed),
            pl.BlockSpec((count, hc), fixed),
            pl.BlockSpec((64 * heads, 256), fixed),
            pl.BlockSpec((64 * heads, 128), fixed),
        ],
        out_shape=[
            jax.ShapeDtypeStruct((count, hc), bf16),
            jax.ShapeDtypeStruct((count, hc), bf16),
            jax.ShapeDtypeStruct((count, hc), bf16),
            jax.ShapeDtypeStruct((64 * heads, 256), f32),
            jax.ShapeDtypeStruct((64 * heads, 128), f32),
        ],
        scratch_shapes=[
            pltpu.VMEM((heads, count, 128), bf16),
            pltpu.VMEM((heads, tq, 128), bf16),
            pltpu.VMEM((pairs, 128, tq), bf16),
            pltpu.VMEM((pairs, 128, tq), bf16),
            pltpu.VMEM((heads, tq, width), bf16),
            pltpu.VMEM((pairs, tq, 128), f32),
            pltpu.VMEM((pairs, 128, count), f32),
            pltpu.VMEM((pairs, 128, count), f32),
            pltpu.VMEM((112 * heads, deep), bf16),
            pltpu.VMEM((256, deep), bf16),
            pltpu.VMEM((128, deep), bf16),
        ],
        compiler_params=pltpu.CompilerParams(vmem_limit_bytes=56 << 20),
        name="attention_backward",
    )(page_lengths, proj, proj, proj, e, code, d_att, att, rinv)


def bucket_sums(raw, heads, left_first, right_bits):
    right = raw.shape[1] // 16
    cube = raw.reshape(4, heads, 16, right, 16)
    traced = jnp.sum(cube * jnp.eye(16, dtype=f32)[None, None, :, None, :], axis=(2, 4))
    if not left_first:
        traced = jnp.concatenate([traced[3:], traced[:3]], axis=0)

    def table(n):
        v = lax.iota(jnp.int32, n)
        both = v[:, None] & v[None, :]
        return (1 - 2 * (lax.population_count(both) & 1)).astype(f32)

    hi = table(right)
    lo = table(4)
    out = jnp.einsum("ahn,ax,ny->yxh", traced, lo, hi, precision=lax.Precision.HIGHEST)
    return out.reshape(4 * right, heads) / (4 * right)


epsilon = 1e-06


def contract_rows(left, right):
    return lax.dot_general(
        left, right, (((0,), (0,)), ((), ())), preferred_element_type=jnp.float32
    )


def contract_cols(left, right):
    return lax.dot_general(
        left, right, (((1,), (1,)), ((), ())), preferred_element_type=jnp.float32
    )


def gated(gate, upward):
    return jax.nn.gelu(gate, approximate=True) * upward


def norm_rows(rows, gain):
    scale = lax.rsqrt(jnp.mean(rows * rows, axis=-1, keepdims=True) + epsilon)
    return (scale, (rows * scale * gain).astype(jnp.bfloat16))


def norm_back(d_normed, rows, scale, gain):
    shaped = d_normed * gain
    gain_term = jnp.sum(d_normed * rows * scale, axis=0)
    cubed = scale * scale * scale
    d_rows = scale * shaped - rows * cubed * jnp.mean(shaped * rows, axis=-1, keepdims=True)
    return (d_rows, gain_term)


def scatter_narrow(array):
    return lax.psum_scatter(array.astype(bf16), "narrow", scatter_dimension=0, tiled=True).astype(f32)


def on_device(
    layer_input,
    out_grad,
    norm_attn_gain,
    w_query,
    w_key,
    w_value,
    w_out,
    rel_table,
    layout_table,
    norm_ffn_gain,
    w_gate,
    w_up,
    down_projection_weight,
    page_lengths,
    key_mask,
    rel_bucket,
    layout_bucket,
):
    head_cols = w_query.shape[1]
    heads = head_cols // DH
    hidden_cols = w_gate.shape[1]
    gain_attn = norm_attn_gain.astype(f32)
    gain_ffn = norm_ffn_gain.astype(f32)
    w_project = jnp.concatenate([w_query, w_key, w_value], axis=1)
    w_gate_up = jnp.concatenate([w_gate, w_up], axis=1)
    resid = layer_input.astype(f32)
    grad_all = lax.all_gather(out_grad, "narrow", axis=0, tiled=True)

    scale_attn, normed_attn = norm_rows(resid, gain_attn)
    normed_attn_all = lax.all_gather(normed_attn, "narrow", axis=0, tiled=True)
    projected = dot(normed_attn_all, w_project).astype(bf16)
    attended, rinv, exps, codes = attention_forward(
        page_lengths, projected, rel_bucket, layout_bucket, bias_words(rel_table, layout_table), key_mask)
    middle = resid + scatter_narrow(dot(attended, w_out))
    scale_ffn, normed_ffn = norm_rows(middle, gain_ffn)
    normed_ffn_all = lax.all_gather(normed_ffn, "narrow", axis=0, tiled=True)
    gate_up = dot(normed_ffn_all, w_gate_up)
    hidden, pullback = jax.vjp(gated, gate_up[:, :hidden_cols], gate_up[:, hidden_cols:])
    hidden = hidden.astype(bf16)
    layer_out = (middle + scatter_narrow(dot(hidden, down_projection_weight))).astype(bf16)

    grad_down = contract_rows(hidden, grad_all)
    d_hidden = contract_cols(grad_all, down_projection_weight)
    d_gate, d_up = pullback(d_hidden)
    d_gate_up = jnp.concatenate([d_gate, d_up], axis=1).astype(bf16)
    grad_gate_up = contract_rows(normed_ffn_all, d_gate_up)
    d_normed_ffn = scatter_narrow(contract_cols(d_gate_up, w_gate_up))
    d_middle_norm, gain_ffn_term = norm_back(d_normed_ffn, middle, scale_ffn, gain_ffn)
    d_middle = out_grad.astype(f32) + d_middle_norm
    d_middle_all = lax.all_gather(d_middle.astype(bf16), "narrow", axis=0, tiled=True)
    grad_wout = contract_rows(attended, d_middle_all)
    d_attended = contract_cols(d_middle_all, w_out).astype(bf16)
    d_query, d_keys, d_values, raw_lay, raw_rel = attention_backward(
        page_lengths, projected, exps, codes, d_attended, attended, rinv)
    grad_relative = bucket_sums(raw_rel, heads, True, 3)
    grad_layout = bucket_sums(raw_lay, heads, False, 4)
    d_project = jnp.concatenate([d_query, d_keys, d_values], axis=1)
    grad_project = contract_rows(normed_attn_all, d_project)
    d_normed_attn = scatter_narrow(contract_cols(d_project, w_project))
    d_resid, gain_attn_term = norm_back(d_normed_attn, resid, scale_attn, gain_attn)
    in_grad = d_middle + d_resid

    def over_wide(array, dim):
        return lax.psum_scatter(array, "wide", scatter_dimension=dim, tiled=True)

    sum_project = over_wide(grad_project, 0)
    sum_wout = over_wide(grad_wout, 1)
    sum_gate_up = over_wide(grad_gate_up, 0)
    sum_down = over_wide(grad_down, 1)
    sum_relative = over_wide(grad_relative, 0)
    sum_layout = over_wide(grad_layout, 0)
    sum_gain_attn = lax.psum_scatter(gain_attn_term, ("wide", "narrow"), scatter_dimension=0, tiled=True)
    sum_gain_ffn = lax.psum_scatter(gain_ffn_term, ("wide", "narrow"), scatter_dimension=0, tiled=True)
    return (
        layer_out,
        in_grad,
        sum_gain_attn,
        sum_project[:, :head_cols],
        sum_project[:, head_cols : 2 * head_cols],
        sum_project[:, 2 * head_cols :],
        sum_wout,
        sum_relative,
        sum_layout,
        sum_gain_ffn,
        sum_gate_up[:, :hidden_cols],
        sum_gate_up[:, hidden_cols:],
        sum_down,
    )


def solution(mesh):
    placed = (
        P(("wide", "narrow"), None),
        P(("wide", "narrow"), None),
        P(),
        P(None, "narrow"),
        P(None, "narrow"),
        P(None, "narrow"),
        P("narrow", None),
        P(None, "narrow"),
        P(None, "narrow"),
        P(),
        P(None, "narrow"),
        P(None, "narrow"),
        P("narrow", None),
        P("wide", None),
        P("wide"),
        P("wide", None),
        P("wide", None),
    )
    return jax.shard_map(
        on_device,
        mesh=mesh,
        in_specs=placed,
        out_specs=(
            P(("wide", "narrow"), None),
            P(("wide", "narrow"), None),
            P(("wide", "narrow")),
            P("wide", "narrow"),
            P("wide", "narrow"),
            P("wide", "narrow"),
            P("narrow", "wide"),
            P("wide", "narrow"),
            P("wide", "narrow"),
            P(("wide", "narrow")),
            P("wide", "narrow"),
            P("wide", "narrow"),
            P("narrow", "wide"),
        ),
        check_vma=False,
    )
```

```python
import functools
import jax
import jax.numpy as jnp
from jax import lax
from jax.experimental import pallas as pl
from jax.experimental.pallas import tpu as pltpu
from jax.sharding import PartitionSpec as P

DH = 64
BIAS_SCALE = 4096.0
LOG2E = 1.4426950408889634
f32 = jnp.float32
bf16 = jnp.bfloat16
NT = (((1,), (1,)), ((), ()))
NN = (((1,), (0,)), ((), ()))


def dot(a, b, dims=NN):
    return lax.dot_general(a, b, dims, preferred_element_type=f32)


def key_window(len_ref, first, last, count, width):
    ends = []
    total = 0
    for p in range(len_ref.shape[1]):
        total = total + len_ref[0, p]
        ends.append(total)
    start = 0
    stop = count
    for e in ends:
        start = jnp.where(e <= first, e, start)
    for e in reversed(ends):
        stop = jnp.where(e > last, e, stop)
    base = (start // 128) * 128
    steps = (stop - base + width - 1) // width
    base = jnp.minimum(base, count - steps * width)
    return ends, base, steps


def own_half(shape, head):
    lane = lax.broadcasted_iota(jnp.int32, shape, len(shape) - 1)
    return (lane < DH) if head % 2 == 0 else (lane >= DH)


def fill_values(vext, v_ref, heads):
    for h in range(heads):
        vp = v_ref[:, (h // 2) * 128:(h // 2 + 1) * 128]
        vext[h] = jnp.where(own_half(vp.shape, h), vp, jnp.ones_like(vp))


def forward_kernel(len_ref, q_ref, k_ref, v_ref, rel_ref, lay_ref, tab_ref, kmask_ref,
                   att_ref, rinv_ref, e_ref, code_ref,
                   s_scr, m_scr, vext, colcode, *, width, heads):
    tq, count = rel_ref.shape
    pairs = heads // 2
    i = pl.program_id(0)
    t0 = i * tq
    ends, base, steps = key_window(len_ref, t0, t0 + tq - 1, count, width)

    @pl.when(i == 0)
    def _():
        fill_values(vext, v_ref, heads)
        pos = lax.broadcasted_iota(jnp.int32, (8, count), 1)
        page = jnp.zeros((8, count), jnp.int32)
        for e in ends:
            page = page + (pos >= e).astype(jnp.int32)
        colcode[...] = jnp.where(kmask_ref[...] == 1, page, -1)

    rowpos = lax.broadcasted_iota(jnp.int32, (tq, 128), 0) + t0
    rowpage = jnp.zeros((tq, 128), jnp.int32)
    for e in ends:
        rowpage = rowpage + (rowpos >= e).astype(jnp.int32)
    lanes = lax.broadcasted_iota(jnp.int32, (tq, 128), 1)
    scaled = []
    for h in range(heads):
        qp = q_ref[:, (h // 2) * 128:(h // 2 + 1) * 128]
        scaled.append(jnp.where(own_half(qp.shape, h), qp * bf16(BIAS_SCALE), jnp.zeros_like(qp)))
        m_scr[h] = jnp.full((tq, 128), -3e38, f32)
    tabs = [[jnp.broadcast_to(tab_ref[2 * p + r:2 * p + r + 1, :], (tq, 128)) for r in range(2)]
            for p in range(pairs)]

    def scores(j, carry):
        c0 = pl.multiple_of(base + j * width, 128)
        raw = [dot(scaled[h], k_ref[pl.ds(c0, width), (h // 2) * 128:(h // 2 + 1) * 128], NT)
               for h in range(heads)]
        for half in range(width // 128):
            cc = pl.multiple_of(c0 + half * 128, 128)
            rel = rel_ref[:, pl.ds(cc, 128)]
            lay = lay_ref[:, pl.ds(cc, 128)]
            code_ref[:, pl.ds(cc, 128)] = (rel + lay * 32).astype(jnp.int16)
            col = jnp.broadcast_to(colcode[0:1, pl.ds(cc, 128)], (tq, 128))
            seen = (rowpage == col) | (rowpos == lanes + cc)
            hide = jnp.where(seen, f32(0.0), f32(-1e30))
            for p in range(pairs):
                word = (jnp.take_along_axis(tabs[p][0], rel, axis=1, mode="promise_in_bounds")
                        + jnp.take_along_axis(tabs[p][1], lay, axis=1, mode="promise_in_bounds"))
                parts = ((word & 0xFFFF).astype(f32), (word >> 16).astype(f32))
                for r in range(2):
                    h = 2 * p + r
                    s = raw[h][:, half * 128:(half + 1) * 128] + parts[r] + hide
                    s_scr[h, :, pl.ds(cc, 128)] = s
                    m_scr[h] = jnp.maximum(m_scr[h], s)
        return carry

    lax.fori_loop(0, steps, scores, 0)

    for p in range(pairs):
        accs = []
        for h in (2 * p, 2 * p + 1):
            top = jnp.max(m_scr[h], axis=1, keepdims=True)

            def values(j, acc):
                c0 = pl.multiple_of(base + j * width, 128)
                e = jnp.exp2((s_scr[h, :, pl.ds(c0, width)] - top) * f32(LOG2E / BIAS_SCALE)).astype(bf16)
                e_ref[h, :, pl.ds(c0, width)] = e
                return acc + dot(e, vext[h, pl.ds(c0, width), :])

            accs.append(lax.fori_loop(0, steps, values, jnp.zeros((tq, 128), f32)))
        low = own_half((tq, 128), 0)
        mixed = jnp.where(low, accs[0], accs[1])
        total = pltpu.roll(jnp.where(low, accs[1], accs[0]), DH, 1)
        rinv = 1.0 / total
        att_ref[:, p * 128:(p + 1) * 128] = (mixed * rinv).astype(bf16)
        rinv_ref[:, p * 128:(p + 1) * 128] = rinv


def attention_forward(page_lengths, proj, rel, lay, tab, kmask, tq=256, width=256):
    count = proj.shape[0]
    hc = proj.shape[1] // 3
    heads = hc // DH
    grid = (count // tq,)
    return pl.pallas_call(
        functools.partial(forward_kernel, width=width, heads=heads),
        grid=grid,
        in_specs=[
            pl.BlockSpec(memory_space=pltpu.SMEM),
            pl.BlockSpec((tq, hc), lambda i: (i, 0)),
            pl.BlockSpec((count, hc), lambda i: (0, 1)),
            pl.BlockSpec((count, hc), lambda i: (0, 2)),
            pl.BlockSpec((tq, count), lambda i: (i, 0)),
            pl.BlockSpec((tq, count), lambda i: (i, 0)),
            pl.BlockSpec(tab.shape, lambda i: (0, 0)),
            pl.BlockSpec((1, count), lambda i: (0, 0)),
        ],
        out_specs=[
            pl.BlockSpec((tq, hc), lambda i: (i, 0)),
            pl.BlockSpec((tq, hc), lambda i: (i, 0)),
            pl.BlockSpec((heads, tq, count), lambda i: (0, i, 0)),
            pl.BlockSpec((tq, count), lambda i: (i, 0)),
        ],
        out_shape=[
            jax.ShapeDtypeStruct((count, hc), bf16),
            jax.ShapeDtypeStruct((count, hc), f32),
            jax.ShapeDtypeStruct((heads, count, count), bf16),
            jax.ShapeDtypeStruct((count, count), jnp.int16),
        ],
        scratch_shapes=[
            pltpu.VMEM((heads, tq, count), f32),
            pltpu.VMEM((heads, tq, 128), f32),
            pltpu.VMEM((heads, count, 128), bf16),
            pltpu.VMEM((8, count), jnp.int32),
        ],
        compiler_params=pltpu.CompilerParams(vmem_limit_bytes=56 << 20),
        cost_estimate=pl.CostEstimate(
            flops=heads * count * count * 256, bytes_accessed=180 << 20, transcendentals=heads * count * count // 2),
        name="attention_forward",
    )(page_lengths, proj, proj, proj, rel, lay, tab, kmask.reshape(1, count))


def bias_words(rel_table, layout_table):
    def pack(table):
        whole = jnp.round(table.astype(f32) * BIAS_SCALE).astype(jnp.int32)
        low = jnp.clip(whole[:, 0::2] + 16384, 0, 32767)
        high = jnp.clip(whole[:, 1::2], -16384, 16383)
        words = (high * 65536 + low).T
        return jnp.pad(words, ((0, 0), (0, 128 - words.shape[1])))
    both = jnp.stack([pack(rel_table), pack(layout_table)], axis=1)
    return both.reshape(-1, 128)


def signs(code, shift, bits):
    return [jnp.where((code & jnp.int16(1 << (shift + b))) == 0, bf16(1.0), bf16(-1.0))
            for b in range(bits)]


def walsh(sign_list):
    out = [None]
    for s in sign_list:
        out = out + [s if o is None else o * s for o in out]
    return out


def backward_kernel(len_ref, q_ref, k_ref, v_ref, e_ref, code_ref, da_ref, att_ref, rinv_ref,
                    dq_ref, dk_ref, dv_ref, hl_ref, hr_ref,
                    vext, lhs_scr, dat_scr, qt_scr, ds_scr, dq_scr, dkt, dvt, left, blay, brel,
                    *, width, heads):
    tq, count = code_ref.shape
    pairs = heads // 2
    i = pl.program_id(0)
    t0 = i * tq
    ends, base, steps = key_window(len_ref, t0, t0 + tq - 1, count, width)

    @pl.when(i == 0)
    def _():
        fill_values(vext, v_ref, heads)
        dkt[...] = jnp.zeros_like(dkt)
        dvt[...] = jnp.zeros_like(dvt)
        hl_ref[...] = jnp.zeros_like(hl_ref)
        hr_ref[...] = jnp.zeros_like(hr_ref)

    low = own_half((tq, 128), 0)
    lane = lax.broadcasted_iota(jnp.int32, (tq, 128), 1)
    first_part = (lane & 32) == 0
    for p in range(pairs):
        cols = slice(p * 128, (p + 1) * 128)
        da = (da_ref[:, cols].astype(f32) * rinv_ref[:, cols]).astype(bf16)
        daf = da.astype(f32)
        prod = daf * att_ref[:, cols].astype(f32)
        for r in range(2):
            own = low if r == 0 else jnp.logical_not(low)
            delta = jnp.sum(jnp.where(own, prod, 0.0), axis=1, keepdims=True) * f32(-1.0 / 32)
            high = delta.astype(bf16).astype(f32)
            rest = delta - high
            lhs_scr[2 * p + r] = jnp.where(own, daf, jnp.where(first_part, high, rest)).astype(bf16)
        dat_scr[p] = daf.T.astype(bf16)
        qt_scr[p] = q_ref[:, cols].astype(f32).T.astype(bf16)
        dq_scr[p] = jnp.zeros((tq, 128), f32)

    def chunk(j, carry):
        c0 = pl.multiple_of(base + j * width, 128)
        here = pl.ds(c0, width)
        for p in range(pairs):
            cols = slice(p * 128, (p + 1) * 128)
            kp = k_ref[here, cols]
            dqs = []
            for r in range(2):
                h = 2 * p + r
                rows = slice(r * DH, (r + 1) * DH)
                e = e_ref[h, :, here]
                d = dot(lhs_scr[h], vext[h, here, :], NT)
                ds = (e.astype(f32) * d).astype(bf16)
                ds_scr[h] = ds
                dqs.append(dot(ds, kp))
                dkt[p, rows, here] += dot(qt_scr[p, rows, :], ds)
                dvt[p, rows, here] += dot(dat_scr[p, rows, :], e)
            dq_scr[p] += jnp.where(low, dqs[0], dqs[1])
        for b in range(tq // 16):
            rows = slice(16 * b, 16 * (b + 1))
            span = slice(b * width, (b + 1) * width)
            code = code_ref[rows, here]
            rel_signs = signs(code, 0, 5)
            lay_signs = signs(code, 5, 6)
            left_lay = walsh(lay_signs[:2])[1:]
            left_rel = walsh(rel_signs[:2])[1:]
            for h in range(heads):
                ds = ds_scr[h, rows, :]
                place = 16 * (3 * heads + h)
                left[place:place + 16, span] = ds
                for a in range(3):
                    place = 16 * (a * heads + h)
                    left[place:place + 16, span] = ds * left_lay[a]
                    place = 16 * ((4 + a) * heads + h)
                    left[place:place + 16, span] = ds * left_rel[a]
            for n, func in enumerate(walsh(lay_signs[2:])):
                blay[16 * n:16 * (n + 1), span] = jnp.ones((16, width), bf16) if func is None else func
            for n, func in enumerate(walsh(rel_signs[2:])):
                brel[16 * n:16 * (n + 1), span] = jnp.ones((16, width), bf16) if func is None else func
        group = 64 * heads
        hl_ref[...] += dot(left[:group, :], blay[...], NT)
        hr_ref[...] += dot(left[48 * heads:48 * heads + group, :], brel[...], NT)
        return carry

    lax.fori_loop(0, steps, chunk, 0)
    for p in range(pairs):
        dq_ref[:, p * 128:(p + 1) * 128] = dq_scr[p].astype(bf16)

    @pl.when(i == pl.num_programs(0) - 1)
    def _():
        for p in range(pairs):
            for c in range(0, count, 256):
                dk_ref[c:c + 256, p * 128:(p + 1) * 128] = dkt[p, :, c:c + 256].T.astype(bf16)
                dv_ref[c:c + 256, p * 128:(p + 1) * 128] = dvt[p, :, c:c + 256].T.astype(bf16)


def attention_backward(page_lengths, proj, e, code, d_att, att, rinv, tq=256, width=256):
    count = proj.shape[0]
    hc = proj.shape[1] // 3
    heads = hc // DH
    pairs = heads // 2
    grid = (count // tq,)
    deep = tq // 16 * width
    tile = lambda i: (i, 0)
    fixed = lambda i: (0, 0)
    return pl.pallas_call(
        functools.partial(backward_kernel, width=width, heads=heads),
        grid=grid,
        in_specs=[
            pl.BlockSpec(memory_space=pltpu.SMEM),
            pl.BlockSpec((tq, hc), tile),
            pl.BlockSpec((count, hc), lambda i: (0, 1)),
            pl.BlockSpec((count, hc), lambda i: (0, 2)),
            pl.BlockSpec((heads, tq, count), lambda i: (0, i, 0)),
            pl.BlockSpec((tq, count), tile),
            pl.BlockSpec((tq, hc), tile),
            pl.BlockSpec((tq, hc), tile),
            pl.BlockSpec((tq, hc), tile),
        ],
        out_specs=[
            pl.BlockSpec((tq, hc), tile),
            pl.BlockSpec((count, hc), fixed),
            pl.BlockSpec((count, hc), fixed),
            pl.BlockSpec((64 * heads, 256), fixed),
            pl.BlockSpec((64 * heads, 128), fixed),
        ],
        out_shape=[
            jax.ShapeDtypeStruct((count, hc), bf16),
            jax.ShapeDtypeStruct((count, hc), bf16),
            jax.ShapeDtypeStruct((count, hc), bf16),
            jax.ShapeDtypeStruct((64 * heads, 256), f32),
            jax.ShapeDtypeStruct((64 * heads, 128), f32),
        ],
        scratch_shapes=[
            pltpu.VMEM((heads, count, 128), bf16),
            pltpu.VMEM((heads, tq, 128), bf16),
            pltpu.VMEM((pairs, 128, tq), bf16),
            pltpu.VMEM((pairs, 128, tq), bf16),
            pltpu.VMEM((heads, tq, width), bf16),
            pltpu.VMEM((pairs, tq, 128), f32),
            pltpu.VMEM((pairs, 128, count), f32),
            pltpu.VMEM((pairs, 128, count), f32),
            pltpu.VMEM((112 * heads, deep), bf16),
            pltpu.VMEM((256, deep), bf16),
            pltpu.VMEM((128, deep), bf16),
        ],
        compiler_params=pltpu.CompilerParams(vmem_limit_bytes=56 << 20),
        cost_estimate=pl.CostEstimate(
            flops=heads * count * count * 768, bytes_accessed=220 << 20, transcendentals=0),
        name="attention_backward",
    )(page_lengths, proj, proj, proj, e, code, d_att, att, rinv)


def bucket_sums(raw, heads, left_first, right_bits):
    right = raw.shape[1] // 16
    cube = raw.reshape(4, heads, 16, right, 16)
    traced = jnp.sum(cube * jnp.eye(16, dtype=f32)[None, None, :, None, :], axis=(2, 4))
    if not left_first:
        traced = jnp.concatenate([traced[3:], traced[:3]], axis=0)

    def table(n):
        v = lax.iota(jnp.int32, n)
        both = v[:, None] & v[None, :]
        return (1 - 2 * (lax.population_count(both) & 1)).astype(f32)

    hi = table(right)
    lo = table(4)
    out = jnp.einsum("ahn,ax,ny->yxh", traced, lo, hi, precision=lax.Precision.HIGHEST)
    return out.reshape(4 * right, heads) / (4 * right)


def weight_grads_kernel(n_pair, *refs):
    x_ref, g_ref, m_ref = refs[:3]
    gate_ups = refs[3:3 + n_pair]
    hiddens = refs[3 + n_pair:3 + 2 * n_pair]
    att_ref, out_ref = refs[3 + 2 * n_pair:]
    rows_in = (((0,), (0,)), ((), ()))
    place = 0
    for left, rights in ((x_ref, gate_ups), (m_ref, (att_ref,)), (g_ref, hiddens)):
        for right in rights:
            size = right.shape[1]
            out_ref[:, place:place + size] = dot(left[...], right[...], rows_in).astype(bf16)
            place += size


def weight_grads(normed_pair, grad_pair, d_middle_low, gate_ups, hiddens, attended_own, tile=256):
    features = normed_pair.shape[1]
    rights = list(gate_ups) + list(hiddens) + [attended_own]
    columns = sum(r.shape[1] for r in rights)
    left = lambda a: pl.BlockSpec((a.shape[0], tile), lambda i: (0, i))
    whole = lambda a: pl.BlockSpec(a.shape, lambda i: (0, 0))
    return pl.pallas_call(
        functools.partial(weight_grads_kernel, len(gate_ups)),
        grid=(features // tile,),
        in_specs=[left(normed_pair), left(grad_pair), left(d_middle_low)] + [whole(r) for r in rights],
        out_specs=pl.BlockSpec((tile, columns), lambda i: (i, 0)),
        out_shape=jax.ShapeDtypeStruct((features, columns), bf16),
        compiler_params=pltpu.CompilerParams(vmem_limit_bytes=56 << 20),
        cost_estimate=pl.CostEstimate(
            flops=2 * features * columns * normed_pair.shape[0], bytes_accessed=26 << 20, transcendentals=0),
        name="weight_grads",
    )(normed_pair, grad_pair, d_middle_low, *rights)


epsilon = 1e-06


def contract_rows(left, right):
    return lax.dot_general(
        left, right, (((0,), (0,)), ((), ())), preferred_element_type=jnp.float32
    )


def contract_cols(left, right):
    return lax.dot_general(
        left, right, (((1,), (1,)), ((), ())), preferred_element_type=jnp.float32
    )


def gated(gate, upward):
    return jax.nn.gelu(gate, approximate=True) * upward


def norm_rows(rows, gain):
    scale = lax.rsqrt(jnp.mean(rows * rows, axis=-1, keepdims=True) + epsilon)
    return (scale, (rows * scale * gain).astype(jnp.bfloat16))


def norm_back(d_normed, rows, scale, gain):
    shaped = d_normed * gain
    cubed = scale * scale * scale
    return scale * shaped - rows * cubed * jnp.mean(shaped * rows, axis=-1, keepdims=True)


def along(array, shift, ring):
    return lax.ppermute(array, "narrow", [(i, (i + shift) % ring) for i in range(ring)])


def swap(array, ring):
    return lax.ppermute(array, "narrow", [(i, i ^ 1) for i in range(ring)])


def rows_of(array, index, count):
    return lax.dynamic_slice_in_dim(array, index * count, count, 0)


def on_device(
    wide,
    ring,
    layer_input,
    out_grad,
    norm_attn_gain,
    w_query,
    w_key,
    w_value,
    w_out,
    rel_table,
    layout_table,
    norm_ffn_gain,
    w_gate,
    w_up,
    down_projection_weight,
    page_lengths,
    key_mask,
    rel_bucket,
    layout_bucket,
):
    tokens, width = layer_input.shape
    head_cols = w_query.shape[1]
    heads = head_cols // DH
    units = w_gate.shape[1]
    part = width // wide
    me = lax.axis_index("narrow")
    my_wide = lax.axis_index("wide")
    gain_attn = norm_attn_gain.astype(f32)
    gain_ffn = norm_ffn_gain.astype(f32)
    resid = layer_input.astype(f32)

    scale_attn, normed_attn = norm_rows(resid, gain_attn)
    normed_attn_all = lax.all_gather(normed_attn, "narrow", axis=0, tiled=True)

    w_project = jnp.concatenate([w_query, w_key, w_value], axis=1)
    w_gate_up = jnp.concatenate([w_gate, w_up], axis=1)
    own_rows_gate_up = rows_of(w_gate_up, my_wide, part)
    own_rows_project = rows_of(w_project, my_wide, part)
    down_piece = lax.dynamic_slice_in_dim(down_projection_weight, my_wide * part, part, 1).T
    out_piece = lax.dynamic_slice_in_dim(w_out, my_wide * part, part, 1).T
    ffn_piece = jnp.concatenate([own_rows_gate_up, down_piece], axis=1)
    out_pieces = [out_piece] + [along(out_piece, d, ring) for d in range(1, ring)]
    ffn_pieces = [along(ffn_piece, d, ring) for d in range(2, ring, 2)]
    w_first = lax.all_gather(jnp.concatenate(out_pieces + ffn_pieces, axis=1), "wide", axis=0, tiled=True)
    late_project, late_grad, normed_attn_all = lax.optimization_barrier(
        (own_rows_project, out_grad, normed_attn_all))
    project_pieces = [own_rows_project] + [along(late_project, d, ring) for d in range(1, ring)]
    other_grad = swap(late_grad, ring)
    out_t = w_first[:, : ring * head_cols]
    shards = [(w_gate_up, down_projection_weight.T)]
    for place in range(ring * head_cols, w_first.shape[1], 3 * units):
        shards.append((w_first[:, place : place + 2 * units], w_first[:, place + 2 * units : place + 3 * units]))

    projected = dot(normed_attn_all, w_project).astype(bf16)
    attended, rinv, exps, codes = attention_forward(
        page_lengths, projected, rel_bucket, layout_bucket, bias_words(rel_table, layout_table), key_mask)
    attended, other_grad, project_pieces = lax.optimization_barrier((attended, other_grad, project_pieces))
    w_project_all = lax.all_gather(jnp.concatenate(project_pieces, axis=1), "wide", axis=0, tiled=True)
    grad_pair = jnp.concatenate([out_grad, other_grad], axis=0)
    mine = [along(rows_of(attended, (me + d) % ring, tokens), d, ring) for d in range(1, ring)]
    attended_own = jnp.concatenate([rows_of(attended, me, tokens)] + mine, axis=1)
    middle = resid + contract_cols(attended_own, out_t)

    scale_ffn, normed_ffn = norm_rows(middle, gain_ffn)
    normed_pair = jnp.concatenate([normed_ffn, swap(normed_ffn, ring)], axis=0)
    d_normed = 0.0
    kept = []
    for gate_up_weight, down_t in shards:
        gate_up = dot(normed_pair, gate_up_weight)
        hidden, pullback = jax.vjp(gated, gate_up[:, :units], gate_up[:, units:])
        hidden = hidden.astype(bf16)
        d_hidden = dot(grad_pair, down_t)
        d_gate, d_up = pullback(d_hidden)
        d_gate_up = jnp.concatenate([d_gate, d_up], axis=1).astype(bf16)
        d_normed = d_normed + contract_cols(d_gate_up, gate_up_weight)
        kept.append((hidden, d_gate_up))
    own_d_normed, other_d_normed, hiddens = lax.optimization_barrier(
        (d_normed[:tokens], d_normed[tokens:].astype(bf16), [k[0] for k in kept]))
    other_d_normed = swap(other_d_normed, ring)
    out_sum = 0.0
    for hidden, (_, down_t) in zip(hiddens, shards):
        out_sum = out_sum + contract_cols(hidden, down_t)
    other_d_normed, other_out = lax.optimization_barrier((other_d_normed, out_sum[tokens:].astype(bf16)))
    layer_out = (middle + out_sum[:tokens] + swap(other_out, ring).astype(f32)).astype(bf16)
    d_normed_ffn = own_d_normed + other_d_normed.astype(f32)
    d_middle = out_grad.astype(f32) + norm_back(d_normed_ffn, middle, scale_ffn, gain_ffn)
    d_middle_low = d_middle.astype(bf16)
    d_attended_own = dot(d_middle_low, out_t).astype(bf16)

    def block(d):
        return d_attended_own[:, d * head_cols : (d + 1) * head_cols]

    d_attended = jnp.zeros((ring * tokens, head_cols), bf16)
    d_attended = lax.dynamic_update_slice_in_dim(d_attended, block(0), me * tokens, 0)
    for d in range(1, ring):
        d_attended = lax.dynamic_update_slice_in_dim(
            d_attended, along(block(d), -d, ring), ((me + d) % ring) * tokens, 0)

    ffn_sums = weight_grads(
        normed_pair, grad_pair, d_middle_low, [k[1] for k in kept], hiddens, attended_own)
    ffn_sums, d_attended, w_project_all = lax.optimization_barrier((ffn_sums, d_attended, w_project_all))
    ffn_sums = lax.psum_scatter(ffn_sums, "wide", scatter_dimension=0, tiled=True)

    d_query, d_keys, d_values, raw_lay, raw_rel = attention_backward(
        page_lengths, projected, exps, codes, d_attended, attended, rinv)
    d_project = jnp.concatenate([d_query, d_keys, d_values], axis=1)
    mine = [along(rows_of(d_project, (me + d) % ring, tokens), d, ring) for d in range(1, ring)]
    d_project_own = jnp.concatenate([rows_of(d_project, me, tokens)] + mine, axis=1)
    d_normed_attn = contract_cols(d_project_own, w_project_all)
    in_grad = d_middle + norm_back(d_normed_attn, resid, scale_attn, gain_attn)

    grad_relative = bucket_sums(raw_rel, heads, True, 3)
    grad_layout = bucket_sums(raw_lay, heads, False, 4)
    tables = jnp.concatenate(
        [grad_relative.reshape(wide, -1, heads), grad_layout.reshape(wide, -1, heads)], axis=1)
    n_rel = grad_relative.shape[0] // wide
    n_both = tables.shape[1]
    tables = jnp.pad(tables, ((0, 0), (0, part - n_both), (0, 128 - heads))).reshape(width, 128)
    last_sums = jnp.concatenate([contract_rows(normed_attn_all, d_project), tables], axis=1)
    last_sums, ffn_sums = lax.optimization_barrier((last_sums.astype(bf16), ffn_sums))
    last_sums = lax.psum_scatter(last_sums, "wide", scatter_dimension=0, tiled=True).astype(f32)
    n_shards = len(kept)
    first = 2 * units * n_shards
    second = first + ring * head_cols
    sum_gate_up = ffn_sums[:, : 2 * units].astype(f32)
    sum_down = ffn_sums[:, second : second + units].astype(f32)
    for n in range(1, n_shards):
        sum_gate_up += along(ffn_sums[:, 2 * units * n : 2 * units * (n + 1)], -2 * n, ring).astype(f32)
        sum_down += along(ffn_sums[:, second + units * n : second + units * (n + 1)], -2 * n, ring).astype(f32)
    sum_wout = ffn_sums[:, first : first + head_cols].astype(f32)
    for d in range(1, ring):
        place = first + d * head_cols
        sum_wout += along(ffn_sums[:, place : place + head_cols], -d, ring).astype(f32)

    sum_project = last_sums[:, : 3 * head_cols]
    sum_tables = last_sums[:n_both, 3 * head_cols : 3 * head_cols + heads]

    gain_terms = jnp.stack(
        [
            jnp.sum(own_rows_project.astype(f32) * sum_project, axis=1),
            jnp.sum(own_rows_gate_up.astype(f32) * sum_gate_up, axis=1),
        ]
    )
    share = part // ring

    def gain_share(index):
        return lax.dynamic_slice_in_dim(gain_terms, index * share, share, 1)

    gain_sum = gain_share(me)
    for d in range(1, ring):
        gain_sum = gain_sum + along(gain_share((me + d) % ring), d, ring)
    place = my_wide * part + me * share
    gains = lax.dynamic_slice_in_dim(jnp.stack([gain_attn, gain_ffn]), place, share, 1)
    gain_grads = gain_sum / gains
    return (
        layer_out,
        in_grad,
        gain_grads[0],
        sum_project[:, :head_cols],
        sum_project[:, head_cols : 2 * head_cols],
        sum_project[:, 2 * head_cols :],
        sum_wout.T,
        sum_tables[:n_rel],
        sum_tables[n_rel:],
        gain_grads[1],
        sum_gate_up[:, :units],
        sum_gate_up[:, units:],
        sum_down.T,
    )


def solution(mesh):
    placed = (
        P(("wide", "narrow"), None),
        P(("wide", "narrow"), None),
        P(),
        P(None, "narrow"),
        P(None, "narrow"),
        P(None, "narrow"),
        P("narrow", None),
        P(None, "narrow"),
        P(None, "narrow"),
        P(),
        P(None, "narrow"),
        P(None, "narrow"),
        P("narrow", None),
        P("wide", None),
        P("wide"),
        P("wide", None),
        P("wide", None),
    )
    return jax.shard_map(
        functools.partial(on_device, mesh.shape["wide"], mesh.shape["narrow"]),
        mesh=mesh,
        in_specs=placed,
        out_specs=(
            P(("wide", "narrow"), None),
            P(("wide", "narrow"), None),
            P(("wide", "narrow")),
            P("wide", "narrow"),
            P("wide", "narrow"),
            P("wide", "narrow"),
            P("narrow", "wide"),
            P("wide", "narrow"),
            P("wide", "narrow"),
            P(("wide", "narrow")),
            P("wide", "narrow"),
            P("wide", "narrow"),
            P("narrow", "wide"),
        ),
        check_vma=False,
    )
```

```python
import functools
import jax
import jax.numpy as jnp
from jax import lax
from jax.experimental import pallas as pl
from jax.experimental.pallas import tpu as pltpu
from jax.sharding import PartitionSpec as P

DH = 64
BIAS_SCALE = 4096.0
LOG2E = 1.4426950408889634
f32 = jnp.float32
bf16 = jnp.bfloat16
NT = (((1,), (1,)), ((), ()))
NN = (((1,), (0,)), ((), ()))


def dot(a, b, dims=NN):
    return lax.dot_general(a, b, dims, preferred_element_type=f32)


def key_window(len_ref, first, last, count, width):
    ends = []
    total = 0
    for p in range(len_ref.shape[1]):
        total = total + len_ref[0, p]
        ends.append(total)
    start = 0
    stop = count
    for e in ends:
        start = jnp.where(e <= first, e, start)
    for e in reversed(ends):
        stop = jnp.where(e > last, e, stop)
    base = (start // 128) * 128
    steps = (stop - base + width - 1) // width
    base = jnp.minimum(base, count - steps * width)
    return ends, base, steps


def for_chunks(base, steps, width, group, body):
    def many(j, carry):
        body(pl.multiple_of(base + j * (group * width), 128), group * width)
        return carry

    def single(j, carry):
        body(pl.multiple_of(base + j * width, 128), width)
        return carry

    if group > 1:
        lax.fori_loop(0, steps // group, many, 0)
    lax.fori_loop((steps // group) * group if group > 1 else 0, steps, single, 0)


def own_half(shape, head):
    lane = lax.broadcasted_iota(jnp.int32, shape, len(shape) - 1)
    return (lane < DH) if head % 2 == 0 else (lane >= DH)


def fill_values(vext, v_ref, heads):
    for h in range(heads):
        vp = v_ref[:, (h // 2) * 128:(h // 2 + 1) * 128]
        vext[h] = jnp.where(own_half(vp.shape, h), vp, jnp.ones_like(vp))


def half_norms(rows):
    lane = lax.broadcasted_iota(jnp.int32, (128, 128), 0)
    column = lax.broadcasted_iota(jnp.int32, (128, 128), 1)
    same = ((lane < DH) == (column < DH)).astype(bf16)
    squares = (rows.astype(f32) * rows.astype(f32)).astype(bf16)
    return jnp.max(dot(squares, same)) * f32(1.02)


def forward_kernel(len_ref, q_ref, k_ref, v_ref, rel_ref, lay_ref, tab_ref, kmask_ref,
                   att_ref, rinv_ref, e_ref, code_ref,
                   s_scr, m_scr, acc_scr, vext, colcode, knorm, *, width, heads, group):
    tq, count = rel_ref.shape
    pairs = heads // 2
    i = pl.program_id(0)
    t0 = i * tq
    ends, base, steps = key_window(len_ref, t0, t0 + tq - 1, count, width)

    @pl.when(i == 0)
    def _():
        fill_values(vext, v_ref, heads)
        pos = lax.broadcasted_iota(jnp.int32, (8, count), 1)
        page = jnp.zeros((8, count), jnp.int32)
        for e in ends:
            page = page + (pos >= e).astype(jnp.int32)
        colcode[...] = jnp.where(kmask_ref[...] == 1, page, -1)
        for p in range(pairs):
            knorm[p] = half_norms(k_ref[:, p * 128:(p + 1) * 128])

    rowpos = lax.broadcasted_iota(jnp.int32, (tq, 128), 0) + t0
    rowpage = jnp.zeros((tq, 128), jnp.int32)
    for e in ends:
        rowpage = rowpage + (rowpos >= e).astype(jnp.int32)
    lanes = lax.broadcasted_iota(jnp.int32, (tq, 128), 1)
    scaled = []
    largest = f32(0.0)
    for h in range(heads):
        qp = q_ref[:, (h // 2) * 128:(h // 2 + 1) * 128]
        scaled.append(jnp.where(own_half(qp.shape, h), qp * bf16(BIAS_SCALE), jnp.zeros_like(qp)))
        if h % 2 == 0:
            largest = jnp.maximum(largest, half_norms(qp) * knorm[h // 2])
    tabs = [[jnp.broadcast_to(tab_ref[2 * p + r:2 * p + r + 1, :], (tq, 128)) for r in range(2)]
            for p in range(pairs)]

    def scores(c0, width, use):
        raw = [dot(scaled[h], k_ref[pl.ds(c0, width), (h // 2) * 128:(h // 2 + 1) * 128], NT)
               for h in range(heads)]
        for half in range(width // 128):
            cc = pl.multiple_of(c0 + half * 128, 128)
            rel = rel_ref[:, pl.ds(cc, 128)]
            lay = lay_ref[:, pl.ds(cc, 128)]
            code_ref[:, pl.ds(cc, 128)] = (rel + lay * 32).astype(jnp.int16)
            col = jnp.broadcast_to(colcode[0:1, pl.ds(cc, 128)], (tq, 128))
            seen = (rowpage == col) | (rowpos == lanes + cc)
            hide = jnp.where(seen, f32(0.0), f32(-1e30))
            for p in range(pairs):
                word = (jnp.take_along_axis(tabs[p][0], rel, axis=1, mode="promise_in_bounds")
                        + jnp.take_along_axis(tabs[p][1], lay, axis=1, mode="promise_in_bounds"))
                parts = ((word & 0xFFFF).astype(f32), (word >> 16).astype(f32))
                for r in range(2):
                    h = 2 * p + r
                    use(h, half, cc, raw[h][:, half * 128:(half + 1) * 128] + parts[r] + hide)

    for h in range(heads):
        acc_scr[h] = jnp.zeros((tq, 128), f32)
    bounded = jnp.sqrt(largest) + 8.0 <= 60.0

    @pl.when(bounded)
    def _():
        def chunk(c0, size):
            pieces = {}

            def use(h, half, cc, s):
                e = jnp.exp2(s * f32(LOG2E / BIAS_SCALE)).astype(bf16)
                e_ref[h, :, pl.ds(cc, 128)] = e
                pieces[h, half] = e

            scores(c0, size, use)
            for h in range(heads):
                e = jnp.concatenate([pieces[h, half] for half in range(size // 128)], axis=1)
                acc_scr[h] += dot(e, vext[h, pl.ds(c0, size), :])

        for_chunks(base, steps, width, group, chunk)

    @pl.when(jnp.logical_not(bounded))
    def _():
        for h in range(heads):
            m_scr[h] = jnp.full((tq, 128), -3e38, f32)

        def first(j, carry):
            def use(h, half, cc, s):
                s_scr[h, :, pl.ds(cc, 128)] = s
                m_scr[h] = jnp.maximum(m_scr[h], s)

            scores(pl.multiple_of(base + j * width, 128), width, use)
            return carry

        lax.fori_loop(0, steps, first, 0)
        for h in range(heads):
            top = jnp.max(m_scr[h], axis=1, keepdims=True)

            def second(j, carry):
                c0 = pl.multiple_of(base + j * width, 128)
                e = jnp.exp2((s_scr[h, :, pl.ds(c0, width)] - top) * f32(LOG2E / BIAS_SCALE)).astype(bf16)
                e_ref[h, :, pl.ds(c0, width)] = e
                acc_scr[h] += dot(e, vext[h, pl.ds(c0, width), :])
                return carry

            lax.fori_loop(0, steps, second, 0)

    low = own_half((tq, 128), 0)
    for p in range(pairs):
        even, odd = acc_scr[2 * p], acc_scr[2 * p + 1]
        rinv = 1.0 / pltpu.roll(jnp.where(low, odd, even), DH, 1)
        att_ref[:, p * 128:(p + 1) * 128] = (jnp.where(low, even, odd) * rinv).astype(bf16)
        rinv_ref[:, p * 128:(p + 1) * 128] = rinv


def attention_forward(page_lengths, proj, rel, lay, tab, kmask, tq=256, width=256, group=1):
    count = proj.shape[0]
    hc = proj.shape[1] // 3
    heads = hc // DH
    grid = (count // tq,)
    return pl.pallas_call(
        functools.partial(forward_kernel, width=width, heads=heads, group=group),
        grid=grid,
        in_specs=[
            pl.BlockSpec(memory_space=pltpu.SMEM),
            pl.BlockSpec((tq, hc), lambda i: (i, 0)),
            pl.BlockSpec((count, hc), lambda i: (0, 1)),
            pl.BlockSpec((count, hc), lambda i: (0, 2)),
            pl.BlockSpec((tq, count), lambda i: (i, 0)),
            pl.BlockSpec((tq, count), lambda i: (i, 0)),
            pl.BlockSpec(tab.shape, lambda i: (0, 0)),
            pl.BlockSpec((1, count), lambda i: (0, 0)),
        ],
        out_specs=[
            pl.BlockSpec((tq, hc), lambda i: (i, 0)),
            pl.BlockSpec((tq, hc), lambda i: (i, 0)),
            pl.BlockSpec((heads, tq, count), lambda i: (0, i, 0)),
            pl.BlockSpec((tq, count), lambda i: (i, 0)),
        ],
        out_shape=[
            jax.ShapeDtypeStruct((count, hc), bf16),
            jax.ShapeDtypeStruct((count, hc), f32),
            jax.ShapeDtypeStruct((heads, count, count), bf16),
            jax.ShapeDtypeStruct((count, count), jnp.int16),
        ],
        scratch_shapes=[
            pltpu.VMEM((heads, tq, count), f32),
            pltpu.VMEM((heads, tq, 128), f32),
            pltpu.VMEM((heads, tq, 128), f32),
            pltpu.VMEM((heads, count, 128), bf16),
            pltpu.VMEM((8, count), jnp.int32),
            pltpu.SMEM((heads // 2,), f32),
        ],
        compiler_params=pltpu.CompilerParams(vmem_limit_bytes=56 << 20),
        cost_estimate=pl.CostEstimate(
            flops=heads * count * count * 256, bytes_accessed=150 << 20, transcendentals=heads * count * count // 2),
        name="attention_forward",
    )(page_lengths, proj, proj, proj, rel, lay, tab, kmask.reshape(1, count))


def bias_words(rel_table, layout_table):
    def pack(table):
        whole = jnp.round(table.astype(f32) * BIAS_SCALE).astype(jnp.int32)
        low = jnp.clip(whole[:, 0::2] + 16384, 0, 32767)
        high = jnp.clip(whole[:, 1::2], -16384, 16383)
        words = (high * 65536 + low).T
        return jnp.pad(words, ((0, 0), (0, 128 - words.shape[1])))
    both = jnp.stack([pack(rel_table), pack(layout_table)], axis=1)
    return both.reshape(-1, 128)


def signs(code, shift, bits):
    return [jnp.where((code & jnp.int16(1 << (shift + b))) == 0, bf16(1.0), bf16(-1.0))
            for b in range(bits)]


def walsh(sign_list):
    out = [None]
    for s in sign_list:
        out = out + [s if o is None else o * s for o in out]
    return out


def backward_kernel(len_ref, q_ref, k_ref, v_ref, e_ref, da_ref, att_ref, rinv_ref,
                    dq_ref, dk_ref, dv_ref, ds_ref,
                    vext, lhs_scr, dat_scr, qt_scr, dq_scr, dkt, dvt, *, width, heads, group):
    tq = q_ref.shape[0]
    count = k_ref.shape[0]
    pairs = heads // 2
    i = pl.program_id(0)
    t0 = i * tq
    ends, base, steps = key_window(len_ref, t0, t0 + tq - 1, count, width)

    @pl.when(i == 0)
    def _():
        fill_values(vext, v_ref, heads)
        dkt[...] = jnp.zeros_like(dkt)
        dvt[...] = jnp.zeros_like(dvt)

    low = own_half((tq, 128), 0)
    lane = lax.broadcasted_iota(jnp.int32, (tq, 128), 1)
    first_part = (lane & 32) == 0
    for p in range(pairs):
        cols = slice(p * 128, (p + 1) * 128)
        da = (da_ref[:, cols].astype(f32) * rinv_ref[:, cols]).astype(bf16)
        daf = da.astype(f32)
        prod = daf * att_ref[:, cols].astype(f32)
        for r in range(2):
            own = low if r == 0 else jnp.logical_not(low)
            delta = jnp.sum(jnp.where(own, prod, 0.0), axis=1, keepdims=True) * f32(-1.0 / 32)
            high = delta.astype(bf16).astype(f32)
            rest = delta - high
            lhs_scr[2 * p + r] = jnp.where(own, daf, jnp.where(first_part, high, rest)).astype(bf16)
        dat_scr[p] = daf.T.astype(bf16)
        qt_scr[p] = q_ref[:, cols].astype(f32).T.astype(bf16)
        dq_scr[p] = jnp.zeros((tq, 128), f32)

    def chunk(c0, size):
        here = pl.ds(c0, size)
        for p in range(pairs):
            kp = k_ref[here, p * 128:(p + 1) * 128]
            dqs = []
            for r in range(2):
                h = 2 * p + r
                rows = slice(r * DH, (r + 1) * DH)
                e = e_ref[h, :, here]
                d = dot(lhs_scr[h], vext[h, here, :], NT)
                ds = (e.astype(f32) * d).astype(bf16)
                ds_ref[h, :, here] = ds
                dqs.append(dot(ds, kp))
                dkt[p, rows, here] += dot(qt_scr[p, rows, :], ds)
                dvt[p, rows, here] += dot(dat_scr[p, rows, :], e)
            dq_scr[p] += jnp.where(low, dqs[0], dqs[1])

    for_chunks(base, steps, width, group, chunk)
    for p in range(pairs):
        dq_ref[:, p * 128:(p + 1) * 128] = dq_scr[p].astype(bf16)

    @pl.when(i == pl.num_programs(0) - 1)
    def _():
        for p in range(pairs):
            for c in range(0, count, 256):
                dk_ref[c:c + 256, p * 128:(p + 1) * 128] = dkt[p, :, c:c + 256].T.astype(bf16)
                dv_ref[c:c + 256, p * 128:(p + 1) * 128] = dvt[p, :, c:c + 256].T.astype(bf16)


def attention_backward(page_lengths, proj, e, d_att, att, rinv, tq=256, width=256, group=2):
    count = proj.shape[0]
    hc = proj.shape[1] // 3
    heads = hc // DH
    pairs = heads // 2
    grid = (count // tq,)
    tile = lambda i: (i, 0)
    fixed = lambda i: (0, 0)
    return pl.pallas_call(
        functools.partial(backward_kernel, width=width, heads=heads, group=group),
        grid=grid,
        in_specs=[
            pl.BlockSpec(memory_space=pltpu.SMEM),
            pl.BlockSpec((tq, hc), tile),
            pl.BlockSpec((count, hc), lambda i: (0, 1)),
            pl.BlockSpec((count, hc), lambda i: (0, 2)),
            pl.BlockSpec((heads, tq, count), lambda i: (0, i, 0)),
            pl.BlockSpec((tq, hc), tile),
            pl.BlockSpec((tq, hc), tile),
            pl.BlockSpec((tq, hc), tile),
        ],
        out_specs=[
            pl.BlockSpec((tq, hc), tile),
            pl.BlockSpec((count, hc), fixed),
            pl.BlockSpec((count, hc), fixed),
            pl.BlockSpec((heads, tq, count), lambda i: (0, i, 0)),
        ],
        out_shape=[
            jax.ShapeDtypeStruct((count, hc), bf16),
            jax.ShapeDtypeStruct((count, hc), bf16),
            jax.ShapeDtypeStruct((count, hc), bf16),
            jax.ShapeDtypeStruct((heads, count, count), bf16),
        ],
        scratch_shapes=[
            pltpu.VMEM((heads, count, 128), bf16),
            pltpu.VMEM((heads, tq, 128), bf16),
            pltpu.VMEM((pairs, 128, tq), bf16),
            pltpu.VMEM((pairs, 128, tq), bf16),
            pltpu.VMEM((pairs, tq, 128), f32),
            pltpu.VMEM((pairs, 128, count), f32),
            pltpu.VMEM((pairs, 128, count), f32),
        ],
        compiler_params=pltpu.CompilerParams(vmem_limit_bytes=56 << 20),
        cost_estimate=pl.CostEstimate(
            flops=heads * count * count * 512, bytes_accessed=150 << 20, transcendentals=0),
        name="attention_backward",
    )(page_lengths, proj, proj, proj, e, d_att, att, rinv)


def table_kernel(len_ref, ds_ref, code_ref, hl_ref, hr_ref, *bufs, width, parts):
    heads, tq, count = ds_ref.shape
    i = pl.program_id(0)
    t0 = i * tq
    ends, base, steps = key_window(len_ref, t0, t0 + tq - 1, count, width)

    @pl.when(i == 0)
    def _():
        hl_ref[...] = jnp.zeros_like(hl_ref)
        hr_ref[...] = jnp.zeros_like(hr_ref)

    one = jnp.ones((16, width), bf16)

    def chunk(j, carry):
        c0 = pl.multiple_of(base + j * width, 128)
        here = pl.ds(c0, width)
        blocks = tq // 16 // parts
        for part in range(parts):
            left, blay, brel = bufs[3 * part:3 * part + 3]
            for b in range(blocks):
                at = 16 * (part * blocks + b)
                rows = slice(at, at + 16)
                span = slice(b * width, (b + 1) * width)
                code = code_ref[rows, here]
                rel_signs = signs(code, 0, 5)
                lay_signs = signs(code, 5, 6)
                left_lay = walsh(lay_signs[:2])[1:]
                for h in range(heads):
                    ds = ds_ref[h, rows, here]
                    for a, func in enumerate(left_lay + [None, rel_signs[0]]):
                        place = 16 * (a * heads + h)
                        left[place:place + 16, span] = ds if func is None else ds * func
                for n, func in enumerate(walsh(lay_signs[2:])):
                    blay[16 * n:16 * (n + 1), span] = one if func is None else func
                for n, func in enumerate(walsh(rel_signs[1:])):
                    brel[16 * n:16 * (n + 1), span] = one if func is None else func
            hl_ref[...] += dot(left[:64 * heads, :], blay[...], NT)
            hr_ref[...] += dot(left[48 * heads:80 * heads, :], brel[...], NT)
        return carry

    lax.fori_loop(0, steps, chunk, 0)


def table_grads(page_lengths, ds, code, tq=256, width=256, parts=2):
    heads, count, _ = ds.shape
    deep = tq // 16 * width // parts
    fixed = lambda i: (0, 0)
    return pl.pallas_call(
        functools.partial(table_kernel, width=width, parts=parts),
        grid=(count // tq,),
        in_specs=[
            pl.BlockSpec(memory_space=pltpu.SMEM),
            pl.BlockSpec((heads, tq, count), lambda i: (0, i, 0)),
            pl.BlockSpec((tq, count), lambda i: (i, 0)),
        ],
        out_specs=[
            pl.BlockSpec((64 * heads, 256), fixed),
            pl.BlockSpec((32 * heads, 256), fixed),
        ],
        out_shape=[
            jax.ShapeDtypeStruct((64 * heads, 256), f32),
            jax.ShapeDtypeStruct((32 * heads, 256), f32),
        ],
        scratch_shapes=[
            pltpu.VMEM((80 * heads, deep), bf16),
            pltpu.VMEM((256, deep), bf16),
            pltpu.VMEM((256, deep), bf16),
        ] * parts,
        compiler_params=pltpu.CompilerParams(vmem_limit_bytes=56 << 20),
        cost_estimate=pl.CostEstimate(
            flops=heads * count * count * 512, bytes_accessed=150 << 20, transcendentals=0),
        name="table_grads",
    )(page_lengths, ds, code)


def bucket_sums(raw, heads):
    right = raw.shape[1] // 16
    left = raw.shape[0] // (16 * heads)
    cube = raw.reshape(left, heads, 16, right, 16)
    traced = jnp.sum(cube * jnp.eye(16, dtype=f32)[None, None, :, None, :], axis=(2, 4))
    if left == 4:
        traced = jnp.concatenate([traced[3:], traced[:3]], axis=0)

    def table(n):
        v = lax.iota(jnp.int32, n)
        both = v[:, None] & v[None, :]
        return (1 - 2 * (lax.population_count(both) & 1)).astype(f32)

    out = jnp.einsum("ahn,ax,ny->yxh", traced, table(left), table(right), precision=lax.Precision.HIGHEST)
    return out.reshape(left * right, heads) / (left * right)


TANH_SLOPE = 0.7978845608028654
CUBE = 0.044715


def feed_forward_kernel(skip, shards, x_ref, g_ref, wg_ref, wu_ref, wd_ref, far_ref, *outs):
    units = wg_ref.shape[0]
    step = pad_lanes(units)
    dn_ref = outs[-1]
    x = x_ref[...]
    g = g_ref[...]
    total = None
    for s in range(shards):
        if s == 0:
            wg, wu = wg_ref[...], wu_ref[...]
            d_hidden = dot(g, wd_ref[...], NT)
            ahead, back = NT, NN
        else:
            at = skip + 3 * step * (s - 1)
            wg = far_ref[:, at:at + units]
            wu = far_ref[:, at + step:at + step + units]
            d_hidden = dot(g, far_ref[:, at + 2 * step:at + 2 * step + units])
            ahead, back = NN, NT
        gate = dot(x, wg, ahead)
        up = dot(x, wu, ahead)
        square = gate * gate
        t = jnp.tanh(TANH_SLOPE * gate * (1.0 + CUBE * square))
        half = 0.5 + 0.5 * t
        gelu = gate * half
        slope = half + (0.5 * TANH_SLOPE) * gate * (1.0 - t * t) * (1.0 + (3 * CUBE) * square)
        d_gate = (d_hidden * up * slope).astype(bf16)
        d_up = (d_hidden * gelu).astype(bf16)
        outs[3 * s][...] = (gelu * up).astype(bf16)
        outs[3 * s + 1][...] = d_gate
        outs[3 * s + 2][...] = d_up
        value = dot(d_gate, wg, back) + dot(d_up, wu, back)
        total = value if total is None else total + value
    dn_ref[...] = total


def feed_forward(x, g, w_gate_t, w_up_t, w_down, far, skip, tile=256):
    tokens, features = x.shape
    units = w_down.shape[0]
    shards = 1 + (far.shape[1] - skip) // (3 * pad_lanes(units))
    tile = min(tile, tokens)
    rows = lambda n: pl.BlockSpec((tile, n), lambda i: (i, 0))
    whole = lambda a: pl.BlockSpec(a.shape, lambda i: (0, 0))
    return pl.pallas_call(
        functools.partial(feed_forward_kernel, skip, shards),
        grid=(tokens // tile,),
        in_specs=[rows(features), rows(features), whole(w_gate_t), whole(w_up_t), whole(w_down), whole(far)],
        out_specs=[rows(units)] * (3 * shards) + [rows(features)],
        out_shape=[jax.ShapeDtypeStruct((tokens, units), bf16)] * (3 * shards)
        + [jax.ShapeDtypeStruct((tokens, features), f32)],
        compiler_params=pltpu.CompilerParams(vmem_limit_bytes=56 << 20),
        cost_estimate=pl.CostEstimate(
            flops=10 * tokens * features * units * shards, bytes_accessed=14 << 20,
            transcendentals=tokens * units * shards),
        name="feed_forward",
    )(x, g, w_gate_t, w_up_t, w_down, far)


def pad_lanes(n):
    return (n + 127) // 128 * 128


def weight_grads_kernel(skip, n_left, n_right, *refs):
    lefts = refs[:2 * n_left]
    rights = refs[2 * n_left:-1]
    out_ref = refs[-1]
    rows_in = (((0,), (0,)), ((), ()))
    place = skip
    for n, left in enumerate(n_right):
        a, b = rights[2 * n], rights[2 * n + 1]
        size = a.shape[1]
        value = dot(lefts[2 * left][...], a[...], rows_in) + dot(lefts[2 * left + 1][...], b[...], rows_in)
        out_ref[:, place:place + size] = value.astype(bf16)
        if pad_lanes(size) > size:
            out_ref[:, place + size:place + pad_lanes(size)] = jnp.zeros(
                (out_ref.shape[0], pad_lanes(size) - size), bf16)
        place += pad_lanes(size)


def weight_grads(lefts, rights, groups, skip, tile=256):
    features = lefts[0].shape[1]
    columns = skip + sum(pad_lanes(r.shape[1]) for r in rights[::2])
    column = lambda a: pl.BlockSpec((a.shape[0], tile), lambda i: (0, i))
    whole = lambda a: pl.BlockSpec(a.shape, lambda i: (0, 0))
    return pl.pallas_call(
        functools.partial(weight_grads_kernel, skip, len(lefts) // 2, groups),
        grid=(features // tile,),
        in_specs=[column(a) for a in lefts] + [whole(a) for a in rights],
        out_specs=pl.BlockSpec((tile, columns), lambda i: (i, 0)),
        out_shape=jax.ShapeDtypeStruct((features, columns), bf16),
        compiler_params=pltpu.CompilerParams(vmem_limit_bytes=56 << 20),
        cost_estimate=pl.CostEstimate(
            flops=4 * features * columns * lefts[0].shape[0], bytes_accessed=26 << 20, transcendentals=0),
        name="weight_grads",
    )(*lefts, *rights)


epsilon = 1e-06


def contract_rows(left, right):
    return lax.dot_general(
        left, right, (((0,), (0,)), ((), ())), preferred_element_type=jnp.float32
    )


def contract_cols(left, right):
    return lax.dot_general(
        left, right, (((1,), (1,)), ((), ())), preferred_element_type=jnp.float32
    )


def norm_rows(rows, gain):
    scale = lax.rsqrt(jnp.mean(rows * rows, axis=-1, keepdims=True) + epsilon)
    return (scale, (rows * scale * gain).astype(jnp.bfloat16))


def norm_back(d_normed, rows, scale, gain):
    shaped = d_normed * gain
    cubed = scale * scale * scale
    return scale * shaped - rows * cubed * jnp.mean(shaped * rows, axis=-1, keepdims=True)


def along(array, shift, ring):
    return lax.ppermute(array, "narrow", [(i, (i + shift) % ring) for i in range(ring)])


def swap(array, ring):
    return lax.ppermute(array, "narrow", [(i, i ^ 1) for i in range(ring)])


def rows_of(array, index, count):
    return lax.dynamic_slice_in_dim(array, index * count, count, 0)


def on_device(
    wide,
    ring,
    layer_input,
    out_grad,
    norm_attn_gain,
    w_query,
    w_key,
    w_value,
    w_out,
    rel_table,
    layout_table,
    norm_ffn_gain,
    w_gate,
    w_up,
    down_projection_weight,
    page_lengths,
    key_mask,
    rel_bucket,
    layout_bucket,
):
    tokens, width = layer_input.shape
    head_cols = w_query.shape[1]
    heads = head_cols // DH
    units = w_gate.shape[1]
    padded = pad_lanes(units)
    part = width // wide
    me = lax.axis_index("narrow")
    my_wide = lax.axis_index("wide")
    gain_attn = norm_attn_gain.astype(f32)
    gain_ffn = norm_ffn_gain.astype(f32)
    resid = layer_input.astype(f32)

    scale_attn, normed_attn = norm_rows(resid, gain_attn)
    normed_attn_all = lax.all_gather(normed_attn, "narrow", axis=0, tiled=True)

    w_project = jnp.concatenate([w_query, w_key, w_value], axis=1)
    own_rows_gate = rows_of(w_gate, my_wide, part)
    own_rows_up = rows_of(w_up, my_wide, part)
    own_rows_project = rows_of(w_project, my_wide, part)
    down_piece = lax.dynamic_slice_in_dim(down_projection_weight, my_wide * part, part, 1).T
    out_piece = lax.dynamic_slice_in_dim(w_out, my_wide * part, part, 1).T
    ffn_piece = jnp.concatenate(
        [jnp.pad(piece, ((0, 0), (0, padded - units))) for piece in (own_rows_gate, own_rows_up, down_piece)], axis=1)
    normed_attn_all, out_piece, ffn_piece = lax.optimization_barrier((normed_attn_all, out_piece, ffn_piece))
    ffn_pieces = [along(ffn_piece, d, ring) for d in range(2, ring, 2)]
    out_pieces = [out_piece] + [along(out_piece, d, ring) for d in range(1, ring)]
    w_first = lax.all_gather(jnp.concatenate(out_pieces + ffn_pieces, axis=1), "wide", axis=0, tiled=True)
    late_project, late_grad, ffn_pieces = lax.optimization_barrier((own_rows_project, out_grad, ffn_pieces))
    project_pieces = [own_rows_project] + [along(late_project, d, ring) for d in range(1, ring)]
    other_grad = swap(late_grad, ring)
    out_t = w_first[:, : ring * head_cols]

    projected = dot(normed_attn_all, w_project).astype(bf16)
    attended, rinv, exps, codes = attention_forward(
        page_lengths, projected, rel_bucket, layout_bucket, bias_words(rel_table, layout_table), key_mask)
    attended, other_grad, project_pieces = lax.optimization_barrier((attended, other_grad, project_pieces))
    w_project_all = lax.all_gather(jnp.concatenate(project_pieces, axis=1), "wide", axis=0, tiled=True)
    mine = [along(rows_of(attended, (me + d) % ring, tokens), d, ring) for d in range(1, ring)]
    attended_own = jnp.concatenate([rows_of(attended, me, tokens)] + mine, axis=1)
    middle = resid + contract_cols(attended_own, out_t)

    scale_ffn, normed_ffn = norm_rows(middle, gain_ffn)
    other_normed = swap(normed_ffn, ring)
    ffn_weights = (w_gate.T, w_up.T, down_projection_weight, w_first, ring * head_cols)
    own = feed_forward(normed_ffn, out_grad, *ffn_weights)
    other = feed_forward(other_normed, other_grad, *ffn_weights)
    shards = (len(own) - 1) // 3
    other_d_normed = swap(other[-1].astype(bf16), ring)
    rights, groups = [], []
    for s in range(shards):
        for n in range(1, 4):
            rights += [own[3 * s + n % 3], other[3 * s + n % 3]]
            groups.append(n // 3)
    sums = weight_grads(
        (normed_ffn, other_normed, out_grad, other_grad), rights, tuple(groups), ring * head_cols)
    sums, other_d_normed = lax.optimization_barrier((sums, other_d_normed))
    d_normed_ffn = own[-1] + other_d_normed.astype(f32)
    d_middle = out_grad.astype(f32) + norm_back(d_normed_ffn, middle, scale_ffn, gain_ffn)
    d_middle_low = d_middle.astype(bf16)
    d_attended_own = dot(d_middle_low, out_t).astype(bf16)

    def block(d):
        return d_attended_own[:, d * head_cols : (d + 1) * head_cols]

    d_attended = jnp.zeros((ring * tokens, head_cols), bf16)
    d_attended = lax.dynamic_update_slice_in_dim(d_attended, block(0), me * tokens, 0)
    for d in range(1, ring):
        d_attended = lax.dynamic_update_slice_in_dim(
            d_attended, along(block(d), -d, ring), ((me + d) % ring) * tokens, 0)

    d_middle_late, attended_late, hiddens = lax.optimization_barrier(
        (d_middle_low, attended_own, [(own[3 * s], other[3 * s]) for s in range(shards)]))
    sums = lax.dynamic_update_slice(sums, contract_rows(d_middle_late, attended_late).astype(bf16), (0, 0))
    own_out, other_out = 0.0, 0.0
    for s, (own_hidden, other_hidden) in enumerate(hiddens):
        if s == 0:
            down, dims = down_projection_weight, NN
        else:
            at = ring * head_cols + 3 * padded * (s - 1) + 2 * padded
            down, dims = w_first[:, at : at + units], NT
        own_out = own_out + dot(own_hidden, down, dims)
        other_out = other_out + dot(other_hidden, down, dims)
    other_out = other_out.astype(bf16)
    sums, d_attended, w_project_all, other_out, own_out = lax.optimization_barrier(
        (sums, d_attended, w_project_all, other_out, own_out))
    ffn_sums = lax.psum_scatter(sums, "wide", scatter_dimension=0, tiled=True)
    other_out = swap(other_out, ring)

    d_query, d_keys, d_values, d_scores = attention_backward(
        page_lengths, projected, exps, d_attended, attended, rinv)
    d_project = jnp.concatenate([d_query, d_keys, d_values], axis=1)
    d_project, other_out, middle_late = lax.optimization_barrier((d_project, other_out, middle))
    layer_out = (middle_late + own_out + other_out.astype(f32)).astype(bf16)
    mine = [along(rows_of(d_project, (me + d) % ring, tokens), d, ring) for d in range(1, ring)]
    last_sums = contract_rows(normed_attn_all, d_project).astype(bf16)
    last_sums, ffn_sums = lax.optimization_barrier((last_sums, ffn_sums))
    sum_project = lax.psum_scatter(last_sums, "wide", scatter_dimension=0, tiled=True).astype(f32)

    last_sums, d_scores = lax.optimization_barrier((last_sums, d_scores))
    raw_lay, raw_rel = table_grads(page_lengths, d_scores, codes)
    raw_lay, raw_rel, mine, sum_project = lax.optimization_barrier((raw_lay, raw_rel, mine, sum_project))
    d_project_own = jnp.concatenate([rows_of(d_project, me, tokens)] + mine, axis=1)
    d_normed_attn = contract_cols(d_project_own, w_project_all)
    in_grad = d_middle + norm_back(d_normed_attn, resid, scale_attn, gain_attn)
    grad_relative = bucket_sums(raw_rel, heads)
    grad_layout = bucket_sums(raw_lay, heads)
    tables = jnp.concatenate(
        [grad_relative.reshape(wide, -1, heads), grad_layout.reshape(wide, -1, heads)], axis=1)
    n_rel = grad_relative.shape[0] // wide
    reach = wide // 2
    while reach >= 1:
        bit = (my_wide // reach) % 2
        keep = lax.dynamic_slice_in_dim(tables, bit * reach, reach, 0)
        give = lax.dynamic_slice_in_dim(tables, (1 - bit) * reach, reach, 0)
        tables = keep + lax.ppermute(give, "wide", [(i, i ^ reach) for i in range(wide)])
        reach //= 2
    sum_tables = tables[0]

    first = ring * head_cols

    def stripe(shard, n):
        at = first + padded * (3 * shard + n)
        return ffn_sums[:, at : at + units]

    sum_gate, sum_up, sum_down = [stripe(0, n).astype(f32) for n in range(3)]
    for s in range(1, shards):
        at = first + 3 * padded * s
        block = along(ffn_sums[:, at : at + 3 * padded], -2 * s, ring).astype(f32)
        sum_gate += block[:, :units]
        sum_up += block[:, padded : padded + units]
        sum_down += block[:, 2 * padded : 2 * padded + units]
    sum_wout = ffn_sums[:, :head_cols].astype(f32)
    for d in range(1, ring):
        sum_wout += along(ffn_sums[:, d * head_cols : (d + 1) * head_cols], -d, ring).astype(f32)

    gain_terms = jnp.stack(
        [
            jnp.sum(own_rows_project.astype(f32) * sum_project, axis=1),
            jnp.sum(own_rows_gate.astype(f32) * sum_gate + own_rows_up.astype(f32) * sum_up, axis=1),
        ]
    )
    share = part // ring

    def gain_share(index):
        return lax.dynamic_slice_in_dim(gain_terms, index * share, share, 1)

    gain_sum = gain_share(me)
    for d in range(1, ring):
        gain_sum = gain_sum + along(gain_share((me + d) % ring), d, ring)
    place = my_wide * part + me * share
    gains = lax.dynamic_slice_in_dim(jnp.stack([gain_attn, gain_ffn]), place, share, 1)
    gain_grads = gain_sum / gains
    return (
        layer_out,
        in_grad,
        gain_grads[0],
        sum_project[:, :head_cols],
        sum_project[:, head_cols : 2 * head_cols],
        sum_project[:, 2 * head_cols :],
        sum_wout.T,
        sum_tables[:n_rel],
        sum_tables[n_rel:],
        gain_grads[1],
        sum_gate,
        sum_up,
        sum_down.T,
    )


def solution(mesh):
    placed = (
        P(("wide", "narrow"), None),
        P(("wide", "narrow"), None),
        P(),
        P(None, "narrow"),
        P(None, "narrow"),
        P(None, "narrow"),
        P("narrow", None),
        P(None, "narrow"),
        P(None, "narrow"),
        P(),
        P(None, "narrow"),
        P(None, "narrow"),
        P("narrow", None),
        P("wide", None),
        P("wide"),
        P("wide", None),
        P("wide", None),
    )
    return jax.shard_map(
        functools.partial(on_device, mesh.shape["wide"], mesh.shape["narrow"]),
        mesh=mesh,
        in_specs=placed,
        out_specs=(
            P(("wide", "narrow"), None),
            P(("wide", "narrow"), None),
            P(("wide", "narrow")),
            P("wide", "narrow"),
            P("wide", "narrow"),
            P("wide", "narrow"),
            P("narrow", "wide"),
            P("wide", "narrow"),
            P("wide", "narrow"),
            P(("wide", "narrow")),
            P("wide", "narrow"),
            P("wide", "narrow"),
            P("narrow", "wide"),
        ),
        check_vma=False,
    )
```

```python
import functools
import jax
import jax.numpy as jnp
from jax import lax
from jax.experimental import pallas as pl
from jax.experimental.pallas import tpu as pltpu
from jax.sharding import PartitionSpec as P

DH = 64
BIAS_SCALE = 4096.0
LOG2E = 1.4426950408889634
f32 = jnp.float32
bf16 = jnp.bfloat16
NT = (((1,), (1,)), ((), ()))
NN = (((1,), (0,)), ((), ()))


def dot(a, b, dims=NN):
    return lax.dot_general(a, b, dims, preferred_element_type=f32)


def key_window(len_ref, first, last, count, width):
    ends = []
    total = 0
    for p in range(len_ref.shape[1]):
        total = total + len_ref[0, p]
        ends.append(total)
    start = 0
    stop = count
    for e in ends:
        start = jnp.where(e <= first, e, start)
    for e in reversed(ends):
        stop = jnp.where(e > last, e, stop)
    base = (start // 128) * 128
    steps = (stop - base + width - 1) // width
    base = jnp.minimum(base, count - steps * width)
    return ends, base, steps


def for_chunks(base, steps, width, group, body):
    def many(j, carry):
        body(pl.multiple_of(base + j * (group * width), 128), group * width)
        return carry

    def single(j, carry):
        body(pl.multiple_of(base + j * width, 128), width)
        return carry

    if group > 1:
        lax.fori_loop(0, steps // group, many, 0)
    lax.fori_loop((steps // group) * group if group > 1 else 0, steps, single, 0)


def own_half(shape, head):
    lane = lax.broadcasted_iota(jnp.int32, shape, len(shape) - 1)
    return (lane < DH) if head % 2 == 0 else (lane >= DH)


def fill_values(vext, v_ref, heads):
    for h in range(heads):
        vp = v_ref[:, (h // 2) * 128:(h // 2 + 1) * 128]
        vext[h] = jnp.where(own_half(vp.shape, h), vp, jnp.ones_like(vp))


def half_norms(rows):
    lane = lax.broadcasted_iota(jnp.int32, (128, 128), 0)
    column = lax.broadcasted_iota(jnp.int32, (128, 128), 1)
    same = ((lane < DH) == (column < DH)).astype(bf16)
    squares = (rows.astype(f32) * rows.astype(f32)).astype(bf16)
    return jnp.max(dot(squares, same)) * f32(1.02)


def forward_kernel(len_ref, q_ref, k_ref, v_ref, rel_ref, lay_ref, tab_ref, kmask_ref,
                   att_ref, rinv_ref, e_ref, *rest, width, group, pair):
    code_ref = rest[0] if len(rest) == 7 else None
    s_scr, m_scr, acc_scr, vext, colcode, knorm = rest[-6:]
    tq, count = rel_ref.shape
    heads, pairs = 2, 1
    i = pl.program_id(0)
    t0 = i * tq
    ends, base, steps = key_window(len_ref, t0, t0 + tq - 1, count, width)

    @pl.when(i == 0)
    def _():
        fill_values(vext, v_ref, heads)
        pos = lax.broadcasted_iota(jnp.int32, (8, count), 1)
        page = jnp.zeros((8, count), jnp.int32)
        for e in ends:
            page = page + (pos >= e).astype(jnp.int32)
        colcode[...] = jnp.where(kmask_ref[...] == 1, page, -1)
        for p in range(pairs):
            knorm[p] = half_norms(k_ref[:, p * 128:(p + 1) * 128])

    rowpos = lax.broadcasted_iota(jnp.int32, (tq, 128), 0) + t0
    rowpage = jnp.zeros((tq, 128), jnp.int32)
    for e in ends:
        rowpage = rowpage + (rowpos >= e).astype(jnp.int32)
    lanes = lax.broadcasted_iota(jnp.int32, (tq, 128), 1)
    scaled = []
    largest = f32(0.0)
    for h in range(heads):
        qp = q_ref[:, (h // 2) * 128:(h // 2 + 1) * 128]
        scaled.append(jnp.where(own_half(qp.shape, h), qp * bf16(BIAS_SCALE), jnp.zeros_like(qp)))
        if h % 2 == 0:
            largest = jnp.maximum(largest, half_norms(qp) * knorm[h // 2])
    tabs = [[jnp.broadcast_to(tab_ref[2 * (pair + p) + r:2 * (pair + p) + r + 1, :], (tq, 128)) for r in range(2)]
            for p in range(pairs)]

    def scores(c0, width, use):
        raw = [dot(scaled[h], k_ref[pl.ds(c0, width), (h // 2) * 128:(h // 2 + 1) * 128], NT)
               for h in range(heads)]
        for half in range(width // 128):
            cc = pl.multiple_of(c0 + half * 128, 128)
            rel = rel_ref[:, pl.ds(cc, 128)]
            lay = lay_ref[:, pl.ds(cc, 128)]
            if code_ref is not None:
                code_ref[:, pl.ds(cc, 128)] = (rel + lay * 32).astype(jnp.int16)
            col = jnp.broadcast_to(colcode[0:1, pl.ds(cc, 128)], (tq, 128))
            seen = (rowpage == col) | (rowpos == lanes + cc)
            hide = jnp.where(seen, f32(0.0), f32(-1e30))
            for p in range(pairs):
                word = (jnp.take_along_axis(tabs[p][0], rel, axis=1, mode="promise_in_bounds")
                        + jnp.take_along_axis(tabs[p][1], lay, axis=1, mode="promise_in_bounds"))
                parts = ((word & 0xFFFF).astype(f32), (word >> 16).astype(f32))
                for r in range(2):
                    h = 2 * p + r
                    use(h, half, cc, raw[h][:, half * 128:(half + 1) * 128] + parts[r] + hide)

    for h in range(heads):
        acc_scr[h] = jnp.zeros((tq, 128), f32)
    bounded = jnp.sqrt(largest) + 8.0 <= 60.0

    @pl.when(bounded)
    def _():
        def chunk(c0, size):
            pieces = {}

            def use(h, half, cc, s):
                e = jnp.exp2(s * f32(LOG2E / BIAS_SCALE)).astype(bf16)
                e_ref[h, :, pl.ds(cc, 128)] = e
                pieces[h, half] = e

            scores(c0, size, use)
            for h in range(heads):
                e = jnp.concatenate([pieces[h, half] for half in range(size // 128)], axis=1)
                acc_scr[h] += dot(e, vext[h, pl.ds(c0, size), :])

        for_chunks(base, steps, width, group, chunk)

    @pl.when(jnp.logical_not(bounded))
    def _():
        for h in range(heads):
            m_scr[h] = jnp.full((tq, 128), -3e38, f32)

        def first(j, carry):
            def use(h, half, cc, s):
                s_scr[h, :, pl.ds(cc, 128)] = s
                m_scr[h] = jnp.maximum(m_scr[h], s)

            scores(pl.multiple_of(base + j * width, 128), width, use)
            return carry

        lax.fori_loop(0, steps, first, 0)
        for h in range(heads):
            top = jnp.max(m_scr[h], axis=1, keepdims=True)

            def second(j, carry):
                c0 = pl.multiple_of(base + j * width, 128)
                e = jnp.exp2((s_scr[h, :, pl.ds(c0, width)] - top) * f32(LOG2E / BIAS_SCALE)).astype(bf16)
                e_ref[h, :, pl.ds(c0, width)] = e
                acc_scr[h] += dot(e, vext[h, pl.ds(c0, width), :])
                return carry

            lax.fori_loop(0, steps, second, 0)

    low = own_half((tq, 128), 0)
    for p in range(pairs):
        even, odd = acc_scr[2 * p], acc_scr[2 * p + 1]
        rinv = 1.0 / pltpu.roll(jnp.where(low, odd, even), DH, 1)
        att_ref[:, p * 128:(p + 1) * 128] = (jnp.where(low, even, odd) * rinv).astype(bf16)
        rinv_ref[:, p * 128:(p + 1) * 128] = rinv


def attention_forward(page_lengths, proj, rel, lay, tab, kmask, pair, tq=256, width=256, group=1):
    count = proj.shape[0]
    pairs = proj.shape[1] // (3 * 128)
    tile = lambda i: (i, 0)
    return pl.pallas_call(
        functools.partial(forward_kernel, width=width, group=group, pair=pair),
        grid=(count // tq,),
        in_specs=[
            pl.BlockSpec(memory_space=pltpu.SMEM),
            pl.BlockSpec((tq, 128), lambda i: (i, pair)),
            pl.BlockSpec((count, 128), lambda i: (0, pairs + pair)),
            pl.BlockSpec((count, 128), lambda i: (0, 2 * pairs + pair)),
            pl.BlockSpec((tq, count), tile),
            pl.BlockSpec((tq, count), tile),
            pl.BlockSpec(tab.shape, lambda i: (0, 0)),
            pl.BlockSpec((1, count), lambda i: (0, 0)),
        ],
        out_specs=[
            pl.BlockSpec((tq, 128), tile),
            pl.BlockSpec((tq, 128), tile),
            pl.BlockSpec((2, tq, count), lambda i: (0, i, 0)),
        ] + [pl.BlockSpec((tq, count), tile)] * (pair == 0),
        out_shape=[
            jax.ShapeDtypeStruct((count, 128), bf16),
            jax.ShapeDtypeStruct((count, 128), f32),
            jax.ShapeDtypeStruct((2, count, count), bf16),
        ] + [jax.ShapeDtypeStruct((count, count), jnp.int16)] * (pair == 0),
        scratch_shapes=[
            pltpu.VMEM((2, tq, count), f32),
            pltpu.VMEM((2, tq, 128), f32),
            pltpu.VMEM((2, tq, 128), f32),
            pltpu.VMEM((2, count, 128), bf16),
            pltpu.VMEM((8, count), jnp.int32),
            pltpu.SMEM((1,), f32),
        ],
        compiler_params=pltpu.CompilerParams(vmem_limit_bytes=56 << 20),
        cost_estimate=pl.CostEstimate(
            flops=count * count * 512, bytes_accessed=80 << 20, transcendentals=count * count),
        name="attention_forward",
    )(page_lengths, proj, proj, proj, rel, lay, tab, kmask.reshape(1, count))


def bias_words(rel_table, layout_table):
    def pack(table):
        whole = jnp.round(table.astype(f32) * BIAS_SCALE).astype(jnp.int32)
        low = jnp.clip(whole[:, 0::2] + 16384, 0, 32767)
        high = jnp.clip(whole[:, 1::2], -16384, 16383)
        words = (high * 65536 + low).T
        return jnp.pad(words, ((0, 0), (0, 128 - words.shape[1])))
    both = jnp.stack([pack(rel_table), pack(layout_table)], axis=1)
    return both.reshape(-1, 128)


def signs(code, shift, bits):
    return [jnp.where((code & jnp.int16(1 << (shift + b))) == 0, bf16(1.0), bf16(-1.0))
            for b in range(bits)]


def walsh(sign_list):
    out = [None]
    for s in sign_list:
        out = out + [s if o is None else o * s for o in out]
    return out


def backward_kernel(len_ref, q_ref, k_ref, v_ref, da_ref, *refs, width, heads, group):
    tq = q_ref.shape[0]
    count = k_ref.shape[0]
    pairs = heads // 2
    e_refs, att_refs, rinv_refs = refs[:pairs], refs[pairs:2 * pairs], refs[2 * pairs:3 * pairs]
    dq_ref, dk_ref, dv_ref, ds_ref = refs[3 * pairs:3 * pairs + 4]
    vext, lhs_scr, dat_scr, qt_scr, dq_scr, dkt, dvt = refs[3 * pairs + 4:]
    i = pl.program_id(0)
    t0 = i * tq
    ends, base, steps = key_window(len_ref, t0, t0 + tq - 1, count, width)

    @pl.when(i == 0)
    def _():
        fill_values(vext, v_ref, heads)
        dkt[...] = jnp.zeros_like(dkt)
        dvt[...] = jnp.zeros_like(dvt)

    low = own_half((tq, 128), 0)
    lane = lax.broadcasted_iota(jnp.int32, (tq, 128), 1)
    first_part = (lane & 32) == 0
    for p in range(pairs):
        cols = slice(p * 128, (p + 1) * 128)
        da = (da_ref[:, cols].astype(f32) * rinv_refs[p][...]).astype(bf16)
        daf = da.astype(f32)
        prod = daf * att_refs[p][...].astype(f32)
        for r in range(2):
            own = low if r == 0 else jnp.logical_not(low)
            delta = jnp.sum(jnp.where(own, prod, 0.0), axis=1, keepdims=True) * f32(-1.0 / 32)
            high = delta.astype(bf16).astype(f32)
            rest = delta - high
            lhs_scr[2 * p + r] = jnp.where(own, daf, jnp.where(first_part, high, rest)).astype(bf16)
        dat_scr[p] = daf.T.astype(bf16)
        qt_scr[p] = q_ref[:, cols].astype(f32).T.astype(bf16)
        dq_scr[p] = jnp.zeros((tq, 128), f32)

    def chunk(c0, size):
        here = pl.ds(c0, size)
        for p in range(pairs):
            kp = k_ref[here, p * 128:(p + 1) * 128]
            dqs = []
            for r in range(2):
                h = 2 * p + r
                rows = slice(r * DH, (r + 1) * DH)
                e = e_refs[p][r, :, here]
                d = dot(lhs_scr[h], vext[h, here, :], NT)
                ds = (e.astype(f32) * d).astype(bf16)
                ds_ref[h, :, here] = ds
                dqs.append(dot(ds, kp))
                dkt[p, rows, here] += dot(qt_scr[p, rows, :], ds)
                dvt[p, rows, here] += dot(dat_scr[p, rows, :], e)
            dq_scr[p] += jnp.where(low, dqs[0], dqs[1])

    for_chunks(base, steps, width, group, chunk)
    for p in range(pairs):
        dq_ref[:, p * 128:(p + 1) * 128] = dq_scr[p].astype(bf16)

    @pl.when(i == pl.num_programs(0) - 1)
    def _():
        for p in range(pairs):
            for c in range(0, count, 256):
                dk_ref[c:c + 256, p * 128:(p + 1) * 128] = dkt[p, :, c:c + 256].T.astype(bf16)
                dv_ref[c:c + 256, p * 128:(p + 1) * 128] = dvt[p, :, c:c + 256].T.astype(bf16)


def attention_backward(page_lengths, proj, exps, d_att, atts, rinvs, tq=256, width=256, group=2):
    count = proj.shape[0]
    hc = proj.shape[1] // 3
    heads = hc // DH
    pairs = heads // 2
    grid = (count // tq,)
    tile = lambda i: (i, 0)
    fixed = lambda i: (0, 0)
    return pl.pallas_call(
        functools.partial(backward_kernel, width=width, heads=heads, group=group),
        grid=grid,
        in_specs=[
            pl.BlockSpec(memory_space=pltpu.SMEM),
            pl.BlockSpec((tq, hc), tile),
            pl.BlockSpec((count, hc), lambda i: (0, 1)),
            pl.BlockSpec((count, hc), lambda i: (0, 2)),
            pl.BlockSpec((tq, hc), tile),
        ] + [pl.BlockSpec((2, tq, count), lambda i: (0, i, 0))] * pairs + [pl.BlockSpec((tq, 128), tile)] * (2 * pairs),
        out_specs=[
            pl.BlockSpec((tq, hc), tile),
            pl.BlockSpec((count, hc), fixed),
            pl.BlockSpec((count, hc), fixed),
            pl.BlockSpec((heads, tq, count), lambda i: (0, i, 0)),
        ],
        out_shape=[
            jax.ShapeDtypeStruct((count, hc), bf16),
            jax.ShapeDtypeStruct((count, hc), bf16),
            jax.ShapeDtypeStruct((count, hc), bf16),
            jax.ShapeDtypeStruct((heads, count, count), bf16),
        ],
        scratch_shapes=[
            pltpu.VMEM((heads, count, 128), bf16),
            pltpu.VMEM((heads, tq, 128), bf16),
            pltpu.VMEM((pairs, 128, tq), bf16),
            pltpu.VMEM((pairs, 128, tq), bf16),
            pltpu.VMEM((pairs, tq, 128), f32),
            pltpu.VMEM((pairs, 128, count), f32),
            pltpu.VMEM((pairs, 128, count), f32),
        ],
        compiler_params=pltpu.CompilerParams(vmem_limit_bytes=56 << 20),
        cost_estimate=pl.CostEstimate(
            flops=heads * count * count * 512, bytes_accessed=150 << 20, transcendentals=0),
        name="attention_backward",
    )(page_lengths, proj, proj, proj, d_att, *exps, *atts, *rinvs)


def table_kernel(len_ref, ds_ref, code_ref, hl_ref, hr_ref, *bufs, width, parts):
    heads, tq, count = ds_ref.shape
    i = pl.program_id(0)
    t0 = i * tq
    ends, base, steps = key_window(len_ref, t0, t0 + tq - 1, count, width)

    @pl.when(i == 0)
    def _():
        hl_ref[...] = jnp.zeros_like(hl_ref)
        hr_ref[...] = jnp.zeros_like(hr_ref)

    one = jnp.ones((16, width), bf16)

    def chunk(j, carry):
        c0 = pl.multiple_of(base + j * width, 128)
        here = pl.ds(c0, width)
        blocks = tq // 16 // parts
        for part in range(parts):
            left, blay, brel = bufs[3 * part:3 * part + 3]
            for b in range(blocks):
                at = 16 * (part * blocks + b)
                rows = slice(at, at + 16)
                span = slice(b * width, (b + 1) * width)
                code = code_ref[rows, here]
                rel_signs = signs(code, 0, 5)
                lay_signs = signs(code, 5, 6)
                left_lay = walsh(lay_signs[:2])[1:]
                for h in range(heads):
                    ds = ds_ref[h, rows, here]
                    for a, func in enumerate(left_lay + [None, rel_signs[0]]):
                        place = 16 * (a * heads + h)
                        left[place:place + 16, span] = ds if func is None else ds * func
                for n, func in enumerate(walsh(lay_signs[2:])):
                    blay[16 * n:16 * (n + 1), span] = one if func is None else func
                for n, func in enumerate(walsh(rel_signs[1:])):
                    brel[16 * n:16 * (n + 1), span] = one if func is None else func
            hl_ref[...] += dot(left[:64 * heads, :], blay[...], NT)
            hr_ref[...] += dot(left[48 * heads:80 * heads, :], brel[...], NT)
        return carry

    lax.fori_loop(0, steps, chunk, 0)


def table_grads(page_lengths, ds, code, tq=256, width=256, parts=2):
    heads, count, _ = ds.shape
    deep = tq // 16 * width // parts
    fixed = lambda i: (0, 0)
    return pl.pallas_call(
        functools.partial(table_kernel, width=width, parts=parts),
        grid=(count // tq,),
        in_specs=[
            pl.BlockSpec(memory_space=pltpu.SMEM),
            pl.BlockSpec((heads, tq, count), lambda i: (0, i, 0)),
            pl.BlockSpec((tq, count), lambda i: (i, 0)),
        ],
        out_specs=[
            pl.BlockSpec((64 * heads, 256), fixed),
            pl.BlockSpec((32 * heads, 256), fixed),
        ],
        out_shape=[
            jax.ShapeDtypeStruct((64 * heads, 256), f32),
            jax.ShapeDtypeStruct((32 * heads, 256), f32),
        ],
        scratch_shapes=[
            pltpu.VMEM((80 * heads, deep), bf16),
            pltpu.VMEM((256, deep), bf16),
            pltpu.VMEM((256, deep), bf16),
        ] * parts,
        compiler_params=pltpu.CompilerParams(vmem_limit_bytes=56 << 20),
        cost_estimate=pl.CostEstimate(
            flops=heads * count * count * 512, bytes_accessed=150 << 20, transcendentals=0),
        name="table_grads",
    )(page_lengths, ds, code)


def bucket_sums(raw, heads):
    right = raw.shape[1] // 16
    left = raw.shape[0] // (16 * heads)
    cube = raw.reshape(left, heads, 16, right, 16)
    traced = jnp.sum(cube * jnp.eye(16, dtype=f32)[None, None, :, None, :], axis=(2, 4))
    if left == 4:
        traced = jnp.concatenate([traced[3:], traced[:3]], axis=0)

    def table(n):
        v = lax.iota(jnp.int32, n)
        both = v[:, None] & v[None, :]
        return (1 - 2 * (lax.population_count(both) & 1)).astype(f32)

    out = jnp.einsum("ahn,ax,ny->yxh", traced, table(left), table(right), precision=lax.Precision.HIGHEST)
    return out.reshape(left * right, heads) / (left * right)


TANH_SLOPE = 0.7978845608028654
CUBE = 0.044715


def feed_forward_kernel(skip, shards, x_ref, g_ref, wg_ref, wu_ref, wd_ref, far_ref, *outs):
    units = wg_ref.shape[0]
    step = pad_lanes(units)
    dn_ref = outs[-1]
    x = x_ref[...]
    g = g_ref[...]
    total = None
    for s in range(shards):
        if s == 0:
            wg, wu = wg_ref[...], wu_ref[...]
            d_hidden = dot(g, wd_ref[...], NT)
            ahead, back = NT, NN
        else:
            at = skip + 3 * step * (s - 1)
            wg = far_ref[:, at:at + units]
            wu = far_ref[:, at + step:at + step + units]
            d_hidden = dot(g, far_ref[:, at + 2 * step:at + 2 * step + units])
            ahead, back = NN, NT
        gate = dot(x, wg, ahead)
        up = dot(x, wu, ahead)
        square = gate * gate
        t = jnp.tanh(TANH_SLOPE * gate * (1.0 + CUBE * square))
        half = 0.5 + 0.5 * t
        gelu = gate * half
        slope = half + (0.5 * TANH_SLOPE) * gate * (1.0 - t * t) * (1.0 + (3 * CUBE) * square)
        d_gate = (d_hidden * up * slope).astype(bf16)
        d_up = (d_hidden * gelu).astype(bf16)
        outs[3 * s][...] = (gelu * up).astype(bf16)
        outs[3 * s + 1][...] = d_gate
        outs[3 * s + 2][...] = d_up
        value = dot(d_gate, wg, back) + dot(d_up, wu, back)
        total = value if total is None else total + value
    dn_ref[...] = total


def feed_forward(x, g, w_gate_t, w_up_t, w_down, far, skip, tile=256):
    tokens, features = x.shape
    units = w_down.shape[0]
    shards = 1 + (far.shape[1] - skip) // (3 * pad_lanes(units))
    tile = min(tile, tokens)
    rows = lambda n: pl.BlockSpec((tile, n), lambda i: (i, 0))
    whole = lambda a: pl.BlockSpec(a.shape, lambda i: (0, 0))
    return pl.pallas_call(
        functools.partial(feed_forward_kernel, skip, shards),
        grid=(tokens // tile,),
        in_specs=[rows(features), rows(features), whole(w_gate_t), whole(w_up_t), whole(w_down), whole(far)],
        out_specs=[rows(units)] * (3 * shards) + [rows(features)],
        out_shape=[jax.ShapeDtypeStruct((tokens, units), bf16)] * (3 * shards)
        + [jax.ShapeDtypeStruct((tokens, features), f32)],
        compiler_params=pltpu.CompilerParams(vmem_limit_bytes=56 << 20),
        cost_estimate=pl.CostEstimate(
            flops=10 * tokens * features * units * shards, bytes_accessed=14 << 20,
            transcendentals=tokens * units * shards),
        name="feed_forward",
    )(x, g, w_gate_t, w_up_t, w_down, far)


def pad_lanes(n):
    return (n + 127) // 128 * 128


def weight_grads_kernel(skip, n_left, n_right, *refs):
    lefts = refs[:2 * n_left]
    rights = refs[2 * n_left:-1]
    out_ref = refs[-1]
    rows_in = (((0,), (0,)), ((), ()))
    place = skip
    for n, left in enumerate(n_right):
        a, b = rights[2 * n], rights[2 * n + 1]
        size = a.shape[1]
        value = dot(lefts[2 * left][...], a[...], rows_in) + dot(lefts[2 * left + 1][...], b[...], rows_in)
        out_ref[:, place:place + size] = value.astype(bf16)
        if pad_lanes(size) > size:
            out_ref[:, place + size:place + pad_lanes(size)] = jnp.zeros(
                (out_ref.shape[0], pad_lanes(size) - size), bf16)
        place += pad_lanes(size)


def weight_grads(lefts, rights, groups, skip, tile=256):
    features = lefts[0].shape[1]
    columns = skip + sum(pad_lanes(r.shape[1]) for r in rights[::2])
    column = lambda a: pl.BlockSpec((a.shape[0], tile), lambda i: (0, i))
    whole = lambda a: pl.BlockSpec(a.shape, lambda i: (0, 0))
    return pl.pallas_call(
        functools.partial(weight_grads_kernel, skip, len(lefts) // 2, groups),
        grid=(features // tile,),
        in_specs=[column(a) for a in lefts] + [whole(a) for a in rights],
        out_specs=pl.BlockSpec((tile, columns), lambda i: (i, 0)),
        out_shape=jax.ShapeDtypeStruct((features, columns), bf16),
        compiler_params=pltpu.CompilerParams(vmem_limit_bytes=56 << 20),
        cost_estimate=pl.CostEstimate(
            flops=4 * features * columns * lefts[0].shape[0], bytes_accessed=26 << 20, transcendentals=0),
        name="weight_grads",
    )(*lefts, *rights)


epsilon = 1e-06


def contract_rows(left, right):
    return lax.dot_general(
        left, right, (((0,), (0,)), ((), ())), preferred_element_type=jnp.float32
    )


def contract_cols(left, right):
    return lax.dot_general(
        left, right, (((1,), (1,)), ((), ())), preferred_element_type=jnp.float32
    )


def norm_rows(rows, gain):
    scale = lax.rsqrt(jnp.mean(rows * rows, axis=-1, keepdims=True) + epsilon)
    return (scale, (rows * scale * gain).astype(jnp.bfloat16))


def norm_back(d_normed, rows, scale, gain):
    shaped = d_normed * gain
    cubed = scale * scale * scale
    return scale * shaped - rows * cubed * jnp.mean(shaped * rows, axis=-1, keepdims=True)


def along(array, shift, ring):
    return lax.ppermute(array, "narrow", [(i, (i + shift) % ring) for i in range(ring)])


def swap(array, ring):
    return lax.ppermute(array, "narrow", [(i, i ^ 1) for i in range(ring)])


def rows_of(array, index, count):
    return lax.dynamic_slice_in_dim(array, index * count, count, 0)


def on_device(
    wide,
    ring,
    layer_input,
    out_grad,
    norm_attn_gain,
    w_query,
    w_key,
    w_value,
    w_out,
    rel_table,
    layout_table,
    norm_ffn_gain,
    w_gate,
    w_up,
    down_projection_weight,
    page_lengths,
    key_mask,
    rel_bucket,
    layout_bucket,
):
    tokens, width = layer_input.shape
    head_cols = w_query.shape[1]
    heads = head_cols // DH
    units = w_gate.shape[1]
    padded = pad_lanes(units)
    part = width // wide
    me = lax.axis_index("narrow")
    my_wide = lax.axis_index("wide")
    gain_attn = norm_attn_gain.astype(f32)
    gain_ffn = norm_ffn_gain.astype(f32)
    resid = layer_input.astype(f32)

    scale_attn, normed_attn = norm_rows(resid, gain_attn)
    normed_attn_all = lax.all_gather(normed_attn, "narrow", axis=0, tiled=True)

    w_project = jnp.concatenate([w_query, w_key, w_value], axis=1)
    own_rows_gate = rows_of(w_gate, my_wide, part)
    own_rows_up = rows_of(w_up, my_wide, part)
    own_rows_project = rows_of(w_project, my_wide, part)
    down_piece = lax.dynamic_slice_in_dim(down_projection_weight, my_wide * part, part, 1).T
    out_piece = lax.dynamic_slice_in_dim(w_out, my_wide * part, part, 1).T
    ffn_piece = jnp.concatenate(
        [jnp.pad(piece, ((0, 0), (0, padded - units))) for piece in (own_rows_gate, own_rows_up, down_piece)], axis=1)
    normed_attn_all, out_piece, ffn_piece, late_grad = lax.optimization_barrier(
        (normed_attn_all, out_piece, ffn_piece, out_grad))
    ffn_pieces = [along(ffn_piece, d, ring) for d in range(2, ring, 2)]
    out_pieces = [out_piece] + [along(out_piece, d, ring) for d in range(1, ring)]
    other_grad = swap(late_grad, ring)

    projected = dot(normed_attn_all, w_project).astype(bf16)
    words = bias_words(rel_table, layout_table)
    pairs = head_cols // 128
    bucket_args = (rel_bucket, layout_bucket, words, key_mask)
    *first_pair, codes = attention_forward(page_lengths, projected, *bucket_args, 0)
    first_pair[0], out_pieces, ffn_pieces, other_grad, late_project = lax.optimization_barrier(
        (first_pair[0], out_pieces, ffn_pieces, other_grad, own_rows_project))
    first_weights = jnp.concatenate(out_pieces + ffn_pieces, axis=1)

    def to_owners(a):
        return [rows_of(a, me, tokens)] + [
            along(rows_of(a, (me + d) % ring, tokens), d, ring) for d in range(1, ring)]

    sent = [to_owners(first_pair[0])]
    project_pieces = [own_rows_project] + [along(late_project, d, ring) for d in range(1, ring)]
    results = [first_pair]
    if pairs > 1:
        late_projected, first_weights = lax.optimization_barrier((projected, first_weights))
        results += [list(attention_forward(page_lengths, late_projected, *bucket_args, p)) for p in range(1, pairs)]
    w_first = lax.all_gather(first_weights, "wide", axis=0, tiled=True)
    out_t = w_first[:, : ring * head_cols]
    if pairs > 1:
        results[1][0], project_pieces, sent[0] = lax.optimization_barrier((results[1][0], project_pieces, sent[0]))
    w_project_all = lax.all_gather(jnp.concatenate(project_pieces, axis=1), "wide", axis=0, tiled=True)
    attended = [r[0] for r in results]
    sent += [to_owners(a) for a in attended[1:]]
    mine = [pieces[d] for d in range(ring) for pieces in sent]
    attended_own = jnp.concatenate(mine, axis=1)
    middle = resid + contract_cols(attended_own, out_t)

    scale_ffn, normed_ffn = norm_rows(middle, gain_ffn)
    other_normed = swap(normed_ffn, ring)
    ffn_weights = (w_gate.T, w_up.T, down_projection_weight, w_first, ring * head_cols)
    own = feed_forward(normed_ffn, out_grad, *ffn_weights)
    other = feed_forward(other_normed, other_grad, *ffn_weights)
    shards = (len(own) - 1) // 3
    other_d_normed = swap(other[-1].astype(bf16), ring)
    rights, groups = [], []
    for s in range(shards):
        for n in range(1, 4):
            rights += [own[3 * s + n % 3], other[3 * s + n % 3]]
            groups.append(n // 3)
    sums = weight_grads(
        (normed_ffn, other_normed, out_grad, other_grad), rights, tuple(groups), ring * head_cols)
    sums, other_d_normed = lax.optimization_barrier((sums, other_d_normed))
    d_normed_ffn = own[-1] + other_d_normed.astype(f32)
    d_middle = out_grad.astype(f32) + norm_back(d_normed_ffn, middle, scale_ffn, gain_ffn)
    d_middle_low = d_middle.astype(bf16)
    d_attended_own = dot(d_middle_low, out_t).astype(bf16)

    def block(d):
        return d_attended_own[:, d * head_cols : (d + 1) * head_cols]

    d_attended = jnp.zeros((ring * tokens, head_cols), bf16)
    d_attended = lax.dynamic_update_slice_in_dim(d_attended, block(0), me * tokens, 0)
    for d in range(1, ring):
        d_attended = lax.dynamic_update_slice_in_dim(
            d_attended, along(block(d), -d, ring), ((me + d) % ring) * tokens, 0)

    d_middle_late, attended_late, hiddens = lax.optimization_barrier(
        (d_middle_low, attended_own, [(own[3 * s], other[3 * s]) for s in range(shards)]))
    sums = lax.dynamic_update_slice(sums, contract_rows(d_middle_late, attended_late).astype(bf16), (0, 0))
    own_out, other_out = 0.0, 0.0
    for s, (own_hidden, other_hidden) in enumerate(hiddens):
        if s == 0:
            down, dims = down_projection_weight, NN
        else:
            at = ring * head_cols + 3 * padded * (s - 1) + 2 * padded
            down, dims = w_first[:, at : at + units], NT
        own_out = own_out + dot(own_hidden, down, dims)
        other_out = other_out + dot(other_hidden, down, dims)
    other_out = other_out.astype(bf16)
    sums, d_attended, w_project_all, other_out, own_out = lax.optimization_barrier(
        (sums, d_attended, w_project_all, other_out, own_out))
    ffn_sums = lax.psum_scatter(sums, "wide", scatter_dimension=0, tiled=True)
    other_out = swap(other_out, ring)

    d_query, d_keys, d_values, d_scores = attention_backward(
        page_lengths, projected, [r[2] for r in results], d_attended, attended, [r[1] for r in results])
    d_project = jnp.concatenate([d_query, d_keys, d_values], axis=1)
    d_project, other_out, middle_late = lax.optimization_barrier((d_project, other_out, middle))
    layer_out = (middle_late + own_out + other_out.astype(f32)).astype(bf16)
    mine = [along(rows_of(d_project, (me + d) % ring, tokens), d, ring) for d in range(1, ring)]
    last_sums = contract_rows(normed_attn_all, d_project).astype(bf16)

    last_sums, d_scores = lax.optimization_barrier((last_sums, d_scores))
    raw_lay, raw_rel = table_grads(page_lengths, d_scores, codes)
    raw_lay, raw_rel, mine, ffn_sums, last_sums = lax.optimization_barrier(
        (raw_lay, raw_rel, mine, ffn_sums, last_sums))
    sum_project = lax.psum_scatter(last_sums, "wide", scatter_dimension=0, tiled=True).astype(f32)
    d_project_own = jnp.concatenate([rows_of(d_project, me, tokens)] + mine, axis=1)
    d_normed_attn = contract_cols(d_project_own, w_project_all)
    in_grad = d_middle + norm_back(d_normed_attn, resid, scale_attn, gain_attn)
    grad_relative = bucket_sums(raw_rel, heads)
    grad_layout = bucket_sums(raw_lay, heads)
    tables = jnp.concatenate(
        [grad_relative.reshape(wide, -1, heads), grad_layout.reshape(wide, -1, heads)], axis=1)
    n_rel = grad_relative.shape[0] // wide
    reach = wide // 2
    while reach >= 1:
        bit = (my_wide // reach) % 2
        keep = lax.dynamic_slice_in_dim(tables, bit * reach, reach, 0)
        give = lax.dynamic_slice_in_dim(tables, (1 - bit) * reach, reach, 0)
        tables = keep + lax.ppermute(give, "wide", [(i, i ^ reach) for i in range(wide)])
        reach //= 2
    sum_tables = tables[0]

    first = ring * head_cols

    def stripe(shard, n):
        at = first + padded * (3 * shard + n)
        return ffn_sums[:, at : at + units]

    sum_gate, sum_up, sum_down = [stripe(0, n).astype(f32) for n in range(3)]
    for s in range(1, shards):
        at = first + 3 * padded * s
        block = along(ffn_sums[:, at : at + 3 * padded], -2 * s, ring).astype(f32)
        sum_gate += block[:, :units]
        sum_up += block[:, padded : padded + units]
        sum_down += block[:, 2 * padded : 2 * padded + units]
    sum_wout = ffn_sums[:, :head_cols].astype(f32)
    for d in range(1, ring):
        sum_wout += along(ffn_sums[:, d * head_cols : (d + 1) * head_cols], -d, ring).astype(f32)

    gain_terms = jnp.stack(
        [
            jnp.sum(own_rows_project.astype(f32) * sum_project, axis=1),
            jnp.sum(own_rows_gate.astype(f32) * sum_gate + own_rows_up.astype(f32) * sum_up, axis=1),
        ]
    )
    share = part // ring

    def gain_share(index):
        return lax.dynamic_slice_in_dim(gain_terms, index * share, share, 1)

    gain_sum = gain_share(me)
    for d in range(1, ring):
        gain_sum = gain_sum + along(gain_share((me + d) % ring), d, ring)
    place = my_wide * part + me * share
    gains = lax.dynamic_slice_in_dim(jnp.stack([gain_attn, gain_ffn]), place, share, 1)
    gain_grads = gain_sum / gains
    return (
        layer_out,
        in_grad,
        gain_grads[0],
        sum_project[:, :head_cols],
        sum_project[:, head_cols : 2 * head_cols],
        sum_project[:, 2 * head_cols :],
        sum_wout.T,
        sum_tables[:n_rel],
        sum_tables[n_rel:],
        gain_grads[1],
        sum_gate,
        sum_up,
        sum_down.T,
    )


def solution(mesh):
    placed = (
        P(("wide", "narrow"), None),
        P(("wide", "narrow"), None),
        P(),
        P(None, "narrow"),
        P(None, "narrow"),
        P(None, "narrow"),
        P("narrow", None),
        P(None, "narrow"),
        P(None, "narrow"),
        P(),
        P(None, "narrow"),
        P(None, "narrow"),
        P("narrow", None),
        P("wide", None),
        P("wide"),
        P("wide", None),
        P("wide", None),
    )
    return jax.shard_map(
        functools.partial(on_device, mesh.shape["wide"], mesh.shape["narrow"]),
        mesh=mesh,
        in_specs=placed,
        out_specs=(
            P(("wide", "narrow"), None),
            P(("wide", "narrow"), None),
            P(("wide", "narrow")),
            P("wide", "narrow"),
            P("wide", "narrow"),
            P("wide", "narrow"),
            P("narrow", "wide"),
            P("wide", "narrow"),
            P("wide", "narrow"),
            P(("wide", "narrow")),
            P("wide", "narrow"),
            P("wide", "narrow"),
            P("narrow", "wide"),
        ),
        check_vma=False,
    )
```

```python
import functools
import jax
import jax.numpy as jnp
from jax import lax
from jax.experimental import pallas as pl
from jax.experimental.pallas import tpu as pltpu
from jax.sharding import PartitionSpec as P

DH = 64
BIAS_SCALE = 4096.0
LOG2E = 1.4426950408889634
f32 = jnp.float32
bf16 = jnp.bfloat16
NT = (((1,), (1,)), ((), ()))
NN = (((1,), (0,)), ((), ()))


def dot(a, b, dims=NN):
    return lax.dot_general(a, b, dims, preferred_element_type=f32)


def key_window(len_ref, first, last, count, width):
    ends = []
    total = 0
    for p in range(len_ref.shape[1]):
        total = total + len_ref[0, p]
        ends.append(total)
    start = 0
    stop = count
    for e in ends:
        start = jnp.where(e <= first, e, start)
    for e in reversed(ends):
        stop = jnp.where(e > last, e, stop)
    base = (start // 128) * 128
    steps = (stop - base + width - 1) // width
    base = jnp.minimum(base, count - steps * width)
    return ends, base, steps


def for_chunks(base, steps, width, group, body):
    def many(j, carry):
        body(pl.multiple_of(base + j * (group * width), 128), group * width)
        return carry

    def single(j, carry):
        body(pl.multiple_of(base + j * width, 128), width)
        return carry

    if group > 1:
        lax.fori_loop(0, steps // group, many, 0)
    lax.fori_loop((steps // group) * group if group > 1 else 0, steps, single, 0)


def own_half(shape, head):
    lane = lax.broadcasted_iota(jnp.int32, shape, len(shape) - 1)
    return (lane < DH) if head % 2 == 0 else (lane >= DH)


def fill_values(vext, v_ref, heads):
    for h in range(heads):
        vp = v_ref[:, (h // 2) * 128:(h // 2 + 1) * 128]
        vext[h] = jnp.where(own_half(vp.shape, h), vp, jnp.ones_like(vp))


def half_norms(rows):
    lane = lax.broadcasted_iota(jnp.int32, (128, 128), 0)
    column = lax.broadcasted_iota(jnp.int32, (128, 128), 1)
    same = ((lane < DH) == (column < DH)).astype(bf16)
    squares = (rows.astype(f32) * rows.astype(f32)).astype(bf16)
    return jnp.max(dot(squares, same)) * f32(1.02)


HIDDEN_PAIR = -(1 << 31)


def pair_bias_kernel(len_ref, rel_ref, lay_ref, tab_ref, kmask_ref, word_ref, code_ref, colcode, *, width, group):
    tq, count = rel_ref.shape
    pairs = word_ref.shape[0]
    i = pl.program_id(0)
    t0 = i * tq
    ends, base, steps = key_window(len_ref, t0, t0 + tq - 1, count, width)

    @pl.when(i == 0)
    def _():
        pos = lax.broadcasted_iota(jnp.int32, (8, count), 1)
        page = jnp.zeros((8, count), jnp.int32)
        for e in ends:
            page = page + (pos >= e).astype(jnp.int32)
        colcode[...] = jnp.where(kmask_ref[...] == 1, page, -1)

    rowpos = lax.broadcasted_iota(jnp.int32, (tq, 128), 0) + t0
    rowpage = jnp.zeros((tq, 128), jnp.int32)
    for e in ends:
        rowpage = rowpage + (rowpos >= e).astype(jnp.int32)
    lanes = lax.broadcasted_iota(jnp.int32, (tq, 128), 1)
    tabs = [jnp.broadcast_to(tab_ref[n:n + 1, :], (tq, 128)) for n in range(2 * pairs)]

    def chunk(c0, size):
        for half in range(size // 128):
            cc = pl.multiple_of(c0 + half * 128, 128)
            here = pl.ds(cc, 128)
            rel = rel_ref[:, here]
            lay = lay_ref[:, here]
            code_ref[:, here] = (rel + lay * 32).astype(jnp.int16)
            col = jnp.broadcast_to(colcode[0:1, here], (tq, 128))
            seen = (rowpage == col) | (rowpos == lanes + cc)
            for p in range(pairs):
                word = (jnp.take_along_axis(tabs[2 * p], rel, axis=1, mode="promise_in_bounds")
                        + jnp.take_along_axis(tabs[2 * p + 1], lay, axis=1, mode="promise_in_bounds"))
                word_ref[p, :, here] = jnp.where(seen, word, HIDDEN_PAIR)

    for_chunks(base, steps, width, group, chunk)


def pair_bias(page_lengths, rel, lay, tab, kmask, tq=256, width=256, group=2):
    count = rel.shape[0]
    pairs = tab.shape[0] // 2
    tile = lambda i: (i, 0)
    return pl.pallas_call(
        functools.partial(pair_bias_kernel, width=width, group=group),
        grid=(count // tq,),
        in_specs=[
            pl.BlockSpec(memory_space=pltpu.SMEM),
            pl.BlockSpec((tq, count), tile),
            pl.BlockSpec((tq, count), tile),
            pl.BlockSpec(tab.shape, lambda i: (0, 0)),
            pl.BlockSpec((1, count), lambda i: (0, 0)),
        ],
        out_specs=[
            pl.BlockSpec((pairs, tq, count), lambda i: (0, i, 0)),
            pl.BlockSpec((tq, count), tile),
        ],
        out_shape=[
            jax.ShapeDtypeStruct((pairs, count, count), jnp.int32),
            jax.ShapeDtypeStruct((count, count), jnp.int16),
        ],
        scratch_shapes=[pltpu.VMEM((8, count), jnp.int32)],
        compiler_params=pltpu.CompilerParams(vmem_limit_bytes=56 << 20),
        cost_estimate=pl.CostEstimate(flops=count * count * 1024, bytes_accessed=120 << 20, transcendentals=0),
        name="pair_bias",
    )(page_lengths, rel, lay, tab, kmask.reshape(1, count))


def forward_kernel(len_ref, q_ref, k_ref, v_ref, word_ref, att_ref, rinv_ref, e_ref,
                   s_scr, m_scr, acc_scr, vext, knorm, *, width, group):
    tq, count = word_ref.shape[1:]
    heads, pairs = 2, 1
    i = pl.program_id(0)
    t0 = i * tq
    ends, base, steps = key_window(len_ref, t0, t0 + tq - 1, count, width)

    @pl.when(i == 0)
    def _():
        fill_values(vext, v_ref, heads)
        for p in range(pairs):
            knorm[p] = half_norms(k_ref[:, p * 128:(p + 1) * 128])

    scaled = []
    largest = f32(0.0)
    for h in range(heads):
        qp = q_ref[:, (h // 2) * 128:(h // 2 + 1) * 128]
        scaled.append(jnp.where(own_half(qp.shape, h), qp * bf16(BIAS_SCALE), jnp.zeros_like(qp)))
        if h % 2 == 0:
            largest = jnp.maximum(largest, half_norms(qp) * knorm[h // 2])
    def scores(c0, width, use):
        raw = [dot(scaled[h], k_ref[pl.ds(c0, width), (h // 2) * 128:(h // 2 + 1) * 128], NT)
               for h in range(heads)]
        for half in range(width // 128):
            cc = pl.multiple_of(c0 + half * 128, 128)
            word = word_ref[0, :, pl.ds(cc, 128)]
            hidden = word == HIDDEN_PAIR
            parts = ((word & 0xFFFF).astype(f32), (word >> 16).astype(f32))
            for h in range(heads):
                bias = jnp.where(hidden, f32(-1e30), parts[h])
                use(h, half, cc, raw[h][:, half * 128:(half + 1) * 128] + bias)

    for h in range(heads):
        acc_scr[h] = jnp.zeros((tq, 128), f32)
    bounded = jnp.sqrt(largest) + 8.0 <= 60.0

    @pl.when(bounded)
    def _():
        def chunk(c0, size):
            pieces = {}

            def use(h, half, cc, s):
                e = jnp.exp2(s * f32(LOG2E / BIAS_SCALE)).astype(bf16)
                e_ref[h, :, pl.ds(cc, 128)] = e
                pieces[h, half] = e

            scores(c0, size, use)
            for h in range(heads):
                e = jnp.concatenate([pieces[h, half] for half in range(size // 128)], axis=1)
                acc_scr[h] += dot(e, vext[h, pl.ds(c0, size), :])

        for_chunks(base, steps, width, group, chunk)

    @pl.when(jnp.logical_not(bounded))
    def _():
        for h in range(heads):
            m_scr[h] = jnp.full((tq, 128), -3e38, f32)

        def first(j, carry):
            def use(h, half, cc, s):
                s_scr[h, :, pl.ds(cc, 128)] = s
                m_scr[h] = jnp.maximum(m_scr[h], s)

            scores(pl.multiple_of(base + j * width, 128), width, use)
            return carry

        lax.fori_loop(0, steps, first, 0)
        for h in range(heads):
            top = jnp.max(m_scr[h], axis=1, keepdims=True)

            def second(j, carry):
                c0 = pl.multiple_of(base + j * width, 128)
                e = jnp.exp2((s_scr[h, :, pl.ds(c0, width)] - top) * f32(LOG2E / BIAS_SCALE)).astype(bf16)
                e_ref[h, :, pl.ds(c0, width)] = e
                acc_scr[h] += dot(e, vext[h, pl.ds(c0, width), :])
                return carry

            lax.fori_loop(0, steps, second, 0)

    low = own_half((tq, 128), 0)
    for p in range(pairs):
        even, odd = acc_scr[2 * p], acc_scr[2 * p + 1]
        rinv = 1.0 / pltpu.roll(jnp.where(low, odd, even), DH, 1)
        att_ref[:, p * 128:(p + 1) * 128] = (jnp.where(low, even, odd) * rinv).astype(bf16)
        rinv_ref[:, p * 128:(p + 1) * 128] = rinv


def attention_forward(page_lengths, proj, words, pair, tq=256, width=256, group=2):
    count = proj.shape[0]
    pairs = proj.shape[1] // (3 * 128)
    tile = lambda i: (i, 0)
    return pl.pallas_call(
        functools.partial(forward_kernel, width=width, group=group),
        grid=(count // tq,),
        in_specs=[
            pl.BlockSpec(memory_space=pltpu.SMEM),
            pl.BlockSpec((tq, 128), lambda i: (i, pair)),
            pl.BlockSpec((count, 128), lambda i: (0, pairs + pair)),
            pl.BlockSpec((count, 128), lambda i: (0, 2 * pairs + pair)),
            pl.BlockSpec((1, tq, count), lambda i: (pair, i, 0)),
        ],
        out_specs=[
            pl.BlockSpec((tq, 128), tile),
            pl.BlockSpec((tq, 128), tile),
            pl.BlockSpec((2, tq, count), lambda i: (0, i, 0)),
        ],
        out_shape=[
            jax.ShapeDtypeStruct((count, 128), bf16),
            jax.ShapeDtypeStruct((count, 128), f32),
            jax.ShapeDtypeStruct((2, count, count), bf16),
        ],
        scratch_shapes=[
            pltpu.VMEM((2, tq, count), f32),
            pltpu.VMEM((2, tq, 128), f32),
            pltpu.VMEM((2, tq, 128), f32),
            pltpu.VMEM((2, count, 128), bf16),
            pltpu.SMEM((1,), f32),
        ],
        compiler_params=pltpu.CompilerParams(vmem_limit_bytes=56 << 20),
        cost_estimate=pl.CostEstimate(
            flops=count * count * 512, bytes_accessed=80 << 20, transcendentals=count * count),
        name="attention_forward",
    )(page_lengths, proj, proj, proj, words)


def bias_words(rel_table, layout_table):
    def pack(table):
        whole = jnp.round(table.astype(f32) * BIAS_SCALE).astype(jnp.int32)
        low = jnp.clip(whole[:, 0::2] + 16384, 0, 32767)
        high = jnp.clip(whole[:, 1::2], -16383, 16383)
        words = (high * 65536 + low).T
        return jnp.pad(words, ((0, 0), (0, 128 - words.shape[1])))
    both = jnp.stack([pack(rel_table), pack(layout_table)], axis=1)
    return both.reshape(-1, 128)


def signs(code, shift, bits):
    return [jnp.where((code & jnp.int16(1 << (shift + b))) == 0, bf16(1.0), bf16(-1.0))
            for b in range(bits)]


def walsh(sign_list):
    out = [None]
    for s in sign_list:
        out = out + [s if o is None else o * s for o in out]
    return out


def backward_kernel(len_ref, q_ref, k_ref, v_ref, da_ref, *refs, width, heads, group):
    tq = q_ref.shape[0]
    count = k_ref.shape[0]
    pairs = heads // 2
    e_refs, att_refs, rinv_refs = refs[:pairs], refs[pairs:2 * pairs], refs[2 * pairs:3 * pairs]
    dq_ref, dk_ref, dv_ref, ds_ref = refs[3 * pairs:3 * pairs + 4]
    vext, lhs_scr, dat_scr, qt_scr, dq_scr, dkt, dvt = refs[3 * pairs + 4:]
    i = pl.program_id(0)
    t0 = i * tq
    ends, base, steps = key_window(len_ref, t0, t0 + tq - 1, count, width)

    @pl.when(i == 0)
    def _():
        fill_values(vext, v_ref, heads)
        dkt[...] = jnp.zeros_like(dkt)
        dvt[...] = jnp.zeros_like(dvt)

    low = own_half((tq, 128), 0)
    lane = lax.broadcasted_iota(jnp.int32, (tq, 128), 1)
    first_part = (lane & 32) == 0
    for p in range(pairs):
        cols = slice(p * 128, (p + 1) * 128)
        da = (da_ref[:, cols].astype(f32) * rinv_refs[p][...]).astype(bf16)
        daf = da.astype(f32)
        prod = daf * att_refs[p][...].astype(f32)
        for r in range(2):
            own = low if r == 0 else jnp.logical_not(low)
            delta = jnp.sum(jnp.where(own, prod, 0.0), axis=1, keepdims=True) * f32(-1.0 / 32)
            high = delta.astype(bf16).astype(f32)
            rest = delta - high
            lhs_scr[2 * p + r] = jnp.where(own, daf, jnp.where(first_part, high, rest)).astype(bf16)
        dat_scr[p] = daf.T.astype(bf16)
        qt_scr[p] = q_ref[:, cols].astype(f32).T.astype(bf16)
        dq_scr[p] = jnp.zeros((tq, 128), f32)

    def chunk(c0, size):
        here = pl.ds(c0, size)
        for p in range(pairs):
            kp = k_ref[here, p * 128:(p + 1) * 128]
            dqs = []
            for r in range(2):
                h = 2 * p + r
                rows = slice(r * DH, (r + 1) * DH)
                e = e_refs[p][r, :, here]
                d = dot(lhs_scr[h], vext[h, here, :], NT)
                ds = (e.astype(f32) * d).astype(bf16)
                ds_ref[h, :, here] = ds
                dqs.append(dot(ds, kp))
                dkt[p, rows, here] += dot(qt_scr[p, rows, :], ds)
                dvt[p, rows, here] += dot(dat_scr[p, rows, :], e)
            dq_scr[p] += jnp.where(low, dqs[0], dqs[1])

    for_chunks(base, steps, width, group, chunk)
    for p in range(pairs):
        dq_ref[:, p * 128:(p + 1) * 128] = dq_scr[p].astype(bf16)

    @pl.when(i == pl.num_programs(0) - 1)
    def _():
        for p in range(pairs):
            for c in range(0, count, 256):
                dk_ref[c:c + 256, p * 128:(p + 1) * 128] = dkt[p, :, c:c + 256].T.astype(bf16)
                dv_ref[c:c + 256, p * 128:(p + 1) * 128] = dvt[p, :, c:c + 256].T.astype(bf16)


def attention_backward(page_lengths, proj, exps, d_att, atts, rinvs, tq=256, width=256, group=2):
    count = proj.shape[0]
    hc = proj.shape[1] // 3
    heads = hc // DH
    pairs = heads // 2
    grid = (count // tq,)
    tile = lambda i: (i, 0)
    fixed = lambda i: (0, 0)
    return pl.pallas_call(
        functools.partial(backward_kernel, width=width, heads=heads, group=group),
        grid=grid,
        in_specs=[
            pl.BlockSpec(memory_space=pltpu.SMEM),
            pl.BlockSpec((tq, hc), tile),
            pl.BlockSpec((count, hc), lambda i: (0, 1)),
            pl.BlockSpec((count, hc), lambda i: (0, 2)),
            pl.BlockSpec((tq, hc), tile),
        ] + [pl.BlockSpec((2, tq, count), lambda i: (0, i, 0))] * pairs + [pl.BlockSpec((tq, 128), tile)] * (2 * pairs),
        out_specs=[
            pl.BlockSpec((tq, hc), tile),
            pl.BlockSpec((count, hc), fixed),
            pl.BlockSpec((count, hc), fixed),
            pl.BlockSpec((heads, tq, count), lambda i: (0, i, 0)),
        ],
        out_shape=[
            jax.ShapeDtypeStruct((count, hc), bf16),
            jax.ShapeDtypeStruct((count, hc), bf16),
            jax.ShapeDtypeStruct((count, hc), bf16),
            jax.ShapeDtypeStruct((heads, count, count), bf16),
        ],
        scratch_shapes=[
            pltpu.VMEM((heads, count, 128), bf16),
            pltpu.VMEM((heads, tq, 128), bf16),
            pltpu.VMEM((pairs, 128, tq), bf16),
            pltpu.VMEM((pairs, 128, tq), bf16),
            pltpu.VMEM((pairs, tq, 128), f32),
            pltpu.VMEM((pairs, 128, count), f32),
            pltpu.VMEM((pairs, 128, count), f32),
        ],
        compiler_params=pltpu.CompilerParams(vmem_limit_bytes=56 << 20),
        cost_estimate=pl.CostEstimate(
            flops=heads * count * count * 512, bytes_accessed=150 << 20, transcendentals=0),
        name="attention_backward",
    )(page_lengths, proj, proj, proj, d_att, *exps, *atts, *rinvs)


def table_kernel(len_ref, ds_ref, code_ref, hl_ref, hr_ref, *bufs, width, parts):
    heads, tq, count = ds_ref.shape
    i = pl.program_id(0)
    t0 = i * tq
    ends, base, steps = key_window(len_ref, t0, t0 + tq - 1, count, width)

    @pl.when(i == 0)
    def _():
        hl_ref[...] = jnp.zeros_like(hl_ref)
        hr_ref[...] = jnp.zeros_like(hr_ref)

    one = jnp.ones((16, width), bf16)

    def chunk(j, carry):
        c0 = pl.multiple_of(base + j * width, 128)
        here = pl.ds(c0, width)
        blocks = tq // 16 // parts
        for part in range(parts):
            left, blay, brel = bufs[3 * part:3 * part + 3]
            for b in range(blocks):
                at = 16 * (part * blocks + b)
                rows = slice(at, at + 16)
                span = slice(b * width, (b + 1) * width)
                code = code_ref[rows, here]
                rel_signs = signs(code, 0, 5)
                lay_signs = signs(code, 5, 6)
                left_lay = walsh(lay_signs[:2])[1:]
                for h in range(heads):
                    ds = ds_ref[h, rows, here]
                    for a, func in enumerate(left_lay + [None, rel_signs[0]]):
                        place = 16 * (a * heads + h)
                        left[place:place + 16, span] = ds if func is None else ds * func
                for n, func in enumerate(walsh(lay_signs[2:])):
                    blay[16 * n:16 * (n + 1), span] = one if func is None else func
                for n, func in enumerate(walsh(rel_signs[1:])):
                    brel[16 * n:16 * (n + 1), span] = one if func is None else func
            hl_ref[...] += dot(left[:64 * heads, :], blay[...], NT)
            hr_ref[...] += dot(left[48 * heads:80 * heads, :], brel[...], NT)
        return carry

    lax.fori_loop(0, steps, chunk, 0)


def table_grads(page_lengths, ds, code, tq=256, width=256, parts=2):
    heads, count, _ = ds.shape
    deep = tq // 16 * width // parts
    fixed = lambda i: (0, 0)
    return pl.pallas_call(
        functools.partial(table_kernel, width=width, parts=parts),
        grid=(count // tq,),
        in_specs=[
            pl.BlockSpec(memory_space=pltpu.SMEM),
            pl.BlockSpec((heads, tq, count), lambda i: (0, i, 0)),
            pl.BlockSpec((tq, count), lambda i: (i, 0)),
        ],
        out_specs=[
            pl.BlockSpec((64 * heads, 256), fixed),
            pl.BlockSpec((32 * heads, 256), fixed),
        ],
        out_shape=[
            jax.ShapeDtypeStruct((64 * heads, 256), f32),
            jax.ShapeDtypeStruct((32 * heads, 256), f32),
        ],
        scratch_shapes=[
            pltpu.VMEM((80 * heads, deep), bf16),
            pltpu.VMEM((256, deep), bf16),
            pltpu.VMEM((256, deep), bf16),
        ] * parts,
        compiler_params=pltpu.CompilerParams(vmem_limit_bytes=56 << 20),
        cost_estimate=pl.CostEstimate(
            flops=heads * count * count * 512, bytes_accessed=150 << 20, transcendentals=0),
        name="table_grads",
    )(page_lengths, ds, code)


def bucket_sums(raw, heads):
    right = raw.shape[1] // 16
    left = raw.shape[0] // (16 * heads)
    cube = raw.reshape(left, heads, 16, right, 16)
    traced = jnp.sum(cube * jnp.eye(16, dtype=f32)[None, None, :, None, :], axis=(2, 4))
    if left == 4:
        traced = jnp.concatenate([traced[3:], traced[:3]], axis=0)

    def table(n):
        v = lax.iota(jnp.int32, n)
        both = v[:, None] & v[None, :]
        return (1 - 2 * (lax.population_count(both) & 1)).astype(f32)

    out = jnp.einsum("ahn,ax,ny->yxh", traced, table(left), table(right), precision=lax.Precision.HIGHEST)
    return out.reshape(left * right, heads) / (left * right)


TANH_SLOPE = 0.7978845608028654
CUBE = 0.044715


def feed_forward_kernel(far, x_ref, g_ref, *refs):
    weights, (hidden_ref, d_gate_ref, d_up_ref, dn_ref) = refs[:-4], refs[-4:]
    units = hidden_ref.shape[1]
    if far:
        step = pad_lanes(units)
        gate_weight, up_weight, down = [weights[0][:, n * step:n * step + units] for n in range(3)]
        ahead, back = NN, NT
    else:
        gate_weight, up_weight, down = [w[...] for w in weights]
        ahead, back = NT, NN
    x = x_ref[...]
    d_hidden = dot(g_ref[...], down, ahead)
    gate = dot(x, gate_weight, ahead)
    up = dot(x, up_weight, ahead)
    square = gate * gate
    t = jnp.tanh(TANH_SLOPE * gate * (1.0 + CUBE * square))
    half = 0.5 + 0.5 * t
    gelu = gate * half
    slope = half + (0.5 * TANH_SLOPE) * gate * (1.0 - t * t) * (1.0 + (3 * CUBE) * square)
    d_gate = (d_hidden * up * slope).astype(bf16)
    d_up = (d_hidden * gelu).astype(bf16)
    hidden_ref[...] = (gelu * up).astype(bf16)
    d_gate_ref[...] = d_gate
    d_up_ref[...] = d_up
    dn_ref[...] = dot(d_gate, gate_weight, back) + dot(d_up, up_weight, back)


def feed_forward(x, g, units, weights, shard=None, tile=256):
    tokens, features = x.shape
    tile = min(tile, tokens)
    rows = lambda n: pl.BlockSpec((tile, n), lambda i: (i, 0))
    if shard is None:
        weight_specs = [pl.BlockSpec(w.shape, lambda i: (0, 0)) for w in weights]
    else:
        weight_specs = [pl.BlockSpec((features, 3 * pad_lanes(units)), lambda i: (0, shard))]
    return pl.pallas_call(
        functools.partial(feed_forward_kernel, shard is not None),
        grid=(tokens // tile,),
        in_specs=[rows(features), rows(features)] + weight_specs,
        out_specs=[rows(units)] * 3 + [rows(features)],
        out_shape=[jax.ShapeDtypeStruct((tokens, units), bf16)] * 3
        + [jax.ShapeDtypeStruct((tokens, features), f32)],
        compiler_params=pltpu.CompilerParams(vmem_limit_bytes=56 << 20),
        cost_estimate=pl.CostEstimate(
            flops=10 * tokens * features * units, bytes_accessed=10 << 20, transcendentals=tokens * units),
        name="feed_forward",
    )(x, g, *weights)


def pad_lanes(n):
    return (n + 127) // 128 * 128


def weight_grads_kernel(n_left, n_right, *refs):
    lefts = refs[:2 * n_left]
    rights = refs[2 * n_left:-1]
    out_ref = refs[-1]
    rows_in = (((0,), (0,)), ((), ()))
    place = 0
    for n, left in enumerate(n_right):
        a, b = rights[2 * n], rights[2 * n + 1]
        size = a.shape[1]
        value = dot(lefts[2 * left][...], a[...], rows_in) + dot(lefts[2 * left + 1][...], b[...], rows_in)
        out_ref[:, place:place + size] = value.astype(bf16)
        if pad_lanes(size) > size:
            out_ref[:, place + size:place + pad_lanes(size)] = jnp.zeros(
                (out_ref.shape[0], pad_lanes(size) - size), bf16)
        place += pad_lanes(size)


def weight_grads(lefts, rights, groups, tile=256):
    features = lefts[0].shape[1]
    columns = sum(pad_lanes(r.shape[1]) for r in rights[::2])
    column = lambda a: pl.BlockSpec((a.shape[0], tile), lambda i: (0, i))
    whole = lambda a: pl.BlockSpec(a.shape, lambda i: (0, 0))
    return pl.pallas_call(
        functools.partial(weight_grads_kernel, len(lefts) // 2, groups),
        grid=(features // tile,),
        in_specs=[column(a) for a in lefts] + [whole(a) for a in rights],
        out_specs=pl.BlockSpec((tile, columns), lambda i: (i, 0)),
        out_shape=jax.ShapeDtypeStruct((features, columns), bf16),
        compiler_params=pltpu.CompilerParams(vmem_limit_bytes=56 << 20),
        cost_estimate=pl.CostEstimate(
            flops=4 * features * columns * lefts[0].shape[0], bytes_accessed=26 << 20, transcendentals=0),
        name="weight_grads",
    )(*lefts, *rights)


epsilon = 1e-06


def contract_rows(left, right):
    return lax.dot_general(
        left, right, (((0,), (0,)), ((), ())), preferred_element_type=jnp.float32
    )


def contract_cols(left, right):
    return lax.dot_general(
        left, right, (((1,), (1,)), ((), ())), preferred_element_type=jnp.float32
    )


def norm_rows(rows, gain):
    scale = lax.rsqrt(jnp.mean(rows * rows, axis=-1, keepdims=True) + epsilon)
    return (scale, (rows * scale * gain).astype(jnp.bfloat16))


def norm_back(d_normed, rows, scale, gain):
    shaped = d_normed * gain
    cubed = scale * scale * scale
    return scale * shaped - rows * cubed * jnp.mean(shaped * rows, axis=-1, keepdims=True)


def along(array, shift, ring):
    return lax.ppermute(array, "narrow", [(i, (i + shift) % ring) for i in range(ring)])


def swap(array, ring):
    return lax.ppermute(array, "narrow", [(i, i ^ 1) for i in range(ring)])


def rows_of(array, index, count):
    return lax.dynamic_slice_in_dim(array, index * count, count, 0)


def on_device(
    wide,
    ring,
    layer_input,
    out_grad,
    norm_attn_gain,
    w_query,
    w_key,
    w_value,
    w_out,
    rel_table,
    layout_table,
    norm_ffn_gain,
    w_gate,
    w_up,
    down_projection_weight,
    page_lengths,
    key_mask,
    rel_bucket,
    layout_bucket,
):
    tokens, width = layer_input.shape
    head_cols = w_query.shape[1]
    heads = head_cols // DH
    units = w_gate.shape[1]
    padded = pad_lanes(units)
    part = width // wide
    me = lax.axis_index("narrow")
    my_wide = lax.axis_index("wide")
    gain_attn = norm_attn_gain.astype(f32)
    gain_ffn = norm_ffn_gain.astype(f32)
    resid = layer_input.astype(f32)

    scale_attn, normed_attn = norm_rows(resid, gain_attn)
    normed_attn_all = lax.all_gather(normed_attn, "narrow", axis=0, tiled=True)

    w_project = jnp.concatenate([w_query, w_key, w_value], axis=1)
    own_rows_gate = rows_of(w_gate, my_wide, part)
    own_rows_up = rows_of(w_up, my_wide, part)
    own_rows_project = rows_of(w_project, my_wide, part)
    down_piece = lax.dynamic_slice_in_dim(down_projection_weight, my_wide * part, part, 1).T
    out_piece = lax.dynamic_slice_in_dim(w_out, my_wide * part, part, 1).T
    ffn_piece = jnp.concatenate(
        [jnp.pad(piece, ((0, 0), (0, padded - units))) for piece in (own_rows_gate, own_rows_up, down_piece)], axis=1)
    out_pieces = [out_piece] + [along(out_piece, d, ring) for d in range(1, ring)]
    words, codes = pair_bias(page_lengths, rel_bucket, layout_bucket, bias_words(rel_table, layout_table), key_mask)
    normed_attn_all, ffn_piece, late_grad, words = lax.optimization_barrier(
        (normed_attn_all, ffn_piece, out_grad, words))
    ffn_pieces = [along(ffn_piece, d, ring) for d in range(2, ring, 2)]
    out_t = lax.all_gather(jnp.concatenate(out_pieces, axis=1), "wide", axis=0, tiled=True)
    other_grad = swap(late_grad, ring)

    projected = dot(normed_attn_all, w_project).astype(bf16)
    pairs = head_cols // 128
    first_pair = list(attention_forward(page_lengths, projected, words, 0))
    first_pair[0], ffn_pieces, other_grad, late_project = lax.optimization_barrier(
        (first_pair[0], ffn_pieces, other_grad, own_rows_project))
    far_pieces = jnp.concatenate(ffn_pieces, axis=1)

    def to_owners(a):
        return [rows_of(a, me, tokens)] + [
            along(rows_of(a, (me + d) % ring, tokens), d, ring) for d in range(1, ring)]

    sent = [to_owners(first_pair[0])]
    project_pieces = [own_rows_project] + [along(late_project, d, ring) for d in range(1, ring)]
    results = [first_pair]
    if pairs > 1:
        late_projected, far_pieces = lax.optimization_barrier((projected, far_pieces))
        results += [list(attention_forward(page_lengths, late_projected, words, p)) for p in range(1, pairs)]
    far = lax.all_gather(far_pieces, "wide", axis=0, tiled=True)
    if pairs > 1:
        results[1][0], project_pieces, sent[0] = lax.optimization_barrier((results[1][0], project_pieces, sent[0]))
    w_project_all = lax.all_gather(jnp.concatenate(project_pieces, axis=1), "wide", axis=0, tiled=True)
    attended = [r[0] for r in results]
    sent += [to_owners(a) for a in attended[1:]]
    mine = [pieces[d] for d in range(ring) for pieces in sent]
    attended_own = jnp.concatenate(mine, axis=1)
    middle = resid + contract_cols(attended_own, out_t)

    scale_ffn, normed_ffn = norm_rows(middle, gain_ffn)
    other_normed = swap(normed_ffn, ring)
    near = (w_gate.T, w_up.T, down_projection_weight)
    shards = ring // 2
    own = [feed_forward(normed_ffn, out_grad, units, near)]
    other = [feed_forward(other_normed, other_grad, units, near)]
    other += [feed_forward(other_normed, other_grad, units, (far,), s) for s in range(shards - 1)]
    other_d_normed = swap(sum(o[3] for o in other).astype(bf16), ring)
    own += [feed_forward(normed_ffn, out_grad, units, (far,), s) for s in range(shards - 1)]
    rights, groups = [], []
    for s in range(shards):
        for n in range(1, 4):
            rights += [own[s][n % 3], other[s][n % 3]]
            groups.append(n // 3)
    sums = weight_grads((normed_ffn, other_normed, out_grad, other_grad), rights, tuple(groups))
    sums, other_d_normed = lax.optimization_barrier((sums, other_d_normed))
    ffn_sums = lax.psum_scatter(sums, "wide", scatter_dimension=0, tiled=True)
    d_normed_ffn = sum(o[3] for o in own) + other_d_normed.astype(f32)
    d_middle = out_grad.astype(f32) + norm_back(d_normed_ffn, middle, scale_ffn, gain_ffn)
    d_middle_low = d_middle.astype(bf16)
    d_attended_own = dot(d_middle_low, out_t).astype(bf16)

    def block(d):
        return d_attended_own[:, d * head_cols : (d + 1) * head_cols]

    d_attended = jnp.zeros((ring * tokens, head_cols), bf16)
    d_attended = lax.dynamic_update_slice_in_dim(d_attended, block(0), me * tokens, 0)
    for d in range(1, ring):
        d_attended = lax.dynamic_update_slice_in_dim(
            d_attended, along(block(d), -d, ring), ((me + d) % ring) * tokens, 0)

    d_middle_late, attended_late, hiddens = lax.optimization_barrier(
        (d_middle_low, attended_own, [(own[s][0], other[s][0]) for s in range(shards)]))
    wout_sums = contract_rows(d_middle_late, attended_late).astype(bf16)
    own_out, other_out = 0.0, 0.0
    for s, (own_hidden, other_hidden) in enumerate(hiddens):
        if s == 0:
            down, dims = down_projection_weight, NN
        else:
            at = 3 * padded * (s - 1) + 2 * padded
            down, dims = far[:, at : at + units], NT
        own_out = own_out + dot(own_hidden, down, dims)
        other_out = other_out + dot(other_hidden, down, dims)
    other_out = other_out.astype(bf16)
    wout_sums, d_attended, w_project_all, other_out, own_out = lax.optimization_barrier(
        (wout_sums, d_attended, w_project_all, other_out, own_out))
    other_out = swap(other_out, ring)

    d_query, d_keys, d_values, d_scores = attention_backward(
        page_lengths, projected, [r[2] for r in results], d_attended, attended, [r[1] for r in results])
    d_project = jnp.concatenate([d_query, d_keys, d_values], axis=1)
    d_project, other_out, middle_late = lax.optimization_barrier((d_project, other_out, middle))
    layer_out = (middle_late + own_out + other_out.astype(f32)).astype(bf16)
    mine = [along(rows_of(d_project, (me + d) % ring, tokens), d, ring) for d in range(1, ring)]
    last_sums = jnp.concatenate([contract_rows(normed_attn_all, d_project).astype(bf16), wout_sums], axis=1)
    last_sums, ffn_sums = lax.optimization_barrier((last_sums, ffn_sums))
    last_sums = lax.psum_scatter(last_sums, "wide", scatter_dimension=0, tiled=True)
    sum_project = last_sums[:, : 3 * head_cols].astype(f32)
    wout_sums = last_sums[:, 3 * head_cols :]

    raw_lay, raw_rel = table_grads(page_lengths, d_scores, codes)
    raw_lay, raw_rel, mine = lax.optimization_barrier((raw_lay, raw_rel, mine))
    d_project_own = jnp.concatenate([rows_of(d_project, me, tokens)] + mine, axis=1)
    d_normed_attn = contract_cols(d_project_own, w_project_all)
    in_grad = d_middle + norm_back(d_normed_attn, resid, scale_attn, gain_attn)
    grad_relative = bucket_sums(raw_rel, heads)
    grad_layout = bucket_sums(raw_lay, heads)
    tables = jnp.concatenate(
        [grad_relative.reshape(wide, -1, heads), grad_layout.reshape(wide, -1, heads)], axis=1)
    n_rel = grad_relative.shape[0] // wide
    reach = wide // 2
    while reach >= 1:
        bit = (my_wide // reach) % 2
        keep = lax.dynamic_slice_in_dim(tables, bit * reach, reach, 0)
        give = lax.dynamic_slice_in_dim(tables, (1 - bit) * reach, reach, 0)
        tables = keep + lax.ppermute(give, "wide", [(i, i ^ reach) for i in range(wide)])
        reach //= 2
    sum_tables = tables[0]

    def stripe(shard, n):
        at = padded * (3 * shard + n)
        return ffn_sums[:, at : at + units]

    sum_gate, sum_up, sum_down = [stripe(0, n).astype(f32) for n in range(3)]
    for s in range(1, shards):
        at = 3 * padded * s
        block = along(ffn_sums[:, at : at + 3 * padded], -2 * s, ring).astype(f32)
        sum_gate += block[:, :units]
        sum_up += block[:, padded : padded + units]
        sum_down += block[:, 2 * padded : 2 * padded + units]
    sum_wout = wout_sums[:, :head_cols].astype(f32)
    for d in range(1, ring):
        sum_wout += along(wout_sums[:, d * head_cols : (d + 1) * head_cols], -d, ring).astype(f32)

    gain_terms = jnp.stack(
        [
            jnp.sum(own_rows_project.astype(f32) * sum_project, axis=1),
            jnp.sum(own_rows_gate.astype(f32) * sum_gate + own_rows_up.astype(f32) * sum_up, axis=1),
        ]
    )
    share = part // ring

    def gain_share(index):
        return lax.dynamic_slice_in_dim(gain_terms, index * share, share, 1)

    gain_sum = gain_share(me)
    for d in range(1, ring):
        gain_sum = gain_sum + along(gain_share((me + d) % ring), d, ring)
    place = my_wide * part + me * share
    gains = lax.dynamic_slice_in_dim(jnp.stack([gain_attn, gain_ffn]), place, share, 1)
    gain_grads = gain_sum / gains
    return (
        layer_out,
        in_grad,
        gain_grads[0],
        sum_project[:, :head_cols],
        sum_project[:, head_cols : 2 * head_cols],
        sum_project[:, 2 * head_cols :],
        sum_wout.T,
        sum_tables[:n_rel],
        sum_tables[n_rel:],
        gain_grads[1],
        sum_gate,
        sum_up,
        sum_down.T,
    )


def solution(mesh):
    placed = (
        P(("wide", "narrow"), None),
        P(("wide", "narrow"), None),
        P(),
        P(None, "narrow"),
        P(None, "narrow"),
        P(None, "narrow"),
        P("narrow", None),
        P(None, "narrow"),
        P(None, "narrow"),
        P(),
        P(None, "narrow"),
        P(None, "narrow"),
        P("narrow", None),
        P("wide", None),
        P("wide"),
        P("wide", None),
        P("wide", None),
    )
    return jax.shard_map(
        functools.partial(on_device, mesh.shape["wide"], mesh.shape["narrow"]),
        mesh=mesh,
        in_specs=placed,
        out_specs=(
            P(("wide", "narrow"), None),
            P(("wide", "narrow"), None),
            P(("wide", "narrow")),
            P("wide", "narrow"),
            P("wide", "narrow"),
            P("wide", "narrow"),
            P("narrow", "wide"),
            P("wide", "narrow"),
            P("wide", "narrow"),
            P(("wide", "narrow")),
            P("wide", "narrow"),
            P("wide", "narrow"),
            P("narrow", "wide"),
        ),
        check_vma=False,
    )
```

```python
import functools
import jax
import jax.numpy as jnp
from jax import lax
from jax.experimental import pallas as pl
from jax.experimental.pallas import tpu as pltpu
from jax.sharding import PartitionSpec as P

DH = 64
BIAS_SCALE = 4096.0
LOG2E = 1.4426950408889634
f32 = jnp.float32
bf16 = jnp.bfloat16
NT = (((1,), (1,)), ((), ()))
NN = (((1,), (0,)), ((), ()))


def dot(a, b, dims=NN):
    return lax.dot_general(a, b, dims, preferred_element_type=f32)


def key_window(len_ref, first, last, count, width):
    ends = []
    total = 0
    for p in range(len_ref.shape[1]):
        total = total + len_ref[0, p]
        ends.append(total)
    start = 0
    stop = count
    for e in ends:
        start = jnp.where(e <= first, e, start)
    for e in reversed(ends):
        stop = jnp.where(e > last, e, stop)
    base = (start // 128) * 128
    steps = (stop - base + width - 1) // width
    base = jnp.minimum(base, count - steps * width)
    return ends, base, steps


def for_chunks(base, steps, width, group, body):
    def many(j, carry):
        body(pl.multiple_of(base + j * (group * width), 128), group * width)
        return carry

    def single(j, carry):
        body(pl.multiple_of(base + j * width, 128), width)
        return carry

    if group > 1:
        lax.fori_loop(0, steps // group, many, 0)
    lax.fori_loop((steps // group) * group if group > 1 else 0, steps, single, 0)


def own_half(shape, head):
    lane = lax.broadcasted_iota(jnp.int32, shape, len(shape) - 1)
    return (lane < DH) if head % 2 == 0 else (lane >= DH)


def fill_values(vext, v_ref, heads):
    for h in range(heads):
        vp = v_ref[:, (h // 2) * 128:(h // 2 + 1) * 128]
        vext[h] = jnp.where(own_half(vp.shape, h), vp, jnp.ones_like(vp))


def half_norms(rows):
    lane = lax.broadcasted_iota(jnp.int32, (128, 128), 0)
    column = lax.broadcasted_iota(jnp.int32, (128, 128), 1)
    same = ((lane < DH) == (column < DH)).astype(bf16)
    squares = (rows.astype(f32) * rows.astype(f32)).astype(bf16)
    return jnp.max(dot(squares, same)) * f32(1.02)


HIDDEN_PAIR = -(1 << 31)


def pair_bias_kernel(len_ref, rel_ref, lay_ref, tab_ref, kmask_ref, word_ref, code_ref, colcode, *, width, group):
    tq, count = rel_ref.shape
    pairs = word_ref.shape[0]
    i = pl.program_id(0)
    t0 = i * tq
    ends, base, steps = key_window(len_ref, t0, t0 + tq - 1, count, width)

    @pl.when(i == 0)
    def _():
        pos = lax.broadcasted_iota(jnp.int32, (8, count), 1)
        page = jnp.zeros((8, count), jnp.int32)
        for e in ends:
            page = page + (pos >= e).astype(jnp.int32)
        colcode[...] = jnp.where(kmask_ref[...] == 1, page, -1)

    rowpos = lax.broadcasted_iota(jnp.int32, (tq, 128), 0) + t0
    rowpage = jnp.zeros((tq, 128), jnp.int32)
    for e in ends:
        rowpage = rowpage + (rowpos >= e).astype(jnp.int32)
    lanes = lax.broadcasted_iota(jnp.int32, (tq, 128), 1)
    tabs = [jnp.broadcast_to(tab_ref[n:n + 1, :], (tq, 128)) for n in range(2 * pairs)]

    def chunk(c0, size):
        for half in range(size // 128):
            cc = pl.multiple_of(c0 + half * 128, 128)
            here = pl.ds(cc, 128)
            rel = rel_ref[:, here]
            lay = lay_ref[:, here]
            code_ref[:, here] = (rel + lay * 32).astype(jnp.int16)
            col = jnp.broadcast_to(colcode[0:1, here], (tq, 128))
            seen = (rowpage == col) | (rowpos == lanes + cc)
            for p in range(pairs):
                word = (jnp.take_along_axis(tabs[2 * p], rel, axis=1, mode="promise_in_bounds")
                        + jnp.take_along_axis(tabs[2 * p + 1], lay, axis=1, mode="promise_in_bounds"))
                word_ref[p, :, here] = jnp.where(seen, word, HIDDEN_PAIR)

    for_chunks(base, steps, width, group, chunk)


def pair_bias(page_lengths, rel, lay, tab, kmask, tq=256, width=256, group=2):
    count = rel.shape[0]
    pairs = tab.shape[0] // 2
    tile = lambda i: (i, 0)
    return pl.pallas_call(
        functools.partial(pair_bias_kernel, width=width, group=group),
        grid=(count // tq,),
        in_specs=[
            pl.BlockSpec(memory_space=pltpu.SMEM),
            pl.BlockSpec((tq, count), tile),
            pl.BlockSpec((tq, count), tile),
            pl.BlockSpec(tab.shape, lambda i: (0, 0)),
            pl.BlockSpec((1, count), lambda i: (0, 0)),
        ],
        out_specs=[
            pl.BlockSpec((pairs, tq, count), lambda i: (0, i, 0)),
            pl.BlockSpec((tq, count), tile),
        ],
        out_shape=[
            jax.ShapeDtypeStruct((pairs, count, count), jnp.int32),
            jax.ShapeDtypeStruct((count, count), jnp.int16),
        ],
        scratch_shapes=[pltpu.VMEM((8, count), jnp.int32)],
        compiler_params=pltpu.CompilerParams(vmem_limit_bytes=56 << 20),
        cost_estimate=pl.CostEstimate(flops=count * count * 1024, bytes_accessed=120 << 20, transcendentals=0),
        name="pair_bias",
    )(page_lengths, rel, lay, tab, kmask.reshape(1, count))


def forward_kernel(len_ref, q_ref, k_ref, v_ref, word_ref, att_ref, rinv_ref, e_ref,
                   s_scr, m_scr, acc_scr, vext, knorm, *, width, group):
    tq, count = word_ref.shape[1:]
    heads, pairs = 2, 1
    i = pl.program_id(0)
    t0 = i * tq
    ends, base, steps = key_window(len_ref, t0, t0 + tq - 1, count, width)

    @pl.when(i == 0)
    def _():
        fill_values(vext, v_ref, heads)
        for p in range(pairs):
            knorm[p] = half_norms(k_ref[:, p * 128:(p + 1) * 128])

    scaled = []
    largest = f32(0.0)
    for h in range(heads):
        qp = q_ref[:, (h // 2) * 128:(h // 2 + 1) * 128]
        scaled.append(jnp.where(own_half(qp.shape, h), qp * bf16(BIAS_SCALE), jnp.zeros_like(qp)))
        if h % 2 == 0:
            largest = jnp.maximum(largest, half_norms(qp) * knorm[h // 2])
    def scores(c0, width, use):
        raw = [dot(scaled[h], k_ref[pl.ds(c0, width), (h // 2) * 128:(h // 2 + 1) * 128], NT)
               for h in range(heads)]
        for half in range(width // 128):
            cc = pl.multiple_of(c0 + half * 128, 128)
            word = word_ref[0, :, pl.ds(cc, 128)]
            hidden = word == HIDDEN_PAIR
            parts = ((word & 0xFFFF).astype(f32), (word >> 16).astype(f32))
            for h in range(heads):
                bias = jnp.where(hidden, f32(-1e30), parts[h])
                use(h, half, cc, raw[h][:, half * 128:(half + 1) * 128] + bias)

    for h in range(heads):
        acc_scr[h] = jnp.zeros((tq, 128), f32)
    bounded = jnp.sqrt(largest) + 8.0 <= 60.0

    @pl.when(bounded)
    def _():
        def chunk(c0, size):
            pieces = {}

            def use(h, half, cc, s):
                e = jnp.exp2(s * f32(LOG2E / BIAS_SCALE)).astype(bf16)
                e_ref[h, :, pl.ds(cc, 128)] = e
                pieces[h, half] = e

            scores(c0, size, use)
            for h in range(heads):
                e = jnp.concatenate([pieces[h, half] for half in range(size // 128)], axis=1)
                acc_scr[h] += dot(e, vext[h, pl.ds(c0, size), :])

        for_chunks(base, steps, width, group, chunk)

    @pl.when(jnp.logical_not(bounded))
    def _():
        for h in range(heads):
            m_scr[h] = jnp.full((tq, 128), -3e38, f32)

        def first(j, carry):
            def use(h, half, cc, s):
                s_scr[h, :, pl.ds(cc, 128)] = s
                m_scr[h] = jnp.maximum(m_scr[h], s)

            scores(pl.multiple_of(base + j * width, 128), width, use)
            return carry

        lax.fori_loop(0, steps, first, 0)
        for h in range(heads):
            top = jnp.max(m_scr[h], axis=1, keepdims=True)

            def second(j, carry):
                c0 = pl.multiple_of(base + j * width, 128)
                e = jnp.exp2((s_scr[h, :, pl.ds(c0, width)] - top) * f32(LOG2E / BIAS_SCALE)).astype(bf16)
                e_ref[h, :, pl.ds(c0, width)] = e
                acc_scr[h] += dot(e, vext[h, pl.ds(c0, width), :])
                return carry

            lax.fori_loop(0, steps, second, 0)

    low = own_half((tq, 128), 0)
    for p in range(pairs):
        even, odd = acc_scr[2 * p], acc_scr[2 * p + 1]
        rinv = 1.0 / pltpu.roll(jnp.where(low, odd, even), DH, 1)
        att_ref[:, p * 128:(p + 1) * 128] = (jnp.where(low, even, odd) * rinv).astype(bf16)
        rinv_ref[:, p * 128:(p + 1) * 128] = rinv


def attention_forward(page_lengths, proj, words, pair, tq=256, width=256, group=2):
    count = proj.shape[0]
    pairs = proj.shape[1] // (3 * 128)
    tile = lambda i: (i, 0)
    return pl.pallas_call(
        functools.partial(forward_kernel, width=width, group=group),
        grid=(count // tq,),
        in_specs=[
            pl.BlockSpec(memory_space=pltpu.SMEM),
            pl.BlockSpec((tq, 128), lambda i: (i, pair)),
            pl.BlockSpec((count, 128), lambda i: (0, pairs + pair)),
            pl.BlockSpec((count, 128), lambda i: (0, 2 * pairs + pair)),
            pl.BlockSpec((1, tq, count), lambda i: (pair, i, 0)),
        ],
        out_specs=[
            pl.BlockSpec((tq, 128), tile),
            pl.BlockSpec((tq, 128), tile),
            pl.BlockSpec((2, tq, count), lambda i: (0, i, 0)),
        ],
        out_shape=[
            jax.ShapeDtypeStruct((count, 128), bf16),
            jax.ShapeDtypeStruct((count, 128), f32),
            jax.ShapeDtypeStruct((2, count, count), bf16),
        ],
        scratch_shapes=[
            pltpu.VMEM((2, tq, count), f32),
            pltpu.VMEM((2, tq, 128), f32),
            pltpu.VMEM((2, tq, 128), f32),
            pltpu.VMEM((2, count, 128), bf16),
            pltpu.SMEM((1,), f32),
        ],
        compiler_params=pltpu.CompilerParams(vmem_limit_bytes=56 << 20),
        cost_estimate=pl.CostEstimate(
            flops=count * count * 512, bytes_accessed=80 << 20, transcendentals=count * count),
        name="attention_forward",
    )(page_lengths, proj, proj, proj, words)


def bias_words(rel_table, layout_table):
    def pack(table):
        whole = jnp.round(table.astype(f32) * BIAS_SCALE).astype(jnp.int32)
        low = jnp.clip(whole[:, 0::2] + 16384, 0, 32767)
        high = jnp.clip(whole[:, 1::2], -16383, 16383)
        words = (high * 65536 + low).T
        return jnp.pad(words, ((0, 0), (0, 128 - words.shape[1])))
    both = jnp.stack([pack(rel_table), pack(layout_table)], axis=1)
    return both.reshape(-1, 128)


def signs(code, shift, bits):
    return [jnp.where((code & jnp.int16(1 << (shift + b))) == 0, bf16(1.0), bf16(-1.0))
            for b in range(bits)]


def walsh(sign_list):
    out = [None]
    for s in sign_list:
        out = out + [s if o is None else o * s for o in out]
    return out


def backward_kernel(len_ref, q_ref, k_ref, v_ref, da_ref, *refs, width, heads, group):
    tq = q_ref.shape[0]
    count = k_ref.shape[0]
    pairs = heads // 2
    e_refs, att_refs, rinv_refs = refs[:pairs], refs[pairs:2 * pairs], refs[2 * pairs:3 * pairs]
    dp_ref, ds_ref = refs[3 * pairs:3 * pairs + 2]
    vext, lhs_scr, dat_scr, qt_scr, dq_scr, dkt, dvt = refs[3 * pairs + 2:]
    i = pl.program_id(0)
    t0 = i * tq
    ends, base, steps = key_window(len_ref, t0, t0 + tq - 1, count, width)

    @pl.when(i == 0)
    def _():
        fill_values(vext, v_ref, heads)
        dkt[...] = jnp.zeros_like(dkt)
        dvt[...] = jnp.zeros_like(dvt)

    low = own_half((tq, 128), 0)
    lane = lax.broadcasted_iota(jnp.int32, (tq, 128), 1)
    first_part = (lane & 32) == 0
    for p in range(pairs):
        cols = slice(p * 128, (p + 1) * 128)
        da = (da_ref[:, cols].astype(f32) * rinv_refs[p][...]).astype(bf16)
        daf = da.astype(f32)
        prod = daf * att_refs[p][...].astype(f32)
        for r in range(2):
            own = low if r == 0 else jnp.logical_not(low)
            delta = jnp.sum(jnp.where(own, prod, 0.0), axis=1, keepdims=True) * f32(-1.0 / 32)
            high = delta.astype(bf16).astype(f32)
            rest = delta - high
            lhs_scr[2 * p + r] = jnp.where(own, daf, jnp.where(first_part, high, rest)).astype(bf16)
        dat_scr[p] = daf.T.astype(bf16)
        qt_scr[p] = q_ref[:, cols].astype(f32).T.astype(bf16)
        dq_scr[p] = jnp.zeros((tq, 128), f32)

    def chunk(c0, size):
        here = pl.ds(c0, size)
        for p in range(pairs):
            kp = k_ref[here, p * 128:(p + 1) * 128]
            dqs = []
            for r in range(2):
                h = 2 * p + r
                rows = slice(r * DH, (r + 1) * DH)
                e = e_refs[p][r, :, here]
                d = dot(lhs_scr[h], vext[h, here, :], NT)
                ds = (e.astype(f32) * d).astype(bf16)
                ds_ref[h, :, here] = ds
                dqs.append(dot(ds, kp))
                dkt[p, rows, here] += dot(qt_scr[p, rows, :], ds)
                dvt[p, rows, here] += dot(dat_scr[p, rows, :], e)
            dq_scr[p] += jnp.where(low, dqs[0], dqs[1])

    for_chunks(base, steps, width, group, chunk)
    for p in range(pairs):
        dp_ref[pl.ds(pl.multiple_of(t0, tq), tq), p * 128:(p + 1) * 128] = dq_scr[p].astype(bf16)

    @pl.when(i == pl.num_programs(0) - 1)
    def _():
        for n, grads in enumerate((dkt, dvt)):
            for p in range(pairs):
                at = ((n + 1) * pairs + p) * 128
                for c in range(0, count, 256):
                    dp_ref[c:c + 256, at:at + 128] = grads[p, :, c:c + 256].T.astype(bf16)


def attention_backward(page_lengths, proj, exps, d_att, atts, rinvs, tq=256, width=256, group=2):
    count = proj.shape[0]
    hc = proj.shape[1] // 3
    heads = hc // DH
    pairs = heads // 2
    grid = (count // tq,)
    tile = lambda i: (i, 0)
    fixed = lambda i: (0, 0)
    return pl.pallas_call(
        functools.partial(backward_kernel, width=width, heads=heads, group=group),
        grid=grid,
        in_specs=[
            pl.BlockSpec(memory_space=pltpu.SMEM),
            pl.BlockSpec((tq, hc), tile),
            pl.BlockSpec((count, hc), lambda i: (0, 1)),
            pl.BlockSpec((count, hc), lambda i: (0, 2)),
            pl.BlockSpec((tq, hc), tile),
        ] + [pl.BlockSpec((2, tq, count), lambda i: (0, i, 0))] * pairs + [pl.BlockSpec((tq, 128), tile)] * (2 * pairs),
        out_specs=[
            pl.BlockSpec((count, 3 * hc), fixed),
            pl.BlockSpec((heads, tq, count), lambda i: (0, i, 0)),
        ],
        out_shape=[
            jax.ShapeDtypeStruct((count, 3 * hc), bf16),
            jax.ShapeDtypeStruct((heads, count, count), bf16),
        ],
        scratch_shapes=[
            pltpu.VMEM((heads, count, 128), bf16),
            pltpu.VMEM((heads, tq, 128), bf16),
            pltpu.VMEM((pairs, 128, tq), bf16),
            pltpu.VMEM((pairs, 128, tq), bf16),
            pltpu.VMEM((pairs, tq, 128), f32),
            pltpu.VMEM((pairs, 128, count), f32),
            pltpu.VMEM((pairs, 128, count), f32),
        ],
        compiler_params=pltpu.CompilerParams(vmem_limit_bytes=56 << 20),
        cost_estimate=pl.CostEstimate(
            flops=heads * count * count * 512, bytes_accessed=150 << 20, transcendentals=0),
        name="attention_backward",
    )(page_lengths, proj, proj, proj, d_att, *exps, *atts, *rinvs)


def table_kernel(len_ref, ds_ref, code_ref, hl_ref, hr_ref, *bufs, width, parts):
    heads, tq, count = ds_ref.shape
    i = pl.program_id(0)
    t0 = i * tq
    ends, base, steps = key_window(len_ref, t0, t0 + tq - 1, count, width)

    @pl.when(i == 0)
    def _():
        hl_ref[...] = jnp.zeros_like(hl_ref)
        hr_ref[...] = jnp.zeros_like(hr_ref)

    one = jnp.ones((16, width), bf16)

    def chunk(j, carry):
        c0 = pl.multiple_of(base + j * width, 128)
        here = pl.ds(c0, width)
        blocks = tq // 16 // parts
        for part in range(parts):
            left, blay, brel = bufs[3 * part:3 * part + 3]
            for b in range(blocks):
                at = 16 * (part * blocks + b)
                rows = slice(at, at + 16)
                span = slice(b * width, (b + 1) * width)
                code = code_ref[rows, here]
                rel_signs = signs(code, 0, 5)
                lay_signs = signs(code, 5, 6)
                left_lay = walsh(lay_signs[:2])[1:]
                for h in range(heads):
                    ds = ds_ref[h, rows, here]
                    for a, func in enumerate(left_lay + [None, rel_signs[0]]):
                        place = 16 * (a * heads + h)
                        left[place:place + 16, span] = ds if func is None else ds * func
                for n, func in enumerate(walsh(lay_signs[2:])):
                    blay[16 * n:16 * (n + 1), span] = one if func is None else func
                for n, func in enumerate(walsh(rel_signs[1:])):
                    brel[16 * n:16 * (n + 1), span] = one if func is None else func
            hl_ref[...] += dot(left[:64 * heads, :], blay[...], NT)
            hr_ref[...] += dot(left[48 * heads:80 * heads, :], brel[...], NT)
        return carry

    lax.fori_loop(0, steps, chunk, 0)


def table_grads(page_lengths, ds, code, tq=256, width=256, parts=2):
    heads, count, _ = ds.shape
    deep = tq // 16 * width // parts
    fixed = lambda i: (0, 0)
    return pl.pallas_call(
        functools.partial(table_kernel, width=width, parts=parts),
        grid=(count // tq,),
        in_specs=[
            pl.BlockSpec(memory_space=pltpu.SMEM),
            pl.BlockSpec((heads, tq, count), lambda i: (0, i, 0)),
            pl.BlockSpec((tq, count), lambda i: (i, 0)),
        ],
        out_specs=[
            pl.BlockSpec((64 * heads, 256), fixed),
            pl.BlockSpec((32 * heads, 256), fixed),
        ],
        out_shape=[
            jax.ShapeDtypeStruct((64 * heads, 256), f32),
            jax.ShapeDtypeStruct((32 * heads, 256), f32),
        ],
        scratch_shapes=[
            pltpu.VMEM((80 * heads, deep), bf16),
            pltpu.VMEM((256, deep), bf16),
            pltpu.VMEM((256, deep), bf16),
        ] * parts,
        compiler_params=pltpu.CompilerParams(vmem_limit_bytes=56 << 20),
        cost_estimate=pl.CostEstimate(
            flops=heads * count * count * 512, bytes_accessed=150 << 20, transcendentals=0),
        name="table_grads",
    )(page_lengths, ds, code)


def bucket_sums(raw, heads):
    right = raw.shape[1] // 16
    left = raw.shape[0] // (16 * heads)
    cube = raw.reshape(left, heads, 16, right, 16)
    traced = jnp.sum(cube * jnp.eye(16, dtype=f32)[None, None, :, None, :], axis=(2, 4))
    if left == 4:
        traced = jnp.concatenate([traced[3:], traced[:3]], axis=0)

    def table(n):
        v = lax.iota(jnp.int32, n)
        both = v[:, None] & v[None, :]
        return (1 - 2 * (lax.population_count(both) & 1)).astype(f32)

    out = jnp.einsum("ahn,ax,ny->yxh", traced, table(left), table(right), precision=lax.Precision.HIGHEST)
    return out.reshape(left * right, heads) / (left * right)


TANH_SLOPE = 0.7978845608028654
CUBE = 0.044715


def feed_forward_kernel(far, x_ref, g_ref, *refs):
    weights, (hidden_ref, d_gate_ref, d_up_ref, dn_ref) = refs[:-4], refs[-4:]
    units = hidden_ref.shape[1]
    if far:
        step = pad_lanes(units)
        gate_weight, up_weight, down = [weights[0][:, n * step:n * step + units] for n in range(3)]
        ahead, back = NN, NT
    else:
        gate_weight, up_weight, down = [w[...] for w in weights]
        ahead, back = NT, NN
    x = x_ref[...]
    d_hidden = dot(g_ref[...], down, ahead)
    gate = dot(x, gate_weight, ahead)
    up = dot(x, up_weight, ahead)
    square = gate * gate
    t = jnp.tanh(TANH_SLOPE * gate * (1.0 + CUBE * square))
    half = 0.5 + 0.5 * t
    gelu = gate * half
    slope = half + (0.5 * TANH_SLOPE) * gate * (1.0 - t * t) * (1.0 + (3 * CUBE) * square)
    d_gate = (d_hidden * up * slope).astype(bf16)
    d_up = (d_hidden * gelu).astype(bf16)
    hidden_ref[...] = (gelu * up).astype(bf16)
    d_gate_ref[...] = d_gate
    d_up_ref[...] = d_up
    dn_ref[...] = dot(d_gate, gate_weight, back) + dot(d_up, up_weight, back)


def feed_forward(x, g, units, weights, shard=None, tile=256):
    tokens, features = x.shape
    tile = min(tile, tokens)
    rows = lambda n: pl.BlockSpec((tile, n), lambda i: (i, 0))
    if shard is None:
        weight_specs = [pl.BlockSpec(w.shape, lambda i: (0, 0)) for w in weights]
    else:
        weight_specs = [pl.BlockSpec((features, 3 * pad_lanes(units)), lambda i: (0, shard))]
    return pl.pallas_call(
        functools.partial(feed_forward_kernel, shard is not None),
        grid=(tokens // tile,),
        in_specs=[rows(features), rows(features)] + weight_specs,
        out_specs=[rows(units)] * 3 + [rows(features)],
        out_shape=[jax.ShapeDtypeStruct((tokens, units), bf16)] * 3
        + [jax.ShapeDtypeStruct((tokens, features), f32)],
        compiler_params=pltpu.CompilerParams(vmem_limit_bytes=56 << 20),
        cost_estimate=pl.CostEstimate(
            flops=10 * tokens * features * units, bytes_accessed=10 << 20, transcendentals=tokens * units),
        name="feed_forward",
    )(x, g, *weights)


def pad_lanes(n):
    return (n + 127) // 128 * 128


def weight_grads_kernel(n_left, n_right, *refs):
    lefts = refs[:2 * n_left]
    rights = refs[2 * n_left:-1]
    out_ref = refs[-1]
    rows_in = (((0,), (0,)), ((), ()))
    place = 0
    for n, left in enumerate(n_right):
        a, b = rights[2 * n], rights[2 * n + 1]
        size = a.shape[1]
        value = dot(lefts[2 * left][...], a[...], rows_in) + dot(lefts[2 * left + 1][...], b[...], rows_in)
        out_ref[:, place:place + size] = value.astype(bf16)
        if pad_lanes(size) > size:
            out_ref[:, place + size:place + pad_lanes(size)] = jnp.zeros(
                (out_ref.shape[0], pad_lanes(size) - size), bf16)
        place += pad_lanes(size)


def weight_grads(lefts, rights, groups, tile=256):
    features = lefts[0].shape[1]
    columns = sum(pad_lanes(r.shape[1]) for r in rights[::2])
    column = lambda a: pl.BlockSpec((a.shape[0], tile), lambda i: (0, i))
    whole = lambda a: pl.BlockSpec(a.shape, lambda i: (0, 0))
    return pl.pallas_call(
        functools.partial(weight_grads_kernel, len(lefts) // 2, groups),
        grid=(features // tile,),
        in_specs=[column(a) for a in lefts] + [whole(a) for a in rights],
        out_specs=pl.BlockSpec((tile, columns), lambda i: (i, 0)),
        out_shape=jax.ShapeDtypeStruct((features, columns), bf16),
        compiler_params=pltpu.CompilerParams(vmem_limit_bytes=56 << 20),
        cost_estimate=pl.CostEstimate(
            flops=4 * features * columns * lefts[0].shape[0], bytes_accessed=26 << 20, transcendentals=0),
        name="weight_grads",
    )(*lefts, *rights)


epsilon = 1e-06


def contract_rows(left, right):
    return lax.dot_general(
        left, right, (((0,), (0,)), ((), ())), preferred_element_type=jnp.float32
    )


def contract_cols(left, right):
    return lax.dot_general(
        left, right, (((1,), (1,)), ((), ())), preferred_element_type=jnp.float32
    )


def norm_rows(rows, gain):
    scale = lax.rsqrt(jnp.mean(rows * rows, axis=-1, keepdims=True) + epsilon)
    return (scale, (rows * scale * gain).astype(jnp.bfloat16))


def norm_back(d_normed, rows, scale, gain):
    shaped = d_normed * gain
    cubed = scale * scale * scale
    return scale * shaped - rows * cubed * jnp.mean(shaped * rows, axis=-1, keepdims=True)


def along(array, shift, ring):
    return lax.ppermute(array, "narrow", [(i, (i + shift) % ring) for i in range(ring)])


def swap(array, ring):
    return lax.ppermute(array, "narrow", [(i, i ^ 1) for i in range(ring)])


def rows_of(array, index, count):
    return lax.dynamic_slice_in_dim(array, index * count, count, 0)


def on_device(
    wide,
    ring,
    layer_input,
    out_grad,
    norm_attn_gain,
    w_query,
    w_key,
    w_value,
    w_out,
    rel_table,
    layout_table,
    norm_ffn_gain,
    w_gate,
    w_up,
    down_projection_weight,
    page_lengths,
    key_mask,
    rel_bucket,
    layout_bucket,
):
    tokens, width = layer_input.shape
    head_cols = w_query.shape[1]
    heads = head_cols // DH
    units = w_gate.shape[1]
    padded = pad_lanes(units)
    part = width // wide
    me = lax.axis_index("narrow")
    my_wide = lax.axis_index("wide")
    gain_attn = norm_attn_gain.astype(f32)
    gain_ffn = norm_ffn_gain.astype(f32)
    resid = layer_input.astype(f32)

    scale_attn, normed_attn = norm_rows(resid, gain_attn)
    normed_attn_all = lax.all_gather(normed_attn, "narrow", axis=0, tiled=True)

    w_project = jnp.concatenate([w_query, w_key, w_value], axis=1)
    own_rows_gate = rows_of(w_gate, my_wide, part)
    own_rows_up = rows_of(w_up, my_wide, part)
    own_rows_project = rows_of(w_project, my_wide, part)
    down_piece = lax.dynamic_slice_in_dim(down_projection_weight, my_wide * part, part, 1).T
    out_piece = lax.dynamic_slice_in_dim(w_out, my_wide * part, part, 1).T
    ffn_piece = jnp.concatenate(
        [jnp.pad(piece, ((0, 0), (0, padded - units))) for piece in (own_rows_gate, own_rows_up, down_piece)], axis=1)
    out_pieces = [out_piece] + [along(out_piece, d, ring) for d in range(1, ring)]
    words, codes = pair_bias(page_lengths, rel_bucket, layout_bucket, bias_words(rel_table, layout_table), key_mask)
    normed_attn_all, ffn_piece, words = lax.optimization_barrier((normed_attn_all, ffn_piece, words))
    ffn_pieces = [along(ffn_piece, d, ring) for d in range(2, ring, 2)]
    out_t = lax.all_gather(jnp.concatenate(out_pieces, axis=1), "wide", axis=0, tiled=True)

    projected, late_grad = lax.optimization_barrier((dot(normed_attn_all, w_project).astype(bf16), out_grad))
    other_grad = swap(late_grad, ring)
    pairs = head_cols // 128
    first_pair = list(attention_forward(page_lengths, projected, words, 0))
    first_pair[0], ffn_pieces, other_grad, late_project = lax.optimization_barrier(
        (first_pair[0], ffn_pieces, other_grad, own_rows_project))
    far_pieces = jnp.concatenate(ffn_pieces, axis=1)

    def to_owners(a):
        return [rows_of(a, me, tokens)] + [
            along(rows_of(a, (me + d) % ring, tokens), d, ring) for d in range(1, ring)]

    sent = [to_owners(first_pair[0])]
    project_pieces = [own_rows_project] + [along(late_project, d, ring) for d in range(1, ring)]
    results = [first_pair]
    if pairs > 1:
        late_projected, far_pieces = lax.optimization_barrier((projected, far_pieces))
        results += [list(attention_forward(page_lengths, late_projected, words, p)) for p in range(1, pairs)]
    far = lax.all_gather(far_pieces, "wide", axis=0, tiled=True)
    if pairs > 1:
        results[1][0], project_pieces, sent[0] = lax.optimization_barrier((results[1][0], project_pieces, sent[0]))
    w_project_all = lax.all_gather(jnp.concatenate(project_pieces, axis=1), "wide", axis=0, tiled=True)
    attended = [r[0] for r in results]
    sent += [to_owners(a) for a in attended[1:]]
    mine = [pieces[d] for d in range(ring) for pieces in sent]
    attended_own = jnp.concatenate(mine, axis=1)
    middle = resid + contract_cols(attended_own, out_t)

    scale_ffn, normed_ffn = norm_rows(middle, gain_ffn)
    other_normed = swap(normed_ffn, ring)
    near = (w_gate.T, w_up.T, down_projection_weight)
    shards = ring // 2
    own = [feed_forward(normed_ffn, out_grad, units, near)]
    own += [feed_forward(normed_ffn, out_grad, units, (far,), s) for s in range(shards - 1)]
    own, other_normed = lax.optimization_barrier((own, other_normed))
    other = [feed_forward(other_normed, other_grad, units, near)]
    other += [feed_forward(other_normed, other_grad, units, (far,), s) for s in range(shards - 1)]
    other_d_normed = swap(sum(o[3] for o in other).astype(bf16), ring)
    rights, groups = [], []
    for s in range(shards):
        for n in range(1, 4):
            rights += [own[s][n % 3], other[s][n % 3]]
            groups.append(n // 3)
    sums = weight_grads((normed_ffn, other_normed, out_grad, other_grad), rights, tuple(groups))
    own_out, other_out = 0.0, 0.0
    for s in range(shards):
        if s == 0:
            down, dims = down_projection_weight, NN
        else:
            at = 3 * padded * (s - 1) + 2 * padded
            down, dims = far[:, at : at + units], NT
        own_out = own_out + dot(own[s][0], down, dims)
        other_out = other_out + dot(other[s][0], down, dims)
    own_out = own_out + middle
    sums, other_d_normed, own_out, other_out = lax.optimization_barrier(
        (sums, other_d_normed, own_out, other_out.astype(bf16)))
    ffn_sums = lax.psum_scatter(sums, "wide", scatter_dimension=0, tiled=True)
    d_normed_ffn = sum(o[3] for o in own) + other_d_normed.astype(f32)
    d_middle = out_grad.astype(f32) + norm_back(d_normed_ffn, middle, scale_ffn, gain_ffn)
    d_middle_low = d_middle.astype(bf16)
    d_attended_own = dot(d_middle_low, out_t).astype(bf16)

    def block(d):
        return d_attended_own[:, d * head_cols : (d + 1) * head_cols]

    d_attended = jnp.zeros((ring * tokens, head_cols), bf16)
    d_attended = lax.dynamic_update_slice_in_dim(d_attended, block(0), me * tokens, 0)
    for d in range(1, ring):
        d_attended = lax.dynamic_update_slice_in_dim(
            d_attended, along(block(d), -d, ring), ((me + d) % ring) * tokens, 0)

    d_middle_late, attended_late = lax.optimization_barrier((d_middle_low, attended_own))
    wout_sums = contract_rows(d_middle_late, attended_late).astype(bf16)
    wout_sums, d_attended, w_project_all, other_out = lax.optimization_barrier(
        (wout_sums, d_attended, w_project_all, other_out))
    other_out = swap(other_out, ring)

    d_project, d_scores = attention_backward(
        page_lengths, projected, [r[2] for r in results], d_attended, attended, [r[1] for r in results])
    d_project, other_out = lax.optimization_barrier((d_project, other_out))
    leaving = [rows_of(d_project, (me + d) % ring, tokens) for d in range(ring)]
    leaving, d_project, own_out = lax.optimization_barrier((leaving, d_project, own_out))
    mine = leaving[:1] + [along(leaving[d], d, ring) for d in range(1, ring)]
    layer_out = (own_out + other_out.astype(f32)).astype(bf16)
    last_sums = jnp.concatenate([contract_rows(normed_attn_all, d_project).astype(bf16), wout_sums], axis=1)
    last_sums, ffn_sums = lax.optimization_barrier((last_sums, ffn_sums))
    last_sums = lax.psum_scatter(last_sums, "wide", scatter_dimension=0, tiled=True)

    raw_lay, raw_rel = table_grads(page_lengths, d_scores, codes)
    raw_lay, raw_rel, ffn_sums = lax.optimization_barrier((raw_lay, raw_rel, ffn_sums))
    raw_lay, raw_rel, mine = lax.optimization_barrier((raw_lay, raw_rel, mine))
    far_sums = [along(ffn_sums[:, 3 * padded * s : 3 * padded * (s + 1)], -2 * s, ring) for s in range(1, shards)]
    grad_relative = bucket_sums(raw_rel, heads)
    grad_layout = bucket_sums(raw_lay, heads)
    tables = jnp.concatenate(
        [grad_relative.reshape(wide, -1, heads), grad_layout.reshape(wide, -1, heads)], axis=1)
    n_rel = grad_relative.shape[0] // wide
    reach = wide // 2
    while reach >= 1:
        bit = (my_wide // reach) % 2
        keep = lax.dynamic_slice_in_dim(tables, bit * reach, reach, 0)
        give = lax.dynamic_slice_in_dim(tables, (1 - bit) * reach, reach, 0)
        tables = keep + lax.ppermute(give, "wide", [(i, i ^ reach) for i in range(wide)])
        reach //= 2
    sum_project = last_sums[:, : 3 * head_cols].astype(f32)
    wout_sums = last_sums[:, 3 * head_cols :]
    far_wout = [along(wout_sums[:, d * head_cols : (d + 1) * head_cols], -d, ring) for d in range(1, ring)]
    sum_tables = tables[0]
    d_project_own = jnp.concatenate(mine, axis=1)
    d_normed_attn = contract_cols(d_project_own, w_project_all)
    in_grad = d_middle + norm_back(d_normed_attn, resid, scale_attn, gain_attn)

    def stripe(shard, n):
        at = padded * (3 * shard + n)
        return ffn_sums[:, at : at + units]

    sum_gate, sum_up, sum_down = [stripe(0, n).astype(f32) for n in range(3)]
    for s in range(1, shards):
        block = far_sums[s - 1].astype(f32)
        sum_gate += block[:, :units]
        sum_up += block[:, padded : padded + units]
        sum_down += block[:, 2 * padded : 2 * padded + units]
    sum_wout = wout_sums[:, :head_cols].astype(f32) + sum(w.astype(f32) for w in far_wout)

    gain_terms = jnp.stack(
        [
            jnp.sum(own_rows_project.astype(f32) * sum_project, axis=1),
            jnp.sum(own_rows_gate.astype(f32) * sum_gate + own_rows_up.astype(f32) * sum_up, axis=1),
        ]
    )
    share = part // ring

    def gain_share(index):
        return lax.dynamic_slice_in_dim(gain_terms, index * share, share, 1)

    gain_sum = gain_share(me)
    for d in range(1, ring):
        gain_sum = gain_sum + along(gain_share((me + d) % ring), d, ring)
    place = my_wide * part + me * share
    gains = lax.dynamic_slice_in_dim(jnp.stack([gain_attn, gain_ffn]), place, share, 1)
    gain_grads = gain_sum / gains
    return (
        layer_out,
        in_grad,
        gain_grads[0],
        sum_project[:, :head_cols],
        sum_project[:, head_cols : 2 * head_cols],
        sum_project[:, 2 * head_cols :],
        sum_wout.T,
        sum_tables[:n_rel],
        sum_tables[n_rel:],
        gain_grads[1],
        sum_gate,
        sum_up,
        sum_down.T,
    )


def solution(mesh):
    placed = (
        P(("wide", "narrow"), None),
        P(("wide", "narrow"), None),
        P(),
        P(None, "narrow"),
        P(None, "narrow"),
        P(None, "narrow"),
        P("narrow", None),
        P(None, "narrow"),
        P(None, "narrow"),
        P(),
        P(None, "narrow"),
        P(None, "narrow"),
        P("narrow", None),
        P("wide", None),
        P("wide"),
        P("wide", None),
        P("wide", None),
    )
    return jax.shard_map(
        functools.partial(on_device, mesh.shape["wide"], mesh.shape["narrow"]),
        mesh=mesh,
        in_specs=placed,
        out_specs=(
            P(("wide", "narrow"), None),
            P(("wide", "narrow"), None),
            P(("wide", "narrow")),
            P("wide", "narrow"),
            P("wide", "narrow"),
            P("wide", "narrow"),
            P("narrow", "wide"),
            P("wide", "narrow"),
            P("wide", "narrow"),
            P(("wide", "narrow")),
            P("wide", "narrow"),
            P("wide", "narrow"),
            P("narrow", "wide"),
        ),
        check_vma=False,
    )
```

```python
import functools
import jax
import jax.numpy as jnp
from jax import lax
from jax.experimental import pallas as pl
from jax.experimental.pallas import tpu as pltpu
from jax.sharding import PartitionSpec as P

DH = 64
BIAS_SCALE = 4096.0
LOG2E = 1.4426950408889634
f32 = jnp.float32
bf16 = jnp.bfloat16
NT = (((1,), (1,)), ((), ()))
NN = (((1,), (0,)), ((), ()))


def dot(a, b, dims=NN):
    return lax.dot_general(a, b, dims, preferred_element_type=f32)


def key_window(len_ref, first, last, count, width):
    ends = []
    total = 0
    for p in range(len_ref.shape[1]):
        total = total + len_ref[0, p]
        ends.append(total)
    start = 0
    stop = count
    for e in ends:
        start = jnp.where(e <= first, e, start)
    for e in reversed(ends):
        stop = jnp.where(e > last, e, stop)
    base = (start // 128) * 128
    steps = (stop - base + width - 1) // width
    base = jnp.minimum(base, count - steps * width)
    return ends, base, steps


def for_chunks(base, steps, width, group, body):
    def many(j, carry):
        body(pl.multiple_of(base + j * (group * width), 128), group * width)
        return carry

    def single(j, carry):
        body(pl.multiple_of(base + j * width, 128), width)
        return carry

    if group > 1:
        lax.fori_loop(0, steps // group, many, 0)
    lax.fori_loop((steps // group) * group if group > 1 else 0, steps, single, 0)


def own_half(shape, head):
    lane = lax.broadcasted_iota(jnp.int32, shape, len(shape) - 1)
    return (lane < DH) if head % 2 == 0 else (lane >= DH)


def fill_values(vext, v_ref, heads):
    for h in range(heads):
        vp = v_ref[:, (h // 2) * 128:(h // 2 + 1) * 128]
        vext[h] = jnp.where(own_half(vp.shape, h), vp, jnp.ones_like(vp))


def half_norms(rows):
    lane = lax.broadcasted_iota(jnp.int32, (128, 128), 0)
    column = lax.broadcasted_iota(jnp.int32, (128, 128), 1)
    same = ((lane < DH) == (column < DH)).astype(bf16)
    squares = (rows.astype(f32) * rows.astype(f32)).astype(bf16)
    return jnp.max(dot(squares, same)) * f32(1.02)


HIDDEN_PAIR = -(1 << 31)


def pair_bias_kernel(len_ref, rel_ref, lay_ref, tab_ref, kmask_ref, word_ref, code_ref, colcode, *, width, group):
    tq, count = rel_ref.shape
    pairs = word_ref.shape[0]
    i = pl.program_id(0)
    t0 = i * tq
    ends, base, steps = key_window(len_ref, t0, t0 + tq - 1, count, width)

    @pl.when(i == 0)
    def _():
        pos = lax.broadcasted_iota(jnp.int32, (8, count), 1)
        page = jnp.zeros((8, count), jnp.int32)
        for e in ends:
            page = page + (pos >= e).astype(jnp.int32)
        colcode[...] = jnp.where(kmask_ref[...] == 1, page, -1)

    rowpos = lax.broadcasted_iota(jnp.int32, (tq, 128), 0) + t0
    rowpage = jnp.zeros((tq, 128), jnp.int32)
    for e in ends:
        rowpage = rowpage + (rowpos >= e).astype(jnp.int32)
    lanes = lax.broadcasted_iota(jnp.int32, (tq, 128), 1)
    tabs = [jnp.broadcast_to(tab_ref[n:n + 1, :], (tq, 128)) for n in range(2 * pairs)]

    def chunk(c0, size):
        for half in range(size // 128):
            cc = pl.multiple_of(c0 + half * 128, 128)
            here = pl.ds(cc, 128)
            rel = rel_ref[:, here]
            lay = lay_ref[:, here]
            code_ref[:, here] = (rel + lay * 32).astype(jnp.int16)
            col = jnp.broadcast_to(colcode[0:1, here], (tq, 128))
            seen = (rowpage == col) | (rowpos == lanes + cc)
            for p in range(pairs):
                word = (jnp.take_along_axis(tabs[2 * p], rel, axis=1, mode="promise_in_bounds")
                        + jnp.take_along_axis(tabs[2 * p + 1], lay, axis=1, mode="promise_in_bounds"))
                word_ref[p, :, here] = jnp.where(seen, word, HIDDEN_PAIR)

    for_chunks(base, steps, width, group, chunk)


def pair_bias(page_lengths, rel, lay, tab, kmask, tq=256, width=256, group=2):
    count = rel.shape[0]
    pairs = tab.shape[0] // 2
    tile = lambda i: (i, 0)
    return pl.pallas_call(
        functools.partial(pair_bias_kernel, width=width, group=group),
        grid=(count // tq,),
        in_specs=[
            pl.BlockSpec(memory_space=pltpu.SMEM),
            pl.BlockSpec((tq, count), tile),
            pl.BlockSpec((tq, count), tile),
            pl.BlockSpec(tab.shape, lambda i: (0, 0)),
            pl.BlockSpec((1, count), lambda i: (0, 0)),
        ],
        out_specs=[
            pl.BlockSpec((pairs, tq, count), lambda i: (0, i, 0)),
            pl.BlockSpec((tq, count), tile),
        ],
        out_shape=[
            jax.ShapeDtypeStruct((pairs, count, count), jnp.int32),
            jax.ShapeDtypeStruct((count, count), jnp.int16),
        ],
        scratch_shapes=[pltpu.VMEM((8, count), jnp.int32)],
        compiler_params=pltpu.CompilerParams(vmem_limit_bytes=56 << 20),
        cost_estimate=pl.CostEstimate(flops=count * count * 1024, bytes_accessed=120 << 20, transcendentals=0),
        name="pair_bias",
    )(page_lengths, rel, lay, tab, kmask.reshape(1, count))


def forward_kernel(len_ref, q_ref, k_ref, v_ref, word_ref, att_ref, rinv_ref, e_ref,
                   s_scr, m_scr, acc_scr, vext, knorm, *, width, group):
    tq, count = word_ref.shape[1:]
    heads, pairs = 2, 1
    i = pl.program_id(0)
    t0 = i * tq
    ends, base, steps = key_window(len_ref, t0, t0 + tq - 1, count, width)

    @pl.when(i == 0)
    def _():
        fill_values(vext, v_ref, heads)
        for p in range(pairs):
            knorm[p] = half_norms(k_ref[:, p * 128:(p + 1) * 128])

    scaled = []
    largest = f32(0.0)
    for h in range(heads):
        qp = q_ref[:, (h // 2) * 128:(h // 2 + 1) * 128]
        scaled.append(jnp.where(own_half(qp.shape, h), qp * bf16(BIAS_SCALE), jnp.zeros_like(qp)))
        if h % 2 == 0:
            largest = jnp.maximum(largest, half_norms(qp) * knorm[h // 2])
    def scores(c0, width, use):
        raw = [dot(scaled[h], k_ref[pl.ds(c0, width), (h // 2) * 128:(h // 2 + 1) * 128], NT)
               for h in range(heads)]
        for half in range(width // 128):
            cc = pl.multiple_of(c0 + half * 128, 128)
            word = word_ref[0, :, pl.ds(cc, 128)]
            hidden = word == HIDDEN_PAIR
            parts = ((word & 0xFFFF).astype(f32), (word >> 16).astype(f32))
            for h in range(heads):
                bias = jnp.where(hidden, f32(-1e30), parts[h])
                use(h, half, cc, raw[h][:, half * 128:(half + 1) * 128] + bias)

    for h in range(heads):
        acc_scr[h] = jnp.zeros((tq, 128), f32)
    bounded = jnp.sqrt(largest) + 8.0 <= 60.0

    @pl.when(bounded)
    def _():
        def chunk(c0, size):
            pieces = {}

            def use(h, half, cc, s):
                e = jnp.exp2(s * f32(LOG2E / BIAS_SCALE)).astype(bf16)
                e_ref[h, :, pl.ds(cc, 128)] = e
                pieces[h, half] = e

            scores(c0, size, use)
            for h in range(heads):
                e = jnp.concatenate([pieces[h, half] for half in range(size // 128)], axis=1)
                acc_scr[h] += dot(e, vext[h, pl.ds(c0, size), :])

        for_chunks(base, steps, width, group, chunk)

    @pl.when(jnp.logical_not(bounded))
    def _():
        for h in range(heads):
            m_scr[h] = jnp.full((tq, 128), -3e38, f32)

        def first(j, carry):
            def use(h, half, cc, s):
                s_scr[h, :, pl.ds(cc, 128)] = s
                m_scr[h] = jnp.maximum(m_scr[h], s)

            scores(pl.multiple_of(base + j * width, 128), width, use)
            return carry

        lax.fori_loop(0, steps, first, 0)
        for h in range(heads):
            top = jnp.max(m_scr[h], axis=1, keepdims=True)

            def second(j, carry):
                c0 = pl.multiple_of(base + j * width, 128)
                e = jnp.exp2((s_scr[h, :, pl.ds(c0, width)] - top) * f32(LOG2E / BIAS_SCALE)).astype(bf16)
                e_ref[h, :, pl.ds(c0, width)] = e
                acc_scr[h] += dot(e, vext[h, pl.ds(c0, width), :])
                return carry

            lax.fori_loop(0, steps, second, 0)

    low = own_half((tq, 128), 0)
    for p in range(pairs):
        even, odd = acc_scr[2 * p], acc_scr[2 * p + 1]
        rinv = 1.0 / pltpu.roll(jnp.where(low, odd, even), DH, 1)
        att_ref[:, p * 128:(p + 1) * 128] = (jnp.where(low, even, odd) * rinv).astype(bf16)
        rinv_ref[:, p * 128:(p + 1) * 128] = rinv


def attention_forward(page_lengths, proj, words, pair, tq=256, width=256, group=2):
    count = proj.shape[0]
    pairs = proj.shape[1] // (3 * 128)
    tile = lambda i: (i, 0)
    return pl.pallas_call(
        functools.partial(forward_kernel, width=width, group=group),
        grid=(count // tq,),
        in_specs=[
            pl.BlockSpec(memory_space=pltpu.SMEM),
            pl.BlockSpec((tq, 128), lambda i: (i, pair)),
            pl.BlockSpec((count, 128), lambda i: (0, pairs + pair)),
            pl.BlockSpec((count, 128), lambda i: (0, 2 * pairs + pair)),
            pl.BlockSpec((1, tq, count), lambda i: (pair, i, 0)),
        ],
        out_specs=[
            pl.BlockSpec((tq, 128), tile),
            pl.BlockSpec((tq, 128), tile),
            pl.BlockSpec((2, tq, count), lambda i: (0, i, 0)),
        ],
        out_shape=[
            jax.ShapeDtypeStruct((count, 128), bf16),
            jax.ShapeDtypeStruct((count, 128), f32),
            jax.ShapeDtypeStruct((2, count, count), bf16),
        ],
        scratch_shapes=[
            pltpu.VMEM((2, tq, count), f32),
            pltpu.VMEM((2, tq, 128), f32),
            pltpu.VMEM((2, tq, 128), f32),
            pltpu.VMEM((2, count, 128), bf16),
            pltpu.SMEM((1,), f32),
        ],
        compiler_params=pltpu.CompilerParams(vmem_limit_bytes=56 << 20),
        cost_estimate=pl.CostEstimate(
            flops=count * count * 512, bytes_accessed=80 << 20, transcendentals=count * count),
        name="attention_forward",
    )(page_lengths, proj, proj, proj, words)


def bias_words(rel_table, layout_table):
    def pack(table):
        whole = jnp.round(table.astype(f32) * BIAS_SCALE).astype(jnp.int32)
        low = jnp.clip(whole[:, 0::2] + 16384, 0, 32767)
        high = jnp.clip(whole[:, 1::2], -16383, 16383)
        words = (high * 65536 + low).T
        return jnp.pad(words, ((0, 0), (0, 128 - words.shape[1])))
    both = jnp.stack([pack(rel_table), pack(layout_table)], axis=1)
    return both.reshape(-1, 128)


def signs(code, shift, bits):
    return [jnp.where((code & jnp.int16(1 << (shift + b))) == 0, bf16(1.0), bf16(-1.0))
            for b in range(bits)]


def walsh(sign_list):
    out = [None]
    for s in sign_list:
        out = out + [s if o is None else o * s for o in out]
    return out


def backward_kernel(len_ref, q_ref, k_ref, v_ref, da_ref, *refs, width, heads, group):
    tq = q_ref.shape[0]
    count = k_ref.shape[0]
    pairs = heads // 2
    e_refs, att_refs, rinv_refs = refs[:pairs], refs[pairs:2 * pairs], refs[2 * pairs:3 * pairs]
    dp_ref, ds_ref = refs[3 * pairs:3 * pairs + 2]
    vext, lhs_scr, dat_scr, qt_scr, dq_scr, dkt, dvt = refs[3 * pairs + 2:]
    i = pl.program_id(0)
    t0 = i * tq
    ends, base, steps = key_window(len_ref, t0, t0 + tq - 1, count, width)

    @pl.when(i == 0)
    def _():
        fill_values(vext, v_ref, heads)
        dkt[...] = jnp.zeros_like(dkt)
        dvt[...] = jnp.zeros_like(dvt)

    low = own_half((tq, 128), 0)
    lane = lax.broadcasted_iota(jnp.int32, (tq, 128), 1)
    first_part = (lane & 32) == 0
    for p in range(pairs):
        cols = slice(p * 128, (p + 1) * 128)
        da = (da_ref[:, cols].astype(f32) * rinv_refs[p][...]).astype(bf16)
        daf = da.astype(f32)
        prod = daf * att_refs[p][...].astype(f32)
        for r in range(2):
            own = low if r == 0 else jnp.logical_not(low)
            delta = jnp.sum(jnp.where(own, prod, 0.0), axis=1, keepdims=True) * f32(-1.0 / 32)
            high = delta.astype(bf16).astype(f32)
            rest = delta - high
            lhs_scr[2 * p + r] = jnp.where(own, daf, jnp.where(first_part, high, rest)).astype(bf16)
        dat_scr[p] = daf.T.astype(bf16)
        qt_scr[p] = q_ref[:, cols].astype(f32).T.astype(bf16)
        dq_scr[p] = jnp.zeros((tq, 128), f32)

    def chunk(c0, size):
        here = pl.ds(c0, size)
        for p in range(pairs):
            kp = k_ref[here, p * 128:(p + 1) * 128]
            dqs = []
            for r in range(2):
                h = 2 * p + r
                rows = slice(r * DH, (r + 1) * DH)
                e = e_refs[p][r, :, here]
                d = dot(lhs_scr[h], vext[h, here, :], NT)
                ds = (e.astype(f32) * d).astype(bf16)
                ds_ref[h, :, here] = ds
                dqs.append(dot(ds, kp))
                dkt[p, rows, here] += dot(qt_scr[p, rows, :], ds)
                dvt[p, rows, here] += dot(dat_scr[p, rows, :], e)
            dq_scr[p] += jnp.where(low, dqs[0], dqs[1])

    for_chunks(base, steps, width, group, chunk)
    for p in range(pairs):
        dp_ref[pl.ds(pl.multiple_of(t0, tq), tq), p * 128:(p + 1) * 128] = dq_scr[p].astype(bf16)

    @pl.when(i == pl.num_programs(0) - 1)
    def _():
        for n, grads in enumerate((dkt, dvt)):
            for p in range(pairs):
                at = ((n + 1) * pairs + p) * 128
                for c in range(0, count, 256):
                    dp_ref[c:c + 256, at:at + 128] = grads[p, :, c:c + 256].T.astype(bf16)


def attention_backward(page_lengths, proj, exps, d_att, atts, rinvs, tq=256, width=256, group=2):
    count = proj.shape[0]
    hc = proj.shape[1] // 3
    heads = hc // DH
    pairs = heads // 2
    grid = (count // tq,)
    tile = lambda i: (i, 0)
    fixed = lambda i: (0, 0)
    return pl.pallas_call(
        functools.partial(backward_kernel, width=width, heads=heads, group=group),
        grid=grid,
        in_specs=[
            pl.BlockSpec(memory_space=pltpu.SMEM),
            pl.BlockSpec((tq, hc), tile),
            pl.BlockSpec((count, hc), lambda i: (0, 1)),
            pl.BlockSpec((count, hc), lambda i: (0, 2)),
            pl.BlockSpec((tq, hc), tile),
        ] + [pl.BlockSpec((2, tq, count), lambda i: (0, i, 0))] * pairs + [pl.BlockSpec((tq, 128), tile)] * (2 * pairs),
        out_specs=[
            pl.BlockSpec((count, 3 * hc), fixed),
            pl.BlockSpec((heads, tq, count), lambda i: (0, i, 0)),
        ],
        out_shape=[
            jax.ShapeDtypeStruct((count, 3 * hc), bf16),
            jax.ShapeDtypeStruct((heads, count, count), bf16),
        ],
        scratch_shapes=[
            pltpu.VMEM((heads, count, 128), bf16),
            pltpu.VMEM((heads, tq, 128), bf16),
            pltpu.VMEM((pairs, 128, tq), bf16),
            pltpu.VMEM((pairs, 128, tq), bf16),
            pltpu.VMEM((pairs, tq, 128), f32),
            pltpu.VMEM((pairs, 128, count), f32),
            pltpu.VMEM((pairs, 128, count), f32),
        ],
        compiler_params=pltpu.CompilerParams(vmem_limit_bytes=56 << 20),
        cost_estimate=pl.CostEstimate(
            flops=heads * count * count * 512, bytes_accessed=150 << 20, transcendentals=0),
        name="attention_backward",
    )(page_lengths, proj, proj, proj, d_att, *exps, *atts, *rinvs)


def table_kernel(len_ref, ds_ref, code_ref, hl_ref, hr_ref, *bufs, width, parts):
    heads, tq, count = ds_ref.shape
    i = pl.program_id(0)
    t0 = i * tq
    ends, base, steps = key_window(len_ref, t0, t0 + tq - 1, count, width)

    @pl.when(i == 0)
    def _():
        hl_ref[...] = jnp.zeros_like(hl_ref)
        hr_ref[...] = jnp.zeros_like(hr_ref)

    one = jnp.ones((16, width), bf16)

    def chunk(j, carry):
        c0 = pl.multiple_of(base + j * width, 128)
        here = pl.ds(c0, width)
        blocks = tq // 16 // parts
        for part in range(parts):
            left, blay, brel = bufs[3 * part:3 * part + 3]
            for b in range(blocks):
                at = 16 * (part * blocks + b)
                rows = slice(at, at + 16)
                span = slice(b * width, (b + 1) * width)
                code = code_ref[rows, here]
                rel_signs = signs(code, 0, 5)
                lay_signs = signs(code, 5, 6)
                left_lay = walsh(lay_signs[:2])[1:]
                for h in range(heads):
                    ds = ds_ref[h, rows, here]
                    for a, func in enumerate(left_lay + [None, rel_signs[0]]):
                        place = 16 * (a * heads + h)
                        left[place:place + 16, span] = ds if func is None else ds * func
                for n, func in enumerate(walsh(lay_signs[2:])):
                    blay[16 * n:16 * (n + 1), span] = one if func is None else func
                for n, func in enumerate(walsh(rel_signs[1:])):
                    brel[16 * n:16 * (n + 1), span] = one if func is None else func
            hl_ref[...] += dot(left[:64 * heads, :], blay[...], NT)
            hr_ref[...] += dot(left[48 * heads:80 * heads, :], brel[...], NT)
        return carry

    lax.fori_loop(0, steps, chunk, 0)


def table_grads(page_lengths, ds, code, tq=256, width=256, parts=2):
    heads, count, _ = ds.shape
    deep = tq // 16 * width // parts
    fixed = lambda i: (0, 0)
    return pl.pallas_call(
        functools.partial(table_kernel, width=width, parts=parts),
        grid=(count // tq,),
        in_specs=[
            pl.BlockSpec(memory_space=pltpu.SMEM),
            pl.BlockSpec((heads, tq, count), lambda i: (0, i, 0)),
            pl.BlockSpec((tq, count), lambda i: (i, 0)),
        ],
        out_specs=[
            pl.BlockSpec((64 * heads, 256), fixed),
            pl.BlockSpec((32 * heads, 256), fixed),
        ],
        out_shape=[
            jax.ShapeDtypeStruct((64 * heads, 256), f32),
            jax.ShapeDtypeStruct((32 * heads, 256), f32),
        ],
        scratch_shapes=[
            pltpu.VMEM((80 * heads, deep), bf16),
            pltpu.VMEM((256, deep), bf16),
            pltpu.VMEM((256, deep), bf16),
        ] * parts,
        compiler_params=pltpu.CompilerParams(vmem_limit_bytes=56 << 20),
        cost_estimate=pl.CostEstimate(
            flops=heads * count * count * 512, bytes_accessed=150 << 20, transcendentals=0),
        name="table_grads",
    )(page_lengths, ds, code)


def bucket_sums(raw, heads):
    right = raw.shape[1] // 16
    left = raw.shape[0] // (16 * heads)
    cube = raw.reshape(left, heads, 16, right, 16)
    traced = jnp.sum(cube * jnp.eye(16, dtype=f32)[None, None, :, None, :], axis=(2, 4))
    if left == 4:
        traced = jnp.concatenate([traced[3:], traced[:3]], axis=0)

    def table(n):
        v = lax.iota(jnp.int32, n)
        both = v[:, None] & v[None, :]
        return (1 - 2 * (lax.population_count(both) & 1)).astype(f32)

    out = jnp.einsum("ahn,ax,ny->yxh", traced, table(left), table(right), precision=lax.Precision.HIGHEST)
    return out.reshape(left * right, heads) / (left * right)


TANH_SLOPE = 0.7978845608028654
CUBE = 0.044715


def feed_forward_kernel(far, x_ref, g_ref, *refs):
    weights, (hidden_ref, d_gate_ref, d_up_ref, dn_ref) = refs[:-4], refs[-4:]
    units = hidden_ref.shape[1]
    if far:
        step = pad_lanes(units)
        gate_weight, up_weight, down = [weights[0][:, n * step:n * step + units] for n in range(3)]
        ahead, back = NN, NT
    else:
        gate_weight, up_weight, down = [w[...] for w in weights]
        ahead, back = NT, NN
    x = x_ref[...]
    d_hidden = dot(g_ref[...], down, ahead)
    gate = dot(x, gate_weight, ahead)
    up = dot(x, up_weight, ahead)
    square = gate * gate
    t = jnp.tanh(TANH_SLOPE * gate * (1.0 + CUBE * square))
    half = 0.5 + 0.5 * t
    gelu = gate * half
    slope = half + (0.5 * TANH_SLOPE) * gate * (1.0 - t * t) * (1.0 + (3 * CUBE) * square)
    d_gate = (d_hidden * up * slope).astype(bf16)
    d_up = (d_hidden * gelu).astype(bf16)
    hidden_ref[...] = (gelu * up).astype(bf16)
    d_gate_ref[...] = d_gate
    d_up_ref[...] = d_up
    dn_ref[...] = dot(d_gate, gate_weight, back) + dot(d_up, up_weight, back)


def feed_forward(x, g, units, weights, shard=None, tile=256):
    tokens, features = x.shape
    tile = min(tile, tokens)
    rows = lambda n: pl.BlockSpec((tile, n), lambda i: (i, 0))
    if shard is None:
        weight_specs = [pl.BlockSpec(w.shape, lambda i: (0, 0)) for w in weights]
    else:
        weight_specs = [pl.BlockSpec((features, 3 * pad_lanes(units)), lambda i: (0, shard))]
    return pl.pallas_call(
        functools.partial(feed_forward_kernel, shard is not None),
        grid=(tokens // tile,),
        in_specs=[rows(features), rows(features)] + weight_specs,
        out_specs=[rows(units)] * 3 + [rows(features)],
        out_shape=[jax.ShapeDtypeStruct((tokens, units), bf16)] * 3
        + [jax.ShapeDtypeStruct((tokens, features), f32)],
        compiler_params=pltpu.CompilerParams(vmem_limit_bytes=56 << 20),
        cost_estimate=pl.CostEstimate(
            flops=10 * tokens * features * units, bytes_accessed=10 << 20, transcendentals=tokens * units),
        name="feed_forward",
    )(x, g, *weights)


def pad_lanes(n):
    return (n + 127) // 128 * 128


def weight_grads_kernel(n_left, n_right, *refs):
    lefts = refs[:2 * n_left]
    rights = refs[2 * n_left:-1]
    out_ref = refs[-1]
    rows_in = (((0,), (0,)), ((), ()))
    place = 0
    for n, left in enumerate(n_right):
        a, b = rights[2 * n], rights[2 * n + 1]
        size = a.shape[1]
        value = dot(lefts[2 * left][...], a[...], rows_in) + dot(lefts[2 * left + 1][...], b[...], rows_in)
        out_ref[:, place:place + size] = value.astype(bf16)
        if pad_lanes(size) > size:
            out_ref[:, place + size:place + pad_lanes(size)] = jnp.zeros(
                (out_ref.shape[0], pad_lanes(size) - size), bf16)
        place += pad_lanes(size)


def weight_grads(lefts, rights, groups, tile=256):
    features = lefts[0].shape[1]
    columns = sum(pad_lanes(r.shape[1]) for r in rights[::2])
    column = lambda a: pl.BlockSpec((a.shape[0], tile), lambda i: (0, i))
    whole = lambda a: pl.BlockSpec(a.shape, lambda i: (0, 0))
    return pl.pallas_call(
        functools.partial(weight_grads_kernel, len(lefts) // 2, groups),
        grid=(features // tile,),
        in_specs=[column(a) for a in lefts] + [whole(a) for a in rights],
        out_specs=pl.BlockSpec((tile, columns), lambda i: (i, 0)),
        out_shape=jax.ShapeDtypeStruct((features, columns), bf16),
        compiler_params=pltpu.CompilerParams(vmem_limit_bytes=56 << 20),
        cost_estimate=pl.CostEstimate(
            flops=4 * features * columns * lefts[0].shape[0], bytes_accessed=26 << 20, transcendentals=0),
        name="weight_grads",
    )(*lefts, *rights)


epsilon = 1e-06


def contract_rows(left, right):
    return lax.dot_general(
        left, right, (((0,), (0,)), ((), ())), preferred_element_type=jnp.float32
    )


def contract_cols(left, right):
    return lax.dot_general(
        left, right, (((1,), (1,)), ((), ())), preferred_element_type=jnp.float32
    )


def norm_rows(rows, gain):
    scale = lax.rsqrt(jnp.mean(rows * rows, axis=-1, keepdims=True) + epsilon)
    return (scale, (rows * scale * gain).astype(jnp.bfloat16))


def norm_back(d_normed, rows, scale, gain):
    shaped = d_normed * gain
    cubed = scale * scale * scale
    return scale * shaped - rows * cubed * jnp.mean(shaped * rows, axis=-1, keepdims=True)


def along(array, shift, ring):
    return lax.ppermute(array, "narrow", [(i, (i + shift) % ring) for i in range(ring)])


def swap(array, ring):
    return lax.ppermute(array, "narrow", [(i, i ^ 1) for i in range(ring)])


def rows_of(array, index, count):
    return lax.dynamic_slice_in_dim(array, index * count, count, 0)


def on_device(
    wide,
    ring,
    layer_input,
    out_grad,
    norm_attn_gain,
    w_query,
    w_key,
    w_value,
    w_out,
    rel_table,
    layout_table,
    norm_ffn_gain,
    w_gate,
    w_up,
    down_projection_weight,
    page_lengths,
    key_mask,
    rel_bucket,
    layout_bucket,
):
    tokens, width = layer_input.shape
    head_cols = w_query.shape[1]
    heads = head_cols // DH
    units = w_gate.shape[1]
    padded = pad_lanes(units)
    part = width // wide
    me = lax.axis_index("narrow")
    my_wide = lax.axis_index("wide")
    gain_attn = norm_attn_gain.astype(f32)
    gain_ffn = norm_ffn_gain.astype(f32)
    resid = layer_input.astype(f32)

    scale_attn, normed_attn = norm_rows(resid, gain_attn)
    normed_attn_all = lax.all_gather(normed_attn, "narrow", axis=0, tiled=True)

    w_project = jnp.concatenate([w_query, w_key, w_value], axis=1)
    own_rows_gate = rows_of(w_gate, my_wide, part)
    own_rows_up = rows_of(w_up, my_wide, part)
    own_rows_project = rows_of(w_project, my_wide, part)
    down_piece = lax.dynamic_slice_in_dim(down_projection_weight, my_wide * part, part, 1).T
    out_piece = lax.dynamic_slice_in_dim(w_out, my_wide * part, part, 1).T
    ffn_piece = jnp.concatenate(
        [jnp.pad(piece, ((0, 0), (0, padded - units))) for piece in (own_rows_gate, own_rows_up, down_piece)], axis=1)
    out_pieces = [out_piece] + [along(out_piece, d, ring) for d in range(1, ring)]
    words, codes = pair_bias(page_lengths, rel_bucket, layout_bucket, bias_words(rel_table, layout_table), key_mask)
    normed_attn_all, ffn_piece, words = lax.optimization_barrier((normed_attn_all, ffn_piece, words))
    ffn_pieces = [along(ffn_piece, d, ring) for d in range(2, ring, 2)]
    out_t = lax.all_gather(jnp.concatenate(out_pieces, axis=1), "wide", axis=0, tiled=True)

    projected = dot(normed_attn_all, w_project).astype(bf16)
    pairs = head_cols // 128
    first_pair = list(attention_forward(page_lengths, projected, words, 0))
    first_pair[0], ffn_pieces, late_grad = lax.optimization_barrier((first_pair[0], ffn_pieces, out_grad))
    far_pieces = jnp.concatenate(ffn_pieces, axis=1)
    other_grad = swap(late_grad, ring)

    def to_owners(a):
        return [rows_of(a, me, tokens)] + [
            along(rows_of(a, (me + d) % ring, tokens), d, ring) for d in range(1, ring)]

    sent = [to_owners(first_pair[0])]
    results = [first_pair]
    if pairs > 1:
        late_projected, far_pieces = lax.optimization_barrier((projected, far_pieces))
        results += [list(attention_forward(page_lengths, late_projected, words, p)) for p in range(1, pairs)]
    far = lax.all_gather(far_pieces, "wide", axis=0, tiled=True)
    results[-1][0], other_grad, sent[0] = lax.optimization_barrier((results[-1][0], other_grad, sent[0]))
    attended = [r[0] for r in results]
    sent += [to_owners(a) for a in attended[1:]]
    mine = [pieces[d] for d in range(ring) for pieces in sent]
    attended_own = jnp.concatenate(mine, axis=1)
    middle = resid + contract_cols(attended_own, out_t)

    scale_ffn, normed_ffn = norm_rows(middle, gain_ffn)
    other_normed = swap(normed_ffn, ring)
    near = (w_gate.T, w_up.T, down_projection_weight)
    shards = ring // 2
    own = [feed_forward(normed_ffn, out_grad, units, near)]
    own, other_normed, late_project = lax.optimization_barrier((own, other_normed, own_rows_project))
    project_pieces = [along(late_project, d, ring) for d in range(1, ring)]
    other = [feed_forward(other_normed, other_grad, units, near)]
    other += [feed_forward(other_normed, other_grad, units, (far,), s) for s in range(shards - 1)]
    other, project_pieces = lax.optimization_barrier((other, project_pieces))
    w_project_all = lax.all_gather(
        jnp.concatenate([own_rows_project] + project_pieces, axis=1), "wide", axis=0, tiled=True)
    other_d_normed = sum(o[3] for o in other).astype(bf16)
    late_normed, other_d_normed = lax.optimization_barrier((normed_ffn, other_d_normed))
    other_d_normed = swap(other_d_normed, ring)
    own += [feed_forward(late_normed, out_grad, units, (far,), s) for s in range(shards - 1)]
    rights, groups = [], []
    for s in range(shards):
        for n in range(1, 4):
            rights += [own[s][n % 3], other[s][n % 3]]
            groups.append(n // 3)
    sums = weight_grads((normed_ffn, other_normed, out_grad, other_grad), rights, tuple(groups))
    sums, other_d_normed = lax.optimization_barrier((sums, other_d_normed))
    ffn_sums = lax.psum_scatter(sums, "wide", scatter_dimension=0, tiled=True)
    d_normed_ffn = sum(o[3] for o in own) + other_d_normed.astype(f32)
    d_middle = out_grad.astype(f32) + norm_back(d_normed_ffn, middle, scale_ffn, gain_ffn)
    d_middle_low = d_middle.astype(bf16)
    d_attended_own = dot(d_middle_low, out_t).astype(bf16)

    def block(d):
        return d_attended_own[:, d * head_cols : (d + 1) * head_cols]

    d_attended = jnp.zeros((ring * tokens, head_cols), bf16)
    d_attended = lax.dynamic_update_slice_in_dim(d_attended, block(0), me * tokens, 0)
    for d in range(1, ring):
        d_attended = lax.dynamic_update_slice_in_dim(
            d_attended, along(block(d), -d, ring), ((me + d) % ring) * tokens, 0)

    d_middle_late, attended_late, own_hidden, other_hidden = lax.optimization_barrier(
        (d_middle_low, attended_own, [o[0] for o in own], [o[0] for o in other]))
    wout_sums = contract_rows(d_middle_late, attended_late).astype(bf16)
    own_out, other_out = 0.0, 0.0
    for s in range(shards):
        if s == 0:
            down, dims = down_projection_weight, NN
        else:
            at = 3 * padded * (s - 1) + 2 * padded
            down, dims = far[:, at : at + units], NT
        own_out = own_out + dot(own_hidden[s], down, dims)
        other_out = other_out + dot(other_hidden[s], down, dims)
    own_out = own_out + middle
    wout_sums, d_attended, w_project_all, own_out, other_out = lax.optimization_barrier(
        (wout_sums, d_attended, w_project_all, own_out, other_out.astype(bf16)))
    other_out = swap(other_out, ring)

    d_project, d_scores = attention_backward(
        page_lengths, projected, [r[2] for r in results], d_attended, attended, [r[1] for r in results])
    d_project, other_out = lax.optimization_barrier((d_project, other_out))
    leaving = [rows_of(d_project, (me + d) % ring, tokens) for d in range(ring)]
    leaving, d_project, own_out = lax.optimization_barrier((leaving, d_project, own_out))
    mine = leaving[:1] + [along(leaving[d], d, ring) for d in range(1, ring)]
    layer_out = (own_out + other_out.astype(f32)).astype(bf16)
    last_sums = jnp.concatenate([contract_rows(normed_attn_all, d_project).astype(bf16), wout_sums], axis=1)
    last_sums, ffn_sums = lax.optimization_barrier((last_sums, ffn_sums))
    last_sums = lax.psum_scatter(last_sums, "wide", scatter_dimension=0, tiled=True)

    raw_lay, raw_rel = table_grads(page_lengths, d_scores, codes)
    far_sums = [along(ffn_sums[:, 3 * padded * s : 3 * padded * (s + 1)], -2 * s, ring) for s in range(1, shards)]
    raw_lay, raw_rel, mine, far_sums, last_sums = lax.optimization_barrier(
        (raw_lay, raw_rel, mine, far_sums, last_sums))
    grad_relative = bucket_sums(raw_rel, heads)
    grad_layout = bucket_sums(raw_lay, heads)
    tables = jnp.concatenate(
        [grad_relative.reshape(wide, -1, heads), grad_layout.reshape(wide, -1, heads)], axis=1)
    n_rel = grad_relative.shape[0] // wide
    reach = wide // 2
    while reach >= 1:
        bit = (my_wide // reach) % 2
        keep = lax.dynamic_slice_in_dim(tables, bit * reach, reach, 0)
        give = lax.dynamic_slice_in_dim(tables, (1 - bit) * reach, reach, 0)
        tables = keep + lax.ppermute(give, "wide", [(i, i ^ reach) for i in range(wide)])
        reach //= 2
    sum_project = last_sums[:, : 3 * head_cols].astype(f32)
    wout_sums = last_sums[:, 3 * head_cols :]
    far_wout = [along(wout_sums[:, d * head_cols : (d + 1) * head_cols], -d, ring) for d in range(1, ring)]
    sum_tables = tables[0]
    d_project_own = jnp.concatenate(mine, axis=1)
    d_normed_attn = contract_cols(d_project_own, w_project_all)
    in_grad = d_middle + norm_back(d_normed_attn, resid, scale_attn, gain_attn)

    def stripe(shard, n):
        at = padded * (3 * shard + n)
        return ffn_sums[:, at : at + units]

    sum_gate, sum_up, sum_down = [stripe(0, n).astype(f32) for n in range(3)]
    for s in range(1, shards):
        block = far_sums[s - 1].astype(f32)
        sum_gate += block[:, :units]
        sum_up += block[:, padded : padded + units]
        sum_down += block[:, 2 * padded : 2 * padded + units]
    sum_wout = wout_sums[:, :head_cols].astype(f32) + sum(w.astype(f32) for w in far_wout)

    gain_terms = jnp.stack(
        [
            jnp.sum(own_rows_project.astype(f32) * sum_project, axis=1),
            jnp.sum(own_rows_gate.astype(f32) * sum_gate + own_rows_up.astype(f32) * sum_up, axis=1),
        ]
    )
    share = part // ring

    def gain_share(index):
        return lax.dynamic_slice_in_dim(gain_terms, index * share, share, 1)

    gain_sum = gain_share(me)
    for d in range(1, ring):
        gain_sum = gain_sum + along(gain_share((me + d) % ring), d, ring)
    place = my_wide * part + me * share
    gains = lax.dynamic_slice_in_dim(jnp.stack([gain_attn, gain_ffn]), place, share, 1)
    gain_grads = gain_sum / gains
    return (
        layer_out,
        in_grad,
        gain_grads[0],
        sum_project[:, :head_cols],
        sum_project[:, head_cols : 2 * head_cols],
        sum_project[:, 2 * head_cols :],
        sum_wout.T,
        sum_tables[:n_rel],
        sum_tables[n_rel:],
        gain_grads[1],
        sum_gate,
        sum_up,
        sum_down.T,
    )


def solution(mesh):
    placed = (
        P(("wide", "narrow"), None),
        P(("wide", "narrow"), None),
        P(),
        P(None, "narrow"),
        P(None, "narrow"),
        P(None, "narrow"),
        P("narrow", None),
        P(None, "narrow"),
        P(None, "narrow"),
        P(),
        P(None, "narrow"),
        P(None, "narrow"),
        P("narrow", None),
        P("wide", None),
        P("wide"),
        P("wide", None),
        P("wide", None),
    )
    return jax.shard_map(
        functools.partial(on_device, mesh.shape["wide"], mesh.shape["narrow"]),
        mesh=mesh,
        in_specs=placed,
        out_specs=(
            P(("wide", "narrow"), None),
            P(("wide", "narrow"), None),
            P(("wide", "narrow")),
            P("wide", "narrow"),
            P("wide", "narrow"),
            P("wide", "narrow"),
            P("narrow", "wide"),
            P("wide", "narrow"),
            P("wide", "narrow"),
            P(("wide", "narrow")),
            P("wide", "narrow"),
            P("wide", "narrow"),
            P("narrow", "wide"),
        ),
        check_vma=False,
    )
```

```python
import functools
import jax
import jax.numpy as jnp
from jax import lax
from jax.experimental import pallas as pl
from jax.experimental.pallas import tpu as pltpu
from jax.sharding import PartitionSpec as P

DH = 64
BIAS_SCALE = 4096.0
LOG2E = 1.4426950408889634
f32 = jnp.float32
bf16 = jnp.bfloat16
NT = (((1,), (1,)), ((), ()))
NN = (((1,), (0,)), ((), ()))


def dot(a, b, dims=NN):
    return lax.dot_general(a, b, dims, preferred_element_type=f32)


def key_window(len_ref, first, last, count, width):
    ends = []
    total = 0
    for p in range(len_ref.shape[1]):
        total = total + len_ref[0, p]
        ends.append(total)
    start = 0
    stop = count
    for e in ends:
        start = jnp.where(e <= first, e, start)
    for e in reversed(ends):
        stop = jnp.where(e > last, e, stop)
    base = (start // 128) * 128
    steps = (stop - base + width - 1) // width
    base = jnp.minimum(base, count - steps * width)
    return ends, base, steps


def for_chunks(base, steps, width, group, body):
    def many(j, carry):
        body(pl.multiple_of(base + j * (group * width), 128), group * width)
        return carry

    def single(j, carry):
        body(pl.multiple_of(base + j * width, 128), width)
        return carry

    if group > 1:
        lax.fori_loop(0, steps // group, many, 0)
    lax.fori_loop((steps // group) * group if group > 1 else 0, steps, single, 0)


def own_half(shape, head):
    lane = lax.broadcasted_iota(jnp.int32, shape, len(shape) - 1)
    return (lane < DH) if head % 2 == 0 else (lane >= DH)


def fill_values(vext, v_ref, heads):
    for h in range(heads):
        vp = v_ref[:, (h // 2) * 128:(h // 2 + 1) * 128]
        vext[h] = jnp.where(own_half(vp.shape, h), vp, jnp.ones_like(vp))


def half_norms(rows):
    lane = lax.broadcasted_iota(jnp.int32, (128, 128), 0)
    column = lax.broadcasted_iota(jnp.int32, (128, 128), 1)
    same = ((lane < DH) == (column < DH)).astype(bf16)
    squares = (rows.astype(f32) * rows.astype(f32)).astype(bf16)
    return jnp.max(dot(squares, same)) * f32(1.02)


HIDDEN_PAIR = -(1 << 31)


def pair_bias_kernel(len_ref, rel_ref, lay_ref, tab_ref, kmask_ref, word_ref, code_ref, colcode, *, width, group):
    tq, count = rel_ref.shape
    pairs = word_ref.shape[0]
    i = pl.program_id(0)
    t0 = i * tq
    ends, base, steps = key_window(len_ref, t0, t0 + tq - 1, count, width)

    @pl.when(i == 0)
    def _():
        pos = lax.broadcasted_iota(jnp.int32, (8, count), 1)
        page = jnp.zeros((8, count), jnp.int32)
        for e in ends:
            page = page + (pos >= e).astype(jnp.int32)
        colcode[...] = jnp.where(kmask_ref[...] == 1, page, -1)

    rowpos = lax.broadcasted_iota(jnp.int32, (tq, 128), 0) + t0
    rowpage = jnp.zeros((tq, 128), jnp.int32)
    for e in ends:
        rowpage = rowpage + (rowpos >= e).astype(jnp.int32)
    lanes = lax.broadcasted_iota(jnp.int32, (tq, 128), 1)
    tabs = [jnp.broadcast_to(tab_ref[n:n + 1, :], (tq, 128)) for n in range(2 * pairs)]

    def chunk(c0, size):
        for half in range(size // 128):
            cc = pl.multiple_of(c0 + half * 128, 128)
            here = pl.ds(cc, 128)
            rel = rel_ref[:, here]
            lay = lay_ref[:, here]
            code_ref[:, here] = (rel + lay * 32).astype(jnp.int16)
            col = jnp.broadcast_to(colcode[0:1, here], (tq, 128))
            seen = (rowpage == col) | (rowpos == lanes + cc)
            for p in range(pairs):
                word = (jnp.take_along_axis(tabs[2 * p], rel, axis=1, mode="promise_in_bounds")
                        + jnp.take_along_axis(tabs[2 * p + 1], lay, axis=1, mode="promise_in_bounds"))
                word_ref[p, :, here] = jnp.where(seen, word, HIDDEN_PAIR)

    for_chunks(base, steps, width, group, chunk)


def pair_bias(page_lengths, rel, lay, tab, kmask, tq=256, width=256, group=2):
    count = rel.shape[0]
    pairs = tab.shape[0] // 2
    tile = lambda i: (i, 0)
    return pl.pallas_call(
        functools.partial(pair_bias_kernel, width=width, group=group),
        grid=(count // tq,),
        in_specs=[
            pl.BlockSpec(memory_space=pltpu.SMEM),
            pl.BlockSpec((tq, count), tile),
            pl.BlockSpec((tq, count), tile),
            pl.BlockSpec(tab.shape, lambda i: (0, 0)),
            pl.BlockSpec((1, count), lambda i: (0, 0)),
        ],
        out_specs=[
            pl.BlockSpec((pairs, tq, count), lambda i: (0, i, 0)),
            pl.BlockSpec((tq, count), tile),
        ],
        out_shape=[
            jax.ShapeDtypeStruct((pairs, count, count), jnp.int32),
            jax.ShapeDtypeStruct((count, count), jnp.int16),
        ],
        scratch_shapes=[pltpu.VMEM((8, count), jnp.int32)],
        compiler_params=pltpu.CompilerParams(vmem_limit_bytes=56 << 20),
        cost_estimate=pl.CostEstimate(flops=count * count * 1024, bytes_accessed=120 << 20, transcendentals=0),
        name="pair_bias",
    )(page_lengths, rel, lay, tab, kmask.reshape(1, count))


def forward_kernel(len_ref, q_ref, k_ref, v_ref, word_ref, att_ref, rinv_ref, e_ref,
                   s_scr, m_scr, acc_scr, vext, knorm, *, width, group):
    tq, count = word_ref.shape[1:]
    heads, pairs = 2, 1
    i = pl.program_id(0)
    t0 = i * tq
    ends, base, steps = key_window(len_ref, t0, t0 + tq - 1, count, width)

    @pl.when(i == 0)
    def _():
        fill_values(vext, v_ref, heads)
        for p in range(pairs):
            knorm[p] = half_norms(k_ref[:, p * 128:(p + 1) * 128])

    scaled = []
    largest = f32(0.0)
    for h in range(heads):
        qp = q_ref[:, (h // 2) * 128:(h // 2 + 1) * 128]
        scaled.append(jnp.where(own_half(qp.shape, h), qp * bf16(BIAS_SCALE), jnp.zeros_like(qp)))
        if h % 2 == 0:
            largest = jnp.maximum(largest, half_norms(qp) * knorm[h // 2])
    def scores(c0, width, use):
        raw = [dot(scaled[h], k_ref[pl.ds(c0, width), (h // 2) * 128:(h // 2 + 1) * 128], NT)
               for h in range(heads)]
        for half in range(width // 128):
            cc = pl.multiple_of(c0 + half * 128, 128)
            word = word_ref[0, :, pl.ds(cc, 128)]
            hidden = word == HIDDEN_PAIR
            parts = ((word & 0xFFFF).astype(f32), (word >> 16).astype(f32))
            for h in range(heads):
                bias = jnp.where(hidden, f32(-1e30), parts[h])
                use(h, half, cc, raw[h][:, half * 128:(half + 1) * 128] + bias)

    for h in range(heads):
        acc_scr[h] = jnp.zeros((tq, 128), f32)
    bounded = jnp.sqrt(largest) + 8.0 <= 60.0

    @pl.when(bounded)
    def _():
        def chunk(c0, size):
            pieces = {}

            def use(h, half, cc, s):
                e = jnp.exp2(s * f32(LOG2E / BIAS_SCALE)).astype(bf16)
                e_ref[h, :, pl.ds(cc, 128)] = e
                pieces[h, half] = e

            scores(c0, size, use)
            for h in range(heads):
                e = jnp.concatenate([pieces[h, half] for half in range(size // 128)], axis=1)
                acc_scr[h] += dot(e, vext[h, pl.ds(c0, size), :])

        for_chunks(base, steps, width, group, chunk)

    @pl.when(jnp.logical_not(bounded))
    def _():
        for h in range(heads):
            m_scr[h] = jnp.full((tq, 128), -3e38, f32)

        def first(j, carry):
            def use(h, half, cc, s):
                s_scr[h, :, pl.ds(cc, 128)] = s
                m_scr[h] = jnp.maximum(m_scr[h], s)

            scores(pl.multiple_of(base + j * width, 128), width, use)
            return carry

        lax.fori_loop(0, steps, first, 0)
        for h in range(heads):
            top = jnp.max(m_scr[h], axis=1, keepdims=True)

            def second(j, carry):
                c0 = pl.multiple_of(base + j * width, 128)
                e = jnp.exp2((s_scr[h, :, pl.ds(c0, width)] - top) * f32(LOG2E / BIAS_SCALE)).astype(bf16)
                e_ref[h, :, pl.ds(c0, width)] = e
                acc_scr[h] += dot(e, vext[h, pl.ds(c0, width), :])
                return carry

            lax.fori_loop(0, steps, second, 0)

    low = own_half((tq, 128), 0)
    for p in range(pairs):
        even, odd = acc_scr[2 * p], acc_scr[2 * p + 1]
        rinv = 1.0 / pltpu.roll(jnp.where(low, odd, even), DH, 1)
        att_ref[:, p * 128:(p + 1) * 128] = (jnp.where(low, even, odd) * rinv).astype(bf16)
        rinv_ref[:, p * 128:(p + 1) * 128] = rinv


def attention_forward(page_lengths, proj, words, pair, tq=256, width=256, group=2):
    count = proj.shape[0]
    pairs = proj.shape[1] // (3 * 128)
    tile = lambda i: (i, 0)
    return pl.pallas_call(
        functools.partial(forward_kernel, width=width, group=group),
        grid=(count // tq,),
        in_specs=[
            pl.BlockSpec(memory_space=pltpu.SMEM),
            pl.BlockSpec((tq, 128), lambda i: (i, pair)),
            pl.BlockSpec((count, 128), lambda i: (0, pairs + pair)),
            pl.BlockSpec((count, 128), lambda i: (0, 2 * pairs + pair)),
            pl.BlockSpec((1, tq, count), lambda i: (pair, i, 0)),
        ],
        out_specs=[
            pl.BlockSpec((tq, 128), tile),
            pl.BlockSpec((tq, 128), tile),
            pl.BlockSpec((2, tq, count), lambda i: (0, i, 0)),
        ],
        out_shape=[
            jax.ShapeDtypeStruct((count, 128), bf16),
            jax.ShapeDtypeStruct((count, 128), f32),
            jax.ShapeDtypeStruct((2, count, count), bf16),
        ],
        scratch_shapes=[
            pltpu.VMEM((2, tq, count), f32),
            pltpu.VMEM((2, tq, 128), f32),
            pltpu.VMEM((2, tq, 128), f32),
            pltpu.VMEM((2, count, 128), bf16),
            pltpu.SMEM((1,), f32),
        ],
        compiler_params=pltpu.CompilerParams(vmem_limit_bytes=56 << 20),
        cost_estimate=pl.CostEstimate(
            flops=count * count * 512, bytes_accessed=80 << 20, transcendentals=count * count),
        name="attention_forward",
    )(page_lengths, proj, proj, proj, words)


def bias_words(rel_table, layout_table):
    def pack(table):
        whole = jnp.round(table.astype(f32) * BIAS_SCALE).astype(jnp.int32)
        low = jnp.clip(whole[:, 0::2] + 16384, 0, 32767)
        high = jnp.clip(whole[:, 1::2], -16383, 16383)
        words = (high * 65536 + low).T
        return jnp.pad(words, ((0, 0), (0, 128 - words.shape[1])))
    both = jnp.stack([pack(rel_table), pack(layout_table)], axis=1)
    return both.reshape(-1, 128)


def signs(code, shift, bits):
    return [jnp.where((code & jnp.int16(1 << (shift + b))) == 0, bf16(1.0), bf16(-1.0))
            for b in range(bits)]


def walsh(sign_list):
    out = [None]
    for s in sign_list:
        out = out + [s if o is None else o * s for o in out]
    return out


def backward_kernel(len_ref, q_ref, k_ref, v_ref, da_ref, *refs, width, heads, group):
    tq = q_ref.shape[0]
    count = k_ref.shape[0]
    pairs = heads // 2
    e_refs, att_refs, rinv_refs = refs[:pairs], refs[pairs:2 * pairs], refs[2 * pairs:3 * pairs]
    dp_ref, ds_ref = refs[3 * pairs:3 * pairs + 2]
    vext, lhs_scr, dat_scr, qt_scr, dq_scr, dkt, dvt = refs[3 * pairs + 2:]
    i = pl.program_id(0)
    t0 = i * tq
    ends, base, steps = key_window(len_ref, t0, t0 + tq - 1, count, width)

    @pl.when(i == 0)
    def _():
        fill_values(vext, v_ref, heads)
        dkt[...] = jnp.zeros_like(dkt)
        dvt[...] = jnp.zeros_like(dvt)

    low = own_half((tq, 128), 0)
    lane = lax.broadcasted_iota(jnp.int32, (tq, 128), 1)
    first_part = (lane & 32) == 0
    for p in range(pairs):
        cols = slice(p * 128, (p + 1) * 128)
        da = (da_ref[:, cols].astype(f32) * rinv_refs[p][...]).astype(bf16)
        daf = da.astype(f32)
        prod = daf * att_refs[p][...].astype(f32)
        for r in range(2):
            own = low if r == 0 else jnp.logical_not(low)
            delta = jnp.sum(jnp.where(own, prod, 0.0), axis=1, keepdims=True) * f32(-1.0 / 32)
            high = delta.astype(bf16).astype(f32)
            rest = delta - high
            lhs_scr[2 * p + r] = jnp.where(own, daf, jnp.where(first_part, high, rest)).astype(bf16)
        dat_scr[p] = daf.T.astype(bf16)
        qt_scr[p] = q_ref[:, cols].astype(f32).T.astype(bf16)
        dq_scr[p] = jnp.zeros((tq, 128), f32)

    def chunk(c0, size):
        here = pl.ds(c0, size)
        for p in range(pairs):
            kp = k_ref[here, p * 128:(p + 1) * 128]
            dqs = []
            for r in range(2):
                h = 2 * p + r
                rows = slice(r * DH, (r + 1) * DH)
                e = e_refs[p][r, :, here]
                d = dot(lhs_scr[h], vext[h, here, :], NT)
                ds = (e.astype(f32) * d).astype(bf16)
                ds_ref[h, :, here] = ds
                dqs.append(dot(ds, kp))
                dkt[p, rows, here] += dot(qt_scr[p, rows, :], ds)
                dvt[p, rows, here] += dot(dat_scr[p, rows, :], e)
            dq_scr[p] += jnp.where(low, dqs[0], dqs[1])

    for_chunks(base, steps, width, group, chunk)
    for p in range(pairs):
        dp_ref[pl.ds(pl.multiple_of(t0, tq), tq), p * 128:(p + 1) * 128] = dq_scr[p].astype(bf16)

    @pl.when(i == pl.num_programs(0) - 1)
    def _():
        for n, grads in enumerate((dkt, dvt)):
            for p in range(pairs):
                at = ((n + 1) * pairs + p) * 128
                for c in range(0, count, 256):
                    dp_ref[c:c + 256, at:at + 128] = grads[p, :, c:c + 256].T.astype(bf16)


def attention_backward(page_lengths, proj, exps, d_att, atts, rinvs, tq=256, width=256, group=2):
    count = proj.shape[0]
    hc = proj.shape[1] // 3
    heads = hc // DH
    pairs = heads // 2
    grid = (count // tq,)
    tile = lambda i: (i, 0)
    fixed = lambda i: (0, 0)
    return pl.pallas_call(
        functools.partial(backward_kernel, width=width, heads=heads, group=group),
        grid=grid,
        in_specs=[
            pl.BlockSpec(memory_space=pltpu.SMEM),
            pl.BlockSpec((tq, hc), tile),
            pl.BlockSpec((count, hc), lambda i: (0, 1)),
            pl.BlockSpec((count, hc), lambda i: (0, 2)),
            pl.BlockSpec((tq, hc), tile),
        ] + [pl.BlockSpec((2, tq, count), lambda i: (0, i, 0))] * pairs + [pl.BlockSpec((tq, 128), tile)] * (2 * pairs),
        out_specs=[
            pl.BlockSpec((count, 3 * hc), fixed),
            pl.BlockSpec((heads, tq, count), lambda i: (0, i, 0)),
        ],
        out_shape=[
            jax.ShapeDtypeStruct((count, 3 * hc), bf16),
            jax.ShapeDtypeStruct((heads, count, count), bf16),
        ],
        scratch_shapes=[
            pltpu.VMEM((heads, count, 128), bf16),
            pltpu.VMEM((heads, tq, 128), bf16),
            pltpu.VMEM((pairs, 128, tq), bf16),
            pltpu.VMEM((pairs, 128, tq), bf16),
            pltpu.VMEM((pairs, tq, 128), f32),
            pltpu.VMEM((pairs, 128, count), f32),
            pltpu.VMEM((pairs, 128, count), f32),
        ],
        compiler_params=pltpu.CompilerParams(vmem_limit_bytes=56 << 20),
        cost_estimate=pl.CostEstimate(
            flops=heads * count * count * 512, bytes_accessed=150 << 20, transcendentals=0),
        name="attention_backward",
    )(page_lengths, proj, proj, proj, d_att, *exps, *atts, *rinvs)


def table_kernel(len_ref, ds_ref, code_ref, hl_ref, hr_ref, *bufs, width, parts):
    heads, tq, count = ds_ref.shape
    i = pl.program_id(0)
    t0 = i * tq
    ends, base, steps = key_window(len_ref, t0, t0 + tq - 1, count, width)

    @pl.when(i == 0)
    def _():
        hl_ref[...] = jnp.zeros_like(hl_ref)
        hr_ref[...] = jnp.zeros_like(hr_ref)

    one = jnp.ones((16, width), bf16)

    def chunk(j, carry):
        c0 = pl.multiple_of(base + j * width, 128)
        here = pl.ds(c0, width)
        blocks = tq // 16 // parts
        for part in range(parts):
            left, blay, brel = bufs[3 * part:3 * part + 3]
            for b in range(blocks):
                at = 16 * (part * blocks + b)
                rows = slice(at, at + 16)
                span = slice(b * width, (b + 1) * width)
                code = code_ref[rows, here]
                rel_signs = signs(code, 0, 5)
                lay_signs = signs(code, 5, 6)
                left_lay = walsh(lay_signs[:2])[1:]
                for h in range(heads):
                    ds = ds_ref[h, rows, here]
                    for a, func in enumerate(left_lay + [None, rel_signs[0]]):
                        place = 16 * (a * heads + h)
                        left[place:place + 16, span] = ds if func is None else ds * func
                for n, func in enumerate(walsh(lay_signs[2:])):
                    blay[16 * n:16 * (n + 1), span] = one if func is None else func
                for n, func in enumerate(walsh(rel_signs[1:])):
                    brel[16 * n:16 * (n + 1), span] = one if func is None else func
            hl_ref[...] += dot(left[:64 * heads, :], blay[...], NT)
            hr_ref[...] += dot(left[48 * heads:80 * heads, :], brel[...], NT)
        return carry

    lax.fori_loop(0, steps, chunk, 0)


def table_grads(page_lengths, ds, code, tq=256, width=256, parts=2):
    heads, count, _ = ds.shape
    deep = tq // 16 * width // parts
    fixed = lambda i: (0, 0)
    return pl.pallas_call(
        functools.partial(table_kernel, width=width, parts=parts),
        grid=(count // tq,),
        in_specs=[
            pl.BlockSpec(memory_space=pltpu.SMEM),
            pl.BlockSpec((heads, tq, count), lambda i: (0, i, 0)),
            pl.BlockSpec((tq, count), lambda i: (i, 0)),
        ],
        out_specs=[
            pl.BlockSpec((64 * heads, 256), fixed),
            pl.BlockSpec((32 * heads, 256), fixed),
        ],
        out_shape=[
            jax.ShapeDtypeStruct((64 * heads, 256), f32),
            jax.ShapeDtypeStruct((32 * heads, 256), f32),
        ],
        scratch_shapes=[
            pltpu.VMEM((80 * heads, deep), bf16),
            pltpu.VMEM((256, deep), bf16),
            pltpu.VMEM((256, deep), bf16),
        ] * parts,
        compiler_params=pltpu.CompilerParams(vmem_limit_bytes=56 << 20),
        cost_estimate=pl.CostEstimate(
            flops=heads * count * count * 512, bytes_accessed=150 << 20, transcendentals=0),
        name="table_grads",
    )(page_lengths, ds, code)


def bucket_sums(raw, heads):
    right = raw.shape[1] // 16
    left = raw.shape[0] // (16 * heads)
    cube = raw.reshape(left, heads, 16, right, 16)
    traced = jnp.sum(cube * jnp.eye(16, dtype=f32)[None, None, :, None, :], axis=(2, 4))
    if left == 4:
        traced = jnp.concatenate([traced[3:], traced[:3]], axis=0)

    def table(n):
        v = lax.iota(jnp.int32, n)
        both = v[:, None] & v[None, :]
        return (1 - 2 * (lax.population_count(both) & 1)).astype(f32)

    out = jnp.einsum("ahn,ax,ny->yxh", traced, table(left), table(right), precision=lax.Precision.HIGHEST)
    return out.reshape(left * right, heads) / (left * right)


TANH_SLOPE = 0.7978845608028654
CUBE = 0.044715


def feed_forward_kernel(far, x_ref, g_ref, *refs):
    weights, (hidden_ref, d_gate_ref, d_up_ref, dn_ref) = refs[:-4], refs[-4:]
    units = hidden_ref.shape[1]
    if far:
        step = pad_lanes(units)
        gate_weight, up_weight, down = [weights[0][:, n * step:n * step + units] for n in range(3)]
        ahead, back = NN, NT
    else:
        gate_weight, up_weight, down = [w[...] for w in weights]
        ahead, back = NT, NN
    x = x_ref[...]
    d_hidden = dot(g_ref[...], down, ahead)
    gate = dot(x, gate_weight, ahead)
    up = dot(x, up_weight, ahead)
    square = gate * gate
    t = jnp.tanh(TANH_SLOPE * gate * (1.0 + CUBE * square))
    half = 0.5 + 0.5 * t
    gelu = gate * half
    slope = half + (0.5 * TANH_SLOPE) * gate * (1.0 - t * t) * (1.0 + (3 * CUBE) * square)
    d_gate = (d_hidden * up * slope).astype(bf16)
    d_up = (d_hidden * gelu).astype(bf16)
    hidden_ref[...] = (gelu * up).astype(bf16)
    d_gate_ref[...] = d_gate
    d_up_ref[...] = d_up
    dn_ref[...] = dot(d_gate, gate_weight, back) + dot(d_up, up_weight, back)


def feed_forward(x, g, units, weights, shard=None, tile=256):
    tokens, features = x.shape
    tile = min(tile, tokens)
    rows = lambda n: pl.BlockSpec((tile, n), lambda i: (i, 0))
    if shard is None:
        weight_specs = [pl.BlockSpec(w.shape, lambda i: (0, 0)) for w in weights]
    else:
        weight_specs = [pl.BlockSpec((features, 3 * pad_lanes(units)), lambda i: (0, shard))]
    return pl.pallas_call(
        functools.partial(feed_forward_kernel, shard is not None),
        grid=(tokens // tile,),
        in_specs=[rows(features), rows(features)] + weight_specs,
        out_specs=[rows(units)] * 3 + [rows(features)],
        out_shape=[jax.ShapeDtypeStruct((tokens, units), bf16)] * 3
        + [jax.ShapeDtypeStruct((tokens, features), f32)],
        compiler_params=pltpu.CompilerParams(vmem_limit_bytes=56 << 20),
        cost_estimate=pl.CostEstimate(
            flops=10 * tokens * features * units, bytes_accessed=10 << 20, transcendentals=tokens * units),
        name="feed_forward",
    )(x, g, *weights)


def pad_lanes(n):
    return (n + 127) // 128 * 128


def weight_grads_kernel(n_left, n_right, *refs):
    lefts = refs[:2 * n_left]
    rights = refs[2 * n_left:-1]
    out_ref = refs[-1]
    rows_in = (((0,), (0,)), ((), ()))
    place = 0
    for n, left in enumerate(n_right):
        a, b = rights[2 * n], rights[2 * n + 1]
        size = a.shape[1]
        value = dot(lefts[2 * left][...], a[...], rows_in) + dot(lefts[2 * left + 1][...], b[...], rows_in)
        out_ref[:, place:place + size] = value.astype(bf16)
        if pad_lanes(size) > size:
            out_ref[:, place + size:place + pad_lanes(size)] = jnp.zeros(
                (out_ref.shape[0], pad_lanes(size) - size), bf16)
        place += pad_lanes(size)


def weight_grads(lefts, rights, groups, tile=256):
    features = lefts[0].shape[1]
    columns = sum(pad_lanes(r.shape[1]) for r in rights[::2])
    column = lambda a: pl.BlockSpec((a.shape[0], tile), lambda i: (0, i))
    whole = lambda a: pl.BlockSpec(a.shape, lambda i: (0, 0))
    return pl.pallas_call(
        functools.partial(weight_grads_kernel, len(lefts) // 2, groups),
        grid=(features // tile,),
        in_specs=[column(a) for a in lefts] + [whole(a) for a in rights],
        out_specs=pl.BlockSpec((tile, columns), lambda i: (i, 0)),
        out_shape=jax.ShapeDtypeStruct((features, columns), bf16),
        compiler_params=pltpu.CompilerParams(vmem_limit_bytes=56 << 20),
        cost_estimate=pl.CostEstimate(
            flops=4 * features * columns * lefts[0].shape[0], bytes_accessed=26 << 20, transcendentals=0),
        name="weight_grads",
    )(*lefts, *rights)


epsilon = 1e-06


def contract_rows(left, right):
    return lax.dot_general(
        left, right, (((0,), (0,)), ((), ())), preferred_element_type=jnp.float32
    )


def contract_cols(left, right):
    return lax.dot_general(
        left, right, (((1,), (1,)), ((), ())), preferred_element_type=jnp.float32
    )


def norm_rows(rows, gain):
    scale = lax.rsqrt(jnp.mean(rows * rows, axis=-1, keepdims=True) + epsilon)
    return (scale, (rows * scale * gain).astype(jnp.bfloat16))


def norm_back(d_normed, rows, scale, gain):
    shaped = d_normed * gain
    cubed = scale * scale * scale
    return scale * shaped - rows * cubed * jnp.mean(shaped * rows, axis=-1, keepdims=True)


def along(array, shift, ring):
    return lax.ppermute(array, "narrow", [(i, (i + shift) % ring) for i in range(ring)])


def swap(array, ring):
    return lax.ppermute(array, "narrow", [(i, i ^ 1) for i in range(ring)])


def rows_of(array, index, count):
    return lax.dynamic_slice_in_dim(array, index * count, count, 0)


def on_device(
    wide,
    ring,
    layer_input,
    out_grad,
    norm_attn_gain,
    w_query,
    w_key,
    w_value,
    w_out,
    rel_table,
    layout_table,
    norm_ffn_gain,
    w_gate,
    w_up,
    down_projection_weight,
    page_lengths,
    key_mask,
    rel_bucket,
    layout_bucket,
):
    tokens, width = layer_input.shape
    head_cols = w_query.shape[1]
    heads = head_cols // DH
    units = w_gate.shape[1]
    padded = pad_lanes(units)
    part = width // wide
    me = lax.axis_index("narrow")
    my_wide = lax.axis_index("wide")
    gain_attn = norm_attn_gain.astype(f32)
    gain_ffn = norm_ffn_gain.astype(f32)
    resid = layer_input.astype(f32)

    scale_attn, normed_attn = norm_rows(resid, gain_attn)
    normed_attn_all = lax.all_gather(normed_attn, "narrow", axis=0, tiled=True)

    w_project = jnp.concatenate([w_query, w_key, w_value], axis=1)
    own_rows_gate = rows_of(w_gate, my_wide, part)
    own_rows_up = rows_of(w_up, my_wide, part)
    own_rows_project = rows_of(w_project, my_wide, part)
    down_piece = lax.dynamic_slice_in_dim(down_projection_weight, my_wide * part, part, 1).T
    out_piece = lax.dynamic_slice_in_dim(w_out, my_wide * part, part, 1).T
    ffn_piece = jnp.concatenate(
        [jnp.pad(piece, ((0, 0), (0, padded - units))) for piece in (own_rows_gate, own_rows_up, down_piece)], axis=1)
    out_pieces = [out_piece] + [along(out_piece, d, ring) for d in range(1, ring)]
    words, codes = pair_bias(page_lengths, rel_bucket, layout_bucket, bias_words(rel_table, layout_table), key_mask)
    normed_attn_all, ffn_piece, words = lax.optimization_barrier((normed_attn_all, ffn_piece, words))
    ffn_pieces = [along(ffn_piece, d, ring) for d in range(2, ring, 2)]
    out_t = lax.all_gather(jnp.concatenate(out_pieces, axis=1), "wide", axis=0, tiled=True)

    projected = dot(normed_attn_all, w_project).astype(bf16)
    pairs = head_cols // 128
    first_pair = list(attention_forward(page_lengths, projected, words, 0))
    first_pair[0], ffn_pieces, late_grad = lax.optimization_barrier((first_pair[0], ffn_pieces, out_grad))
    far_pieces = jnp.concatenate(ffn_pieces, axis=1)
    other_grad = swap(late_grad, ring)

    def to_owners(a):
        return [rows_of(a, me, tokens)] + [
            along(rows_of(a, (me + d) % ring, tokens), d, ring) for d in range(1, ring)]

    sent = [to_owners(first_pair[0])]
    results = [first_pair]
    if pairs > 1:
        late_projected, far_pieces = lax.optimization_barrier((projected, far_pieces))
        results += [list(attention_forward(page_lengths, late_projected, words, p)) for p in range(1, pairs)]
    far = lax.all_gather(far_pieces, "wide", axis=0, tiled=True)
    results[-1][0], other_grad, sent[0] = lax.optimization_barrier((results[-1][0], other_grad, sent[0]))
    attended = [r[0] for r in results]
    sent += [to_owners(a) for a in attended[1:]]
    mine = [pieces[d] for d in range(ring) for pieces in sent]
    attended_own = jnp.concatenate(mine, axis=1)
    middle = resid + contract_cols(attended_own, out_t)

    scale_ffn, normed_ffn = norm_rows(middle, gain_ffn)
    other_normed = swap(normed_ffn, ring)
    near = (w_gate.T, w_up.T, down_projection_weight)
    shards = ring // 2
    own = [feed_forward(normed_ffn, out_grad, units, near)]
    own, other_normed, late_project = lax.optimization_barrier((own, other_normed, own_rows_project))
    project_pieces = [along(late_project, d, ring) for d in range(1, ring)]
    other = [feed_forward(other_normed, other_grad, units, near)]
    other += [feed_forward(other_normed, other_grad, units, (far,), s) for s in range(shards - 1)]
    other, project_pieces = lax.optimization_barrier((other, project_pieces))
    w_project_all = lax.all_gather(
        jnp.concatenate([own_rows_project] + project_pieces, axis=1), "wide", axis=0, tiled=True)
    other_d_normed = sum(o[3] for o in other).astype(bf16)
    late_normed, other_d_normed = lax.optimization_barrier((normed_ffn, other_d_normed))
    other_d_normed = swap(other_d_normed, ring)
    own += [feed_forward(late_normed, out_grad, units, (far,), s) for s in range(shards - 1)]
    rights, groups = [], []
    for s in range(shards):
        for n in range(1, 4):
            rights += [own[s][n % 3], other[s][n % 3]]
            groups.append(n // 3)
    sums = weight_grads((normed_ffn, other_normed, out_grad, other_grad), rights, tuple(groups))
    sums, other_d_normed = lax.optimization_barrier((sums, other_d_normed))
    ffn_sums = lax.psum_scatter(sums, "wide", scatter_dimension=0, tiled=True)
    d_normed_ffn = sum(o[3] for o in own) + other_d_normed.astype(f32)
    d_middle = out_grad.astype(f32) + norm_back(d_normed_ffn, middle, scale_ffn, gain_ffn)
    d_middle_low = d_middle.astype(bf16)
    d_attended_own = dot(d_middle_low, out_t).astype(bf16)

    def block(d):
        return d_attended_own[:, d * head_cols : (d + 1) * head_cols]

    d_attended = jnp.zeros((ring * tokens, head_cols), bf16)
    d_attended = lax.dynamic_update_slice_in_dim(d_attended, block(0), me * tokens, 0)
    for d in range(1, ring):
        d_attended = lax.dynamic_update_slice_in_dim(
            d_attended, along(block(d), -d, ring), ((me + d) % ring) * tokens, 0)

    d_middle_late, attended_late, own_hidden, other_hidden = lax.optimization_barrier(
        (d_middle_low, attended_own, [o[0] for o in own], [o[0] for o in other]))
    wout_sums = contract_rows(d_middle_late, attended_late).astype(bf16)
    own_out, other_out = 0.0, 0.0
    for s in range(shards):
        if s == 0:
            down, dims = down_projection_weight, NN
        else:
            at = 3 * padded * (s - 1) + 2 * padded
            down, dims = far[:, at : at + units], NT
        own_out = own_out + dot(own_hidden[s], down, dims)
        other_out = other_out + dot(other_hidden[s], down, dims)
    own_out = own_out + middle
    wout_sums, d_attended, w_project_all, own_out, other_out = lax.optimization_barrier(
        (wout_sums, d_attended, w_project_all, own_out, other_out.astype(bf16)))
    other_out = swap(other_out, ring)

    d_project, d_scores = attention_backward(
        page_lengths, projected, [r[2] for r in results], d_attended, attended, [r[1] for r in results])
    d_project, other_out = lax.optimization_barrier((d_project, other_out))
    leaving = [rows_of(d_project, (me + d) % ring, tokens) for d in range(ring)]
    leaving, d_project, own_out = lax.optimization_barrier((leaving, d_project, own_out))
    mine = leaving[:1] + [along(leaving[d], d, ring) for d in range(1, ring)]
    layer_out = (own_out + other_out.astype(f32)).astype(bf16)
    last_sums = jnp.concatenate([contract_rows(normed_attn_all, d_project).astype(bf16), wout_sums], axis=1)
    last_sums = lax.psum_scatter(last_sums, "wide", scatter_dimension=0, tiled=True)

    raw_lay, raw_rel = table_grads(page_lengths, d_scores, codes)
    raw_lay, raw_rel, mine = lax.optimization_barrier((raw_lay, raw_rel, mine))
    raw_lay, raw_rel, ffn_sums = lax.optimization_barrier((raw_lay, raw_rel, ffn_sums))
    far_sums = [along(ffn_sums[:, 3 * padded * s : 3 * padded * (s + 1)], -2 * s, ring) for s in range(1, shards)]
    grad_relative = bucket_sums(raw_rel, heads)
    grad_layout = bucket_sums(raw_lay, heads)
    tables = jnp.concatenate(
        [grad_relative.reshape(wide, -1, heads), grad_layout.reshape(wide, -1, heads)], axis=1)
    n_rel = grad_relative.shape[0] // wide
    reach = wide // 2
    while reach >= 1:
        bit = (my_wide // reach) % 2
        keep = lax.dynamic_slice_in_dim(tables, bit * reach, reach, 0)
        give = lax.dynamic_slice_in_dim(tables, (1 - bit) * reach, reach, 0)
        tables = keep + lax.ppermute(give, "wide", [(i, i ^ reach) for i in range(wide)])
        if reach == wide // 2:
            tables, far_sums, last_sums = lax.optimization_barrier((tables, far_sums, last_sums))
        reach //= 2
    sum_project = last_sums[:, : 3 * head_cols].astype(f32)
    wout_sums = last_sums[:, 3 * head_cols :]
    far_wout = [along(wout_sums[:, d * head_cols : (d + 1) * head_cols], -d, ring) for d in range(1, ring)]
    sum_tables = tables[0]
    d_project_own = jnp.concatenate(mine, axis=1)
    d_normed_attn = contract_cols(d_project_own, w_project_all)
    in_grad = d_middle + norm_back(d_normed_attn, resid, scale_attn, gain_attn)

    def stripe(shard, n):
        at = padded * (3 * shard + n)
        return ffn_sums[:, at : at + units]

    sum_gate, sum_up, sum_down = [stripe(0, n).astype(f32) for n in range(3)]
    for s in range(1, shards):
        block = far_sums[s - 1].astype(f32)
        sum_gate += block[:, :units]
        sum_up += block[:, padded : padded + units]
        sum_down += block[:, 2 * padded : 2 * padded + units]
    sum_wout = wout_sums[:, :head_cols].astype(f32) + sum(w.astype(f32) for w in far_wout)

    gain_terms = jnp.stack(
        [
            jnp.sum(own_rows_project.astype(f32) * sum_project, axis=1),
            jnp.sum(own_rows_gate.astype(f32) * sum_gate + own_rows_up.astype(f32) * sum_up, axis=1),
        ]
    )
    share = part // ring

    def gain_share(index):
        return lax.dynamic_slice_in_dim(gain_terms, index * share, share, 1)

    gain_sum = gain_share(me)
    for d in range(1, ring):
        gain_sum = gain_sum + along(gain_share((me + d) % ring), d, ring)
    place = my_wide * part + me * share
    gains = lax.dynamic_slice_in_dim(jnp.stack([gain_attn, gain_ffn]), place, share, 1)
    gain_grads = gain_sum / gains
    return (
        layer_out,
        in_grad,
        gain_grads[0],
        sum_project[:, :head_cols],
        sum_project[:, head_cols : 2 * head_cols],
        sum_project[:, 2 * head_cols :],
        sum_wout.T,
        sum_tables[:n_rel],
        sum_tables[n_rel:],
        gain_grads[1],
        sum_gate,
        sum_up,
        sum_down.T,
    )


def solution(mesh):
    placed = (
        P(("wide", "narrow"), None),
        P(("wide", "narrow"), None),
        P(),
        P(None, "narrow"),
        P(None, "narrow"),
        P(None, "narrow"),
        P("narrow", None),
        P(None, "narrow"),
        P(None, "narrow"),
        P(),
        P(None, "narrow"),
        P(None, "narrow"),
        P("narrow", None),
        P("wide", None),
        P("wide"),
        P("wide", None),
        P("wide", None),
    )
    return jax.shard_map(
        functools.partial(on_device, mesh.shape["wide"], mesh.shape["narrow"]),
        mesh=mesh,
        in_specs=placed,
        out_specs=(
            P(("wide", "narrow"), None),
            P(("wide", "narrow"), None),
            P(("wide", "narrow")),
            P("wide", "narrow"),
            P("wide", "narrow"),
            P("wide", "narrow"),
            P("narrow", "wide"),
            P("wide", "narrow"),
            P("wide", "narrow"),
            P(("wide", "narrow")),
            P("wide", "narrow"),
            P("wide", "narrow"),
            P("narrow", "wide"),
        ),
        check_vma=False,
    )
```

```python
import functools
import jax
import jax.numpy as jnp
from jax import lax
from jax.experimental import pallas as pl
from jax.experimental.pallas import tpu as pltpu
from jax.sharding import PartitionSpec as P

DH = 64
BIAS_SCALE = 4096.0
LOG2E = 1.4426950408889634
f32 = jnp.float32
bf16 = jnp.bfloat16
NT = (((1,), (1,)), ((), ()))
NN = (((1,), (0,)), ((), ()))


def dot(a, b, dims=NN):
    return lax.dot_general(a, b, dims, preferred_element_type=f32)


def key_window(len_ref, first, last, count, width):
    ends = []
    total = 0
    for p in range(len_ref.shape[1]):
        total = total + len_ref[0, p]
        ends.append(total)
    start = 0
    stop = count
    for e in ends:
        start = jnp.where(e <= first, e, start)
    for e in reversed(ends):
        stop = jnp.where(e > last, e, stop)
    base = (start // 128) * 128
    steps = (stop - base + width - 1) // width
    base = jnp.minimum(base, count - steps * width)
    return ends, base, steps


def for_chunks(base, steps, width, group, body):
    def many(j, carry):
        body(pl.multiple_of(base + j * (group * width), 128), group * width)
        return carry

    def single(j, carry):
        body(pl.multiple_of(base + j * width, 128), width)
        return carry

    if group > 1:
        lax.fori_loop(0, steps // group, many, 0)
    lax.fori_loop((steps // group) * group if group > 1 else 0, steps, single, 0)


def own_half(shape, head):
    lane = lax.broadcasted_iota(jnp.int32, shape, len(shape) - 1)
    return (lane < DH) if head % 2 == 0 else (lane >= DH)


def fill_values(vext, v_ref, heads):
    for h in range(heads):
        vp = v_ref[:, (h // 2) * 128:(h // 2 + 1) * 128]
        vext[h] = jnp.where(own_half(vp.shape, h), vp, jnp.ones_like(vp))


def half_norms(rows):
    lane = lax.broadcasted_iota(jnp.int32, (128, 128), 0)
    column = lax.broadcasted_iota(jnp.int32, (128, 128), 1)
    same = ((lane < DH) == (column < DH)).astype(bf16)
    squares = (rows.astype(f32) * rows.astype(f32)).astype(bf16)
    return jnp.max(dot(squares, same)) * f32(1.02)


HIDDEN_PAIR = -(1 << 31)


def pair_bias_kernel(len_ref, rel_ref, lay_ref, tab_ref, kmask_ref, word_ref, code_ref, colcode, *, width, group):
    tq, count = rel_ref.shape
    pairs = word_ref.shape[0]
    i = pl.program_id(0)
    t0 = i * tq
    ends, base, steps = key_window(len_ref, t0, t0 + tq - 1, count, width)

    @pl.when(i == 0)
    def _():
        pos = lax.broadcasted_iota(jnp.int32, (8, count), 1)
        page = jnp.zeros((8, count), jnp.int32)
        for e in ends:
            page = page + (pos >= e).astype(jnp.int32)
        colcode[...] = jnp.where(kmask_ref[...] == 1, page, -1)

    rowpos = lax.broadcasted_iota(jnp.int32, (tq, 128), 0) + t0
    rowpage = jnp.zeros((tq, 128), jnp.int32)
    for e in ends:
        rowpage = rowpage + (rowpos >= e).astype(jnp.int32)
    lanes = lax.broadcasted_iota(jnp.int32, (tq, 128), 1)
    tabs = [jnp.broadcast_to(tab_ref[n:n + 1, :], (tq, 128)) for n in range(2 * pairs)]

    def chunk(c0, size):
        for half in range(size // 128):
            cc = pl.multiple_of(c0 + half * 128, 128)
            here = pl.ds(cc, 128)
            rel = rel_ref[:, here]
            lay = lay_ref[:, here]
            code_ref[:, here] = (rel + lay * 32).astype(jnp.int16)
            col = jnp.broadcast_to(colcode[0:1, here], (tq, 128))
            seen = (rowpage == col) | (rowpos == lanes + cc)
            for p in range(pairs):
                word = (jnp.take_along_axis(tabs[2 * p], rel, axis=1, mode="promise_in_bounds")
                        + jnp.take_along_axis(tabs[2 * p + 1], lay, axis=1, mode="promise_in_bounds"))
                word_ref[p, :, here] = jnp.where(seen, word, HIDDEN_PAIR)

    for_chunks(base, steps, width, group, chunk)


def pair_bias(page_lengths, rel, lay, tab, kmask, tq=256, width=256, group=2):
    count = rel.shape[0]
    pairs = tab.shape[0] // 2
    tile = lambda i: (i, 0)
    return pl.pallas_call(
        functools.partial(pair_bias_kernel, width=width, group=group),
        grid=(count // tq,),
        in_specs=[
            pl.BlockSpec(memory_space=pltpu.SMEM),
            pl.BlockSpec((tq, count), tile),
            pl.BlockSpec((tq, count), tile),
            pl.BlockSpec(tab.shape, lambda i: (0, 0)),
            pl.BlockSpec((1, count), lambda i: (0, 0)),
        ],
        out_specs=[
            pl.BlockSpec((pairs, tq, count), lambda i: (0, i, 0)),
            pl.BlockSpec((tq, count), tile),
        ],
        out_shape=[
            jax.ShapeDtypeStruct((pairs, count, count), jnp.int32),
            jax.ShapeDtypeStruct((count, count), jnp.int16),
        ],
        scratch_shapes=[pltpu.VMEM((8, count), jnp.int32)],
        compiler_params=pltpu.CompilerParams(vmem_limit_bytes=56 << 20),
        cost_estimate=pl.CostEstimate(flops=count * count * 1024, bytes_accessed=120 << 20, transcendentals=0),
        name="pair_bias",
    )(page_lengths, rel, lay, tab, kmask.reshape(1, count))


def forward_kernel(len_ref, q_ref, k_ref, v_ref, word_ref, att_ref, rinv_ref, e_ref,
                   s_scr, m_scr, acc_scr, vext, knorm, *, width, group):
    tq, count = word_ref.shape[1:]
    heads, pairs = 2, 1
    i = pl.program_id(0)
    t0 = i * tq
    ends, base, steps = key_window(len_ref, t0, t0 + tq - 1, count, width)

    @pl.when(i == 0)
    def _():
        fill_values(vext, v_ref, heads)
        for p in range(pairs):
            knorm[p] = half_norms(k_ref[:, p * 128:(p + 1) * 128])

    scaled = []
    largest = f32(0.0)
    for h in range(heads):
        qp = q_ref[:, (h // 2) * 128:(h // 2 + 1) * 128]
        scaled.append(jnp.where(own_half(qp.shape, h), qp * bf16(BIAS_SCALE), jnp.zeros_like(qp)))
        if h % 2 == 0:
            largest = jnp.maximum(largest, half_norms(qp) * knorm[h // 2])
    def scores(c0, width, use):
        raw = [dot(scaled[h], k_ref[pl.ds(c0, width), (h // 2) * 128:(h // 2 + 1) * 128], NT)
               for h in range(heads)]
        for half in range(width // 128):
            cc = pl.multiple_of(c0 + half * 128, 128)
            word = word_ref[0, :, pl.ds(cc, 128)]
            hidden = word == HIDDEN_PAIR
            parts = ((word & 0xFFFF).astype(f32), (word >> 16).astype(f32))
            for h in range(heads):
                bias = jnp.where(hidden, f32(-1e30), parts[h])
                use(h, half, cc, raw[h][:, half * 128:(half + 1) * 128] + bias)

    for h in range(heads):
        acc_scr[h] = jnp.zeros((tq, 128), f32)
    bounded = jnp.sqrt(largest) + 8.0 <= 60.0

    @pl.when(bounded)
    def _():
        def chunk(c0, size):
            pieces = {}

            def use(h, half, cc, s):
                e = jnp.exp2(s * f32(LOG2E / BIAS_SCALE)).astype(bf16)
                e_ref[h, :, pl.ds(cc, 128)] = e
                pieces[h, half] = e

            scores(c0, size, use)
            for h in range(heads):
                e = jnp.concatenate([pieces[h, half] for half in range(size // 128)], axis=1)
                acc_scr[h] += dot(e, vext[h, pl.ds(c0, size), :])

        for_chunks(base, steps, width, group, chunk)

    @pl.when(jnp.logical_not(bounded))
    def _():
        for h in range(heads):
            m_scr[h] = jnp.full((tq, 128), -3e38, f32)

        def first(j, carry):
            def use(h, half, cc, s):
                s_scr[h, :, pl.ds(cc, 128)] = s
                m_scr[h] = jnp.maximum(m_scr[h], s)

            scores(pl.multiple_of(base + j * width, 128), width, use)
            return carry

        lax.fori_loop(0, steps, first, 0)
        for h in range(heads):
            top = jnp.max(m_scr[h], axis=1, keepdims=True)

            def second(j, carry):
                c0 = pl.multiple_of(base + j * width, 128)
                e = jnp.exp2((s_scr[h, :, pl.ds(c0, width)] - top) * f32(LOG2E / BIAS_SCALE)).astype(bf16)
                e_ref[h, :, pl.ds(c0, width)] = e
                acc_scr[h] += dot(e, vext[h, pl.ds(c0, width), :])
                return carry

            lax.fori_loop(0, steps, second, 0)

    low = own_half((tq, 128), 0)
    for p in range(pairs):
        even, odd = acc_scr[2 * p], acc_scr[2 * p + 1]
        rinv = 1.0 / pltpu.roll(jnp.where(low, odd, even), DH, 1)
        att_ref[:, p * 128:(p + 1) * 128] = (jnp.where(low, even, odd) * rinv).astype(bf16)
        rinv_ref[:, p * 128:(p + 1) * 128] = rinv


def attention_forward(page_lengths, proj, words, pair, tq=256, width=256, group=2):
    count = proj.shape[0]
    pairs = proj.shape[1] // (3 * 128)
    tile = lambda i: (i, 0)
    return pl.pallas_call(
        functools.partial(forward_kernel, width=width, group=group),
        grid=(count // tq,),
        in_specs=[
            pl.BlockSpec(memory_space=pltpu.SMEM),
            pl.BlockSpec((tq, 128), lambda i: (i, pair)),
            pl.BlockSpec((count, 128), lambda i: (0, pairs + pair)),
            pl.BlockSpec((count, 128), lambda i: (0, 2 * pairs + pair)),
            pl.BlockSpec((1, tq, count), lambda i: (pair, i, 0)),
        ],
        out_specs=[
            pl.BlockSpec((tq, 128), tile),
            pl.BlockSpec((tq, 128), tile),
            pl.BlockSpec((2, tq, count), lambda i: (0, i, 0)),
        ],
        out_shape=[
            jax.ShapeDtypeStruct((count, 128), bf16),
            jax.ShapeDtypeStruct((count, 128), f32),
            jax.ShapeDtypeStruct((2, count, count), bf16),
        ],
        scratch_shapes=[
            pltpu.VMEM((2, tq, count), f32),
            pltpu.VMEM((2, tq, 128), f32),
            pltpu.VMEM((2, tq, 128), f32),
            pltpu.VMEM((2, count, 128), bf16),
            pltpu.SMEM((1,), f32),
        ],
        compiler_params=pltpu.CompilerParams(vmem_limit_bytes=56 << 20),
        cost_estimate=pl.CostEstimate(
            flops=count * count * 512, bytes_accessed=80 << 20, transcendentals=count * count),
        name="attention_forward",
    )(page_lengths, proj, proj, proj, words)


def bias_words(rel_table, layout_table):
    def pack(table):
        whole = jnp.round(table.astype(f32) * BIAS_SCALE).astype(jnp.int32)
        low = jnp.clip(whole[:, 0::2] + 16384, 0, 32767)
        high = jnp.clip(whole[:, 1::2], -16383, 16383)
        words = (high * 65536 + low).T
        return jnp.pad(words, ((0, 0), (0, 128 - words.shape[1])))
    both = jnp.stack([pack(rel_table), pack(layout_table)], axis=1)
    return both.reshape(-1, 128)


def signs(code, shift, bits):
    return [jnp.where((code & jnp.int16(1 << (shift + b))) == 0, bf16(1.0), bf16(-1.0))
            for b in range(bits)]


def walsh(sign_list):
    out = [None]
    for s in sign_list:
        out = out + [s if o is None else o * s for o in out]
    return out


def backward_kernel(len_ref, q_ref, k_ref, v_ref, da_ref, *refs, width, heads, group):
    tq = q_ref.shape[0]
    count = k_ref.shape[0]
    pairs = heads // 2
    e_refs, att_refs, rinv_refs = refs[:pairs], refs[pairs:2 * pairs], refs[2 * pairs:3 * pairs]
    dp_ref, ds_ref = refs[3 * pairs:3 * pairs + 2]
    vext, lhs_scr, dat_scr, qt_scr, dq_scr, dkt, dvt = refs[3 * pairs + 2:]
    i = pl.program_id(0)
    t0 = i * tq
    ends, base, steps = key_window(len_ref, t0, t0 + tq - 1, count, width)

    @pl.when(i == 0)
    def _():
        fill_values(vext, v_ref, heads)
        dkt[...] = jnp.zeros_like(dkt)
        dvt[...] = jnp.zeros_like(dvt)

    low = own_half((tq, 128), 0)
    lane = lax.broadcasted_iota(jnp.int32, (tq, 128), 1)
    first_part = (lane & 32) == 0
    for p in range(pairs):
        cols = slice(p * 128, (p + 1) * 128)
        da = (da_ref[:, cols].astype(f32) * rinv_refs[p][...]).astype(bf16)
        daf = da.astype(f32)
        prod = daf * att_refs[p][...].astype(f32)
        for r in range(2):
            own = low if r == 0 else jnp.logical_not(low)
            delta = jnp.sum(jnp.where(own, prod, 0.0), axis=1, keepdims=True) * f32(-1.0 / 32)
            high = delta.astype(bf16).astype(f32)
            rest = delta - high
            lhs_scr[2 * p + r] = jnp.where(own, daf, jnp.where(first_part, high, rest)).astype(bf16)
        dat_scr[p] = daf.T.astype(bf16)
        qt_scr[p] = q_ref[:, cols].astype(f32).T.astype(bf16)
        dq_scr[p] = jnp.zeros((tq, 128), f32)

    def chunk(c0, size):
        here = pl.ds(c0, size)
        for p in range(pairs):
            kp = k_ref[here, p * 128:(p + 1) * 128]
            dqs = []
            for r in range(2):
                h = 2 * p + r
                rows = slice(r * DH, (r + 1) * DH)
                e = e_refs[p][r, :, here]
                d = dot(lhs_scr[h], vext[h, here, :], NT)
                ds = (e.astype(f32) * d).astype(bf16)
                ds_ref[h, :, here] = ds
                dqs.append(dot(ds, kp))
                dkt[p, rows, here] += dot(qt_scr[p, rows, :], ds)
                dvt[p, rows, here] += dot(dat_scr[p, rows, :], e)
            dq_scr[p] += jnp.where(low, dqs[0], dqs[1])

    for_chunks(base, steps, width, group, chunk)
    for p in range(pairs):
        dp_ref[pl.ds(pl.multiple_of(t0, tq), tq), p * 128:(p + 1) * 128] = dq_scr[p].astype(bf16)

    @pl.when(i == pl.num_programs(0) - 1)
    def _():
        for n, grads in enumerate((dkt, dvt)):
            for p in range(pairs):
                at = ((n + 1) * pairs + p) * 128
                for c in range(0, count, 256):
                    dp_ref[c:c + 256, at:at + 128] = grads[p, :, c:c + 256].T.astype(bf16)


def attention_backward(page_lengths, proj, exps, d_att, atts, rinvs, tq=256, width=256, group=2):
    count = proj.shape[0]
    hc = proj.shape[1] // 3
    heads = hc // DH
    pairs = heads // 2
    grid = (count // tq,)
    tile = lambda i: (i, 0)
    fixed = lambda i: (0, 0)
    return pl.pallas_call(
        functools.partial(backward_kernel, width=width, heads=heads, group=group),
        grid=grid,
        in_specs=[
            pl.BlockSpec(memory_space=pltpu.SMEM),
            pl.BlockSpec((tq, hc), tile),
            pl.BlockSpec((count, hc), lambda i: (0, 1)),
            pl.BlockSpec((count, hc), lambda i: (0, 2)),
            pl.BlockSpec((tq, hc), tile),
        ] + [pl.BlockSpec((2, tq, count), lambda i: (0, i, 0))] * pairs + [pl.BlockSpec((tq, 128), tile)] * (2 * pairs),
        out_specs=[
            pl.BlockSpec((count, 3 * hc), fixed),
            pl.BlockSpec((heads, tq, count), lambda i: (0, i, 0)),
        ],
        out_shape=[
            jax.ShapeDtypeStruct((count, 3 * hc), bf16),
            jax.ShapeDtypeStruct((heads, count, count), bf16),
        ],
        scratch_shapes=[
            pltpu.VMEM((heads, count, 128), bf16),
            pltpu.VMEM((heads, tq, 128), bf16),
            pltpu.VMEM((pairs, 128, tq), bf16),
            pltpu.VMEM((pairs, 128, tq), bf16),
            pltpu.VMEM((pairs, tq, 128), f32),
            pltpu.VMEM((pairs, 128, count), f32),
            pltpu.VMEM((pairs, 128, count), f32),
        ],
        compiler_params=pltpu.CompilerParams(vmem_limit_bytes=56 << 20),
        cost_estimate=pl.CostEstimate(
            flops=heads * count * count * 512, bytes_accessed=150 << 20, transcendentals=0),
        name="attention_backward",
    )(page_lengths, proj, proj, proj, d_att, *exps, *atts, *rinvs)


def parity_sign(v):
    v = v ^ (v >> 2)
    v = v ^ (v >> 1)
    return (1 - 2 * (v & 1)).astype(f32)


def bucket_totals(raw, first, heads):
    rows, cols = raw.shape
    low = rows // (16 * heads)
    r = lax.broadcasted_iota(jnp.int32, raw.shape, 0)
    c = lax.broadcasted_iota(jnp.int32, raw.shape, 1)
    kept = jnp.where((r & 15) == (c & 15), raw, 0.0)
    c = lax.broadcasted_iota(jnp.int32, (cols, 128), 0)
    y = lax.broadcasted_iota(jnp.int32, (cols, 128), 1)
    right = jnp.where(y < cols // 16, parity_sign((c >> 4) & y), 0.0)
    r = lax.broadcasted_iota(jnp.int32, (low * heads, rows), 1) >> 4
    x = lax.broadcasted_iota(jnp.int32, (low * heads, rows), 0)
    function = (r // heads + first) & (low - 1)
    left = jnp.where(r % heads == x % heads, parity_sign(function & (x // heads)), 0.0)
    exact = lax.Precision.HIGHEST
    half = lax.dot_general(kept, right, NN, precision=exact, preferred_element_type=f32)
    out = lax.dot_general(left, half, NN, precision=exact, preferred_element_type=f32)
    return out * f32(1.0 / (low * (cols // 16)))


def table_kernel(len_ref, ds_ref, code_ref, out_ref, hl_ref, hr_ref, *bufs, width, parts):
    heads, tq, count = ds_ref.shape
    i = pl.program_id(0)
    t0 = i * tq
    ends, base, steps = key_window(len_ref, t0, t0 + tq - 1, count, width)

    @pl.when(i == 0)
    def _():
        hl_ref[...] = jnp.zeros_like(hl_ref)
        hr_ref[...] = jnp.zeros_like(hr_ref)

    one = jnp.ones((16, width), bf16)

    def chunk(j, carry):
        c0 = pl.multiple_of(base + j * width, 128)
        here = pl.ds(c0, width)
        blocks = tq // 16 // parts
        for part in range(parts):
            left, blay, brel = bufs[3 * part:3 * part + 3]
            for b in range(blocks):
                at = 16 * (part * blocks + b)
                rows = slice(at, at + 16)
                span = slice(b * width, (b + 1) * width)
                code = code_ref[rows, here]
                rel_signs = signs(code, 0, 5)
                lay_signs = signs(code, 5, 6)
                left_lay = walsh(lay_signs[:2])[1:]
                for h in range(heads):
                    ds = ds_ref[h, rows, here]
                    for a, func in enumerate(left_lay + [None, rel_signs[0]]):
                        place = 16 * (a * heads + h)
                        left[place:place + 16, span] = ds if func is None else ds * func
                for n, func in enumerate(walsh(lay_signs[2:])):
                    blay[16 * n:16 * (n + 1), span] = one if func is None else func
                for n, func in enumerate(walsh(rel_signs[1:])):
                    brel[16 * n:16 * (n + 1), span] = one if func is None else func
            hl_ref[...] += dot(left[:64 * heads, :], blay[...], NT)
            hr_ref[...] += dot(left[48 * heads:80 * heads, :], brel[...], NT)
        return carry

    lax.fori_loop(0, steps, chunk, 0)

    @pl.when(i == pl.num_programs(0) - 1)
    def _():
        out_ref[...] = jnp.zeros_like(out_ref)
        out_ref[:4 * heads, :] = bucket_totals(hl_ref[...], 1, heads)
        out_ref[4 * heads:6 * heads, :] = bucket_totals(hr_ref[...], 0, heads)


def table_grads(page_lengths, ds, code, tq=256, width=256, parts=2):
    heads, count, _ = ds.shape
    deep = tq // 16 * width // parts
    fixed = lambda i: (0, 0)
    return pl.pallas_call(
        functools.partial(table_kernel, width=width, parts=parts),
        grid=(count // tq,),
        in_specs=[
            pl.BlockSpec(memory_space=pltpu.SMEM),
            pl.BlockSpec((heads, tq, count), lambda i: (0, i, 0)),
            pl.BlockSpec((tq, count), lambda i: (i, 0)),
        ],
        out_specs=pl.BlockSpec((8 * heads, 128), fixed),
        out_shape=jax.ShapeDtypeStruct((8 * heads, 128), f32),
        scratch_shapes=[pltpu.VMEM((64 * heads, 256), f32), pltpu.VMEM((32 * heads, 256), f32)] + [
            pltpu.VMEM((80 * heads, deep), bf16),
            pltpu.VMEM((256, deep), bf16),
            pltpu.VMEM((256, deep), bf16),
        ] * parts,
        compiler_params=pltpu.CompilerParams(vmem_limit_bytes=56 << 20),
        cost_estimate=pl.CostEstimate(
            flops=heads * count * count * 512, bytes_accessed=150 << 20, transcendentals=0),
        name="table_grads",
    )(page_lengths, ds, code)


def bucket_sums(totals, heads, first, low):
    rows = totals[first * heads:(first + low) * heads, :16].reshape(low, heads, 16)
    return jnp.transpose(rows, (2, 0, 1)).reshape(16 * low, heads)


TANH_SLOPE = 0.7978845608028654
CUBE = 0.044715


def feed_forward_kernel(far, x_ref, g_ref, *refs):
    weights, (hidden_ref, d_gate_ref, d_up_ref, dn_ref) = refs[:-4], refs[-4:]
    units = hidden_ref.shape[1]
    if far:
        step = pad_lanes(units)
        gate_weight, up_weight, down = [weights[0][:, n * step:n * step + units] for n in range(3)]
        ahead, back = NN, NT
    else:
        gate_weight, up_weight, down = [w[...] for w in weights]
        ahead, back = NT, NN
    x = x_ref[...]
    d_hidden = dot(g_ref[...], down, ahead)
    gate = dot(x, gate_weight, ahead)
    up = dot(x, up_weight, ahead)
    square = gate * gate
    t = jnp.tanh(TANH_SLOPE * gate * (1.0 + CUBE * square))
    half = 0.5 + 0.5 * t
    gelu = gate * half
    slope = half + (0.5 * TANH_SLOPE) * gate * (1.0 - t * t) * (1.0 + (3 * CUBE) * square)
    d_gate = (d_hidden * up * slope).astype(bf16)
    d_up = (d_hidden * gelu).astype(bf16)
    hidden_ref[...] = (gelu * up).astype(bf16)
    d_gate_ref[...] = d_gate
    d_up_ref[...] = d_up
    dn_ref[...] = dot(d_gate, gate_weight, back) + dot(d_up, up_weight, back)


def feed_forward(x, g, units, weights, shard=None, tile=256):
    tokens, features = x.shape
    tile = min(tile, tokens)
    rows = lambda n: pl.BlockSpec((tile, n), lambda i: (i, 0))
    if shard is None:
        weight_specs = [pl.BlockSpec(w.shape, lambda i: (0, 0)) for w in weights]
    else:
        weight_specs = [pl.BlockSpec((features, 3 * pad_lanes(units)), lambda i: (0, shard))]
    return pl.pallas_call(
        functools.partial(feed_forward_kernel, shard is not None),
        grid=(tokens // tile,),
        in_specs=[rows(features), rows(features)] + weight_specs,
        out_specs=[rows(units)] * 3 + [rows(features)],
        out_shape=[jax.ShapeDtypeStruct((tokens, units), bf16)] * 3
        + [jax.ShapeDtypeStruct((tokens, features), f32)],
        compiler_params=pltpu.CompilerParams(vmem_limit_bytes=56 << 20),
        cost_estimate=pl.CostEstimate(
            flops=10 * tokens * features * units, bytes_accessed=10 << 20, transcendentals=tokens * units),
        name="feed_forward",
    )(x, g, *weights)


def pad_lanes(n):
    return (n + 127) // 128 * 128


def weight_grads_kernel(n_left, n_right, *refs):
    lefts = refs[:2 * n_left]
    rights = refs[2 * n_left:-1]
    out_ref = refs[-1]
    rows_in = (((0,), (0,)), ((), ()))
    place = 0
    for n, left in enumerate(n_right):
        a, b = rights[2 * n], rights[2 * n + 1]
        size = a.shape[1]
        value = dot(lefts[2 * left][...], a[...], rows_in) + dot(lefts[2 * left + 1][...], b[...], rows_in)
        out_ref[:, place:place + size] = value.astype(bf16)
        if pad_lanes(size) > size:
            out_ref[:, place + size:place + pad_lanes(size)] = jnp.zeros(
                (out_ref.shape[0], pad_lanes(size) - size), bf16)
        place += pad_lanes(size)


def weight_grads(lefts, rights, groups, tile=256):
    features = lefts[0].shape[1]
    columns = sum(pad_lanes(r.shape[1]) for r in rights[::2])
    column = lambda a: pl.BlockSpec((a.shape[0], tile), lambda i: (0, i))
    whole = lambda a: pl.BlockSpec(a.shape, lambda i: (0, 0))
    return pl.pallas_call(
        functools.partial(weight_grads_kernel, len(lefts) // 2, groups),
        grid=(features // tile,),
        in_specs=[column(a) for a in lefts] + [whole(a) for a in rights],
        out_specs=pl.BlockSpec((tile, columns), lambda i: (i, 0)),
        out_shape=jax.ShapeDtypeStruct((features, columns), bf16),
        compiler_params=pltpu.CompilerParams(vmem_limit_bytes=56 << 20),
        cost_estimate=pl.CostEstimate(
            flops=4 * features * columns * lefts[0].shape[0], bytes_accessed=26 << 20, transcendentals=0),
        name="weight_grads",
    )(*lefts, *rights)


epsilon = 1e-06


def contract_rows(left, right):
    return lax.dot_general(
        left, right, (((0,), (0,)), ((), ())), preferred_element_type=jnp.float32
    )


def contract_cols(left, right):
    return lax.dot_general(
        left, right, (((1,), (1,)), ((), ())), preferred_element_type=jnp.float32
    )


def norm_rows(rows, gain):
    scale = lax.rsqrt(jnp.mean(rows * rows, axis=-1, keepdims=True) + epsilon)
    return (scale, (rows * scale * gain).astype(jnp.bfloat16))


def norm_back(d_normed, rows, scale, gain):
    shaped = d_normed * gain
    cubed = scale * scale * scale
    return scale * shaped - rows * cubed * jnp.mean(shaped * rows, axis=-1, keepdims=True)


def along(array, shift, ring):
    return lax.ppermute(array, "narrow", [(i, (i + shift) % ring) for i in range(ring)])


def swap(array, ring):
    return lax.ppermute(array, "narrow", [(i, i ^ 1) for i in range(ring)])


def rows_of(array, index, count):
    return lax.dynamic_slice_in_dim(array, index * count, count, 0)


def on_device(
    wide,
    ring,
    layer_input,
    out_grad,
    norm_attn_gain,
    w_query,
    w_key,
    w_value,
    w_out,
    rel_table,
    layout_table,
    norm_ffn_gain,
    w_gate,
    w_up,
    down_projection_weight,
    page_lengths,
    key_mask,
    rel_bucket,
    layout_bucket,
):
    tokens, width = layer_input.shape
    head_cols = w_query.shape[1]
    heads = head_cols // DH
    units = w_gate.shape[1]
    padded = pad_lanes(units)
    part = width // wide
    me = lax.axis_index("narrow")
    my_wide = lax.axis_index("wide")
    gain_attn = norm_attn_gain.astype(f32)
    gain_ffn = norm_ffn_gain.astype(f32)
    resid = layer_input.astype(f32)

    scale_attn, normed_attn = norm_rows(resid, gain_attn)
    normed_attn_all = lax.all_gather(normed_attn, "narrow", axis=0, tiled=True)

    w_project = jnp.concatenate([w_query, w_key, w_value], axis=1)
    own_rows_gate = rows_of(w_gate, my_wide, part)
    own_rows_up = rows_of(w_up, my_wide, part)
    own_rows_project = rows_of(w_project, my_wide, part)
    down_piece = lax.dynamic_slice_in_dim(down_projection_weight, my_wide * part, part, 1).T
    out_piece = lax.dynamic_slice_in_dim(w_out, my_wide * part, part, 1).T
    ffn_piece = jnp.concatenate(
        [jnp.pad(piece, ((0, 0), (0, padded - units))) for piece in (own_rows_gate, own_rows_up, down_piece)], axis=1)
    out_pieces = [out_piece] + [along(out_piece, d, ring) for d in range(1, ring)]
    words, codes = pair_bias(page_lengths, rel_bucket, layout_bucket, bias_words(rel_table, layout_table), key_mask)
    normed_attn_all, ffn_piece, words = lax.optimization_barrier((normed_attn_all, ffn_piece, words))
    ffn_pieces = [along(ffn_piece, d, ring) for d in range(2, ring, 2)]
    out_t = lax.all_gather(jnp.concatenate(out_pieces, axis=1), "wide", axis=0, tiled=True)

    projected = dot(normed_attn_all, w_project).astype(bf16)
    pairs = head_cols // 128
    first_pair = list(attention_forward(page_lengths, projected, words, 0))
    first_pair[0], ffn_pieces, late_grad = lax.optimization_barrier((first_pair[0], ffn_pieces, out_grad))
    far_pieces = jnp.concatenate(ffn_pieces, axis=1)
    other_grad = swap(late_grad, ring)

    def to_owners(a):
        return [rows_of(a, me, tokens)] + [
            along(rows_of(a, (me + d) % ring, tokens), d, ring) for d in range(1, ring)]

    sent = [to_owners(first_pair[0])]
    results = [first_pair]
    if pairs > 1:
        late_projected, far_pieces = lax.optimization_barrier((projected, far_pieces))
        results += [list(attention_forward(page_lengths, late_projected, words, p)) for p in range(1, pairs)]
    far = lax.all_gather(far_pieces, "wide", axis=0, tiled=True)
    results[-1][0], other_grad, sent[0] = lax.optimization_barrier((results[-1][0], other_grad, sent[0]))
    attended = [r[0] for r in results]
    sent += [to_owners(a) for a in attended[1:]]
    mine = [pieces[d] for d in range(ring) for pieces in sent]
    attended_own = jnp.concatenate(mine, axis=1)
    middle = resid + contract_cols(attended_own, out_t)

    scale_ffn, normed_ffn = norm_rows(middle, gain_ffn)
    other_normed = swap(normed_ffn, ring)
    near = (w_gate.T, w_up.T, down_projection_weight)
    shards = ring // 2
    own = [feed_forward(normed_ffn, out_grad, units, near)]
    own, other_normed = lax.optimization_barrier((own, other_normed))
    other = [feed_forward(other_normed, other_grad, units, near)]
    other += [feed_forward(other_normed, other_grad, units, (far,), s) for s in range(shards - 1)]
    other_d_normed = sum(o[3] for o in other).astype(bf16)
    late_normed, other_d_normed = lax.optimization_barrier((normed_ffn, other_d_normed))
    other_d_normed = swap(other_d_normed, ring)
    own += [feed_forward(late_normed, out_grad, units, (far,), s) for s in range(shards - 1)]
    rights, groups = [], []
    for s in range(shards):
        for n in range(1, 4):
            rights += [own[s][n % 3], other[s][n % 3]]
            groups.append(n // 3)
    sums = weight_grads((normed_ffn, other_normed, out_grad, other_grad), rights, tuple(groups))
    sums, other_d_normed = lax.optimization_barrier((sums, other_d_normed))
    ffn_sums = lax.psum_scatter(sums, "wide", scatter_dimension=0, tiled=True)
    d_normed_ffn = sum(o[3] for o in own) + other_d_normed.astype(f32)
    d_middle = out_grad.astype(f32) + norm_back(d_normed_ffn, middle, scale_ffn, gain_ffn)
    d_middle_low = d_middle.astype(bf16)
    d_attended_own = dot(d_middle_low, out_t).astype(bf16)

    def block(d):
        return d_attended_own[:, d * head_cols : (d + 1) * head_cols]

    d_attended = jnp.zeros((ring * tokens, head_cols), bf16)
    d_attended = lax.dynamic_update_slice_in_dim(d_attended, block(0), me * tokens, 0)
    for d in range(1, ring):
        d_attended = lax.dynamic_update_slice_in_dim(
            d_attended, along(block(d), -d, ring), ((me + d) % ring) * tokens, 0)

    d_middle_late, attended_late, own_hidden, other_hidden = lax.optimization_barrier(
        (d_middle_low, attended_own, [o[0] for o in own], [o[0] for o in other]))
    wout_sums = contract_rows(d_middle_late, attended_late).astype(bf16)
    own_out, other_out = 0.0, 0.0
    for s in range(shards):
        if s == 0:
            down, dims = down_projection_weight, NN
        else:
            at = 3 * padded * (s - 1) + 2 * padded
            down, dims = far[:, at : at + units], NT
        own_out = own_out + dot(own_hidden[s], down, dims)
        other_out = other_out + dot(other_hidden[s], down, dims)
    own_out = own_out + middle
    wout_sums, d_attended, own_out, other_out, late_project = lax.optimization_barrier(
        (wout_sums, d_attended, own_out, other_out.astype(bf16), own_rows_project))
    other_out = swap(other_out, ring)
    project_pieces = [along(late_project, d, ring) for d in range(1, ring)]

    d_project, d_scores = attention_backward(
        page_lengths, projected, [r[2] for r in results], d_attended, attended, [r[1] for r in results])
    d_project, other_out, project_pieces = lax.optimization_barrier((d_project, other_out, project_pieces))
    w_project_all = lax.all_gather(
        jnp.concatenate([own_rows_project] + project_pieces, axis=1), "wide", axis=0, tiled=True)
    leaving = [rows_of(d_project, (me + d) % ring, tokens) for d in range(ring)]
    leaving, d_project, own_out = lax.optimization_barrier((leaving, d_project, own_out))
    mine = leaving[:1] + [along(leaving[d], d, ring) for d in range(1, ring)]
    layer_out = (own_out + other_out.astype(f32)).astype(bf16)
    last_sums = jnp.concatenate([contract_rows(normed_attn_all, d_project).astype(bf16), wout_sums], axis=1)
    last_sums = lax.psum_scatter(last_sums, "wide", scatter_dimension=0, tiled=True)

    totals = table_grads(page_lengths, d_scores, codes)
    far_sums = [along(ffn_sums[:, 3 * padded * s : 3 * padded * (s + 1)], -2 * s, ring) for s in range(1, shards)]
    totals, mine, far_sums = lax.optimization_barrier((totals, mine, far_sums))
    grad_relative = bucket_sums(totals, heads, 4, 2)
    grad_layout = bucket_sums(totals, heads, 0, 4)
    tables = jnp.concatenate(
        [grad_relative.reshape(wide, -1, heads), grad_layout.reshape(wide, -1, heads)], axis=1)
    n_rel = grad_relative.shape[0] // wide
    reach = wide // 2
    while reach >= 1:
        bit = (my_wide // reach) % 2
        keep = lax.dynamic_slice_in_dim(tables, bit * reach, reach, 0)
        give = lax.dynamic_slice_in_dim(tables, (1 - bit) * reach, reach, 0)
        tables = keep + lax.ppermute(give, "wide", [(i, i ^ reach) for i in range(wide)])
        if reach == wide // 2:
            tables, last_sums = lax.optimization_barrier((tables, last_sums))
        reach //= 2
    sum_project = last_sums[:, : 3 * head_cols].astype(f32)
    wout_sums = last_sums[:, 3 * head_cols :]
    far_wout = [along(wout_sums[:, d * head_cols : (d + 1) * head_cols], -d, ring) for d in range(1, ring)]
    sum_tables = tables[0]
    d_project_own = jnp.concatenate(mine, axis=1)
    d_normed_attn = contract_cols(d_project_own, w_project_all)
    in_grad = d_middle + norm_back(d_normed_attn, resid, scale_attn, gain_attn)

    def stripe(shard, n):
        at = padded * (3 * shard + n)
        return ffn_sums[:, at : at + units]

    sum_gate, sum_up, sum_down = [stripe(0, n).astype(f32) for n in range(3)]
    for s in range(1, shards):
        block = far_sums[s - 1].astype(f32)
        sum_gate += block[:, :units]
        sum_up += block[:, padded : padded + units]
        sum_down += block[:, 2 * padded : 2 * padded + units]
    sum_wout = wout_sums[:, :head_cols].astype(f32) + sum(w.astype(f32) for w in far_wout)

    gain_terms = jnp.stack(
        [
            jnp.sum(own_rows_project.astype(f32) * sum_project, axis=1),
            jnp.sum(own_rows_gate.astype(f32) * sum_gate + own_rows_up.astype(f32) * sum_up, axis=1),
        ]
    )
    share = part // ring

    def gain_share(index):
        return lax.dynamic_slice_in_dim(gain_terms, index * share, share, 1)

    gain_sum = gain_share(me)
    for d in range(1, ring):
        gain_sum = gain_sum + along(gain_share((me + d) % ring), d, ring)
    place = my_wide * part + me * share
    gains = lax.dynamic_slice_in_dim(jnp.stack([gain_attn, gain_ffn]), place, share, 1)
    gain_grads = gain_sum / gains
    return (
        layer_out,
        in_grad,
        gain_grads[0],
        sum_project[:, :head_cols],
        sum_project[:, head_cols : 2 * head_cols],
        sum_project[:, 2 * head_cols :],
        sum_wout.T,
        sum_tables[:n_rel],
        sum_tables[n_rel:],
        gain_grads[1],
        sum_gate,
        sum_up,
        sum_down.T,
    )


def solution(mesh):
    placed = (
        P(("wide", "narrow"), None),
        P(("wide", "narrow"), None),
        P(),
        P(None, "narrow"),
        P(None, "narrow"),
        P(None, "narrow"),
        P("narrow", None),
        P(None, "narrow"),
        P(None, "narrow"),
        P(),
        P(None, "narrow"),
        P(None, "narrow"),
        P("narrow", None),
        P("wide", None),
        P("wide"),
        P("wide", None),
        P("wide", None),
    )
    return jax.shard_map(
        functools.partial(on_device, mesh.shape["wide"], mesh.shape["narrow"]),
        mesh=mesh,
        in_specs=placed,
        out_specs=(
            P(("wide", "narrow"), None),
            P(("wide", "narrow"), None),
            P(("wide", "narrow")),
            P("wide", "narrow"),
            P("wide", "narrow"),
            P("wide", "narrow"),
            P("narrow", "wide"),
            P("wide", "narrow"),
            P("wide", "narrow"),
            P(("wide", "narrow")),
            P("wide", "narrow"),
            P("wide", "narrow"),
            P("narrow", "wide"),
        ),
        check_vma=False,
    )
```

```python
import functools
import jax
import jax.numpy as jnp
from jax import lax
from jax.experimental import pallas as pl
from jax.experimental.pallas import tpu as pltpu
from jax.sharding import PartitionSpec as P

DH = 64
BIAS_SCALE = 4096.0
LOG2E = 1.4426950408889634
f32 = jnp.float32
bf16 = jnp.bfloat16
NT = (((1,), (1,)), ((), ()))
NN = (((1,), (0,)), ((), ()))


def dot(a, b, dims=NN):
    return lax.dot_general(a, b, dims, preferred_element_type=f32)


def key_window(len_ref, first, last, count, width):
    ends = []
    total = 0
    for p in range(len_ref.shape[1]):
        total = total + len_ref[0, p]
        ends.append(total)
    start = 0
    stop = count
    for e in ends:
        start = jnp.where(e <= first, e, start)
    for e in reversed(ends):
        stop = jnp.where(e > last, e, stop)
    base = (start // 128) * 128
    steps = (stop - base + width - 1) // width
    base = jnp.minimum(base, count - steps * width)
    return ends, base, steps


def for_chunks(base, steps, width, group, body):
    def many(j, carry):
        body(pl.multiple_of(base + j * (group * width), 128), group * width)
        return carry

    def single(j, carry):
        body(pl.multiple_of(base + j * width, 128), width)
        return carry

    if group > 1:
        lax.fori_loop(0, steps // group, many, 0)
    lax.fori_loop((steps // group) * group if group > 1 else 0, steps, single, 0)


def own_half(shape, head):
    lane = lax.broadcasted_iota(jnp.int32, shape, len(shape) - 1)
    return (lane < DH) if head % 2 == 0 else (lane >= DH)


def fill_values(vext, v_ref, heads):
    for h in range(heads):
        vp = v_ref[:, (h // 2) * 128:(h // 2 + 1) * 128]
        vext[h] = jnp.where(own_half(vp.shape, h), vp, jnp.ones_like(vp))


def half_norms(rows):
    lane = lax.broadcasted_iota(jnp.int32, (128, 128), 0)
    column = lax.broadcasted_iota(jnp.int32, (128, 128), 1)
    same = ((lane < DH) == (column < DH)).astype(bf16)
    squares = (rows.astype(f32) * rows.astype(f32)).astype(bf16)
    return jnp.max(dot(squares, same)) * f32(1.02)


HIDDEN_PAIR = -(1 << 31)


def pair_bias_kernel(len_ref, rel_ref, lay_ref, tab_ref, kmask_ref, word_ref, code_ref, colcode, *, width, group):
    tq, count = rel_ref.shape
    pairs = word_ref.shape[0]
    i = pl.program_id(0)
    t0 = i * tq
    ends, base, steps = key_window(len_ref, t0, t0 + tq - 1, count, width)

    @pl.when(i == 0)
    def _():
        pos = lax.broadcasted_iota(jnp.int32, (8, count), 1)
        page = jnp.zeros((8, count), jnp.int32)
        for e in ends:
            page = page + (pos >= e).astype(jnp.int32)
        colcode[...] = jnp.where(kmask_ref[...] == 1, page, -1)

    rowpos = lax.broadcasted_iota(jnp.int32, (tq, 128), 0) + t0
    rowpage = jnp.zeros((tq, 128), jnp.int32)
    for e in ends:
        rowpage = rowpage + (rowpos >= e).astype(jnp.int32)
    lanes = lax.broadcasted_iota(jnp.int32, (tq, 128), 1)
    tabs = [jnp.broadcast_to(tab_ref[n:n + 1, :], (tq, 128)) for n in range(2 * pairs)]

    def chunk(c0, size):
        for half in range(size // 128):
            cc = pl.multiple_of(c0 + half * 128, 128)
            here = pl.ds(cc, 128)
            rel = rel_ref[:, here]
            lay = lay_ref[:, here]
            code_ref[:, here] = (rel + lay * 32).astype(jnp.int16)
            col = jnp.broadcast_to(colcode[0:1, here], (tq, 128))
            seen = (rowpage == col) | (rowpos == lanes + cc)
            for p in range(pairs):
                word = (jnp.take_along_axis(tabs[2 * p], rel, axis=1, mode="promise_in_bounds")
                        + jnp.take_along_axis(tabs[2 * p + 1], lay, axis=1, mode="promise_in_bounds"))
                word_ref[p, :, here] = jnp.where(seen, word, HIDDEN_PAIR)

    for_chunks(base, steps, width, group, chunk)


def pair_bias(page_lengths, rel, lay, tab, kmask, tq=256, width=256, group=2):
    count = rel.shape[0]
    pairs = tab.shape[0] // 2
    tile = lambda i: (i, 0)
    return pl.pallas_call(
        functools.partial(pair_bias_kernel, width=width, group=group),
        grid=(count // tq,),
        in_specs=[
            pl.BlockSpec(memory_space=pltpu.SMEM),
            pl.BlockSpec((tq, count), tile),
            pl.BlockSpec((tq, count), tile),
            pl.BlockSpec(tab.shape, lambda i: (0, 0)),
            pl.BlockSpec((1, count), lambda i: (0, 0)),
        ],
        out_specs=[
            pl.BlockSpec((pairs, tq, count), lambda i: (0, i, 0)),
            pl.BlockSpec((tq, count), tile),
        ],
        out_shape=[
            jax.ShapeDtypeStruct((pairs, count, count), jnp.int32),
            jax.ShapeDtypeStruct((count, count), jnp.int16),
        ],
        scratch_shapes=[pltpu.VMEM((8, count), jnp.int32)],
        compiler_params=pltpu.CompilerParams(vmem_limit_bytes=56 << 20),
        cost_estimate=pl.CostEstimate(flops=count * count * 1024, bytes_accessed=120 << 20, transcendentals=0),
        name="pair_bias",
    )(page_lengths, rel, lay, tab, kmask.reshape(1, count))


def forward_kernel(len_ref, q_ref, k_ref, v_ref, word_ref, att_ref, rinv_ref, e_ref,
                   s_scr, m_scr, acc_scr, vext, knorm, *, width, group):
    tq, count = word_ref.shape[1:]
    heads, pairs = 2, 1
    i = pl.program_id(0)
    t0 = i * tq
    ends, base, steps = key_window(len_ref, t0, t0 + tq - 1, count, width)

    @pl.when(i == 0)
    def _():
        fill_values(vext, v_ref, heads)
        for p in range(pairs):
            knorm[p] = half_norms(k_ref[:, p * 128:(p + 1) * 128])

    scaled = []
    largest = f32(0.0)
    for h in range(heads):
        qp = q_ref[:, (h // 2) * 128:(h // 2 + 1) * 128]
        scaled.append(jnp.where(own_half(qp.shape, h), qp * bf16(BIAS_SCALE), jnp.zeros_like(qp)))
        if h % 2 == 0:
            largest = jnp.maximum(largest, half_norms(qp) * knorm[h // 2])
    def scores(c0, width, use):
        raw = [dot(scaled[h], k_ref[pl.ds(c0, width), (h // 2) * 128:(h // 2 + 1) * 128], NT)
               for h in range(heads)]
        for half in range(width // 128):
            cc = pl.multiple_of(c0 + half * 128, 128)
            word = word_ref[0, :, pl.ds(cc, 128)]
            hidden = word == HIDDEN_PAIR
            parts = ((word & 0xFFFF).astype(f32), (word >> 16).astype(f32))
            for h in range(heads):
                bias = jnp.where(hidden, f32(-1e30), parts[h])
                use(h, half, cc, raw[h][:, half * 128:(half + 1) * 128] + bias)

    for h in range(heads):
        acc_scr[h] = jnp.zeros((tq, 128), f32)
    bounded = jnp.sqrt(largest) + 8.0 <= 60.0

    @pl.when(bounded)
    def _():
        def chunk(c0, size):
            pieces = {}

            def use(h, half, cc, s):
                e = jnp.exp2(s * f32(LOG2E / BIAS_SCALE)).astype(bf16)
                e_ref[h, :, pl.ds(cc, 128)] = e
                pieces[h, half] = e

            scores(c0, size, use)
            for h in range(heads):
                e = jnp.concatenate([pieces[h, half] for half in range(size // 128)], axis=1)
                acc_scr[h] += dot(e, vext[h, pl.ds(c0, size), :])

        for_chunks(base, steps, width, group, chunk)

    @pl.when(jnp.logical_not(bounded))
    def _():
        for h in range(heads):
            m_scr[h] = jnp.full((tq, 128), -3e38, f32)

        def first(j, carry):
            def use(h, half, cc, s):
                s_scr[h, :, pl.ds(cc, 128)] = s
                m_scr[h] = jnp.maximum(m_scr[h], s)

            scores(pl.multiple_of(base + j * width, 128), width, use)
            return carry

        lax.fori_loop(0, steps, first, 0)
        for h in range(heads):
            top = jnp.max(m_scr[h], axis=1, keepdims=True)

            def second(j, carry):
                c0 = pl.multiple_of(base + j * width, 128)
                e = jnp.exp2((s_scr[h, :, pl.ds(c0, width)] - top) * f32(LOG2E / BIAS_SCALE)).astype(bf16)
                e_ref[h, :, pl.ds(c0, width)] = e
                acc_scr[h] += dot(e, vext[h, pl.ds(c0, width), :])
                return carry

            lax.fori_loop(0, steps, second, 0)

    low = own_half((tq, 128), 0)
    for p in range(pairs):
        even, odd = acc_scr[2 * p], acc_scr[2 * p + 1]
        rinv = 1.0 / pltpu.roll(jnp.where(low, odd, even), DH, 1)
        att_ref[:, p * 128:(p + 1) * 128] = (jnp.where(low, even, odd) * rinv).astype(bf16)
        rinv_ref[:, p * 128:(p + 1) * 128] = rinv


def attention_forward(page_lengths, proj, words, pair, tq=256, width=256, group=2):
    count = proj.shape[0]
    pairs = proj.shape[1] // (3 * 128)
    tile = lambda i: (i, 0)
    return pl.pallas_call(
        functools.partial(forward_kernel, width=width, group=group),
        grid=(count // tq,),
        in_specs=[
            pl.BlockSpec(memory_space=pltpu.SMEM),
            pl.BlockSpec((tq, 128), lambda i: (i, pair)),
            pl.BlockSpec((count, 128), lambda i: (0, pairs + pair)),
            pl.BlockSpec((count, 128), lambda i: (0, 2 * pairs + pair)),
            pl.BlockSpec((1, tq, count), lambda i: (pair, i, 0)),
        ],
        out_specs=[
            pl.BlockSpec((tq, 128), tile),
            pl.BlockSpec((tq, 128), tile),
            pl.BlockSpec((2, tq, count), lambda i: (0, i, 0)),
        ],
        out_shape=[
            jax.ShapeDtypeStruct((count, 128), bf16),
            jax.ShapeDtypeStruct((count, 128), f32),
            jax.ShapeDtypeStruct((2, count, count), bf16),
        ],
        scratch_shapes=[
            pltpu.VMEM((2, tq, count), f32),
            pltpu.VMEM((2, tq, 128), f32),
            pltpu.VMEM((2, tq, 128), f32),
            pltpu.VMEM((2, count, 128), bf16),
            pltpu.SMEM((1,), f32),
        ],
        compiler_params=pltpu.CompilerParams(vmem_limit_bytes=56 << 20),
        cost_estimate=pl.CostEstimate(
            flops=count * count * 512, bytes_accessed=80 << 20, transcendentals=count * count),
        name="attention_forward",
    )(page_lengths, proj, proj, proj, words)


def bias_words(rel_table, layout_table):
    def pack(table):
        whole = jnp.round(table.astype(f32) * BIAS_SCALE).astype(jnp.int32)
        low = jnp.clip(whole[:, 0::2] + 16384, 0, 32767)
        high = jnp.clip(whole[:, 1::2], -16383, 16383)
        words = (high * 65536 + low).T
        return jnp.pad(words, ((0, 0), (0, 128 - words.shape[1])))
    both = jnp.stack([pack(rel_table), pack(layout_table)], axis=1)
    return both.reshape(-1, 128)


def signs(code, shift, bits):
    return [jnp.where((code & jnp.int16(1 << (shift + b))) == 0, bf16(1.0), bf16(-1.0))
            for b in range(bits)]


def walsh(sign_list):
    out = [None]
    for s in sign_list:
        out = out + [s if o is None else o * s for o in out]
    return out


def backward_kernel(len_ref, q_ref, k_ref, v_ref, da_ref, *refs, width, heads, group):
    tq = q_ref.shape[0]
    count = k_ref.shape[0]
    pairs = heads // 2
    e_refs, att_refs, rinv_refs = refs[:pairs], refs[pairs:2 * pairs], refs[2 * pairs:3 * pairs]
    dp_ref, ds_ref = refs[3 * pairs:3 * pairs + 2]
    vext, lhs_scr, dat_scr, qt_scr, dq_scr, dkt, dvt = refs[3 * pairs + 2:]
    i = pl.program_id(0)
    t0 = i * tq
    ends, base, steps = key_window(len_ref, t0, t0 + tq - 1, count, width)

    @pl.when(i == 0)
    def _():
        fill_values(vext, v_ref, heads)
        dkt[...] = jnp.zeros_like(dkt)
        dvt[...] = jnp.zeros_like(dvt)

    low = own_half((tq, 128), 0)
    lane = lax.broadcasted_iota(jnp.int32, (tq, 128), 1)
    first_part = (lane & 32) == 0
    for p in range(pairs):
        cols = slice(p * 128, (p + 1) * 128)
        da = (da_ref[:, cols].astype(f32) * rinv_refs[p][...]).astype(bf16)
        daf = da.astype(f32)
        prod = daf * att_refs[p][...].astype(f32)
        for r in range(2):
            own = low if r == 0 else jnp.logical_not(low)
            delta = jnp.sum(jnp.where(own, prod, 0.0), axis=1, keepdims=True) * f32(-1.0 / 32)
            high = delta.astype(bf16).astype(f32)
            rest = delta - high
            lhs_scr[2 * p + r] = jnp.where(own, daf, jnp.where(first_part, high, rest)).astype(bf16)
        dat_scr[p] = daf.T.astype(bf16)
        qt_scr[p] = q_ref[:, cols].astype(f32).T.astype(bf16)
        dq_scr[p] = jnp.zeros((tq, 128), f32)

    def chunk(c0, size):
        here = pl.ds(c0, size)
        for p in range(pairs):
            kp = k_ref[here, p * 128:(p + 1) * 128]
            dqs = []
            for r in range(2):
                h = 2 * p + r
                rows = slice(r * DH, (r + 1) * DH)
                e = e_refs[p][r, :, here]
                d = dot(lhs_scr[h], vext[h, here, :], NT)
                ds = (e.astype(f32) * d).astype(bf16)
                ds_ref[h, :, here] = ds
                dqs.append(dot(ds, kp))
                dkt[p, rows, here] += dot(qt_scr[p, rows, :], ds)
                dvt[p, rows, here] += dot(dat_scr[p, rows, :], e)
            dq_scr[p] += jnp.where(low, dqs[0], dqs[1])

    for_chunks(base, steps, width, group, chunk)
    for p in range(pairs):
        dp_ref[pl.ds(pl.multiple_of(t0, tq), tq), p * 128:(p + 1) * 128] = dq_scr[p].astype(bf16)

    @pl.when(i == pl.num_programs(0) - 1)
    def _():
        for n, grads in enumerate((dkt, dvt)):
            for p in range(pairs):
                at = ((n + 1) * pairs + p) * 128
                for c in range(0, count, 256):
                    dp_ref[c:c + 256, at:at + 128] = grads[p, :, c:c + 256].T.astype(bf16)


def attention_backward(page_lengths, proj, exps, d_att, att, rinv, pair, tq=256, width=256, group=2):
    count = proj.shape[0]
    pairs = proj.shape[1] // (3 * 128)
    tile = lambda i: (i, 0)
    return pl.pallas_call(
        functools.partial(backward_kernel, width=width, heads=2, group=group),
        grid=(count // tq,),
        in_specs=[
            pl.BlockSpec(memory_space=pltpu.SMEM),
            pl.BlockSpec((tq, 128), lambda i: (i, pair)),
            pl.BlockSpec((count, 128), lambda i: (0, pairs + pair)),
            pl.BlockSpec((count, 128), lambda i: (0, 2 * pairs + pair)),
            pl.BlockSpec((tq, 128), lambda i: (i, pair)),
            pl.BlockSpec((2, tq, count), lambda i: (0, i, 0)),
            pl.BlockSpec((tq, 128), tile),
            pl.BlockSpec((tq, 128), tile),
        ],
        out_specs=[
            pl.BlockSpec((count, 384), lambda i: (0, 0)),
            pl.BlockSpec((2, tq, count), lambda i: (0, i, 0)),
        ],
        out_shape=[
            jax.ShapeDtypeStruct((count, 384), bf16),
            jax.ShapeDtypeStruct((2, count, count), bf16),
        ],
        scratch_shapes=[
            pltpu.VMEM((2, count, 128), bf16),
            pltpu.VMEM((2, tq, 128), bf16),
            pltpu.VMEM((1, 128, tq), bf16),
            pltpu.VMEM((1, 128, tq), bf16),
            pltpu.VMEM((1, tq, 128), f32),
            pltpu.VMEM((1, 128, count), f32),
            pltpu.VMEM((1, 128, count), f32),
        ],
        compiler_params=pltpu.CompilerParams(vmem_limit_bytes=56 << 20),
        cost_estimate=pl.CostEstimate(flops=count * count * 1024, bytes_accessed=80 << 20, transcendentals=0),
        name="attention_backward",
    )(page_lengths, proj, proj, proj, d_att, exps, att, rinv)


def parity_sign(v):
    v = v ^ (v >> 2)
    v = v ^ (v >> 1)
    return (1 - 2 * (v & 1)).astype(f32)


def bucket_totals(raw, first, heads):
    rows, cols = raw.shape
    low = rows // (16 * heads)
    r = lax.broadcasted_iota(jnp.int32, raw.shape, 0)
    c = lax.broadcasted_iota(jnp.int32, raw.shape, 1)
    kept = jnp.where((r & 15) == (c & 15), raw, 0.0)
    c = lax.broadcasted_iota(jnp.int32, (cols, 128), 0)
    y = lax.broadcasted_iota(jnp.int32, (cols, 128), 1)
    right = jnp.where(y < cols // 16, parity_sign((c >> 4) & y), 0.0)
    r = lax.broadcasted_iota(jnp.int32, (low * heads, rows), 1) >> 4
    x = lax.broadcasted_iota(jnp.int32, (low * heads, rows), 0)
    function = (r // heads + first) & (low - 1)
    left = jnp.where(r % heads == x % heads, parity_sign(function & (x // heads)), 0.0)
    exact = lax.Precision.HIGHEST
    half = lax.dot_general(kept, right, NN, precision=exact, preferred_element_type=f32)
    out = lax.dot_general(left, half, NN, precision=exact, preferred_element_type=f32)
    return out * f32(1.0 / (low * (cols // 16)))


def table_kernel(len_ref, code_ref, *refs, width, parts, pairs):
    ds_refs, (out_ref, hl_ref, hr_ref), bufs = refs[:pairs], refs[pairs:pairs + 3], refs[pairs + 3:]
    heads = 2 * pairs
    tq, count = code_ref.shape
    i = pl.program_id(0)
    t0 = i * tq
    ends, base, steps = key_window(len_ref, t0, t0 + tq - 1, count, width)

    @pl.when(i == 0)
    def _():
        hl_ref[...] = jnp.zeros_like(hl_ref)
        hr_ref[...] = jnp.zeros_like(hr_ref)

    one = jnp.ones((16, width), bf16)

    def chunk(j, carry):
        c0 = pl.multiple_of(base + j * width, 128)
        here = pl.ds(c0, width)
        blocks = tq // 16 // parts
        for part in range(parts):
            left, blay, brel = bufs[3 * part:3 * part + 3]
            for b in range(blocks):
                at = 16 * (part * blocks + b)
                rows = slice(at, at + 16)
                span = slice(b * width, (b + 1) * width)
                code = code_ref[rows, here]
                rel_signs = signs(code, 0, 5)
                lay_signs = signs(code, 5, 6)
                left_lay = walsh(lay_signs[:2])[1:]
                for h in range(heads):
                    ds = ds_refs[h // 2][h % 2, rows, here]
                    for a, func in enumerate(left_lay + [None, rel_signs[0]]):
                        place = 16 * (a * heads + h)
                        left[place:place + 16, span] = ds if func is None else ds * func
                for n, func in enumerate(walsh(lay_signs[2:])):
                    blay[16 * n:16 * (n + 1), span] = one if func is None else func
                for n, func in enumerate(walsh(rel_signs[1:])):
                    brel[16 * n:16 * (n + 1), span] = one if func is None else func
            hl_ref[...] += dot(left[:64 * heads, :], blay[...], NT)
            hr_ref[...] += dot(left[48 * heads:80 * heads, :], brel[...], NT)
        return carry

    lax.fori_loop(0, steps, chunk, 0)

    @pl.when(i == pl.num_programs(0) - 1)
    def _():
        out_ref[...] = jnp.zeros_like(out_ref)
        out_ref[:4 * heads, :] = bucket_totals(hl_ref[...], 1, heads)
        out_ref[4 * heads:6 * heads, :] = bucket_totals(hr_ref[...], 0, heads)


def table_grads(page_lengths, ds, code, tq=256, width=256, parts=2):
    heads, count = 2 * len(ds), code.shape[0]
    deep = tq // 16 * width // parts
    fixed = lambda i: (0, 0)
    return pl.pallas_call(
        functools.partial(table_kernel, width=width, parts=parts, pairs=len(ds)),
        grid=(count // tq,),
        in_specs=[
            pl.BlockSpec(memory_space=pltpu.SMEM),
            pl.BlockSpec((tq, count), lambda i: (i, 0)),
        ] + [pl.BlockSpec((2, tq, count), lambda i: (0, i, 0))] * len(ds),
        out_specs=pl.BlockSpec((8 * heads, 128), fixed),
        out_shape=jax.ShapeDtypeStruct((8 * heads, 128), f32),
        scratch_shapes=[pltpu.VMEM((64 * heads, 256), f32), pltpu.VMEM((32 * heads, 256), f32)] + [
            pltpu.VMEM((80 * heads, deep), bf16),
            pltpu.VMEM((256, deep), bf16),
            pltpu.VMEM((256, deep), bf16),
        ] * parts,
        compiler_params=pltpu.CompilerParams(vmem_limit_bytes=56 << 20),
        cost_estimate=pl.CostEstimate(
            flops=heads * count * count * 512, bytes_accessed=150 << 20, transcendentals=0),
        name="table_grads",
    )(page_lengths, code, *ds)


def bucket_sums(totals, heads, first, low):
    rows = totals[first * heads:(first + low) * heads, :16].reshape(low, heads, 16)
    return jnp.transpose(rows, (2, 0, 1)).reshape(16 * low, heads)


TANH_SLOPE = 0.7978845608028654
CUBE = 0.044715


def feed_forward_kernel(far, x_ref, g_ref, *refs):
    weights, (hidden_ref, d_gate_ref, d_up_ref, dn_ref) = refs[:-4], refs[-4:]
    units = hidden_ref.shape[1]
    if far:
        step = pad_lanes(units)
        gate_weight, up_weight, down = [weights[0][:, n * step:n * step + units] for n in range(3)]
        ahead, back = NN, NT
    else:
        gate_weight, up_weight, down = [w[...] for w in weights]
        ahead, back = NT, NN
    x = x_ref[...]
    d_hidden = dot(g_ref[...], down, ahead)
    gate = dot(x, gate_weight, ahead)
    up = dot(x, up_weight, ahead)
    square = gate * gate
    t = jnp.tanh(TANH_SLOPE * gate * (1.0 + CUBE * square))
    half = 0.5 + 0.5 * t
    gelu = gate * half
    slope = half + (0.5 * TANH_SLOPE) * gate * (1.0 - t * t) * (1.0 + (3 * CUBE) * square)
    d_gate = (d_hidden * up * slope).astype(bf16)
    d_up = (d_hidden * gelu).astype(bf16)
    hidden_ref[...] = (gelu * up).astype(bf16)
    d_gate_ref[...] = d_gate
    d_up_ref[...] = d_up
    dn_ref[...] = dot(d_gate, gate_weight, back) + dot(d_up, up_weight, back)


def feed_forward(x, g, units, weights, shard=None, tile=256):
    tokens, features = x.shape
    tile = min(tile, tokens)
    rows = lambda n: pl.BlockSpec((tile, n), lambda i: (i, 0))
    if shard is None:
        weight_specs = [pl.BlockSpec(w.shape, lambda i: (0, 0)) for w in weights]
    else:
        weight_specs = [pl.BlockSpec((features, 3 * pad_lanes(units)), lambda i: (0, shard))]
    return pl.pallas_call(
        functools.partial(feed_forward_kernel, shard is not None),
        grid=(tokens // tile,),
        in_specs=[rows(features), rows(features)] + weight_specs,
        out_specs=[rows(units)] * 3 + [rows(features)],
        out_shape=[jax.ShapeDtypeStruct((tokens, units), bf16)] * 3
        + [jax.ShapeDtypeStruct((tokens, features), f32)],
        compiler_params=pltpu.CompilerParams(vmem_limit_bytes=56 << 20),
        cost_estimate=pl.CostEstimate(
            flops=10 * tokens * features * units, bytes_accessed=10 << 20, transcendentals=tokens * units),
        name="feed_forward",
    )(x, g, *weights)


def pad_lanes(n):
    return (n + 127) // 128 * 128


def weight_grads_kernel(n_left, n_right, *refs):
    lefts = refs[:2 * n_left]
    rights = refs[2 * n_left:-1]
    out_ref = refs[-1]
    rows_in = (((0,), (0,)), ((), ()))
    place = 0
    for n, left in enumerate(n_right):
        a, b = rights[2 * n], rights[2 * n + 1]
        size = a.shape[1]
        value = dot(lefts[2 * left][...], a[...], rows_in) + dot(lefts[2 * left + 1][...], b[...], rows_in)
        out_ref[:, place:place + size] = value.astype(bf16)
        if pad_lanes(size) > size:
            out_ref[:, place + size:place + pad_lanes(size)] = jnp.zeros(
                (out_ref.shape[0], pad_lanes(size) - size), bf16)
        place += pad_lanes(size)


def weight_grads(lefts, rights, groups, tile=256):
    features = lefts[0].shape[1]
    columns = sum(pad_lanes(r.shape[1]) for r in rights[::2])
    column = lambda a: pl.BlockSpec((a.shape[0], tile), lambda i: (0, i))
    whole = lambda a: pl.BlockSpec(a.shape, lambda i: (0, 0))
    return pl.pallas_call(
        functools.partial(weight_grads_kernel, len(lefts) // 2, groups),
        grid=(features // tile,),
        in_specs=[column(a) for a in lefts] + [whole(a) for a in rights],
        out_specs=pl.BlockSpec((tile, columns), lambda i: (i, 0)),
        out_shape=jax.ShapeDtypeStruct((features, columns), bf16),
        compiler_params=pltpu.CompilerParams(vmem_limit_bytes=56 << 20),
        cost_estimate=pl.CostEstimate(
            flops=4 * features * columns * lefts[0].shape[0], bytes_accessed=26 << 20, transcendentals=0),
        name="weight_grads",
    )(*lefts, *rights)


epsilon = 1e-06


def contract_rows(left, right):
    return lax.dot_general(
        left, right, (((0,), (0,)), ((), ())), preferred_element_type=jnp.float32
    )


def contract_cols(left, right):
    return lax.dot_general(
        left, right, (((1,), (1,)), ((), ())), preferred_element_type=jnp.float32
    )


def norm_rows(rows, gain):
    scale = lax.rsqrt(jnp.mean(rows * rows, axis=-1, keepdims=True) + epsilon)
    return (scale, (rows * scale * gain).astype(jnp.bfloat16))


def norm_back(d_normed, rows, scale, gain):
    shaped = d_normed * gain
    cubed = scale * scale * scale
    return scale * shaped - rows * cubed * jnp.mean(shaped * rows, axis=-1, keepdims=True)


def along(array, shift, ring):
    return lax.ppermute(array, "narrow", [(i, (i + shift) % ring) for i in range(ring)])


def swap(array, ring):
    return lax.ppermute(array, "narrow", [(i, i ^ 1) for i in range(ring)])


def rows_of(array, index, count):
    return lax.dynamic_slice_in_dim(array, index * count, count, 0)


def on_device(
    wide,
    ring,
    layer_input,
    out_grad,
    norm_attn_gain,
    w_query,
    w_key,
    w_value,
    w_out,
    rel_table,
    layout_table,
    norm_ffn_gain,
    w_gate,
    w_up,
    down_projection_weight,
    page_lengths,
    key_mask,
    rel_bucket,
    layout_bucket,
):
    tokens, width = layer_input.shape
    head_cols = w_query.shape[1]
    heads = head_cols // DH
    units = w_gate.shape[1]
    padded = pad_lanes(units)
    part = width // wide
    me = lax.axis_index("narrow")
    my_wide = lax.axis_index("wide")
    gain_attn = norm_attn_gain.astype(f32)
    gain_ffn = norm_ffn_gain.astype(f32)
    resid = layer_input.astype(f32)

    scale_attn, normed_attn = norm_rows(resid, gain_attn)
    normed_attn_all = lax.all_gather(normed_attn, "narrow", axis=0, tiled=True)

    w_project = jnp.concatenate([w_query, w_key, w_value], axis=1)
    own_rows_gate = rows_of(w_gate, my_wide, part)
    own_rows_up = rows_of(w_up, my_wide, part)
    pairs = head_cols // 128
    own_rows_project = jnp.concatenate(
        [rows_of(w, my_wide, part)[:, p * 128 : (p + 1) * 128] for p in range(pairs) for w in (w_query, w_key, w_value)],
        axis=1)
    down_piece = lax.dynamic_slice_in_dim(down_projection_weight, my_wide * part, part, 1).T
    out_piece = lax.dynamic_slice_in_dim(w_out, my_wide * part, part, 1).T
    ffn_piece = jnp.concatenate(
        [jnp.pad(piece, ((0, 0), (0, padded - units))) for piece in (own_rows_gate, own_rows_up, down_piece)], axis=1)
    out_pieces = [out_piece] + [along(out_piece, d, ring) for d in range(1, ring)]
    words, codes = pair_bias(page_lengths, rel_bucket, layout_bucket, bias_words(rel_table, layout_table), key_mask)
    normed_attn_all, ffn_piece, words = lax.optimization_barrier((normed_attn_all, ffn_piece, words))
    ffn_pieces = [along(ffn_piece, d, ring) for d in range(2, ring, 2)]
    out_t = lax.all_gather(jnp.concatenate(out_pieces, axis=1), "wide", axis=0, tiled=True)

    projected = dot(normed_attn_all, w_project).astype(bf16)
    first_pair = list(attention_forward(page_lengths, projected, words, 0))
    first_pair[0], ffn_pieces, late_grad = lax.optimization_barrier((first_pair[0], ffn_pieces, out_grad))
    far_pieces = jnp.concatenate(ffn_pieces, axis=1)
    other_grad = swap(late_grad, ring)

    def to_owners(a):
        return [rows_of(a, me, tokens)] + [
            along(rows_of(a, (me + d) % ring, tokens), d, ring) for d in range(1, ring)]

    sent = [to_owners(first_pair[0])]
    results = [first_pair]
    if pairs > 1:
        late_projected, far_pieces = lax.optimization_barrier((projected, far_pieces))
        results += [list(attention_forward(page_lengths, late_projected, words, p)) for p in range(1, pairs)]
    far = lax.all_gather(far_pieces, "wide", axis=0, tiled=True)
    results[-1][0], other_grad, sent[0] = lax.optimization_barrier((results[-1][0], other_grad, sent[0]))
    attended = [r[0] for r in results]
    sent += [to_owners(a) for a in attended[1:]]
    mine = [pieces[d] for d in range(ring) for pieces in sent]
    attended_own = jnp.concatenate(mine, axis=1)
    middle = resid + contract_cols(attended_own, out_t)

    scale_ffn, normed_ffn = norm_rows(middle, gain_ffn)
    other_normed = swap(normed_ffn, ring)
    near = (w_gate.T, w_up.T, down_projection_weight)
    shards = ring // 2
    own = [feed_forward(normed_ffn, out_grad, units, near)]
    own, other_normed, late_project = lax.optimization_barrier((own, other_normed, own_rows_project))
    project_pieces = [along(late_project, d, ring) for d in range(1, ring)]
    other = [feed_forward(other_normed, other_grad, units, near)]
    other += [feed_forward(other_normed, other_grad, units, (far,), s) for s in range(shards - 1)]
    other, project_pieces = lax.optimization_barrier((other, project_pieces))
    other_d_normed = sum(o[3] for o in other).astype(bf16)
    late_normed, other_d_normed = lax.optimization_barrier((normed_ffn, other_d_normed))
    other_d_normed = swap(other_d_normed, ring)
    own += [feed_forward(late_normed, out_grad, units, (far,), s) for s in range(shards - 1)]
    rights, groups = [], []
    for s in range(shards):
        for n in range(1, 4):
            rights += [own[s][n % 3], other[s][n % 3]]
            groups.append(n // 3)
    sums = weight_grads((normed_ffn, other_normed, out_grad, other_grad), rights, tuple(groups))
    sums, other_d_normed = lax.optimization_barrier((sums, other_d_normed))
    ffn_sums = lax.psum_scatter(sums, "wide", scatter_dimension=0, tiled=True)
    d_normed_ffn = sum(o[3] for o in own) + other_d_normed.astype(f32)
    d_middle = out_grad.astype(f32) + norm_back(d_normed_ffn, middle, scale_ffn, gain_ffn)
    d_middle_low = d_middle.astype(bf16)
    d_attended_own = dot(d_middle_low, out_t).astype(bf16)

    def block(d):
        return d_attended_own[:, d * head_cols : (d + 1) * head_cols]

    d_attended = jnp.zeros((ring * tokens, head_cols), bf16)
    d_attended = lax.dynamic_update_slice_in_dim(d_attended, block(0), me * tokens, 0)
    for d in range(1, ring):
        d_attended = lax.dynamic_update_slice_in_dim(
            d_attended, along(block(d), -d, ring), ((me + d) % ring) * tokens, 0)

    d_middle_late, attended_late, own_hidden, other_hidden = lax.optimization_barrier(
        (d_middle_low, attended_own, [o[0] for o in own], [o[0] for o in other]))
    wout_sums = contract_rows(d_middle_late, attended_late).astype(bf16)
    own_out, other_out = 0.0, 0.0
    for s in range(shards):
        if s == 0:
            down, dims = down_projection_weight, NN
        else:
            at = 3 * padded * (s - 1) + 2 * padded
            down, dims = far[:, at : at + units], NT
        own_out = own_out + dot(own_hidden[s], down, dims)
        other_out = other_out + dot(other_hidden[s], down, dims)
    own_out = own_out + middle
    wout_sums, d_attended, own_out, other_out = lax.optimization_barrier(
        (wout_sums, d_attended, own_out, other_out.astype(bf16)))
    other_out = swap(other_out, ring)

    d_scores, leaving, mine, products = [], [], [], []
    for p, (att, rinv, exps) in enumerate(results):
        d_pair, scores = attention_backward(page_lengths, projected, exps, d_attended, att, rinv, p)
        if p == 0:
            d_pair, other_out, project_pieces = lax.optimization_barrier((d_pair, other_out, project_pieces))
        else:
            d_pair, mine[p - 1], products[p - 1] = lax.optimization_barrier((d_pair, mine[p - 1], products[p - 1]))
        sent = [rows_of(d_pair, (me + d) % ring, tokens) for d in range(ring)]
        sent, d_pair, d_attended = lax.optimization_barrier((sent, d_pair, d_attended))
        mine.append(sent[:1] + [along(sent[d], d, ring) for d in range(1, ring)])
        d_scores.append(scores)
        products.append(contract_rows(normed_attn_all, d_pair).astype(bf16))
    w_project_all = lax.all_gather(
        jnp.concatenate([own_rows_project] + project_pieces, axis=1), "wide", axis=0, tiled=True)
    layer_out = (own_out + other_out.astype(f32)).astype(bf16)
    last_sums = jnp.concatenate(products + [wout_sums], axis=1)
    last_sums = lax.psum_scatter(last_sums, "wide", scatter_dimension=0, tiled=True)

    totals = table_grads(page_lengths, d_scores, codes)
    far_sums = [along(ffn_sums[:, 3 * padded * s : 3 * padded * (s + 1)], -2 * s, ring) for s in range(1, shards)]
    totals, mine, far_sums = lax.optimization_barrier((totals, mine, far_sums))
    grad_relative = bucket_sums(totals, heads, 4, 2)
    grad_layout = bucket_sums(totals, heads, 0, 4)
    tables = jnp.concatenate(
        [grad_relative.reshape(wide, -1, heads), grad_layout.reshape(wide, -1, heads)], axis=1)
    n_rel = grad_relative.shape[0] // wide
    reach = wide // 2
    while reach >= 1:
        bit = (my_wide // reach) % 2
        keep = lax.dynamic_slice_in_dim(tables, bit * reach, reach, 0)
        give = lax.dynamic_slice_in_dim(tables, (1 - bit) * reach, reach, 0)
        tables = keep + lax.ppermute(give, "wide", [(i, i ^ reach) for i in range(wide)])
        if reach == wide // 2:
            tables, last_sums = lax.optimization_barrier((tables, last_sums))
        reach //= 2
    sum_project = last_sums[:, : 3 * head_cols].astype(f32)
    wout_sums = last_sums[:, 3 * head_cols :]
    far_wout = [along(wout_sums[:, d * head_cols : (d + 1) * head_cols], -d, ring) for d in range(1, ring)]
    sum_tables = tables[0]
    d_project_own = jnp.concatenate([pieces[d] for d in range(ring) for pieces in mine], axis=1)
    d_normed_attn = contract_cols(d_project_own, w_project_all)
    in_grad = d_middle + norm_back(d_normed_attn, resid, scale_attn, gain_attn)

    def stripe(shard, n):
        at = padded * (3 * shard + n)
        return ffn_sums[:, at : at + units]

    sum_gate, sum_up, sum_down = [stripe(0, n).astype(f32) for n in range(3)]
    for s in range(1, shards):
        block = far_sums[s - 1].astype(f32)
        sum_gate += block[:, :units]
        sum_up += block[:, padded : padded + units]
        sum_down += block[:, 2 * padded : 2 * padded + units]
    sum_wout = wout_sums[:, :head_cols].astype(f32) + sum(w.astype(f32) for w in far_wout)

    gain_terms = jnp.stack(
        [
            jnp.sum(own_rows_project.astype(f32) * sum_project, axis=1),
            jnp.sum(own_rows_gate.astype(f32) * sum_gate + own_rows_up.astype(f32) * sum_up, axis=1),
        ]
    )
    share = part // ring

    def gain_share(index):
        return lax.dynamic_slice_in_dim(gain_terms, index * share, share, 1)

    gain_sum = gain_share(me)
    for d in range(1, ring):
        gain_sum = gain_sum + along(gain_share((me + d) % ring), d, ring)
    place = my_wide * part + me * share
    gains = lax.dynamic_slice_in_dim(jnp.stack([gain_attn, gain_ffn]), place, share, 1)
    gain_grads = gain_sum / gains

    def whole_project(n):
        return jnp.concatenate([sum_project[:, (3 * p + n) * 128 : (3 * p + n + 1) * 128] for p in range(pairs)], axis=1)

    return (
        layer_out,
        in_grad,
        gain_grads[0],
        whole_project(0),
        whole_project(1),
        whole_project(2),
        sum_wout.T,
        sum_tables[:n_rel],
        sum_tables[n_rel:],
        gain_grads[1],
        sum_gate,
        sum_up,
        sum_down.T,
    )


def solution(mesh):
    placed = (
        P(("wide", "narrow"), None),
        P(("wide", "narrow"), None),
        P(),
        P(None, "narrow"),
        P(None, "narrow"),
        P(None, "narrow"),
        P("narrow", None),
        P(None, "narrow"),
        P(None, "narrow"),
        P(),
        P(None, "narrow"),
        P(None, "narrow"),
        P("narrow", None),
        P("wide", None),
        P("wide"),
        P("wide", None),
        P("wide", None),
    )
    return jax.shard_map(
        functools.partial(on_device, mesh.shape["wide"], mesh.shape["narrow"]),
        mesh=mesh,
        in_specs=placed,
        out_specs=(
            P(("wide", "narrow"), None),
            P(("wide", "narrow"), None),
            P(("wide", "narrow")),
            P("wide", "narrow"),
            P("wide", "narrow"),
            P("wide", "narrow"),
            P("narrow", "wide"),
            P("wide", "narrow"),
            P("wide", "narrow"),
            P(("wide", "narrow")),
            P("wide", "narrow"),
            P("wide", "narrow"),
            P("narrow", "wide"),
        ),
        check_vma=False,
    )
```

```python
import functools
import jax
import jax.numpy as jnp
from jax import lax
from jax.experimental import pallas as pl
from jax.experimental.pallas import tpu as pltpu
from jax.sharding import PartitionSpec as P

DH = 64
BIAS_SCALE = 4096.0
LOG2E = 1.4426950408889634
f32 = jnp.float32
bf16 = jnp.bfloat16
NT = (((1,), (1,)), ((), ()))
NN = (((1,), (0,)), ((), ()))


def dot(a, b, dims=NN):
    return lax.dot_general(a, b, dims, preferred_element_type=f32)


def key_window(len_ref, first, last, count, width):
    ends = []
    total = 0
    for p in range(len_ref.shape[1]):
        total = total + len_ref[0, p]
        ends.append(total)
    start = 0
    stop = count
    for e in ends:
        start = jnp.where(e <= first, e, start)
    for e in reversed(ends):
        stop = jnp.where(e > last, e, stop)
    base = (start // 128) * 128
    steps = (stop - base + width - 1) // width
    base = jnp.minimum(base, count - steps * width)
    return ends, base, steps


def for_chunks(base, steps, width, group, body):
    def many(j, carry):
        body(pl.multiple_of(base + j * (group * width), 128), group * width)
        return carry

    def single(j, carry):
        body(pl.multiple_of(base + j * width, 128), width)
        return carry

    if group > 1:
        lax.fori_loop(0, steps // group, many, 0)
    lax.fori_loop((steps // group) * group if group > 1 else 0, steps, single, 0)


def own_half(shape, head):
    lane = lax.broadcasted_iota(jnp.int32, shape, len(shape) - 1)
    return (lane < DH) if head % 2 == 0 else (lane >= DH)


def fill_values(vext, v_ref, heads):
    for h in range(heads):
        vp = v_ref[:, (h // 2) * 128:(h // 2 + 1) * 128]
        vext[h] = jnp.where(own_half(vp.shape, h), vp, jnp.ones_like(vp))


def half_norms(rows):
    lane = lax.broadcasted_iota(jnp.int32, (128, 128), 0)
    column = lax.broadcasted_iota(jnp.int32, (128, 128), 1)
    same = ((lane < DH) == (column < DH)).astype(bf16)
    squares = (rows.astype(f32) * rows.astype(f32)).astype(bf16)
    return jnp.max(dot(squares, same)) * f32(1.02)


HIDDEN_PAIR = -(1 << 31)


def pair_bias_kernel(len_ref, rel_ref, lay_ref, tab_ref, kmask_ref, word_ref, code_ref, colcode, *, width, group):
    tq, count = rel_ref.shape
    pairs = word_ref.shape[0]
    i = pl.program_id(0)
    t0 = i * tq
    ends, base, steps = key_window(len_ref, t0, t0 + tq - 1, count, width)

    @pl.when(i == 0)
    def _():
        pos = lax.broadcasted_iota(jnp.int32, (8, count), 1)
        page = jnp.zeros((8, count), jnp.int32)
        for e in ends:
            page = page + (pos >= e).astype(jnp.int32)
        colcode[...] = jnp.where(kmask_ref[...] == 1, page, -1)

    rowpos = lax.broadcasted_iota(jnp.int32, (tq, 128), 0) + t0
    rowpage = jnp.zeros((tq, 128), jnp.int32)
    for e in ends:
        rowpage = rowpage + (rowpos >= e).astype(jnp.int32)
    lanes = lax.broadcasted_iota(jnp.int32, (tq, 128), 1)
    tabs = [jnp.broadcast_to(tab_ref[n:n + 1, :], (tq, 128)) for n in range(2 * pairs)]

    def chunk(c0, size):
        for half in range(size // 128):
            cc = pl.multiple_of(c0 + half * 128, 128)
            here = pl.ds(cc, 128)
            rel = rel_ref[:, here]
            lay = lay_ref[:, here]
            code_ref[:, here] = (rel + lay * 32).astype(jnp.int16)
            col = jnp.broadcast_to(colcode[0:1, here], (tq, 128))
            seen = (rowpage == col) | (rowpos == lanes + cc)
            for p in range(pairs):
                word = (jnp.take_along_axis(tabs[2 * p], rel, axis=1, mode="promise_in_bounds")
                        + jnp.take_along_axis(tabs[2 * p + 1], lay, axis=1, mode="promise_in_bounds"))
                word_ref[p, :, here] = jnp.where(seen, word, HIDDEN_PAIR)

    for_chunks(base, steps, width, group, chunk)


def pair_bias(page_lengths, rel, lay, tab, kmask, tq=256, width=256, group=2):
    count = rel.shape[0]
    pairs = tab.shape[0] // 2
    tile = lambda i: (i, 0)
    return pl.pallas_call(
        functools.partial(pair_bias_kernel, width=width, group=group),
        grid=(count // tq,),
        in_specs=[
            pl.BlockSpec(memory_space=pltpu.SMEM),
            pl.BlockSpec((tq, count), tile),
            pl.BlockSpec((tq, count), tile),
            pl.BlockSpec(tab.shape, lambda i: (0, 0)),
            pl.BlockSpec((1, count), lambda i: (0, 0)),
        ],
        out_specs=[
            pl.BlockSpec((pairs, tq, count), lambda i: (0, i, 0)),
            pl.BlockSpec((tq, count), tile),
        ],
        out_shape=[
            jax.ShapeDtypeStruct((pairs, count, count), jnp.int32),
            jax.ShapeDtypeStruct((count, count), jnp.int16),
        ],
        scratch_shapes=[pltpu.VMEM((8, count), jnp.int32)],
        compiler_params=pltpu.CompilerParams(vmem_limit_bytes=56 << 20),
        cost_estimate=pl.CostEstimate(flops=count * count * 1024, bytes_accessed=120 << 20, transcendentals=0),
        name="pair_bias",
    )(page_lengths, rel, lay, tab, kmask.reshape(1, count))


def forward_kernel(len_ref, q_ref, k_ref, v_ref, word_ref, att_ref, rinv_ref, e_ref,
                   s_scr, m_scr, acc_scr, vext, knorm, *, width, group):
    tq, count = word_ref.shape[1:]
    heads, pairs = 2, 1
    i = pl.program_id(0)
    t0 = i * tq
    ends, base, steps = key_window(len_ref, t0, t0 + tq - 1, count, width)

    @pl.when(i == 0)
    def _():
        fill_values(vext, v_ref, heads)
        for p in range(pairs):
            knorm[p] = half_norms(k_ref[:, p * 128:(p + 1) * 128])

    scaled = []
    largest = f32(0.0)
    for h in range(heads):
        qp = q_ref[:, (h // 2) * 128:(h // 2 + 1) * 128]
        scaled.append(jnp.where(own_half(qp.shape, h), qp * bf16(BIAS_SCALE), jnp.zeros_like(qp)))
        if h % 2 == 0:
            largest = jnp.maximum(largest, half_norms(qp) * knorm[h // 2])
    def scores(c0, width, use):
        raw = [dot(scaled[h], k_ref[pl.ds(c0, width), (h // 2) * 128:(h // 2 + 1) * 128], NT)
               for h in range(heads)]
        for half in range(width // 128):
            cc = pl.multiple_of(c0 + half * 128, 128)
            word = word_ref[0, :, pl.ds(cc, 128)]
            hidden = word == HIDDEN_PAIR
            parts = ((word & 0xFFFF).astype(f32), (word >> 16).astype(f32))
            for h in range(heads):
                bias = jnp.where(hidden, f32(-1e30), parts[h])
                use(h, half, cc, raw[h][:, half * 128:(half + 1) * 128] + bias)

    for h in range(heads):
        acc_scr[h] = jnp.zeros((tq, 128), f32)
    bounded = jnp.sqrt(largest) + 8.0 <= 60.0

    @pl.when(bounded)
    def _():
        def chunk(c0, size):
            pieces = {}

            def use(h, half, cc, s):
                e = jnp.exp2(s * f32(LOG2E / BIAS_SCALE)).astype(bf16)
                e_ref[h, :, pl.ds(cc, 128)] = e
                pieces[h, half] = e

            scores(c0, size, use)
            for h in range(heads):
                e = jnp.concatenate([pieces[h, half] for half in range(size // 128)], axis=1)
                acc_scr[h] += dot(e, vext[h, pl.ds(c0, size), :])

        for_chunks(base, steps, width, group, chunk)

    @pl.when(jnp.logical_not(bounded))
    def _():
        for h in range(heads):
            m_scr[h] = jnp.full((tq, 128), -3e38, f32)

        def first(j, carry):
            def use(h, half, cc, s):
                s_scr[h, :, pl.ds(cc, 128)] = s
                m_scr[h] = jnp.maximum(m_scr[h], s)

            scores(pl.multiple_of(base + j * width, 128), width, use)
            return carry

        lax.fori_loop(0, steps, first, 0)
        for h in range(heads):
            top = jnp.max(m_scr[h], axis=1, keepdims=True)

            def second(j, carry):
                c0 = pl.multiple_of(base + j * width, 128)
                e = jnp.exp2((s_scr[h, :, pl.ds(c0, width)] - top) * f32(LOG2E / BIAS_SCALE)).astype(bf16)
                e_ref[h, :, pl.ds(c0, width)] = e
                acc_scr[h] += dot(e, vext[h, pl.ds(c0, width), :])
                return carry

            lax.fori_loop(0, steps, second, 0)

    low = own_half((tq, 128), 0)
    for p in range(pairs):
        even, odd = acc_scr[2 * p], acc_scr[2 * p + 1]
        rinv = 1.0 / pltpu.roll(jnp.where(low, odd, even), DH, 1)
        att_ref[:, p * 128:(p + 1) * 128] = (jnp.where(low, even, odd) * rinv).astype(bf16)
        rinv_ref[:, p * 128:(p + 1) * 128] = rinv


def attention_forward(page_lengths, proj, words, pair, tq=256, width=256, group=2):
    count = proj.shape[0]
    pairs = proj.shape[1] // (3 * 128)
    tile = lambda i: (i, 0)
    return pl.pallas_call(
        functools.partial(forward_kernel, width=width, group=group),
        grid=(count // tq,),
        in_specs=[
            pl.BlockSpec(memory_space=pltpu.SMEM),
            pl.BlockSpec((tq, 128), lambda i: (i, pair)),
            pl.BlockSpec((count, 128), lambda i: (0, pairs + pair)),
            pl.BlockSpec((count, 128), lambda i: (0, 2 * pairs + pair)),
            pl.BlockSpec((1, tq, count), lambda i: (pair, i, 0)),
        ],
        out_specs=[
            pl.BlockSpec((tq, 128), tile),
            pl.BlockSpec((tq, 128), tile),
            pl.BlockSpec((2, tq, count), lambda i: (0, i, 0)),
        ],
        out_shape=[
            jax.ShapeDtypeStruct((count, 128), bf16),
            jax.ShapeDtypeStruct((count, 128), f32),
            jax.ShapeDtypeStruct((2, count, count), bf16),
        ],
        scratch_shapes=[
            pltpu.VMEM((2, tq, count), f32),
            pltpu.VMEM((2, tq, 128), f32),
            pltpu.VMEM((2, tq, 128), f32),
            pltpu.VMEM((2, count, 128), bf16),
            pltpu.SMEM((1,), f32),
        ],
        compiler_params=pltpu.CompilerParams(vmem_limit_bytes=56 << 20),
        cost_estimate=pl.CostEstimate(
            flops=count * count * 512, bytes_accessed=80 << 20, transcendentals=count * count),
        name="attention_forward",
    )(page_lengths, proj, proj, proj, words)


def bias_words(rel_table, layout_table):
    def pack(table):
        whole = jnp.round(table.astype(f32) * BIAS_SCALE).astype(jnp.int32)
        low = jnp.clip(whole[:, 0::2] + 16384, 0, 32767)
        high = jnp.clip(whole[:, 1::2], -16383, 16383)
        words = (high * 65536 + low).T
        return jnp.pad(words, ((0, 0), (0, 128 - words.shape[1])))
    both = jnp.stack([pack(rel_table), pack(layout_table)], axis=1)
    return both.reshape(-1, 128)


def signs(code, shift, bits):
    return [jnp.where((code & jnp.int16(1 << (shift + b))) == 0, bf16(1.0), bf16(-1.0))
            for b in range(bits)]


def walsh(sign_list):
    out = [None]
    for s in sign_list:
        out = out + [s if o is None else o * s for o in out]
    return out


def backward_kernel(len_ref, q_ref, k_ref, v_ref, da_ref, *refs, width, heads, group):
    tq = q_ref.shape[0]
    count = k_ref.shape[0]
    pairs = heads // 2
    e_refs, att_refs, rinv_refs = refs[:pairs], refs[pairs:2 * pairs], refs[2 * pairs:3 * pairs]
    dp_ref, ds_ref = refs[3 * pairs:3 * pairs + 2]
    vext, lhs_scr, dat_scr, qt_scr, dq_scr, dkt, dvt = refs[3 * pairs + 2:]
    i = pl.program_id(0)
    t0 = i * tq
    ends, base, steps = key_window(len_ref, t0, t0 + tq - 1, count, width)

    @pl.when(i == 0)
    def _():
        fill_values(vext, v_ref, heads)
        dkt[...] = jnp.zeros_like(dkt)
        dvt[...] = jnp.zeros_like(dvt)

    low = own_half((tq, 128), 0)
    lane = lax.broadcasted_iota(jnp.int32, (tq, 128), 1)
    first_part = (lane & 32) == 0
    for p in range(pairs):
        cols = slice(p * 128, (p + 1) * 128)
        da = (da_ref[:, cols].astype(f32) * rinv_refs[p][...]).astype(bf16)
        daf = da.astype(f32)
        prod = daf * att_refs[p][...].astype(f32)
        for r in range(2):
            own = low if r == 0 else jnp.logical_not(low)
            delta = jnp.sum(jnp.where(own, prod, 0.0), axis=1, keepdims=True) * f32(-1.0 / 32)
            high = delta.astype(bf16).astype(f32)
            rest = delta - high
            lhs_scr[2 * p + r] = jnp.where(own, daf, jnp.where(first_part, high, rest)).astype(bf16)
        dat_scr[p] = daf.T.astype(bf16)
        qt_scr[p] = q_ref[:, cols].astype(f32).T.astype(bf16)
        dq_scr[p] = jnp.zeros((tq, 128), f32)

    def chunk(c0, size):
        here = pl.ds(c0, size)
        for p in range(pairs):
            kp = k_ref[here, p * 128:(p + 1) * 128]
            dqs = []
            for r in range(2):
                h = 2 * p + r
                rows = slice(r * DH, (r + 1) * DH)
                e = e_refs[p][r, :, here]
                d = dot(lhs_scr[h], vext[h, here, :], NT)
                ds = (e.astype(f32) * d).astype(bf16)
                ds_ref[h, :, here] = ds
                dqs.append(dot(ds, kp))
                dkt[p, rows, here] += dot(qt_scr[p, rows, :], ds)
                dvt[p, rows, here] += dot(dat_scr[p, rows, :], e)
            dq_scr[p] += jnp.where(low, dqs[0], dqs[1])

    for_chunks(base, steps, width, group, chunk)
    for p in range(pairs):
        dp_ref[pl.ds(pl.multiple_of(t0, tq), tq), p * 128:(p + 1) * 128] = dq_scr[p].astype(bf16)

    @pl.when(i == pl.num_programs(0) - 1)
    def _():
        for n, grads in enumerate((dkt, dvt)):
            for p in range(pairs):
                at = ((n + 1) * pairs + p) * 128
                for c in range(0, count, 256):
                    dp_ref[c:c + 256, at:at + 128] = grads[p, :, c:c + 256].T.astype(bf16)


def attention_backward(page_lengths, proj, exps, d_att, att, rinv, pair, tq=256, width=256, group=2):
    count = proj.shape[0]
    pairs = proj.shape[1] // (3 * 128)
    tile = lambda i: (i, 0)
    return pl.pallas_call(
        functools.partial(backward_kernel, width=width, heads=2, group=group),
        grid=(count // tq,),
        in_specs=[
            pl.BlockSpec(memory_space=pltpu.SMEM),
            pl.BlockSpec((tq, 128), lambda i: (i, pair)),
            pl.BlockSpec((count, 128), lambda i: (0, pairs + pair)),
            pl.BlockSpec((count, 128), lambda i: (0, 2 * pairs + pair)),
            pl.BlockSpec((tq, 128), lambda i: (i, pair)),
            pl.BlockSpec((2, tq, count), lambda i: (0, i, 0)),
            pl.BlockSpec((tq, 128), tile),
            pl.BlockSpec((tq, 128), tile),
        ],
        out_specs=[
            pl.BlockSpec((count, 384), lambda i: (0, 0)),
            pl.BlockSpec((2, tq, count), lambda i: (0, i, 0)),
        ],
        out_shape=[
            jax.ShapeDtypeStruct((count, 384), bf16),
            jax.ShapeDtypeStruct((2, count, count), bf16),
        ],
        scratch_shapes=[
            pltpu.VMEM((2, count, 128), bf16),
            pltpu.VMEM((2, tq, 128), bf16),
            pltpu.VMEM((1, 128, tq), bf16),
            pltpu.VMEM((1, 128, tq), bf16),
            pltpu.VMEM((1, tq, 128), f32),
            pltpu.VMEM((1, 128, count), f32),
            pltpu.VMEM((1, 128, count), f32),
        ],
        compiler_params=pltpu.CompilerParams(vmem_limit_bytes=56 << 20),
        cost_estimate=pl.CostEstimate(flops=count * count * 1024, bytes_accessed=80 << 20, transcendentals=0),
        name="attention_backward",
    )(page_lengths, proj, proj, proj, d_att, exps, att, rinv)


def parity_sign(v):
    v = v ^ (v >> 2)
    v = v ^ (v >> 1)
    return (1 - 2 * (v & 1)).astype(f32)


def bucket_totals(raw, first, heads):
    rows, cols = raw.shape
    low = rows // (16 * heads)
    r = lax.broadcasted_iota(jnp.int32, raw.shape, 0)
    c = lax.broadcasted_iota(jnp.int32, raw.shape, 1)
    kept = jnp.where((r & 15) == (c & 15), raw, 0.0)
    c = lax.broadcasted_iota(jnp.int32, (cols, 128), 0)
    y = lax.broadcasted_iota(jnp.int32, (cols, 128), 1)
    right = jnp.where(y < cols // 16, parity_sign((c >> 4) & y), 0.0)
    r = lax.broadcasted_iota(jnp.int32, (low * heads, rows), 1) >> 4
    x = lax.broadcasted_iota(jnp.int32, (low * heads, rows), 0)
    function = (r // heads + first) & (low - 1)
    left = jnp.where(r % heads == x % heads, parity_sign(function & (x // heads)), 0.0)
    exact = lax.Precision.HIGHEST
    half = lax.dot_general(kept, right, NN, precision=exact, preferred_element_type=f32)
    out = lax.dot_general(left, half, NN, precision=exact, preferred_element_type=f32)
    return out * f32(1.0 / (low * (cols // 16)))


def table_kernel(len_ref, code_ref, *refs, width, parts, pairs):
    ds_refs, (out_ref, hl_ref, hr_ref), bufs = refs[:pairs], refs[pairs:pairs + 3], refs[pairs + 3:]
    heads = 2 * pairs
    tq, count = code_ref.shape
    i = pl.program_id(0)
    t0 = i * tq
    ends, base, steps = key_window(len_ref, t0, t0 + tq - 1, count, width)

    @pl.when(i == 0)
    def _():
        hl_ref[...] = jnp.zeros_like(hl_ref)
        hr_ref[...] = jnp.zeros_like(hr_ref)

    one = jnp.ones((16, width), bf16)

    def chunk(j, carry):
        c0 = pl.multiple_of(base + j * width, 128)
        here = pl.ds(c0, width)
        blocks = tq // 16 // parts
        for part in range(parts):
            left, blay, brel = bufs[3 * part:3 * part + 3]
            for b in range(blocks):
                at = 16 * (part * blocks + b)
                rows = slice(at, at + 16)
                span = slice(b * width, (b + 1) * width)
                code = code_ref[rows, here]
                rel_signs = signs(code, 0, 5)
                lay_signs = signs(code, 5, 6)
                left_lay = walsh(lay_signs[:2])[1:]
                for h in range(heads):
                    ds = ds_refs[h // 2][h % 2, rows, here]
                    for a, func in enumerate(left_lay + [None, rel_signs[0]]):
                        place = 16 * (a * heads + h)
                        left[place:place + 16, span] = ds if func is None else ds * func
                for n, func in enumerate(walsh(lay_signs[2:])):
                    blay[16 * n:16 * (n + 1), span] = one if func is None else func
                for n, func in enumerate(walsh(rel_signs[1:])):
                    brel[16 * n:16 * (n + 1), span] = one if func is None else func
            hl_ref[...] += dot(left[:64 * heads, :], blay[...], NT)
            hr_ref[...] += dot(left[48 * heads:80 * heads, :], brel[...], NT)
        return carry

    lax.fori_loop(0, steps, chunk, 0)

    @pl.when(i == pl.num_programs(0) - 1)
    def _():
        out_ref[...] = jnp.zeros_like(out_ref)
        out_ref[:4 * heads, :] = bucket_totals(hl_ref[...], 1, heads)
        out_ref[4 * heads:6 * heads, :] = bucket_totals(hr_ref[...], 0, heads)


def table_grads(page_lengths, ds, code, tq=256, width=256, parts=2):
    heads, count = 2 * len(ds), code.shape[0]
    deep = tq // 16 * width // parts
    fixed = lambda i: (0, 0)
    return pl.pallas_call(
        functools.partial(table_kernel, width=width, parts=parts, pairs=len(ds)),
        grid=(count // tq,),
        in_specs=[
            pl.BlockSpec(memory_space=pltpu.SMEM),
            pl.BlockSpec((tq, count), lambda i: (i, 0)),
        ] + [pl.BlockSpec((2, tq, count), lambda i: (0, i, 0))] * len(ds),
        out_specs=pl.BlockSpec((8 * heads, 128), fixed),
        out_shape=jax.ShapeDtypeStruct((8 * heads, 128), f32),
        scratch_shapes=[pltpu.VMEM((64 * heads, 256), f32), pltpu.VMEM((32 * heads, 256), f32)] + [
            pltpu.VMEM((80 * heads, deep), bf16),
            pltpu.VMEM((256, deep), bf16),
            pltpu.VMEM((256, deep), bf16),
        ] * parts,
        compiler_params=pltpu.CompilerParams(vmem_limit_bytes=56 << 20),
        cost_estimate=pl.CostEstimate(
            flops=heads * count * count * 512, bytes_accessed=150 << 20, transcendentals=0),
        name="table_grads",
    )(page_lengths, code, *ds)


def bucket_sums(totals, heads, first, low):
    rows = totals[first * heads:(first + low) * heads, :16].reshape(low, heads, 16)
    return jnp.transpose(rows, (2, 0, 1)).reshape(16 * low, heads)


TANH_SLOPE = 0.7978845608028654
CUBE = 0.044715


def feed_forward_kernel(far, x_ref, g_ref, *refs):
    weights, (hidden_ref, d_gate_ref, d_up_ref, dn_ref) = refs[:-4], refs[-4:]
    units = hidden_ref.shape[1]
    if far:
        step = pad_lanes(units)
        gate_weight, up_weight, down = [weights[0][:, n * step:n * step + units] for n in range(3)]
        ahead, back = NN, NT
    else:
        gate_weight, up_weight, down = [w[...] for w in weights]
        ahead, back = NT, NN
    x = x_ref[...]
    d_hidden = dot(g_ref[...], down, ahead)
    gate = dot(x, gate_weight, ahead)
    up = dot(x, up_weight, ahead)
    square = gate * gate
    t = jnp.tanh(TANH_SLOPE * gate * (1.0 + CUBE * square))
    half = 0.5 + 0.5 * t
    gelu = gate * half
    slope = half + (0.5 * TANH_SLOPE) * gate * (1.0 - t * t) * (1.0 + (3 * CUBE) * square)
    d_gate = (d_hidden * up * slope).astype(bf16)
    d_up = (d_hidden * gelu).astype(bf16)
    hidden_ref[...] = (gelu * up).astype(bf16)
    d_gate_ref[...] = d_gate
    d_up_ref[...] = d_up
    dn_ref[...] = dot(d_gate, gate_weight, back) + dot(d_up, up_weight, back)


def feed_forward(x, g, units, weights, shard=None, tile=256):
    tokens, features = x.shape
    tile = min(tile, tokens)
    rows = lambda n: pl.BlockSpec((tile, n), lambda i: (i, 0))
    if shard is None:
        weight_specs = [pl.BlockSpec(w.shape, lambda i: (0, 0)) for w in weights]
    else:
        weight_specs = [pl.BlockSpec((features, 3 * pad_lanes(units)), lambda i: (0, shard))]
    return pl.pallas_call(
        functools.partial(feed_forward_kernel, shard is not None),
        grid=(tokens // tile,),
        in_specs=[rows(features), rows(features)] + weight_specs,
        out_specs=[rows(units)] * 3 + [rows(features)],
        out_shape=[jax.ShapeDtypeStruct((tokens, units), bf16)] * 3
        + [jax.ShapeDtypeStruct((tokens, features), f32)],
        compiler_params=pltpu.CompilerParams(vmem_limit_bytes=56 << 20),
        cost_estimate=pl.CostEstimate(
            flops=10 * tokens * features * units, bytes_accessed=10 << 20, transcendentals=tokens * units),
        name="feed_forward",
    )(x, g, *weights)


def pad_lanes(n):
    return (n + 127) // 128 * 128


def weight_grads_kernel(n_left, n_right, *refs):
    lefts = refs[:2 * n_left]
    rights = refs[2 * n_left:-1]
    out_ref = refs[-1]
    rows_in = (((0,), (0,)), ((), ()))
    place = 0
    for n, left in enumerate(n_right):
        a, b = rights[2 * n], rights[2 * n + 1]
        size = a.shape[1]
        value = dot(lefts[2 * left][...], a[...], rows_in) + dot(lefts[2 * left + 1][...], b[...], rows_in)
        out_ref[:, place:place + size] = value.astype(bf16)
        if pad_lanes(size) > size:
            out_ref[:, place + size:place + pad_lanes(size)] = jnp.zeros(
                (out_ref.shape[0], pad_lanes(size) - size), bf16)
        place += pad_lanes(size)


def weight_grads(lefts, rights, groups, tile=256):
    features = lefts[0].shape[1]
    columns = sum(pad_lanes(r.shape[1]) for r in rights[::2])
    column = lambda a: pl.BlockSpec((a.shape[0], tile), lambda i: (0, i))
    whole = lambda a: pl.BlockSpec(a.shape, lambda i: (0, 0))
    return pl.pallas_call(
        functools.partial(weight_grads_kernel, len(lefts) // 2, groups),
        grid=(features // tile,),
        in_specs=[column(a) for a in lefts] + [whole(a) for a in rights],
        out_specs=pl.BlockSpec((tile, columns), lambda i: (i, 0)),
        out_shape=jax.ShapeDtypeStruct((features, columns), bf16),
        compiler_params=pltpu.CompilerParams(vmem_limit_bytes=56 << 20),
        cost_estimate=pl.CostEstimate(
            flops=4 * features * columns * lefts[0].shape[0], bytes_accessed=26 << 20, transcendentals=0),
        name="weight_grads",
    )(*lefts, *rights)


def pieces_product_kernel(*refs):
    pieces, w_ref, out_ref = refs[:-2], refs[-2], refs[-1]
    total = None
    place = 0
    for piece in pieces:
        size = piece.shape[1]
        value = dot(piece[...], w_ref[:, place:place + size], NT)
        total = value if total is None else total + value
        place += size
    out_ref[...] = total


def pieces_product(pieces, w, tile=256):
    rows = pieces[0].shape[0]
    tile = min(tile, rows)
    return pl.pallas_call(
        pieces_product_kernel,
        grid=(rows // tile,),
        in_specs=[pl.BlockSpec((tile, p.shape[1]), lambda i: (i, 0)) for p in pieces]
        + [pl.BlockSpec(w.shape, lambda i: (0, 0))],
        out_specs=pl.BlockSpec((tile, w.shape[0]), lambda i: (i, 0)),
        out_shape=jax.ShapeDtypeStruct((rows, w.shape[0]), f32),
        compiler_params=pltpu.CompilerParams(vmem_limit_bytes=40 << 20),
        cost_estimate=pl.CostEstimate(
            flops=2 * rows * w.shape[0] * w.shape[1], bytes_accessed=12 << 20, transcendentals=0),
        name="pieces_product",
    )(*pieces, w)


epsilon = 1e-06


def contract_rows(left, right):
    return lax.dot_general(
        left, right, (((0,), (0,)), ((), ())), preferred_element_type=jnp.float32
    )


def contract_cols(left, right):
    return lax.dot_general(
        left, right, (((1,), (1,)), ((), ())), preferred_element_type=jnp.float32
    )


def norm_rows(rows, gain):
    scale = lax.rsqrt(jnp.mean(rows * rows, axis=-1, keepdims=True) + epsilon)
    return (scale, (rows * scale * gain).astype(jnp.bfloat16))


def norm_back(d_normed, rows, scale, gain):
    shaped = d_normed * gain
    cubed = scale * scale * scale
    return scale * shaped - rows * cubed * jnp.mean(shaped * rows, axis=-1, keepdims=True)


def along(array, shift, ring):
    return lax.ppermute(array, "narrow", [(i, (i + shift) % ring) for i in range(ring)])


def swap(array, ring):
    return lax.ppermute(array, "narrow", [(i, i ^ 1) for i in range(ring)])


def rows_of(array, index, count):
    return lax.dynamic_slice_in_dim(array, index * count, count, 0)


def on_device(
    wide,
    ring,
    layer_input,
    out_grad,
    norm_attn_gain,
    w_query,
    w_key,
    w_value,
    w_out,
    rel_table,
    layout_table,
    norm_ffn_gain,
    w_gate,
    w_up,
    down_projection_weight,
    page_lengths,
    key_mask,
    rel_bucket,
    layout_bucket,
):
    tokens, width = layer_input.shape
    head_cols = w_query.shape[1]
    heads = head_cols // DH
    units = w_gate.shape[1]
    padded = pad_lanes(units)
    part = width // wide
    me = lax.axis_index("narrow")
    my_wide = lax.axis_index("wide")
    gain_attn = norm_attn_gain.astype(f32)
    gain_ffn = norm_ffn_gain.astype(f32)
    resid = layer_input.astype(f32)

    scale_attn, normed_attn = norm_rows(resid, gain_attn)
    normed_attn_all = lax.all_gather(normed_attn, "narrow", axis=0, tiled=True)

    w_project = jnp.concatenate([w_query, w_key, w_value], axis=1)
    own_rows_gate = rows_of(w_gate, my_wide, part)
    own_rows_up = rows_of(w_up, my_wide, part)
    pairs = head_cols // 128
    own_rows_project = jnp.concatenate(
        [rows_of(w, my_wide, part)[:, p * 128 : (p + 1) * 128] for p in range(pairs) for w in (w_query, w_key, w_value)],
        axis=1)
    down_piece = lax.dynamic_slice_in_dim(down_projection_weight, my_wide * part, part, 1).T
    out_piece = lax.dynamic_slice_in_dim(w_out, my_wide * part, part, 1).T
    ffn_piece = jnp.concatenate(
        [jnp.pad(piece, ((0, 0), (0, padded - units))) for piece in (own_rows_gate, own_rows_up, down_piece)], axis=1)
    out_pieces = [out_piece] + [along(out_piece, d, ring) for d in range(1, ring)]
    words, codes = pair_bias(page_lengths, rel_bucket, layout_bucket, bias_words(rel_table, layout_table), key_mask)
    normed_attn_all, ffn_piece, words = lax.optimization_barrier((normed_attn_all, ffn_piece, words))
    ffn_pieces = [along(ffn_piece, d, ring) for d in range(2, ring, 2)]
    out_t = lax.all_gather(jnp.concatenate(out_pieces, axis=1), "wide", axis=0, tiled=True)

    projected = dot(normed_attn_all, w_project).astype(bf16)
    first_pair = list(attention_forward(page_lengths, projected, words, 0))
    first_pair[0], ffn_pieces, late_grad = lax.optimization_barrier((first_pair[0], ffn_pieces, out_grad))
    far_pieces = jnp.concatenate(ffn_pieces, axis=1)
    other_grad = swap(late_grad, ring)

    def to_owners(a):
        return [rows_of(a, me, tokens)] + [
            along(rows_of(a, (me + d) % ring, tokens), d, ring) for d in range(1, ring)]

    sent = [to_owners(first_pair[0])]
    results = [first_pair]
    if pairs > 1:
        late_projected, far_pieces = lax.optimization_barrier((projected, far_pieces))
        results += [list(attention_forward(page_lengths, late_projected, words, p)) for p in range(1, pairs)]
    far = lax.all_gather(far_pieces, "wide", axis=0, tiled=True)
    results[-1][0], other_grad, sent[0] = lax.optimization_barrier((results[-1][0], other_grad, sent[0]))
    attended = [r[0] for r in results]
    sent += [to_owners(a) for a in attended[1:]]
    mine = [pieces[d] for d in range(ring) for pieces in sent]
    attended_own = jnp.concatenate(mine, axis=1)
    middle = resid + contract_cols(attended_own, out_t)

    scale_ffn, normed_ffn = norm_rows(middle, gain_ffn)
    other_normed = swap(normed_ffn, ring)
    near = (w_gate.T, w_up.T, down_projection_weight)
    shards = ring // 2
    own = [feed_forward(normed_ffn, out_grad, units, near)]
    own, other_normed, late_project = lax.optimization_barrier((own, other_normed, own_rows_project))
    project_pieces = [along(late_project, d, ring) for d in range(1, ring)]
    other = [feed_forward(other_normed, other_grad, units, near)]
    other += [feed_forward(other_normed, other_grad, units, (far,), s) for s in range(shards - 1)]
    other_d_normed = sum(o[3] for o in other).astype(bf16)
    late_normed, other_d_normed = lax.optimization_barrier((normed_ffn, other_d_normed))
    other_d_normed = swap(other_d_normed, ring)
    own += [feed_forward(late_normed, out_grad, units, (far,), s) for s in range(shards - 1)]
    rights, groups = [], []
    for s in range(shards):
        for n in range(1, 4):
            rights += [own[s][n % 3], other[s][n % 3]]
            groups.append(n // 3)
    sums = weight_grads((normed_ffn, other_normed, out_grad, other_grad), rights, tuple(groups))
    sums, other_d_normed, project_pieces = lax.optimization_barrier((sums, other_d_normed, project_pieces))
    ffn_sums = lax.psum_scatter(sums, "wide", scatter_dimension=0, tiled=True)
    d_normed_ffn = sum(o[3] for o in own) + other_d_normed.astype(f32)
    d_middle = out_grad.astype(f32) + norm_back(d_normed_ffn, middle, scale_ffn, gain_ffn)
    d_middle_low = d_middle.astype(bf16)
    d_attended_own = dot(d_middle_low, out_t).astype(bf16)

    def block(d):
        return d_attended_own[:, d * head_cols : (d + 1) * head_cols]

    d_attended = jnp.zeros((ring * tokens, head_cols), bf16)
    d_attended = lax.dynamic_update_slice_in_dim(d_attended, block(0), me * tokens, 0)
    for d in range(1, ring):
        d_attended = lax.dynamic_update_slice_in_dim(
            d_attended, along(block(d), -d, ring), ((me + d) % ring) * tokens, 0)

    d_middle_late, attended_late, own_hidden, other_hidden = lax.optimization_barrier(
        (d_middle_low, attended_own, [o[0] for o in own], [o[0] for o in other]))
    wout_sums = contract_rows(d_middle_late, attended_late).astype(bf16)
    own_out, other_out = 0.0, 0.0
    for s in range(shards):
        if s == 0:
            down, dims = down_projection_weight, NN
        else:
            at = 3 * padded * (s - 1) + 2 * padded
            down, dims = far[:, at : at + units], NT
        own_out = own_out + dot(own_hidden[s], down, dims)
        other_out = other_out + dot(other_hidden[s], down, dims)
    own_out = own_out + middle
    project_pieces = jnp.concatenate([own_rows_project] + project_pieces, axis=1)
    wout_sums, d_attended, own_out, other_out, project_pieces = lax.optimization_barrier(
        (wout_sums, d_attended, own_out, other_out.astype(bf16), project_pieces))
    other_out = swap(other_out, ring)

    d_scores, leaving, mine, products = [], [], [], []
    for p, (att, rinv, exps) in enumerate(results):
        d_pair, scores = attention_backward(page_lengths, projected, exps, d_attended, att, rinv, p)
        if p == 0:
            d_pair, other_out = lax.optimization_barrier((d_pair, other_out))
        else:
            d_pair, mine[-1] = lax.optimization_barrier((d_pair, mine[-1]))
        sent = [rows_of(d_pair, (me + d) % ring, tokens) for d in range(ring)]
        sent, d_pair, d_attended = lax.optimization_barrier((sent, d_pair, d_attended))
        mine.append(sent[:1] + [along(sent[d], d, ring) for d in range(1, ring)])
        d_scores.append(scores)
        products.append(contract_rows(normed_attn_all, d_pair).astype(bf16))
    w_project_all = lax.all_gather(project_pieces, "wide", axis=0, tiled=True)
    layer_out = (own_out + other_out.astype(f32)).astype(bf16)
    last_sums = jnp.concatenate(products + [wout_sums], axis=1)
    last_sums = lax.psum_scatter(last_sums, "wide", scatter_dimension=0, tiled=True)

    totals = table_grads(page_lengths, d_scores, codes)
    far_sums = [along(ffn_sums[:, 3 * padded * s : 3 * padded * (s + 1)], -2 * s, ring) for s in range(1, shards)]
    totals, mine, far_sums = lax.optimization_barrier((totals, mine, far_sums))
    grad_relative = bucket_sums(totals, heads, 4, 2)
    grad_layout = bucket_sums(totals, heads, 0, 4)
    tables = jnp.concatenate(
        [grad_relative.reshape(wide, -1, heads), grad_layout.reshape(wide, -1, heads)], axis=1)
    n_rel = grad_relative.shape[0] // wide
    reach = wide // 2
    while reach >= 1:
        bit = (my_wide // reach) % 2
        keep = lax.dynamic_slice_in_dim(tables, bit * reach, reach, 0)
        give = lax.dynamic_slice_in_dim(tables, (1 - bit) * reach, reach, 0)
        tables = keep + lax.ppermute(give, "wide", [(i, i ^ reach) for i in range(wide)])
        if reach == wide // 2:
            tables, last_sums = lax.optimization_barrier((tables, last_sums))
        reach //= 2
    sum_project = last_sums[:, : 3 * head_cols].astype(f32)
    wout_sums = last_sums[:, 3 * head_cols :]
    far_wout = [along(wout_sums[:, d * head_cols : (d + 1) * head_cols], -d, ring) for d in range(1, ring)]
    sum_tables = tables[0]
    d_normed_attn = pieces_product([pieces[d] for d in range(ring) for pieces in mine], w_project_all)
    in_grad = d_middle + norm_back(d_normed_attn, resid, scale_attn, gain_attn)

    def stripe(shard, n):
        at = padded * (3 * shard + n)
        return ffn_sums[:, at : at + units]

    sum_gate, sum_up, sum_down = [stripe(0, n).astype(f32) for n in range(3)]
    for s in range(1, shards):
        block = far_sums[s - 1].astype(f32)
        sum_gate += block[:, :units]
        sum_up += block[:, padded : padded + units]
        sum_down += block[:, 2 * padded : 2 * padded + units]
    sum_wout = wout_sums[:, :head_cols].astype(f32) + sum(w.astype(f32) for w in far_wout)

    gain_terms = jnp.stack(
        [
            jnp.sum(own_rows_project.astype(f32) * sum_project, axis=1),
            jnp.sum(own_rows_gate.astype(f32) * sum_gate + own_rows_up.astype(f32) * sum_up, axis=1),
        ]
    )
    share = part // ring

    def gain_share(index):
        return lax.dynamic_slice_in_dim(gain_terms, index * share, share, 1)

    gain_sum = gain_share(me)
    for d in range(1, ring):
        gain_sum = gain_sum + along(gain_share((me + d) % ring), d, ring)
    place = my_wide * part + me * share
    gains = lax.dynamic_slice_in_dim(jnp.stack([gain_attn, gain_ffn]), place, share, 1)
    gain_grads = gain_sum / gains

    def whole_project(n):
        return jnp.concatenate([sum_project[:, (3 * p + n) * 128 : (3 * p + n + 1) * 128] for p in range(pairs)], axis=1)

    return (
        layer_out,
        in_grad,
        gain_grads[0],
        whole_project(0),
        whole_project(1),
        whole_project(2),
        sum_wout.T,
        sum_tables[:n_rel],
        sum_tables[n_rel:],
        gain_grads[1],
        sum_gate,
        sum_up,
        sum_down.T,
    )


def solution(mesh):
    placed = (
        P(("wide", "narrow"), None),
        P(("wide", "narrow"), None),
        P(),
        P(None, "narrow"),
        P(None, "narrow"),
        P(None, "narrow"),
        P("narrow", None),
        P(None, "narrow"),
        P(None, "narrow"),
        P(),
        P(None, "narrow"),
        P(None, "narrow"),
        P("narrow", None),
        P("wide", None),
        P("wide"),
        P("wide", None),
        P("wide", None),
    )
    return jax.shard_map(
        functools.partial(on_device, mesh.shape["wide"], mesh.shape["narrow"]),
        mesh=mesh,
        in_specs=placed,
        out_specs=(
            P(("wide", "narrow"), None),
            P(("wide", "narrow"), None),
            P(("wide", "narrow")),
            P("wide", "narrow"),
            P("wide", "narrow"),
            P("wide", "narrow"),
            P("narrow", "wide"),
            P("wide", "narrow"),
            P("wide", "narrow"),
            P(("wide", "narrow")),
            P("wide", "narrow"),
            P("wide", "narrow"),
            P("narrow", "wide"),
        ),
        check_vma=False,
    )
```

```python
import functools
import jax
import jax.numpy as jnp
from jax import lax
from jax.experimental import pallas as pl
from jax.experimental.pallas import tpu as pltpu
from jax.sharding import PartitionSpec as P

DH = 64
BIAS_SCALE = 4096.0
LOG2E = 1.4426950408889634
f32 = jnp.float32
bf16 = jnp.bfloat16
NT = (((1,), (1,)), ((), ()))
NN = (((1,), (0,)), ((), ()))


def dot(a, b, dims=NN):
    return lax.dot_general(a, b, dims, preferred_element_type=f32)


def key_window(len_ref, first, last, count, width):
    ends = []
    total = 0
    for p in range(len_ref.shape[1]):
        total = total + len_ref[0, p]
        ends.append(total)
    start = 0
    stop = count
    for e in ends:
        start = jnp.where(e <= first, e, start)
    for e in reversed(ends):
        stop = jnp.where(e > last, e, stop)
    base = (start // 128) * 128
    steps = (stop - base + width - 1) // width
    base = jnp.minimum(base, count - steps * width)
    return ends, base, steps


def for_chunks(base, steps, width, group, body):
    def many(j, carry):
        body(pl.multiple_of(base + j * (group * width), 128), group * width)
        return carry

    def single(j, carry):
        body(pl.multiple_of(base + j * width, 128), width)
        return carry

    if group > 1:
        lax.fori_loop(0, steps // group, many, 0)
    lax.fori_loop((steps // group) * group if group > 1 else 0, steps, single, 0)


def own_half(shape, head):
    lane = lax.broadcasted_iota(jnp.int32, shape, len(shape) - 1)
    return (lane < DH) if head % 2 == 0 else (lane >= DH)


def fill_values(vext, v_ref, heads):
    for h in range(heads):
        vp = v_ref[:, (h // 2) * 128:(h // 2 + 1) * 128]
        vext[h] = jnp.where(own_half(vp.shape, h), vp, jnp.ones_like(vp))


def half_norms(rows):
    lane = lax.broadcasted_iota(jnp.int32, (128, 128), 0)
    column = lax.broadcasted_iota(jnp.int32, (128, 128), 1)
    same = ((lane < DH) == (column < DH)).astype(bf16)
    squares = (rows.astype(f32) * rows.astype(f32)).astype(bf16)
    return jnp.max(dot(squares, same)) * f32(1.02)


HIDDEN_PAIR = -(1 << 31)


def pair_bias_kernel(len_ref, rel_ref, lay_ref, tab_ref, kmask_ref, word_ref, code_ref, colcode, *, width, group):
    tq, count = rel_ref.shape
    pairs = word_ref.shape[0]
    i = pl.program_id(0)
    t0 = i * tq
    ends, base, steps = key_window(len_ref, t0, t0 + tq - 1, count, width)

    @pl.when(i == 0)
    def _():
        pos = lax.broadcasted_iota(jnp.int32, (8, count), 1)
        page = jnp.zeros((8, count), jnp.int32)
        for e in ends:
            page = page + (pos >= e).astype(jnp.int32)
        colcode[...] = jnp.where(kmask_ref[...] == 1, page, -1)

    rowpos = lax.broadcasted_iota(jnp.int32, (tq, 128), 0) + t0
    rowpage = jnp.zeros((tq, 128), jnp.int32)
    for e in ends:
        rowpage = rowpage + (rowpos >= e).astype(jnp.int32)
    lanes = lax.broadcasted_iota(jnp.int32, (tq, 128), 1)
    tabs = [jnp.broadcast_to(tab_ref[n:n + 1, :], (tq, 128)) for n in range(2 * pairs)]

    def chunk(c0, size):
        for half in range(size // 128):
            cc = pl.multiple_of(c0 + half * 128, 128)
            here = pl.ds(cc, 128)
            rel = rel_ref[:, here]
            lay = lay_ref[:, here]
            code_ref[:, here] = (rel + lay * 32).astype(jnp.int16)
            col = jnp.broadcast_to(colcode[0:1, here], (tq, 128))
            seen = (rowpage == col) | (rowpos == lanes + cc)
            for p in range(pairs):
                word = (jnp.take_along_axis(tabs[2 * p], rel, axis=1, mode="promise_in_bounds")
                        + jnp.take_along_axis(tabs[2 * p + 1], lay, axis=1, mode="promise_in_bounds"))
                word_ref[p, :, here] = jnp.where(seen, word, HIDDEN_PAIR)

    for_chunks(base, steps, width, group, chunk)


def pair_bias(page_lengths, rel, lay, tab, kmask, tq=256, width=256, group=2):
    count = rel.shape[0]
    pairs = tab.shape[0] // 2
    tile = lambda i: (i, 0)
    return pl.pallas_call(
        functools.partial(pair_bias_kernel, width=width, group=group),
        grid=(count // tq,),
        in_specs=[
            pl.BlockSpec(memory_space=pltpu.SMEM),
            pl.BlockSpec((tq, count), tile),
            pl.BlockSpec((tq, count), tile),
            pl.BlockSpec(tab.shape, lambda i: (0, 0)),
            pl.BlockSpec((1, count), lambda i: (0, 0)),
        ],
        out_specs=[
            pl.BlockSpec((pairs, tq, count), lambda i: (0, i, 0)),
            pl.BlockSpec((tq, count), tile),
        ],
        out_shape=[
            jax.ShapeDtypeStruct((pairs, count, count), jnp.int32),
            jax.ShapeDtypeStruct((count, count), jnp.int16),
        ],
        scratch_shapes=[pltpu.VMEM((8, count), jnp.int32)],
        compiler_params=pltpu.CompilerParams(vmem_limit_bytes=56 << 20),
        cost_estimate=pl.CostEstimate(flops=count * count * 1024, bytes_accessed=120 << 20, transcendentals=0),
        name="pair_bias",
    )(page_lengths, rel, lay, tab, kmask.reshape(1, count))


def forward_kernel(len_ref, q_ref, k_ref, v_ref, word_ref, att_ref, rinv_ref, e_ref,
                   s_scr, m_scr, acc_scr, vext, knorm, *, width, group):
    tq, count = word_ref.shape[1:]
    heads, pairs = 2, 1
    i = pl.program_id(0)
    t0 = i * tq
    ends, base, steps = key_window(len_ref, t0, t0 + tq - 1, count, width)

    @pl.when(i == 0)
    def _():
        fill_values(vext, v_ref, heads)
        for p in range(pairs):
            knorm[p] = half_norms(k_ref[:, p * 128:(p + 1) * 128])

    scaled = []
    largest = f32(0.0)
    for h in range(heads):
        qp = q_ref[:, (h // 2) * 128:(h // 2 + 1) * 128]
        scaled.append(jnp.where(own_half(qp.shape, h), qp * bf16(BIAS_SCALE), jnp.zeros_like(qp)))
        if h % 2 == 0:
            largest = jnp.maximum(largest, half_norms(qp) * knorm[h // 2])
    def scores(c0, width, use):
        raw = [dot(scaled[h], k_ref[pl.ds(c0, width), (h // 2) * 128:(h // 2 + 1) * 128], NT)
               for h in range(heads)]
        for half in range(width // 128):
            cc = pl.multiple_of(c0 + half * 128, 128)
            word = word_ref[0, :, pl.ds(cc, 128)]
            hidden = word == HIDDEN_PAIR
            parts = ((word & 0xFFFF).astype(f32), (word >> 16).astype(f32))
            for h in range(heads):
                bias = jnp.where(hidden, f32(-1e30), parts[h])
                use(h, half, cc, raw[h][:, half * 128:(half + 1) * 128] + bias)

    for h in range(heads):
        acc_scr[h] = jnp.zeros((tq, 128), f32)
    bounded = jnp.sqrt(largest) + 8.0 <= 60.0

    @pl.when(bounded)
    def _():
        def chunk(c0, size):
            pieces = {}

            def use(h, half, cc, s):
                e = jnp.exp2(s * f32(LOG2E / BIAS_SCALE)).astype(bf16)
                e_ref[h, :, pl.ds(cc, 128)] = e
                pieces[h, half] = e

            scores(c0, size, use)
            for h in range(heads):
                e = jnp.concatenate([pieces[h, half] for half in range(size // 128)], axis=1)
                acc_scr[h] += dot(e, vext[h, pl.ds(c0, size), :])

        for_chunks(base, steps, width, group, chunk)

    @pl.when(jnp.logical_not(bounded))
    def _():
        for h in range(heads):
            m_scr[h] = jnp.full((tq, 128), -3e38, f32)

        def first(j, carry):
            def use(h, half, cc, s):
                s_scr[h, :, pl.ds(cc, 128)] = s
                m_scr[h] = jnp.maximum(m_scr[h], s)

            scores(pl.multiple_of(base + j * width, 128), width, use)
            return carry

        lax.fori_loop(0, steps, first, 0)
        for h in range(heads):
            top = jnp.max(m_scr[h], axis=1, keepdims=True)

            def second(j, carry):
                c0 = pl.multiple_of(base + j * width, 128)
                e = jnp.exp2((s_scr[h, :, pl.ds(c0, width)] - top) * f32(LOG2E / BIAS_SCALE)).astype(bf16)
                e_ref[h, :, pl.ds(c0, width)] = e
                acc_scr[h] += dot(e, vext[h, pl.ds(c0, width), :])
                return carry

            lax.fori_loop(0, steps, second, 0)

    low = own_half((tq, 128), 0)
    for p in range(pairs):
        even, odd = acc_scr[2 * p], acc_scr[2 * p + 1]
        rinv = 1.0 / pltpu.roll(jnp.where(low, odd, even), DH, 1)
        att_ref[:, p * 128:(p + 1) * 128] = (jnp.where(low, even, odd) * rinv).astype(bf16)
        rinv_ref[:, p * 128:(p + 1) * 128] = rinv


def attention_forward(page_lengths, proj, words, pair, tq=256, width=256, group=2):
    count = proj.shape[0]
    pairs = proj.shape[1] // (3 * 128)
    tile = lambda i: (i, 0)
    return pl.pallas_call(
        functools.partial(forward_kernel, width=width, group=group),
        grid=(count // tq,),
        in_specs=[
            pl.BlockSpec(memory_space=pltpu.SMEM),
            pl.BlockSpec((tq, 128), lambda i: (i, pair)),
            pl.BlockSpec((count, 128), lambda i: (0, pairs + pair)),
            pl.BlockSpec((count, 128), lambda i: (0, 2 * pairs + pair)),
            pl.BlockSpec((1, tq, count), lambda i: (pair, i, 0)),
        ],
        out_specs=[
            pl.BlockSpec((tq, 128), tile),
            pl.BlockSpec((tq, 128), tile),
            pl.BlockSpec((2, tq, count), lambda i: (0, i, 0)),
        ],
        out_shape=[
            jax.ShapeDtypeStruct((count, 128), bf16),
            jax.ShapeDtypeStruct((count, 128), f32),
            jax.ShapeDtypeStruct((2, count, count), bf16),
        ],
        scratch_shapes=[
            pltpu.VMEM((2, tq, count), f32),
            pltpu.VMEM((2, tq, 128), f32),
            pltpu.VMEM((2, tq, 128), f32),
            pltpu.VMEM((2, count, 128), bf16),
            pltpu.SMEM((1,), f32),
        ],
        compiler_params=pltpu.CompilerParams(vmem_limit_bytes=56 << 20),
        cost_estimate=pl.CostEstimate(
            flops=count * count * 512, bytes_accessed=80 << 20, transcendentals=count * count),
        name="attention_forward",
    )(page_lengths, proj, proj, proj, words)


def bias_words(rel_table, layout_table):
    def pack(table):
        whole = jnp.round(table.astype(f32) * BIAS_SCALE).astype(jnp.int32)
        low = jnp.clip(whole[:, 0::2] + 16384, 0, 32767)
        high = jnp.clip(whole[:, 1::2], -16383, 16383)
        words = (high * 65536 + low).T
        return jnp.pad(words, ((0, 0), (0, 128 - words.shape[1])))
    both = jnp.stack([pack(rel_table), pack(layout_table)], axis=1)
    return both.reshape(-1, 128)


def signs(code, shift, bits):
    return [jnp.where((code & jnp.int16(1 << (shift + b))) == 0, bf16(1.0), bf16(-1.0))
            for b in range(bits)]


def walsh(sign_list):
    out = [None]
    for s in sign_list:
        out = out + [s if o is None else o * s for o in out]
    return out


def backward_kernel(len_ref, q_ref, k_ref, v_ref, da_ref, *refs, width, heads, group):
    tq = q_ref.shape[0]
    count = k_ref.shape[0]
    pairs = heads // 2
    e_refs, att_refs, rinv_refs = refs[:pairs], refs[pairs:2 * pairs], refs[2 * pairs:3 * pairs]
    dp_ref, ds_ref = refs[3 * pairs:3 * pairs + 2]
    vext, lhs_scr, dat_scr, qt_scr, dq_scr, dkt, dvt = refs[3 * pairs + 2:]
    i = pl.program_id(0)
    t0 = i * tq
    ends, base, steps = key_window(len_ref, t0, t0 + tq - 1, count, width)

    @pl.when(i == 0)
    def _():
        fill_values(vext, v_ref, heads)
        dkt[...] = jnp.zeros_like(dkt)
        dvt[...] = jnp.zeros_like(dvt)

    low = own_half((tq, 128), 0)
    lane = lax.broadcasted_iota(jnp.int32, (tq, 128), 1)
    first_part = (lane & 32) == 0
    for p in range(pairs):
        cols = slice(p * 128, (p + 1) * 128)
        da = (da_ref[:, cols].astype(f32) * rinv_refs[p][...]).astype(bf16)
        daf = da.astype(f32)
        prod = daf * att_refs[p][...].astype(f32)
        for r in range(2):
            own = low if r == 0 else jnp.logical_not(low)
            delta = jnp.sum(jnp.where(own, prod, 0.0), axis=1, keepdims=True) * f32(-1.0 / 32)
            high = delta.astype(bf16).astype(f32)
            rest = delta - high
            lhs_scr[2 * p + r] = jnp.where(own, daf, jnp.where(first_part, high, rest)).astype(bf16)
        dat_scr[p] = daf.T.astype(bf16)
        qt_scr[p] = q_ref[:, cols].astype(f32).T.astype(bf16)
        dq_scr[p] = jnp.zeros((tq, 128), f32)

    def chunk(c0, size):
        here = pl.ds(c0, size)
        for p in range(pairs):
            kp = k_ref[here, p * 128:(p + 1) * 128]
            dqs = []
            for r in range(2):
                h = 2 * p + r
                rows = slice(r * DH, (r + 1) * DH)
                e = e_refs[p][r, :, here]
                d = dot(lhs_scr[h], vext[h, here, :], NT)
                ds = (e.astype(f32) * d).astype(bf16)
                ds_ref[h, :, here] = ds
                dqs.append(dot(ds, kp))
                dkt[p, rows, here] += dot(qt_scr[p, rows, :], ds)
                dvt[p, rows, here] += dot(dat_scr[p, rows, :], e)
            dq_scr[p] += jnp.where(low, dqs[0], dqs[1])

    for_chunks(base, steps, width, group, chunk)
    for p in range(pairs):
        dp_ref[pl.ds(pl.multiple_of(t0, tq), tq), p * 128:(p + 1) * 128] = dq_scr[p].astype(bf16)

    @pl.when(i == pl.num_programs(0) - 1)
    def _():
        for n, grads in enumerate((dkt, dvt)):
            for p in range(pairs):
                at = ((n + 1) * pairs + p) * 128
                for c in range(0, count, 256):
                    dp_ref[c:c + 256, at:at + 128] = grads[p, :, c:c + 256].T.astype(bf16)


def attention_backward(page_lengths, proj, exps, d_att, att, rinv, pair, tq=256, width=256, group=2):
    count = proj.shape[0]
    pairs = proj.shape[1] // (3 * 128)
    tile = lambda i: (i, 0)
    return pl.pallas_call(
        functools.partial(backward_kernel, width=width, heads=2, group=group),
        grid=(count // tq,),
        in_specs=[
            pl.BlockSpec(memory_space=pltpu.SMEM),
            pl.BlockSpec((tq, 128), lambda i: (i, pair)),
            pl.BlockSpec((count, 128), lambda i: (0, pairs + pair)),
            pl.BlockSpec((count, 128), lambda i: (0, 2 * pairs + pair)),
            pl.BlockSpec((tq, 128), lambda i: (i, pair)),
            pl.BlockSpec((2, tq, count), lambda i: (0, i, 0)),
            pl.BlockSpec((tq, 128), tile),
            pl.BlockSpec((tq, 128), tile),
        ],
        out_specs=[
            pl.BlockSpec((count, 384), lambda i: (0, 0)),
            pl.BlockSpec((2, tq, count), lambda i: (0, i, 0)),
        ],
        out_shape=[
            jax.ShapeDtypeStruct((count, 384), bf16),
            jax.ShapeDtypeStruct((2, count, count), bf16),
        ],
        scratch_shapes=[
            pltpu.VMEM((2, count, 128), bf16),
            pltpu.VMEM((2, tq, 128), bf16),
            pltpu.VMEM((1, 128, tq), bf16),
            pltpu.VMEM((1, 128, tq), bf16),
            pltpu.VMEM((1, tq, 128), f32),
            pltpu.VMEM((1, 128, count), f32),
            pltpu.VMEM((1, 128, count), f32),
        ],
        compiler_params=pltpu.CompilerParams(vmem_limit_bytes=56 << 20),
        cost_estimate=pl.CostEstimate(flops=count * count * 1024, bytes_accessed=80 << 20, transcendentals=0),
        name="attention_backward",
    )(page_lengths, proj, proj, proj, d_att, exps, att, rinv)


def parity_sign(v):
    v = v ^ (v >> 2)
    v = v ^ (v >> 1)
    return (1 - 2 * (v & 1)).astype(f32)


def bucket_totals(raw, first, heads):
    rows, cols = raw.shape
    low = rows // (16 * heads)
    r = lax.broadcasted_iota(jnp.int32, raw.shape, 0)
    c = lax.broadcasted_iota(jnp.int32, raw.shape, 1)
    kept = jnp.where((r & 15) == (c & 15), raw, 0.0)
    c = lax.broadcasted_iota(jnp.int32, (cols, 128), 0)
    y = lax.broadcasted_iota(jnp.int32, (cols, 128), 1)
    right = jnp.where(y < cols // 16, parity_sign((c >> 4) & y), 0.0)
    r = lax.broadcasted_iota(jnp.int32, (low * heads, rows), 1) >> 4
    x = lax.broadcasted_iota(jnp.int32, (low * heads, rows), 0)
    function = (r // heads + first) & (low - 1)
    left = jnp.where(r % heads == x % heads, parity_sign(function & (x // heads)), 0.0)
    exact = lax.Precision.HIGHEST
    half = lax.dot_general(kept, right, NN, precision=exact, preferred_element_type=f32)
    out = lax.dot_general(left, half, NN, precision=exact, preferred_element_type=f32)
    return out * f32(1.0 / (low * (cols // 16)))


def table_kernel(len_ref, code_ref, *refs, width, parts, pairs):
    ds_refs, (out_ref, hl_ref, hr_ref), bufs = refs[:pairs], refs[pairs:pairs + 3], refs[pairs + 3:]
    heads = 2 * pairs
    tq, count = code_ref.shape
    i = pl.program_id(0)
    t0 = i * tq
    ends, base, steps = key_window(len_ref, t0, t0 + tq - 1, count, width)

    @pl.when(i == 0)
    def _():
        hl_ref[...] = jnp.zeros_like(hl_ref)
        hr_ref[...] = jnp.zeros_like(hr_ref)

    one = jnp.ones((16, width), bf16)

    def chunk(j, carry):
        c0 = pl.multiple_of(base + j * width, 128)
        here = pl.ds(c0, width)
        blocks = tq // 16 // parts
        for part in range(parts):
            left, blay, brel = bufs[3 * part:3 * part + 3]
            for b in range(blocks):
                at = 16 * (part * blocks + b)
                rows = slice(at, at + 16)
                span = slice(b * width, (b + 1) * width)
                code = code_ref[rows, here]
                rel_signs = signs(code, 0, 5)
                lay_signs = signs(code, 5, 6)
                left_lay = walsh(lay_signs[:2])[1:]
                for h in range(heads):
                    ds = ds_refs[h // 2][h % 2, rows, here]
                    for a, func in enumerate(left_lay + [None, rel_signs[0]]):
                        place = 16 * (a * heads + h)
                        left[place:place + 16, span] = ds if func is None else ds * func
                for n, func in enumerate(walsh(lay_signs[2:])):
                    blay[16 * n:16 * (n + 1), span] = one if func is None else func
                for n, func in enumerate(walsh(rel_signs[1:])):
                    brel[16 * n:16 * (n + 1), span] = one if func is None else func
            hl_ref[...] += dot(left[:64 * heads, :], blay[...], NT)
            hr_ref[...] += dot(left[48 * heads:80 * heads, :], brel[...], NT)
        return carry

    lax.fori_loop(0, steps, chunk, 0)

    @pl.when(i == pl.num_programs(0) - 1)
    def _():
        out_ref[...] = jnp.zeros_like(out_ref)
        out_ref[:4 * heads, :] = bucket_totals(hl_ref[...], 1, heads)
        out_ref[4 * heads:6 * heads, :] = bucket_totals(hr_ref[...], 0, heads)


def table_grads(page_lengths, ds, code, tq=256, width=256, parts=2):
    heads, count = 2 * len(ds), code.shape[0]
    deep = tq // 16 * width // parts
    fixed = lambda i: (0, 0)
    return pl.pallas_call(
        functools.partial(table_kernel, width=width, parts=parts, pairs=len(ds)),
        grid=(count // tq,),
        in_specs=[
            pl.BlockSpec(memory_space=pltpu.SMEM),
            pl.BlockSpec((tq, count), lambda i: (i, 0)),
        ] + [pl.BlockSpec((2, tq, count), lambda i: (0, i, 0))] * len(ds),
        out_specs=pl.BlockSpec((8 * heads, 128), fixed),
        out_shape=jax.ShapeDtypeStruct((8 * heads, 128), f32),
        scratch_shapes=[pltpu.VMEM((64 * heads, 256), f32), pltpu.VMEM((32 * heads, 256), f32)] + [
            pltpu.VMEM((80 * heads, deep), bf16),
            pltpu.VMEM((256, deep), bf16),
            pltpu.VMEM((256, deep), bf16),
        ] * parts,
        compiler_params=pltpu.CompilerParams(vmem_limit_bytes=56 << 20),
        cost_estimate=pl.CostEstimate(
            flops=heads * count * count * 512, bytes_accessed=150 << 20, transcendentals=0),
        name="table_grads",
    )(page_lengths, code, *ds)


def bucket_sums(totals, heads, first, low):
    rows = totals[first * heads:(first + low) * heads, :16].reshape(low, heads, 16)
    return jnp.transpose(rows, (2, 0, 1)).reshape(16 * low, heads)


TANH_SLOPE = 0.7978845608028654
CUBE = 0.044715


def feed_forward_kernel(far, x_ref, g_ref, *refs):
    weights, (hidden_ref, d_gate_ref, d_up_ref, dn_ref) = refs[:-4], refs[-4:]
    units = hidden_ref.shape[1]
    if far:
        step = pad_lanes(units)
        gate_weight, up_weight, down = [weights[0][:, n * step:n * step + units] for n in range(3)]
        ahead, back = NN, NT
    else:
        gate_weight, up_weight, down = [w[...] for w in weights]
        ahead, back = NT, NN
    x = x_ref[...]
    d_hidden = dot(g_ref[...], down, ahead)
    gate = dot(x, gate_weight, ahead)
    up = dot(x, up_weight, ahead)
    square = gate * gate
    t = jnp.tanh(TANH_SLOPE * gate * (1.0 + CUBE * square))
    half = 0.5 + 0.5 * t
    gelu = gate * half
    slope = half + (0.5 * TANH_SLOPE) * gate * (1.0 - t * t) * (1.0 + (3 * CUBE) * square)
    d_gate = (d_hidden * up * slope).astype(bf16)
    d_up = (d_hidden * gelu).astype(bf16)
    hidden_ref[...] = (gelu * up).astype(bf16)
    d_gate_ref[...] = d_gate
    d_up_ref[...] = d_up
    dn_ref[...] = dot(d_gate, gate_weight, back) + dot(d_up, up_weight, back)


def feed_forward(x, g, units, weights, shard=None, tile=256):
    tokens, features = x.shape
    tile = min(tile, tokens)
    rows = lambda n: pl.BlockSpec((tile, n), lambda i: (i, 0))
    if shard is None:
        weight_specs = [pl.BlockSpec(w.shape, lambda i: (0, 0)) for w in weights]
    else:
        weight_specs = [pl.BlockSpec((features, 3 * pad_lanes(units)), lambda i: (0, shard))]
    return pl.pallas_call(
        functools.partial(feed_forward_kernel, shard is not None),
        grid=(tokens // tile,),
        in_specs=[rows(features), rows(features)] + weight_specs,
        out_specs=[rows(units)] * 3 + [rows(features)],
        out_shape=[jax.ShapeDtypeStruct((tokens, units), bf16)] * 3
        + [jax.ShapeDtypeStruct((tokens, features), f32)],
        compiler_params=pltpu.CompilerParams(vmem_limit_bytes=56 << 20),
        cost_estimate=pl.CostEstimate(
            flops=10 * tokens * features * units, bytes_accessed=10 << 20, transcendentals=tokens * units),
        name="feed_forward",
    )(x, g, *weights)


def pad_lanes(n):
    return (n + 127) // 128 * 128


def weight_grads_kernel(n_left, n_right, *refs):
    lefts = refs[:2 * n_left]
    rights = refs[2 * n_left:-1]
    out_ref = refs[-1]
    rows_in = (((0,), (0,)), ((), ()))
    place = 0
    for n, left in enumerate(n_right):
        a, b = rights[2 * n], rights[2 * n + 1]
        size = a.shape[1]
        value = dot(lefts[2 * left][...], a[...], rows_in) + dot(lefts[2 * left + 1][...], b[...], rows_in)
        out_ref[:, place:place + size] = value.astype(bf16)
        if pad_lanes(size) > size:
            out_ref[:, place + size:place + pad_lanes(size)] = jnp.zeros(
                (out_ref.shape[0], pad_lanes(size) - size), bf16)
        place += pad_lanes(size)


def weight_grads(lefts, rights, groups, tile=256):
    features = lefts[0].shape[1]
    columns = sum(pad_lanes(r.shape[1]) for r in rights[::2])
    column = lambda a: pl.BlockSpec((a.shape[0], tile), lambda i: (0, i))
    whole = lambda a: pl.BlockSpec(a.shape, lambda i: (0, 0))
    return pl.pallas_call(
        functools.partial(weight_grads_kernel, len(lefts) // 2, groups),
        grid=(features // tile,),
        in_specs=[column(a) for a in lefts] + [whole(a) for a in rights],
        out_specs=pl.BlockSpec((tile, columns), lambda i: (i, 0)),
        out_shape=jax.ShapeDtypeStruct((features, columns), bf16),
        compiler_params=pltpu.CompilerParams(vmem_limit_bytes=56 << 20),
        cost_estimate=pl.CostEstimate(
            flops=4 * features * columns * lefts[0].shape[0], bytes_accessed=26 << 20, transcendentals=0),
        name="weight_grads",
    )(*lefts, *rights)


def pieces_product_kernel(*refs):
    pieces, w_ref, out_ref = refs[:-2], refs[-2], refs[-1]
    total = None
    place = 0
    for piece in pieces:
        size = piece.shape[1]
        value = dot(piece[...], w_ref[:, place:place + size], NT)
        total = value if total is None else total + value
        place += size
    out_ref[...] = total


def pieces_product(pieces, w, tile=256):
    rows = pieces[0].shape[0]
    tile = min(tile, rows)
    return pl.pallas_call(
        pieces_product_kernel,
        grid=(rows // tile,),
        in_specs=[pl.BlockSpec((tile, p.shape[1]), lambda i: (i, 0)) for p in pieces]
        + [pl.BlockSpec(w.shape, lambda i: (0, 0))],
        out_specs=pl.BlockSpec((tile, w.shape[0]), lambda i: (i, 0)),
        out_shape=jax.ShapeDtypeStruct((rows, w.shape[0]), f32),
        compiler_params=pltpu.CompilerParams(vmem_limit_bytes=40 << 20),
        cost_estimate=pl.CostEstimate(
            flops=2 * rows * w.shape[0] * w.shape[1], bytes_accessed=12 << 20, transcendentals=0),
        name="pieces_product",
    )(*pieces, w)


epsilon = 1e-06


def contract_rows(left, right):
    return lax.dot_general(
        left, right, (((0,), (0,)), ((), ())), preferred_element_type=jnp.float32
    )


def contract_cols(left, right):
    return lax.dot_general(
        left, right, (((1,), (1,)), ((), ())), preferred_element_type=jnp.float32
    )


def norm_rows(rows, gain):
    scale = lax.rsqrt(jnp.mean(rows * rows, axis=-1, keepdims=True) + epsilon)
    return (scale, (rows * scale * gain).astype(jnp.bfloat16))


def norm_back(d_normed, rows, scale, gain):
    shaped = d_normed * gain
    cubed = scale * scale * scale
    return scale * shaped - rows * cubed * jnp.mean(shaped * rows, axis=-1, keepdims=True)


def along(array, shift, ring):
    return lax.ppermute(array, "narrow", [(i, (i + shift) % ring) for i in range(ring)])


def swap(array, ring):
    return lax.ppermute(array, "narrow", [(i, i ^ 1) for i in range(ring)])


def rows_of(array, index, count):
    return lax.dynamic_slice_in_dim(array, index * count, count, 0)


def on_device(
    wide,
    ring,
    layer_input,
    out_grad,
    norm_attn_gain,
    w_query,
    w_key,
    w_value,
    w_out,
    rel_table,
    layout_table,
    norm_ffn_gain,
    w_gate,
    w_up,
    down_projection_weight,
    page_lengths,
    key_mask,
    rel_bucket,
    layout_bucket,
):
    tokens, width = layer_input.shape
    head_cols = w_query.shape[1]
    heads = head_cols // DH
    units = w_gate.shape[1]
    padded = pad_lanes(units)
    part = width // wide
    me = lax.axis_index("narrow")
    my_wide = lax.axis_index("wide")
    gain_attn = norm_attn_gain.astype(f32)
    gain_ffn = norm_ffn_gain.astype(f32)
    resid = layer_input.astype(f32)

    scale_attn, normed_attn = norm_rows(resid, gain_attn)
    normed_attn_all = lax.all_gather(normed_attn, "narrow", axis=0, tiled=True)

    w_project = jnp.concatenate([w_query, w_key, w_value], axis=1)
    own_rows_gate = rows_of(w_gate, my_wide, part)
    own_rows_up = rows_of(w_up, my_wide, part)
    pairs = head_cols // 128
    own_rows_project = jnp.concatenate(
        [rows_of(w, my_wide, part)[:, p * 128 : (p + 1) * 128] for p in range(pairs) for w in (w_query, w_key, w_value)],
        axis=1)
    down_piece = lax.dynamic_slice_in_dim(down_projection_weight, my_wide * part, part, 1).T
    out_piece = lax.dynamic_slice_in_dim(w_out, my_wide * part, part, 1).T
    ffn_piece = jnp.concatenate(
        [jnp.pad(piece, ((0, 0), (0, padded - units))) for piece in (own_rows_gate, own_rows_up, down_piece)], axis=1)
    out_pieces = [out_piece] + [along(out_piece, d, ring) for d in range(1, ring)]
    words, codes = pair_bias(page_lengths, rel_bucket, layout_bucket, bias_words(rel_table, layout_table), key_mask)
    normed_attn_all, ffn_piece, words, own_rows_project = lax.optimization_barrier(
        (normed_attn_all, ffn_piece, words, own_rows_project))
    ffn_pieces = [along(ffn_piece, d, ring) for d in range(2, ring, 2)]
    out_t = lax.all_gather(jnp.concatenate(out_pieces, axis=1), "wide", axis=0, tiled=True)

    projected = dot(normed_attn_all, w_project).astype(bf16)
    first_pair = list(attention_forward(page_lengths, projected, words, 0))
    first_pair[0], ffn_pieces, late_grad = lax.optimization_barrier((first_pair[0], ffn_pieces, out_grad))
    far_pieces = jnp.concatenate(ffn_pieces, axis=1)
    other_grad = swap(late_grad, ring)

    def to_owners(a):
        return [rows_of(a, me, tokens)] + [
            along(rows_of(a, (me + d) % ring, tokens), d, ring) for d in range(1, ring)]

    sent = [to_owners(first_pair[0])]
    results = [first_pair]
    if pairs > 1:
        late_projected, far_pieces = lax.optimization_barrier((projected, far_pieces))
        results += [list(attention_forward(page_lengths, late_projected, words, p)) for p in range(1, pairs)]
    far = lax.all_gather(far_pieces, "wide", axis=0, tiled=True)
    results[-1][0], other_grad, sent[0] = lax.optimization_barrier((results[-1][0], other_grad, sent[0]))
    attended = [r[0] for r in results]
    sent += [to_owners(a) for a in attended[1:]]
    mine = [pieces[d] for d in range(ring) for pieces in sent]
    attended_own = jnp.concatenate(mine, axis=1)
    middle = resid + contract_cols(attended_own, out_t)

    scale_ffn, normed_ffn = norm_rows(middle, gain_ffn)
    other_normed = swap(normed_ffn, ring)
    near = (w_gate.T, w_up.T, down_projection_weight)
    shards = ring // 2
    own = [feed_forward(normed_ffn, out_grad, units, near)]
    own, other_normed, late_project = lax.optimization_barrier((own, other_normed, own_rows_project))
    project_pieces = [along(late_project, d, ring) for d in range(1, ring)]
    other = [feed_forward(other_normed, other_grad, units, near)]
    other += [feed_forward(other_normed, other_grad, units, (far,), s) for s in range(shards - 1)]
    other_d_normed = sum(o[3] for o in other).astype(bf16)
    late_normed, other_d_normed = lax.optimization_barrier((normed_ffn, other_d_normed))
    other_d_normed = swap(other_d_normed, ring)
    own += [feed_forward(late_normed, out_grad, units, (far,), s) for s in range(shards - 1)]
    rights, groups = [], []
    for s in range(shards):
        for n in range(1, 4):
            rights += [own[s][n % 3], other[s][n % 3]]
            groups.append(n // 3)
    sums = weight_grads((normed_ffn, other_normed, out_grad, other_grad), rights, tuple(groups))
    sums, other_d_normed, project_pieces = lax.optimization_barrier((sums, other_d_normed, project_pieces))
    ffn_sums = lax.psum_scatter(sums, "wide", scatter_dimension=0, tiled=True)
    d_normed_ffn = sum(o[3] for o in own) + other_d_normed.astype(f32)
    d_middle = out_grad.astype(f32) + norm_back(d_normed_ffn, middle, scale_ffn, gain_ffn)
    d_middle_low = d_middle.astype(bf16)
    d_attended_own = dot(d_middle_low, out_t).astype(bf16)

    def block(d):
        return d_attended_own[:, d * head_cols : (d + 1) * head_cols]

    d_attended = jnp.zeros((ring * tokens, head_cols), bf16)
    d_attended = lax.dynamic_update_slice_in_dim(d_attended, block(0), me * tokens, 0)
    for d in range(1, ring):
        d_attended = lax.dynamic_update_slice_in_dim(
            d_attended, along(block(d), -d, ring), ((me + d) % ring) * tokens, 0)

    d_middle_late, attended_late, own_hidden, other_hidden = lax.optimization_barrier(
        (d_middle_low, attended_own, [o[0] for o in own], [o[0] for o in other]))
    wout_sums = contract_rows(d_middle_late, attended_late).astype(bf16)
    own_out, other_out = 0.0, 0.0
    for s in range(shards):
        if s == 0:
            down, dims = down_projection_weight, NN
        else:
            at = 3 * padded * (s - 1) + 2 * padded
            down, dims = far[:, at : at + units], NT
        own_out = own_out + dot(own_hidden[s], down, dims)
        other_out = other_out + dot(other_hidden[s], down, dims)
    own_out = own_out + middle
    project_pieces = jnp.concatenate([own_rows_project] + project_pieces, axis=1)
    wout_sums, d_attended, own_out, other_out, project_pieces = lax.optimization_barrier(
        (wout_sums, d_attended, own_out, other_out.astype(bf16), project_pieces))
    other_out = swap(other_out, ring)

    d_scores, leaving, mine, products = [], [], [], []
    for p, (att, rinv, exps) in enumerate(results):
        d_pair, scores = attention_backward(page_lengths, projected, exps, d_attended, att, rinv, p)
        if p == 0:
            d_pair, other_out = lax.optimization_barrier((d_pair, other_out))
        else:
            d_pair, mine[-1] = lax.optimization_barrier((d_pair, mine[-1]))
        sent = [rows_of(d_pair, (me + d) % ring, tokens) for d in range(ring)]
        sent, d_pair, d_attended = lax.optimization_barrier((sent, d_pair, d_attended))
        mine.append(sent[:1] + [along(sent[d], d, ring) for d in range(1, ring)])
        d_scores.append(scores)
        products.append(contract_rows(normed_attn_all, d_pair).astype(bf16))
    w_project_all = lax.all_gather(project_pieces, "wide", axis=0, tiled=True)
    layer_out = (own_out + other_out.astype(f32)).astype(bf16)
    last_sums = jnp.concatenate(products + [wout_sums], axis=1)
    last_sums = lax.psum_scatter(last_sums, "wide", scatter_dimension=0, tiled=True)

    totals = table_grads(page_lengths, d_scores, codes)
    far_sums = [along(ffn_sums[:, 3 * padded * s : 3 * padded * (s + 1)], -2 * s, ring) for s in range(1, shards)]
    totals, mine, far_sums = lax.optimization_barrier((totals, mine, far_sums))
    grad_relative = bucket_sums(totals, heads, 4, 2)
    grad_layout = bucket_sums(totals, heads, 0, 4)
    tables = jnp.concatenate(
        [grad_relative.reshape(wide, -1, heads), grad_layout.reshape(wide, -1, heads)], axis=1)
    n_rel = grad_relative.shape[0] // wide
    reach = wide // 2
    while reach >= 1:
        bit = (my_wide // reach) % 2
        keep = lax.dynamic_slice_in_dim(tables, bit * reach, reach, 0)
        give = lax.dynamic_slice_in_dim(tables, (1 - bit) * reach, reach, 0)
        tables = keep + lax.ppermute(give, "wide", [(i, i ^ reach) for i in range(wide)])
        if reach == wide // 2:
            tables, last_sums = lax.optimization_barrier((tables, last_sums))
        reach //= 2
    sum_project = last_sums[:, : 3 * head_cols].astype(f32)
    wout_sums = last_sums[:, 3 * head_cols :]
    sum_tables = tables[0]
    d_normed_attn = pieces_product([pieces[d] for d in range(ring) for pieces in mine], w_project_all)
    in_grad = d_middle + norm_back(d_normed_attn, resid, scale_attn, gain_attn)

    def stripe(shard, n):
        at = padded * (3 * shard + n)
        return ffn_sums[:, at : at + units]

    sum_gate, sum_up, sum_down = [stripe(0, n).astype(f32) for n in range(3)]
    for s in range(1, shards):
        block = far_sums[s - 1].astype(f32)
        sum_gate += block[:, :units]
        sum_up += block[:, padded : padded + units]
        sum_down += block[:, 2 * padded : 2 * padded + units]
    gain_terms = jnp.stack(
        [
            jnp.sum(own_rows_project.astype(f32) * sum_project, axis=1),
            jnp.sum(own_rows_gate.astype(f32) * sum_gate + own_rows_up.astype(f32) * sum_up, axis=1),
        ]
    )
    share = part // ring

    high = gain_terms.astype(bf16)
    halves = jnp.concatenate([high, (gain_terms - high.astype(f32)).astype(bf16)], axis=0)
    gain_sum = lax.dynamic_slice_in_dim(gain_terms, me * share, share, 1)
    sum_wout = wout_sums[:, :head_cols].astype(f32)
    for d in range(1, ring):
        its = lax.dynamic_slice_in_dim(halves, ((me - d) % ring) * share, share, 1)
        its = jnp.pad(its, ((0, 12), (0, head_cols - share)))
        got = along(jnp.concatenate([wout_sums[:, d * head_cols : (d + 1) * head_cols], its], axis=0), -d, ring)
        got = got.astype(f32)
        sum_wout = sum_wout + got[:part]
        gain_sum = gain_sum + got[part : part + 2, :share] + got[part + 2 : part + 4, :share]
    place = my_wide * part + me * share
    gains = lax.dynamic_slice_in_dim(jnp.stack([gain_attn, gain_ffn]), place, share, 1)
    gain_grads = gain_sum / gains

    def whole_project(n):
        return jnp.concatenate([sum_project[:, (3 * p + n) * 128 : (3 * p + n + 1) * 128] for p in range(pairs)], axis=1)

    return (
        layer_out,
        in_grad,
        gain_grads[0],
        whole_project(0),
        whole_project(1),
        whole_project(2),
        sum_wout.T,
        sum_tables[:n_rel],
        sum_tables[n_rel:],
        gain_grads[1],
        sum_gate,
        sum_up,
        sum_down.T,
    )


def solution(mesh):
    placed = (
        P(("wide", "narrow"), None),
        P(("wide", "narrow"), None),
        P(),
        P(None, "narrow"),
        P(None, "narrow"),
        P(None, "narrow"),
        P("narrow", None),
        P(None, "narrow"),
        P(None, "narrow"),
        P(),
        P(None, "narrow"),
        P(None, "narrow"),
        P("narrow", None),
        P("wide", None),
        P("wide"),
        P("wide", None),
        P("wide", None),
    )
    return jax.shard_map(
        functools.partial(on_device, mesh.shape["wide"], mesh.shape["narrow"]),
        mesh=mesh,
        in_specs=placed,
        out_specs=(
            P(("wide", "narrow"), None),
            P(("wide", "narrow"), None),
            P(("wide", "narrow")),
            P("wide", "narrow"),
            P("wide", "narrow"),
            P("wide", "narrow"),
            P("narrow", "wide"),
            P("wide", "narrow"),
            P("wide", "narrow"),
            P(("wide", "narrow")),
            P("wide", "narrow"),
            P("wide", "narrow"),
            P("narrow", "wide"),
        ),
        check_vma=False,
    )
```

```python
import functools
import jax
import jax.numpy as jnp
from jax import lax
from jax.experimental import pallas as pl
from jax.experimental.pallas import tpu as pltpu
from jax.sharding import PartitionSpec as P

DH = 64
BIAS_SCALE = 4096.0
LOG2E = 1.4426950408889634
f32 = jnp.float32
bf16 = jnp.bfloat16
NT = (((1,), (1,)), ((), ()))
NN = (((1,), (0,)), ((), ()))


def dot(a, b, dims=NN):
    return lax.dot_general(a, b, dims, preferred_element_type=f32)


def key_window(len_ref, first, last, count, width):
    ends = []
    total = 0
    for p in range(len_ref.shape[1]):
        total = total + len_ref[0, p]
        ends.append(total)
    start = 0
    stop = count
    for e in ends:
        start = jnp.where(e <= first, e, start)
    for e in reversed(ends):
        stop = jnp.where(e > last, e, stop)
    base = (start // 128) * 128
    steps = (stop - base + width - 1) // width
    base = jnp.minimum(base, count - steps * width)
    return ends, base, steps


def for_chunks(base, steps, width, group, body):
    def many(j, carry):
        body(pl.multiple_of(base + j * (group * width), 128), group * width)
        return carry

    def single(j, carry):
        body(pl.multiple_of(base + j * width, 128), width)
        return carry

    if group > 1:
        lax.fori_loop(0, steps // group, many, 0)
    lax.fori_loop((steps // group) * group if group > 1 else 0, steps, single, 0)


def own_half(shape, head):
    lane = lax.broadcasted_iota(jnp.int32, shape, len(shape) - 1)
    return (lane < DH) if head % 2 == 0 else (lane >= DH)


def fill_values(vext, v_ref, heads):
    for h in range(heads):
        vp = v_ref[:, (h // 2) * 128:(h // 2 + 1) * 128]
        vext[h] = jnp.where(own_half(vp.shape, h), vp, jnp.ones_like(vp))


def half_norms(rows):
    lane = lax.broadcasted_iota(jnp.int32, (128, 128), 0)
    column = lax.broadcasted_iota(jnp.int32, (128, 128), 1)
    same = ((lane < DH) == (column < DH)).astype(bf16)
    squares = (rows.astype(f32) * rows.astype(f32)).astype(bf16)
    return jnp.max(dot(squares, same)) * f32(1.02)


HIDDEN_PAIR = -(1 << 31)


def pair_bias_kernel(len_ref, rel_ref, lay_ref, tab_ref, kmask_ref, word_ref, code_ref, colcode, *, width, group):
    tq, count = rel_ref.shape
    pairs = word_ref.shape[0]
    i = pl.program_id(0)
    t0 = i * tq
    ends, base, steps = key_window(len_ref, t0, t0 + tq - 1, count, width)

    @pl.when(i == 0)
    def _():
        pos = lax.broadcasted_iota(jnp.int32, (8, count), 1)
        page = jnp.zeros((8, count), jnp.int32)
        for e in ends:
            page = page + (pos >= e).astype(jnp.int32)
        colcode[...] = jnp.where(kmask_ref[...] == 1, page, -1)

    rowpos = lax.broadcasted_iota(jnp.int32, (tq, 128), 0) + t0
    rowpage = jnp.zeros((tq, 128), jnp.int32)
    for e in ends:
        rowpage = rowpage + (rowpos >= e).astype(jnp.int32)
    lanes = lax.broadcasted_iota(jnp.int32, (tq, 128), 1)
    tabs = [jnp.broadcast_to(tab_ref[n:n + 1, :], (tq, 128)) for n in range(2 * pairs)]

    def chunk(c0, size):
        for half in range(size // 128):
            cc = pl.multiple_of(c0 + half * 128, 128)
            here = pl.ds(cc, 128)
            rel = rel_ref[:, here]
            lay = lay_ref[:, here]
            code_ref[:, here] = (rel + lay * 32).astype(jnp.int16)
            col = jnp.broadcast_to(colcode[0:1, here], (tq, 128))
            seen = (rowpage == col) | (rowpos == lanes + cc)
            for p in range(pairs):
                word = (jnp.take_along_axis(tabs[2 * p], rel, axis=1, mode="promise_in_bounds")
                        + jnp.take_along_axis(tabs[2 * p + 1], lay, axis=1, mode="promise_in_bounds"))
                word_ref[p, :, here] = jnp.where(seen, word, HIDDEN_PAIR)

    for_chunks(base, steps, width, group, chunk)


def pair_bias(page_lengths, rel, lay, tab, kmask, tq=256, width=256, group=2):
    count = rel.shape[0]
    pairs = tab.shape[0] // 2
    tile = lambda i: (i, 0)
    return pl.pallas_call(
        functools.partial(pair_bias_kernel, width=width, group=group),
        grid=(count // tq,),
        in_specs=[
            pl.BlockSpec(memory_space=pltpu.SMEM),
            pl.BlockSpec((tq, count), tile),
            pl.BlockSpec((tq, count), tile),
            pl.BlockSpec(tab.shape, lambda i: (0, 0)),
            pl.BlockSpec((1, count), lambda i: (0, 0)),
        ],
        out_specs=[
            pl.BlockSpec((pairs, tq, count), lambda i: (0, i, 0)),
            pl.BlockSpec((tq, count), tile),
        ],
        out_shape=[
            jax.ShapeDtypeStruct((pairs, count, count), jnp.int32),
            jax.ShapeDtypeStruct((count, count), jnp.int16),
        ],
        scratch_shapes=[pltpu.VMEM((8, count), jnp.int32)],
        compiler_params=pltpu.CompilerParams(vmem_limit_bytes=56 << 20),
        cost_estimate=pl.CostEstimate(flops=count * count * 1024, bytes_accessed=120 << 20, transcendentals=0),
        name="pair_bias",
    )(page_lengths, rel, lay, tab, kmask.reshape(1, count))


def forward_kernel(len_ref, q_ref, k_ref, v_ref, word_ref, att_ref, rinv_ref, e_ref,
                   s_scr, m_scr, acc_scr, vext, knorm, *, width, group):
    tq, count = word_ref.shape[1:]
    heads, pairs = 2, 1
    i = pl.program_id(0)
    t0 = i * tq
    ends, base, steps = key_window(len_ref, t0, t0 + tq - 1, count, width)

    @pl.when(i == 0)
    def _():
        fill_values(vext, v_ref, heads)
        for p in range(pairs):
            knorm[p] = half_norms(k_ref[:, p * 128:(p + 1) * 128])

    scaled = []
    largest = f32(0.0)
    for h in range(heads):
        qp = q_ref[:, (h // 2) * 128:(h // 2 + 1) * 128]
        scaled.append(jnp.where(own_half(qp.shape, h), qp * bf16(BIAS_SCALE), jnp.zeros_like(qp)))
        if h % 2 == 0:
            largest = jnp.maximum(largest, half_norms(qp) * knorm[h // 2])
    def scores(c0, width, use):
        raw = [dot(scaled[h], k_ref[pl.ds(c0, width), (h // 2) * 128:(h // 2 + 1) * 128], NT)
               for h in range(heads)]
        for half in range(width // 128):
            cc = pl.multiple_of(c0 + half * 128, 128)
            word = word_ref[0, :, pl.ds(cc, 128)]
            hidden = word == HIDDEN_PAIR
            parts = ((word & 0xFFFF).astype(f32), (word >> 16).astype(f32))
            for h in range(heads):
                bias = jnp.where(hidden, f32(-1e30), parts[h])
                use(h, half, cc, raw[h][:, half * 128:(half + 1) * 128] + bias)

    for h in range(heads):
        acc_scr[h] = jnp.zeros((tq, 128), f32)
    bounded = jnp.sqrt(largest) + 8.0 <= 60.0

    @pl.when(bounded)
    def _():
        def chunk(c0, size):
            pieces = {}

            def use(h, half, cc, s):
                e = jnp.exp2(s * f32(LOG2E / BIAS_SCALE)).astype(bf16)
                e_ref[h, :, pl.ds(cc, 128)] = e
                pieces[h, half] = e

            scores(c0, size, use)
            for h in range(heads):
                e = jnp.concatenate([pieces[h, half] for half in range(size // 128)], axis=1)
                acc_scr[h] += dot(e, vext[h, pl.ds(c0, size), :])

        for_chunks(base, steps, width, group, chunk)

    @pl.when(jnp.logical_not(bounded))
    def _():
        for h in range(heads):
            m_scr[h] = jnp.full((tq, 128), -3e38, f32)

        def first(j, carry):
            def use(h, half, cc, s):
                s_scr[h, :, pl.ds(cc, 128)] = s
                m_scr[h] = jnp.maximum(m_scr[h], s)

            scores(pl.multiple_of(base + j * width, 128), width, use)
            return carry

        lax.fori_loop(0, steps, first, 0)
        for h in range(heads):
            top = jnp.max(m_scr[h], axis=1, keepdims=True)

            def second(j, carry):
                c0 = pl.multiple_of(base + j * width, 128)
                e = jnp.exp2((s_scr[h, :, pl.ds(c0, width)] - top) * f32(LOG2E / BIAS_SCALE)).astype(bf16)
                e_ref[h, :, pl.ds(c0, width)] = e
                acc_scr[h] += dot(e, vext[h, pl.ds(c0, width), :])
                return carry

            lax.fori_loop(0, steps, second, 0)

    low = own_half((tq, 128), 0)
    for p in range(pairs):
        even, odd = acc_scr[2 * p], acc_scr[2 * p + 1]
        rinv = 1.0 / pltpu.roll(jnp.where(low, odd, even), DH, 1)
        att_ref[:, p * 128:(p + 1) * 128] = (jnp.where(low, even, odd) * rinv).astype(bf16)
        rinv_ref[:, p * 128:(p + 1) * 128] = rinv


def attention_forward(page_lengths, proj, words, pair, tq=256, width=256, group=2):
    count = proj.shape[0]
    pairs = proj.shape[1] // (3 * 128)
    tile = lambda i: (i, 0)
    return pl.pallas_call(
        functools.partial(forward_kernel, width=width, group=group),
        grid=(count // tq,),
        in_specs=[
            pl.BlockSpec(memory_space=pltpu.SMEM),
            pl.BlockSpec((tq, 128), lambda i: (i, pair)),
            pl.BlockSpec((count, 128), lambda i: (0, pairs + pair)),
            pl.BlockSpec((count, 128), lambda i: (0, 2 * pairs + pair)),
            pl.BlockSpec((1, tq, count), lambda i: (pair, i, 0)),
        ],
        out_specs=[
            pl.BlockSpec((tq, 128), tile),
            pl.BlockSpec((tq, 128), tile),
            pl.BlockSpec((2, tq, count), lambda i: (0, i, 0)),
        ],
        out_shape=[
            jax.ShapeDtypeStruct((count, 128), bf16),
            jax.ShapeDtypeStruct((count, 128), f32),
            jax.ShapeDtypeStruct((2, count, count), bf16),
        ],
        scratch_shapes=[
            pltpu.VMEM((2, tq, count), f32),
            pltpu.VMEM((2, tq, 128), f32),
            pltpu.VMEM((2, tq, 128), f32),
            pltpu.VMEM((2, count, 128), bf16),
            pltpu.SMEM((1,), f32),
        ],
        compiler_params=pltpu.CompilerParams(vmem_limit_bytes=56 << 20),
        cost_estimate=pl.CostEstimate(
            flops=count * count * 512, bytes_accessed=80 << 20, transcendentals=count * count),
        name="attention_forward",
    )(page_lengths, proj, proj, proj, words)


def bias_words(rel_table, layout_table):
    def pack(table):
        whole = jnp.round(table.astype(f32) * BIAS_SCALE).astype(jnp.int32)
        low = jnp.clip(whole[:, 0::2] + 16384, 0, 32767)
        high = jnp.clip(whole[:, 1::2], -16383, 16383)
        words = (high * 65536 + low).T
        return jnp.pad(words, ((0, 0), (0, 128 - words.shape[1])))
    both = jnp.stack([pack(rel_table), pack(layout_table)], axis=1)
    return both.reshape(-1, 128)


def signs(code, shift, bits):
    return [jnp.where((code & jnp.int16(1 << (shift + b))) == 0, bf16(1.0), bf16(-1.0))
            for b in range(bits)]


def walsh(sign_list):
    out = [None]
    for s in sign_list:
        out = out + [s if o is None else o * s for o in out]
    return out


def backward_kernel(len_ref, q_ref, k_ref, v_ref, da_ref, *refs, width, heads, group):
    tq = q_ref.shape[0]
    count = k_ref.shape[0]
    pairs = heads // 2
    e_refs, att_refs, rinv_refs = refs[:pairs], refs[pairs:2 * pairs], refs[2 * pairs:3 * pairs]
    dp_ref, ds_ref = refs[3 * pairs:3 * pairs + 2]
    vext, lhs_scr, dat_scr, qt_scr, dq_scr, dkt, dvt = refs[3 * pairs + 2:]
    i = pl.program_id(0)
    t0 = i * tq
    ends, base, steps = key_window(len_ref, t0, t0 + tq - 1, count, width)

    @pl.when(i == 0)
    def _():
        fill_values(vext, v_ref, heads)
        dkt[...] = jnp.zeros_like(dkt)
        dvt[...] = jnp.zeros_like(dvt)

    low = own_half((tq, 128), 0)
    lane = lax.broadcasted_iota(jnp.int32, (tq, 128), 1)
    first_part = (lane & 32) == 0
    for p in range(pairs):
        cols = slice(p * 128, (p + 1) * 128)
        da = (da_ref[:, cols].astype(f32) * rinv_refs[p][...]).astype(bf16)
        daf = da.astype(f32)
        prod = daf * att_refs[p][...].astype(f32)
        for r in range(2):
            own = low if r == 0 else jnp.logical_not(low)
            delta = jnp.sum(jnp.where(own, prod, 0.0), axis=1, keepdims=True) * f32(-1.0 / 32)
            high = delta.astype(bf16).astype(f32)
            rest = delta - high
            lhs_scr[2 * p + r] = jnp.where(own, daf, jnp.where(first_part, high, rest)).astype(bf16)
        dat_scr[p] = daf.T.astype(bf16)
        qt_scr[p] = q_ref[:, cols].astype(f32).T.astype(bf16)
        dq_scr[p] = jnp.zeros((tq, 128), f32)

    def chunk(c0, size):
        here = pl.ds(c0, size)
        for p in range(pairs):
            kp = k_ref[here, p * 128:(p + 1) * 128]
            dqs = []
            for r in range(2):
                h = 2 * p + r
                rows = slice(r * DH, (r + 1) * DH)
                e = e_refs[p][r, :, here]
                d = dot(lhs_scr[h], vext[h, here, :], NT)
                ds = (e.astype(f32) * d).astype(bf16)
                ds_ref[h, :, here] = ds
                dqs.append(dot(ds, kp))
                dkt[p, rows, here] += dot(qt_scr[p, rows, :], ds)
                dvt[p, rows, here] += dot(dat_scr[p, rows, :], e)
            dq_scr[p] += jnp.where(low, dqs[0], dqs[1])

    for_chunks(base, steps, width, group, chunk)
    for p in range(pairs):
        dp_ref[pl.ds(pl.multiple_of(t0, tq), tq), p * 128:(p + 1) * 128] = dq_scr[p].astype(bf16)

    @pl.when(i == pl.num_programs(0) - 1)
    def _():
        for n, grads in enumerate((dkt, dvt)):
            for p in range(pairs):
                at = ((n + 1) * pairs + p) * 128
                for c in range(0, count, 256):
                    dp_ref[c:c + 256, at:at + 128] = grads[p, :, c:c + 256].T.astype(bf16)


def attention_backward(page_lengths, proj, exps, d_att, att, rinv, pair, tq=256, width=256, group=2):
    count = proj.shape[0]
    pairs = proj.shape[1] // (3 * 128)
    tile = lambda i: (i, 0)
    return pl.pallas_call(
        functools.partial(backward_kernel, width=width, heads=2, group=group),
        grid=(count // tq,),
        in_specs=[
            pl.BlockSpec(memory_space=pltpu.SMEM),
            pl.BlockSpec((tq, 128), lambda i: (i, pair)),
            pl.BlockSpec((count, 128), lambda i: (0, pairs + pair)),
            pl.BlockSpec((count, 128), lambda i: (0, 2 * pairs + pair)),
            pl.BlockSpec((tq, 128), lambda i: (i, pair)),
            pl.BlockSpec((2, tq, count), lambda i: (0, i, 0)),
            pl.BlockSpec((tq, 128), tile),
            pl.BlockSpec((tq, 128), tile),
        ],
        out_specs=[
            pl.BlockSpec((count, 384), lambda i: (0, 0)),
            pl.BlockSpec((2, tq, count), lambda i: (0, i, 0)),
        ],
        out_shape=[
            jax.ShapeDtypeStruct((count, 384), bf16),
            jax.ShapeDtypeStruct((2, count, count), bf16),
        ],
        scratch_shapes=[
            pltpu.VMEM((2, count, 128), bf16),
            pltpu.VMEM((2, tq, 128), bf16),
            pltpu.VMEM((1, 128, tq), bf16),
            pltpu.VMEM((1, 128, tq), bf16),
            pltpu.VMEM((1, tq, 128), f32),
            pltpu.VMEM((1, 128, count), f32),
            pltpu.VMEM((1, 128, count), f32),
        ],
        compiler_params=pltpu.CompilerParams(vmem_limit_bytes=56 << 20),
        cost_estimate=pl.CostEstimate(flops=count * count * 1024, bytes_accessed=80 << 20, transcendentals=0),
        name="attention_backward",
    )(page_lengths, proj, proj, proj, d_att, exps, att, rinv)


def parity_sign(v):
    v = v ^ (v >> 2)
    v = v ^ (v >> 1)
    return (1 - 2 * (v & 1)).astype(f32)


def bucket_totals(raw, first, heads):
    rows, cols = raw.shape
    low = rows // (16 * heads)
    r = lax.broadcasted_iota(jnp.int32, raw.shape, 0)
    c = lax.broadcasted_iota(jnp.int32, raw.shape, 1)
    kept = jnp.where((r & 15) == (c & 15), raw, 0.0)
    c = lax.broadcasted_iota(jnp.int32, (cols, 128), 0)
    y = lax.broadcasted_iota(jnp.int32, (cols, 128), 1)
    right = jnp.where(y < cols // 16, parity_sign((c >> 4) & y), 0.0)
    r = lax.broadcasted_iota(jnp.int32, (low * heads, rows), 1) >> 4
    x = lax.broadcasted_iota(jnp.int32, (low * heads, rows), 0)
    function = (r // heads + first) & (low - 1)
    left = jnp.where(r % heads == x % heads, parity_sign(function & (x // heads)), 0.0)
    exact = lax.Precision.HIGHEST
    half = lax.dot_general(kept, right, NN, precision=exact, preferred_element_type=f32)
    out = lax.dot_general(left, half, NN, precision=exact, preferred_element_type=f32)
    return out * f32(1.0 / (low * (cols // 16)))


def table_kernel(len_ref, code_ref, *refs, width, parts, pairs):
    ds_refs, (out_ref, hl_ref, hr_ref), bufs = refs[:pairs], refs[pairs:pairs + 3], refs[pairs + 3:]
    heads = 2 * pairs
    tq, count = code_ref.shape
    i = pl.program_id(0)
    t0 = i * tq
    ends, base, steps = key_window(len_ref, t0, t0 + tq - 1, count, width)

    @pl.when(i == 0)
    def _():
        hl_ref[...] = jnp.zeros_like(hl_ref)
        hr_ref[...] = jnp.zeros_like(hr_ref)

    one = jnp.ones((16, width), bf16)

    def chunk(j, carry):
        c0 = pl.multiple_of(base + j * width, 128)
        here = pl.ds(c0, width)
        blocks = tq // 16 // parts
        for part in range(parts):
            left, blay, brel = bufs[3 * part:3 * part + 3]
            for b in range(blocks):
                at = 16 * (part * blocks + b)
                rows = slice(at, at + 16)
                span = slice(b * width, (b + 1) * width)
                code = code_ref[rows, here]
                rel_signs = signs(code, 0, 5)
                lay_signs = signs(code, 5, 6)
                left_lay = walsh(lay_signs[:2])[1:]
                for h in range(heads):
                    ds = ds_refs[h // 2][h % 2, rows, here]
                    for a, func in enumerate(left_lay + [None, rel_signs[0]]):
                        place = 16 * (a * heads + h)
                        left[place:place + 16, span] = ds if func is None else ds * func
                for n, func in enumerate(walsh(lay_signs[2:])):
                    blay[16 * n:16 * (n + 1), span] = one if func is None else func
                for n, func in enumerate(walsh(rel_signs[1:])):
                    brel[16 * n:16 * (n + 1), span] = one if func is None else func
            hl_ref[...] += dot(left[:64 * heads, :], blay[...], NT)
            hr_ref[...] += dot(left[48 * heads:80 * heads, :], brel[...], NT)
        return carry

    lax.fori_loop(0, steps, chunk, 0)

    @pl.when(i == pl.num_programs(0) - 1)
    def _():
        out_ref[...] = jnp.zeros_like(out_ref)
        out_ref[:4 * heads, :] = bucket_totals(hl_ref[...], 1, heads)
        out_ref[4 * heads:6 * heads, :] = bucket_totals(hr_ref[...], 0, heads)


def table_grads(page_lengths, ds, code, tq=256, width=256, parts=2):
    heads, count = 2 * len(ds), code.shape[0]
    deep = tq // 16 * width // parts
    fixed = lambda i: (0, 0)
    return pl.pallas_call(
        functools.partial(table_kernel, width=width, parts=parts, pairs=len(ds)),
        grid=(count // tq,),
        in_specs=[
            pl.BlockSpec(memory_space=pltpu.SMEM),
            pl.BlockSpec((tq, count), lambda i: (i, 0)),
        ] + [pl.BlockSpec((2, tq, count), lambda i: (0, i, 0))] * len(ds),
        out_specs=pl.BlockSpec((8 * heads, 128), fixed),
        out_shape=jax.ShapeDtypeStruct((8 * heads, 128), f32),
        scratch_shapes=[pltpu.VMEM((64 * heads, 256), f32), pltpu.VMEM((32 * heads, 256), f32)] + [
            pltpu.VMEM((80 * heads, deep), bf16),
            pltpu.VMEM((256, deep), bf16),
            pltpu.VMEM((256, deep), bf16),
        ] * parts,
        compiler_params=pltpu.CompilerParams(vmem_limit_bytes=56 << 20),
        cost_estimate=pl.CostEstimate(
            flops=heads * count * count * 512, bytes_accessed=150 << 20, transcendentals=0),
        name="table_grads",
    )(page_lengths, code, *ds)


def bucket_sums(totals, heads, first, low):
    rows = totals[first * heads:(first + low) * heads, :16].reshape(low, heads, 16)
    return jnp.transpose(rows, (2, 0, 1)).reshape(16 * low, heads)


TANH_SLOPE = 0.7978845608028654
CUBE = 0.044715


def feed_forward_kernel(far, x_ref, g_ref, *refs):
    weights, (hidden_ref, d_gate_ref, d_up_ref, dn_ref) = refs[:-4], refs[-4:]
    units = hidden_ref.shape[1]
    if far:
        step = pad_lanes(units)
        gate_weight, up_weight, down = [weights[0][:, n * step:n * step + units] for n in range(3)]
        ahead, back = NN, NT
    else:
        gate_weight, up_weight, down = [w[...] for w in weights]
        ahead, back = NT, NN
    x = x_ref[...]
    d_hidden = dot(g_ref[...], down, ahead)
    gate = dot(x, gate_weight, ahead)
    up = dot(x, up_weight, ahead)
    square = gate * gate
    t = jnp.tanh(TANH_SLOPE * gate * (1.0 + CUBE * square))
    half = 0.5 + 0.5 * t
    gelu = gate * half
    slope = half + (0.5 * TANH_SLOPE) * gate * (1.0 - t * t) * (1.0 + (3 * CUBE) * square)
    d_gate = (d_hidden * up * slope).astype(bf16)
    d_up = (d_hidden * gelu).astype(bf16)
    hidden_ref[...] = (gelu * up).astype(bf16)
    d_gate_ref[...] = d_gate
    d_up_ref[...] = d_up
    dn_ref[...] = dot(d_gate, gate_weight, back) + dot(d_up, up_weight, back)


def feed_forward(x, g, units, weights, shard=None, tile=256):
    tokens, features = x.shape
    tile = min(tile, tokens)
    rows = lambda n: pl.BlockSpec((tile, n), lambda i: (i, 0))
    if shard is None:
        weight_specs = [pl.BlockSpec(w.shape, lambda i: (0, 0)) for w in weights]
    else:
        weight_specs = [pl.BlockSpec((features, 3 * pad_lanes(units)), lambda i: (0, shard))]
    return pl.pallas_call(
        functools.partial(feed_forward_kernel, shard is not None),
        grid=(tokens // tile,),
        in_specs=[rows(features), rows(features)] + weight_specs,
        out_specs=[rows(units)] * 3 + [rows(features)],
        out_shape=[jax.ShapeDtypeStruct((tokens, units), bf16)] * 3
        + [jax.ShapeDtypeStruct((tokens, features), f32)],
        compiler_params=pltpu.CompilerParams(vmem_limit_bytes=56 << 20),
        cost_estimate=pl.CostEstimate(
            flops=10 * tokens * features * units, bytes_accessed=10 << 20, transcendentals=tokens * units),
        name="feed_forward",
    )(x, g, *weights)


def pad_lanes(n):
    return (n + 127) // 128 * 128


def weight_grads_kernel(n_left, n_right, *refs):
    lefts = refs[:2 * n_left]
    rights = refs[2 * n_left:-1]
    out_ref = refs[-1]
    rows_in = (((0,), (0,)), ((), ()))
    place = 0
    for n, left in enumerate(n_right):
        a, b = rights[2 * n], rights[2 * n + 1]
        size = a.shape[1]
        value = dot(lefts[2 * left][...], a[...], rows_in) + dot(lefts[2 * left + 1][...], b[...], rows_in)
        out_ref[:, place:place + size] = value.astype(bf16)
        if pad_lanes(size) > size:
            out_ref[:, place + size:place + pad_lanes(size)] = jnp.zeros(
                (out_ref.shape[0], pad_lanes(size) - size), bf16)
        place += pad_lanes(size)


def weight_grads(lefts, rights, groups, tile=256):
    features = lefts[0].shape[1]
    columns = sum(pad_lanes(r.shape[1]) for r in rights[::2])
    column = lambda a: pl.BlockSpec((a.shape[0], tile), lambda i: (0, i))
    whole = lambda a: pl.BlockSpec(a.shape, lambda i: (0, 0))
    return pl.pallas_call(
        functools.partial(weight_grads_kernel, len(lefts) // 2, groups),
        grid=(features // tile,),
        in_specs=[column(a) for a in lefts] + [whole(a) for a in rights],
        out_specs=pl.BlockSpec((tile, columns), lambda i: (i, 0)),
        out_shape=jax.ShapeDtypeStruct((features, columns), bf16),
        compiler_params=pltpu.CompilerParams(vmem_limit_bytes=56 << 20),
        cost_estimate=pl.CostEstimate(
            flops=4 * features * columns * lefts[0].shape[0], bytes_accessed=26 << 20, transcendentals=0),
        name="weight_grads",
    )(*lefts, *rights)


def pieces_product_kernel(*refs):
    pieces, w_ref, out_ref = refs[:-2], refs[-2], refs[-1]
    total = None
    place = 0
    for piece in pieces:
        size = piece.shape[1]
        value = dot(piece[...], w_ref[:, place:place + size], NT)
        total = value if total is None else total + value
        place += size
    out_ref[...] = total


def pieces_product(pieces, w, tile=256):
    rows = pieces[0].shape[0]
    tile = min(tile, rows)
    return pl.pallas_call(
        pieces_product_kernel,
        grid=(rows // tile,),
        in_specs=[pl.BlockSpec((tile, p.shape[1]), lambda i: (i, 0)) for p in pieces]
        + [pl.BlockSpec(w.shape, lambda i: (0, 0))],
        out_specs=pl.BlockSpec((tile, w.shape[0]), lambda i: (i, 0)),
        out_shape=jax.ShapeDtypeStruct((rows, w.shape[0]), f32),
        compiler_params=pltpu.CompilerParams(vmem_limit_bytes=40 << 20),
        cost_estimate=pl.CostEstimate(
            flops=2 * rows * w.shape[0] * w.shape[1], bytes_accessed=12 << 20, transcendentals=0),
        name="pieces_product",
    )(*pieces, w)


epsilon = 1e-06


def contract_rows(left, right):
    return lax.dot_general(
        left, right, (((0,), (0,)), ((), ())), preferred_element_type=jnp.float32
    )


def contract_cols(left, right):
    return lax.dot_general(
        left, right, (((1,), (1,)), ((), ())), preferred_element_type=jnp.float32
    )


def norm_rows(rows, gain):
    scale = lax.rsqrt(jnp.mean(rows * rows, axis=-1, keepdims=True) + epsilon)
    return (scale, (rows * scale * gain).astype(jnp.bfloat16))


def norm_back(d_normed, rows, scale, gain):
    shaped = d_normed * gain
    cubed = scale * scale * scale
    return scale * shaped - rows * cubed * jnp.mean(shaped * rows, axis=-1, keepdims=True)


def along(array, shift, ring):
    return lax.ppermute(array, "narrow", [(i, (i + shift) % ring) for i in range(ring)])


def swap(array, ring):
    return lax.ppermute(array, "narrow", [(i, i ^ 1) for i in range(ring)])


def rows_of(array, index, count):
    return lax.dynamic_slice_in_dim(array, index * count, count, 0)


def on_device(
    wide,
    ring,
    layer_input,
    out_grad,
    norm_attn_gain,
    w_query,
    w_key,
    w_value,
    w_out,
    rel_table,
    layout_table,
    norm_ffn_gain,
    w_gate,
    w_up,
    down_projection_weight,
    page_lengths,
    key_mask,
    rel_bucket,
    layout_bucket,
):
    tokens, width = layer_input.shape
    head_cols = w_query.shape[1]
    heads = head_cols // DH
    units = w_gate.shape[1]
    padded = pad_lanes(units)
    part = width // wide
    me = lax.axis_index("narrow")
    my_wide = lax.axis_index("wide")
    gain_attn = norm_attn_gain.astype(f32)
    gain_ffn = norm_ffn_gain.astype(f32)
    resid = layer_input.astype(f32)

    scale_attn, normed_attn = norm_rows(resid, gain_attn)
    normed_attn_all = lax.all_gather(normed_attn, "narrow", axis=0, tiled=True)

    w_project = jnp.concatenate([w_query, w_key, w_value], axis=1)
    own_rows_gate = rows_of(w_gate, my_wide, part)
    own_rows_up = rows_of(w_up, my_wide, part)
    pairs = head_cols // 128
    own_rows_project = jnp.concatenate(
        [rows_of(w, my_wide, part)[:, p * 128 : (p + 1) * 128] for p in range(pairs) for w in (w_query, w_key, w_value)],
        axis=1)
    down_piece = lax.dynamic_slice_in_dim(down_projection_weight, my_wide * part, part, 1).T
    out_piece = lax.dynamic_slice_in_dim(w_out, my_wide * part, part, 1).T
    ffn_piece = jnp.concatenate(
        [jnp.pad(piece, ((0, 0), (0, padded - units))) for piece in (own_rows_gate, own_rows_up, down_piece)], axis=1)
    out_pieces = [out_piece] + [along(out_piece, d, ring) for d in range(1, ring)]
    words, codes = pair_bias(page_lengths, rel_bucket, layout_bucket, bias_words(rel_table, layout_table), key_mask)
    normed_attn_all, ffn_piece, words, own_rows_project = lax.optimization_barrier(
        (normed_attn_all, ffn_piece, words, own_rows_project))
    ffn_pieces = [along(ffn_piece, d, ring) for d in range(2, ring, 2)]
    out_t = lax.all_gather(jnp.concatenate(out_pieces, axis=1), "wide", axis=0, tiled=True)

    projected = dot(normed_attn_all, w_project).astype(bf16)
    first_pair = list(attention_forward(page_lengths, projected, words, 0))
    first_pair[0], ffn_pieces, late_grad = lax.optimization_barrier((first_pair[0], ffn_pieces, out_grad))
    far_pieces = jnp.concatenate(ffn_pieces, axis=1)
    other_grad = swap(late_grad, ring)

    def to_owners(a):
        return [rows_of(a, me, tokens)] + [
            along(rows_of(a, (me + d) % ring, tokens), d, ring) for d in range(1, ring)]

    sent = [to_owners(first_pair[0])]
    results = [first_pair]
    if pairs > 1:
        late_projected, far_pieces = lax.optimization_barrier((projected, far_pieces))
        results += [list(attention_forward(page_lengths, late_projected, words, p)) for p in range(1, pairs)]
    far = lax.all_gather(far_pieces, "wide", axis=0, tiled=True)
    results[-1][0], other_grad, sent[0] = lax.optimization_barrier((results[-1][0], other_grad, sent[0]))
    attended = [r[0] for r in results]
    sent += [to_owners(a) for a in attended[1:]]
    mine = [pieces[d] for d in range(ring) for pieces in sent]
    attended_own = jnp.concatenate(mine, axis=1)
    middle = resid + contract_cols(attended_own, out_t)

    scale_ffn, normed_ffn = norm_rows(middle, gain_ffn)
    other_normed = swap(normed_ffn, ring)
    near = (w_gate.T, w_up.T, down_projection_weight)
    shards = ring // 2
    own = [feed_forward(normed_ffn, out_grad, units, near)]
    own += [feed_forward(normed_ffn, out_grad, units, (far,), s) for s in range(shards - 1)]
    own, other_normed, late_project = lax.optimization_barrier((own, other_normed, own_rows_project))
    project_pieces = [along(late_project, d, ring) for d in range(1, ring)]
    other = [feed_forward(other_normed, other_grad, units, near)]
    other += [feed_forward(other_normed, other_grad, units, (far,), s) for s in range(shards - 1)]
    other, project_pieces = lax.optimization_barrier((other, project_pieces))
    other_d_normed = sum(o[3] for o in other).astype(bf16)
    other_d_normed = swap(other_d_normed, ring)
    rights, groups = [], []
    for s in range(shards):
        for n in range(1, 4):
            rights += [own[s][n % 3], other[s][n % 3]]
            groups.append(n // 3)
    sums = weight_grads((normed_ffn, other_normed, out_grad, other_grad), rights, tuple(groups))
    sums, other_d_normed = lax.optimization_barrier((sums, other_d_normed))
    ffn_sums = lax.psum_scatter(sums, "wide", scatter_dimension=0, tiled=True)
    d_normed_ffn = sum(o[3] for o in own) + other_d_normed.astype(f32)
    d_middle = out_grad.astype(f32) + norm_back(d_normed_ffn, middle, scale_ffn, gain_ffn)
    d_middle_low = d_middle.astype(bf16)
    d_attended_own = dot(d_middle_low, out_t).astype(bf16)

    def block(d):
        return d_attended_own[:, d * head_cols : (d + 1) * head_cols]

    d_attended = jnp.zeros((ring * tokens, head_cols), bf16)
    d_attended = lax.dynamic_update_slice_in_dim(d_attended, block(0), me * tokens, 0)
    for d in range(1, ring):
        d_attended = lax.dynamic_update_slice_in_dim(
            d_attended, along(block(d), -d, ring), ((me + d) % ring) * tokens, 0)

    d_middle_late, attended_late, own_hidden, other_hidden = lax.optimization_barrier(
        (d_middle_low, attended_own, [o[0] for o in own], [o[0] for o in other]))
    wout_sums = contract_rows(d_middle_late, attended_late).astype(bf16)
    own_out, other_out = 0.0, 0.0
    for s in range(shards):
        if s == 0:
            down, dims = down_projection_weight, NN
        else:
            at = 3 * padded * (s - 1) + 2 * padded
            down, dims = far[:, at : at + units], NT
        own_out = own_out + dot(own_hidden[s], down, dims)
        other_out = other_out + dot(other_hidden[s], down, dims)
    own_out = own_out + middle
    project_pieces = jnp.concatenate([own_rows_project] + project_pieces, axis=1)
    wout_sums, d_attended, own_out, other_out, project_pieces = lax.optimization_barrier(
        (wout_sums, d_attended, own_out, other_out.astype(bf16), project_pieces))
    other_out = swap(other_out, ring)

    d_scores, leaving, mine, products = [], [], [], []
    for p, (att, rinv, exps) in enumerate(results):
        d_pair, scores = attention_backward(page_lengths, projected, exps, d_attended, att, rinv, p)
        if p == 0:
            d_pair, other_out = lax.optimization_barrier((d_pair, other_out))
        else:
            d_pair, mine[-1] = lax.optimization_barrier((d_pair, mine[-1]))
        sent = [rows_of(d_pair, (me + d) % ring, tokens) for d in range(ring)]
        sent, d_pair, d_attended = lax.optimization_barrier((sent, d_pair, d_attended))
        mine.append(sent[:1] + [along(sent[d], d, ring) for d in range(1, ring)])
        d_scores.append(scores)
        products.append(contract_rows(normed_attn_all, d_pair).astype(bf16))
    w_project_all = lax.all_gather(project_pieces, "wide", axis=0, tiled=True)
    layer_out = (own_out + other_out.astype(f32)).astype(bf16)
    last_sums = jnp.concatenate(products + [wout_sums], axis=1)
    last_sums = lax.psum_scatter(last_sums, "wide", scatter_dimension=0, tiled=True)

    totals = table_grads(page_lengths, d_scores, codes)
    far_sums = [along(ffn_sums[:, 3 * padded * s : 3 * padded * (s + 1)], -2 * s, ring) for s in range(1, shards)]
    totals, mine, far_sums = lax.optimization_barrier((totals, mine, far_sums))
    grad_relative = bucket_sums(totals, heads, 4, 2)
    grad_layout = bucket_sums(totals, heads, 0, 4)
    tables = jnp.concatenate(
        [grad_relative.reshape(wide, -1, heads), grad_layout.reshape(wide, -1, heads)], axis=1)
    n_rel = grad_relative.shape[0] // wide
    reach = wide // 2
    while reach >= 1:
        bit = (my_wide // reach) % 2
        keep = lax.dynamic_slice_in_dim(tables, bit * reach, reach, 0)
        give = lax.dynamic_slice_in_dim(tables, (1 - bit) * reach, reach, 0)
        tables = keep + lax.ppermute(give, "wide", [(i, i ^ reach) for i in range(wide)])
        if reach == wide // 2:
            tables, last_sums = lax.optimization_barrier((tables, last_sums))
        reach //= 2
    sum_project = last_sums[:, : 3 * head_cols].astype(f32)
    wout_sums = last_sums[:, 3 * head_cols :]
    sum_tables = tables[0]
    d_normed_attn = pieces_product([pieces[d] for d in range(ring) for pieces in mine], w_project_all)
    in_grad = d_middle + norm_back(d_normed_attn, resid, scale_attn, gain_attn)

    def stripe(shard, n):
        at = padded * (3 * shard + n)
        return ffn_sums[:, at : at + units]

    sum_gate, sum_up, sum_down = [stripe(0, n).astype(f32) for n in range(3)]
    for s in range(1, shards):
        block = far_sums[s - 1].astype(f32)
        sum_gate += block[:, :units]
        sum_up += block[:, padded : padded + units]
        sum_down += block[:, 2 * padded : 2 * padded + units]
    gain_terms = jnp.stack(
        [
            jnp.sum(own_rows_project.astype(f32) * sum_project, axis=1),
            jnp.sum(own_rows_gate.astype(f32) * sum_gate + own_rows_up.astype(f32) * sum_up, axis=1),
        ]
    )
    share = part // ring

    high = gain_terms.astype(bf16)
    halves = jnp.concatenate([high, (gain_terms - high.astype(f32)).astype(bf16)], axis=0)
    gain_sum = lax.dynamic_slice_in_dim(gain_terms, me * share, share, 1)
    sum_wout = wout_sums[:, :head_cols].astype(f32)
    for d in range(1, ring):
        its = lax.dynamic_slice_in_dim(halves, ((me - d) % ring) * share, share, 1)
        its = jnp.pad(its, ((0, 12), (0, head_cols - share)))
        got = along(jnp.concatenate([wout_sums[:, d * head_cols : (d + 1) * head_cols], its], axis=0), -d, ring)
        got = got.astype(f32)
        sum_wout = sum_wout + got[:part]
        gain_sum = gain_sum + got[part : part + 2, :share] + got[part + 2 : part + 4, :share]
    place = my_wide * part + me * share
    gains = lax.dynamic_slice_in_dim(jnp.stack([gain_attn, gain_ffn]), place, share, 1)
    gain_grads = gain_sum / gains

    def whole_project(n):
        return jnp.concatenate([sum_project[:, (3 * p + n) * 128 : (3 * p + n + 1) * 128] for p in range(pairs)], axis=1)

    return (
        layer_out,
        in_grad,
        gain_grads[0],
        whole_project(0),
        whole_project(1),
        whole_project(2),
        sum_wout.T,
        sum_tables[:n_rel],
        sum_tables[n_rel:],
        gain_grads[1],
        sum_gate,
        sum_up,
        sum_down.T,
    )


def solution(mesh):
    placed = (
        P(("wide", "narrow"), None),
        P(("wide", "narrow"), None),
        P(),
        P(None, "narrow"),
        P(None, "narrow"),
        P(None, "narrow"),
        P("narrow", None),
        P(None, "narrow"),
        P(None, "narrow"),
        P(),
        P(None, "narrow"),
        P(None, "narrow"),
        P("narrow", None),
        P("wide", None),
        P("wide"),
        P("wide", None),
        P("wide", None),
    )
    return jax.shard_map(
        functools.partial(on_device, mesh.shape["wide"], mesh.shape["narrow"]),
        mesh=mesh,
        in_specs=placed,
        out_specs=(
            P(("wide", "narrow"), None),
            P(("wide", "narrow"), None),
            P(("wide", "narrow")),
            P("wide", "narrow"),
            P("wide", "narrow"),
            P("wide", "narrow"),
            P("narrow", "wide"),
            P("wide", "narrow"),
            P("wide", "narrow"),
            P(("wide", "narrow")),
            P("wide", "narrow"),
            P("wide", "narrow"),
            P("narrow", "wide"),
        ),
        check_vma=False,
    )
```
